32 devices in a mesh: group: 2 (over y), fm: 4 (over z), kl: 2 (over x), pol: 2 (over core).
Axes of the slice: x: 2, y: 2, z: 4, core: 2. Of those that a mesh axis runs over, the one named last changes fastest.
Arguments:
- visibility: bfloat16 [64, 4, 96, 1024], P(('group', 'fm'), None, 'kl', 'pol'), parts along dimension 0, may hold values from -6 to 6
- beam_transfer: bfloat16 [8, 32, 1024, 1024], P(('group', 'fm'), None, 'pol', 'kl'), parts along dimension 0, may hold values from -0.1875 to 0.1875
- tile_mask: int32 [4, 8, 8], P('fm', 'pol', 'kl'), may hold values 0 or 1
- first_block: int32 [4], P('fm'), may hold values from 0 to 7, as said below
- eigen_modes: bfloat16 [8, 32, 24], P(('group', 'fm')), parts along dimension 0, may hold values from -1 to 1
- signal_noise: float32 [8, 24], P(('group', 'fm')), parts along dimension 0, may hold values from 0.1 to 10
Outputs:
- filtered: bfloat16 [64, 4, 96, 1024], P(('group', 'fm'), None, 'pol', 'kl'), parts along dimension 0
The draws below stay inside these ranges and needn't reach their ends.
There are 2 independent parts, one for each index of `group`. The reference program is written for one: setup_inputs(seed, part) draws one part's arguments, and reference() takes and returns one part's arrays. A program takes and returns all parts, laid end to end along the dimension named above; an argument that names none is the same for every part. Nothing has to cross between parts.
Inputs may be any that keep to these rules, and one draw needn't show every extreme that they name: first_block never decreases along the m-modes; the first m-mode starts at block 0 and the last at block 7.
All inputs are finite; a program needn't handle non-finite values. No bound on the sum of `tile_mask` on one device may be relied on, other than what follows from the above.
Results may differ from the reference program's by a relative error of at most 0.01.
Values may be sent and summed in bfloat16 or wider, within the bound.
No kernel may reach another device: no remote copies, remote signals or barrier semaphores. Data moves between devices by JAX's collectives and lax.ppermute only.
A program may use at most 64 MiB of HBM per device.

```python
import math
import jax
import jax.numpy as jnp
from jax import lax

F = 32
NKL = 24
ELL = 1024
TILE = 128
R = 96
BLR = 1024
M = 4
NBB = 8
NLB = 8
N_POL = 2


def draw_first_block(key, part):
    key = jax.random.fold_in(key, 11)
    raw_blocks = jax.random.randint(key, (M,), 0, NLB, dtype=jnp.int32)
    raw_blocks = raw_blocks.at[0].set(0).at[M - 1].set(NLB - 1)
    return jnp.sort(raw_blocks)


def with_ends(values, rng, least, high):
    shape = values.shape
    spot = [jax.random.randint(jax.random.fold_in(rng, axis), (), 0, shape[axis]) for axis in range(len(shape))]
    values = values.at[tuple(spot)].set(least)
    longest = shape.index(max(shape))
    spot[longest] = (spot[longest] + 1) % shape[longest]
    return values.at[tuple(spot)].set(high)


def shard_levels(stream_key, dims, pieces, low, largest):
    level, own = 1.0, jax.random.fold_in(stream_key, 6)
    for dim, shards_of in pieces:
        steps = jnp.exp(jax.random.uniform(jax.random.fold_in(own, dim), (shards_of,), jnp.float32, low / len(pieces), largest / len(pieces)))
        level = level * jnp.repeat(steps, dims[dim] // shards_of).reshape([-1 if axis == dim else 1 for axis in range(len(dims))])
    return level


def scatter_about(key, extent, deviation, most, split=(), held_as=jnp.bfloat16):
    values = deviation * jax.random.normal(key, extent, jnp.float32)
    if split:
        values = values * shard_levels(key, extent, split, -0.22, 0.18)
    return jnp.clip(values, -most, most).astype(held_as)


def setup_inputs(seed: int = 0, part: int = 0) -> dict:
    streams_of = jax.random.split(jax.random.key(seed), 7)
    part_splits = jax.random.split(jax.random.fold_in(streams_of[6], part), 7)
    visibility = scatter_about(part_splits[0], (F, M, R, BLR), 1.0, 6.0, ((0, 4), (2, 2), (3, 2)))
    beam_transfer = scatter_about(part_splits[1], (M, F, BLR, ELL), BLR ** -0.5, 0.1875, ((0, 4), (2, 2), (3, 2)))
    tile_mask = with_ends((jax.random.randint(streams_of[2], (M, NBB, NLB), 0, 4) < 3).astype(jnp.int32), jax.random.fold_in(streams_of[2], 1), 0, 1)
    first_block = draw_first_block(jax.random.fold_in(streams_of[6], 71), part)
    eigen_modes = scatter_about(part_splits[4], (M, F, NKL), F ** -0.5, 1.0, ((0, 4),))
    signal_noise = jnp.clip(jnp.exp(math.log(10.0) - 4.6051702 * jax.random.uniform(part_splits[5], (M, NKL), jnp.float32) ** shard_levels(part_splits[5], (M, NKL), ((0, 4),), -0.2, 0.2)), 0.1, 10.0)
    return dict(visibility=visibility, beam_transfer=beam_transfer, tile_mask=tile_mask, first_block=first_block, eigen_modes=eigen_modes, signal_noise=signal_noise)


def reference(visibility, beam_transfer, tile_mask, first_block, eigen_modes, signal_noise):
    block_ids = jnp.arange(NLB, dtype=jnp.int32)
    base_half = BLR // N_POL

    def per_mode(mode_index):
        mode_vis = lax.dynamic_index_in_dim(visibility, mode_index, 1, keepdims=False).astype(jnp.float32)
        mode_beam = lax.dynamic_index_in_dim(beam_transfer, mode_index, 0, keepdims=False).astype(jnp.float32)
        mode_mask = lax.dynamic_index_in_dim(tile_mask, mode_index, 0, keepdims=False)
        mode_start = lax.dynamic_index_in_dim(first_block, mode_index, 0, keepdims=False)
        keep_tiles = (mode_mask * (mode_start <= block_ids).astype(jnp.int32)[None, :]).astype(jnp.float32)
        masked_beam = (mode_beam.reshape(F, NBB, TILE, NLB, TILE) * keep_tiles[None, :, None, :, None]).reshape(F, BLR, ELL)
        sky_sum = jnp.zeros((F, R, ELL), jnp.float32)
        for half_index in range(N_POL):
            vis_half = mode_vis[:, :, half_index * base_half:(half_index + 1) * base_half]
            beam_half = masked_beam[:, half_index * base_half:(half_index + 1) * base_half, :]
            partial_value = jnp.einsum("frb,fbl->frl", vis_half, beam_half, precision=lax.Precision.HIGHEST)
            sky_sum = sky_sum + lax.optimization_barrier(partial_value.astype(jnp.bfloat16)).astype(jnp.float32)
        modes_float = lax.dynamic_index_in_dim(eigen_modes, mode_index, 0, keepdims=False).astype(jnp.float32)
        ratio_row = lax.dynamic_index_in_dim(signal_noise, mode_index, 0, keepdims=False)
        ratios = ratio_row / (1.0 + ratio_row)
        coeffs = jnp.einsum("fk,frl->krl", modes_float, sky_sum, precision=lax.Precision.HIGHEST)
        weighted = (coeffs * ratios[:, None, None]).astype(jnp.bfloat16)
        result = jnp.einsum("fk,krl->frl", modes_float, weighted.astype(jnp.float32), precision=lax.Precision.HIGHEST)
        return result.astype(jnp.bfloat16)

    stacked = lax.map(per_mode, jnp.arange(M, dtype=jnp.int32))
    return jnp.transpose(stacked, (1, 0, 2, 3))
```

```python
import functools
import jax
import jax.numpy as jnp
from jax import lax
from jax.experimental import pallas as pl
from jax.experimental.pallas import tpu as pltpu
from jax.sharding import PartitionSpec as P

TILE = 128
ROWS = 16
STEP_F = 4
VMEM_LIMIT = 40 * 1024 * 1024


def project_kernel(where, *refs, parts, freqs, rows):
    mine, others = refs[:parts], refs[parts:2 * parts]
    beam_ref, modes_ref, stay_ref, leave_ref, mask, sky, lines = refs[2 * parts:]
    piece, step = pl.program_id(0), pl.program_id(1)
    base_tiles, ell_tiles = mask.shape[0] // TILE, mask.shape[1] // TILE

    @pl.when((piece == 0) & (step == 0))
    def _():
        for b in range(base_tiles):
            for l in range(ell_tiles):
                kept = where[parts + 1 + b * ell_tiles + l].astype(jnp.float32)
                mask[b * TILE:(b + 1) * TILE, l * TILE:(l + 1) * TILE] = jnp.full(
                    (TILE, TILE), kept, jnp.float32
                ).astype(jnp.bfloat16)

    for which in range(parts):

        @pl.when(piece == which)
        def _():
            lines[:, :rows] = mine[which][pl.ds(step * STEP_F, STEP_F)]
            lines[:, rows:] = others[which][pl.ds(step * STEP_F, STEP_F)]

    for u in range(STEP_F):
        sky[piece * freqs + step * STEP_F + u] = jnp.dot(
            lines[u], beam_ref[u] * mask[...], preferred_element_type=jnp.float32
        ).astype(jnp.bfloat16)

    @pl.when((piece == parts - 1) & (step == freqs // STEP_F - 1))
    def _():
        own = where[parts]
        for ref, first in ((stay_ref, (1 - own) * rows), (leave_ref, own * rows)):
            for g in range(rows // ROWS):
                start = pl.multiple_of(first + g * ROWS, ROWS)
                block = sky[:, pl.ds(start, ROWS), :].reshape(sky.shape[0] * ROWS, sky.shape[2])
                value = jnp.dot(modes_ref[...], block, preferred_element_type=jnp.float32)
                ref[:, g * ROWS:(g + 1) * ROWS, :] = value.astype(jnp.bfloat16).reshape(
                    ref.shape[0], ROWS, ref.shape[2]
                )


def project(where, mine, others, beam, modes, n_modes):
    parts = len(mine)
    freqs, rows, base = mine[0].shape
    ell = beam.shape[2]
    whole = pl.BlockSpec((freqs, rows, base), lambda j, i, s: (0, 0, 0))
    out = jax.ShapeDtypeStruct((n_modes, rows, ell), jnp.bfloat16)
    out_spec = pl.BlockSpec((n_modes, rows, ell), lambda j, i, s: (0, 0, 0))
    steps = freqs // STEP_F
    return pl.pallas_call(
        functools.partial(project_kernel, parts=parts, freqs=freqs, rows=rows),
        grid_spec=pltpu.PrefetchScalarGridSpec(
            num_scalar_prefetch=1,
            grid=(parts, steps),
            in_specs=[whole] * (2 * parts)
            + [
                pl.BlockSpec((STEP_F, base, ell), lambda j, i, s: (s[j] * steps + i, 0, 0)),
                pl.BlockSpec(modes.shape, lambda j, i, s: (0, 0)),
            ],
            out_specs=[out_spec, out_spec],
            scratch_shapes=[
                pltpu.VMEM((base, ell), jnp.bfloat16),
                pltpu.VMEM((parts * freqs, 2 * rows, ell), jnp.bfloat16),
                pltpu.VMEM((STEP_F, 2 * rows, base), jnp.bfloat16),
            ],
        ),
        out_shape=[out, out],
        compiler_params=pltpu.CompilerParams(vmem_limit_bytes=VMEM_LIMIT),
        cost_estimate=pl.CostEstimate(
            flops=4 * parts * freqs * rows * base * ell,
            bytes_accessed=2 * beam.size + 4 * parts * mine[0].size,
            transcendentals=0,
        ),
    )(where, *mine, *others, beam, modes)


def restore_kernel(stay_ref, came_ref, ratio_ref, modes_ref, *outs):
    n_modes, rows, ell = stay_ref.shape
    freqs = outs[0].shape[0]
    for g in range(rows // ROWS):
        span = slice(g * ROWS, (g + 1) * ROWS)
        total = stay_ref[:, span, :].astype(jnp.float32) + came_ref[:, span, :].astype(jnp.float32)
        weighted = (total * ratio_ref[...]).astype(jnp.bfloat16).reshape(n_modes * ROWS, ell)
        for which, out in enumerate(outs):
            size = freqs * ROWS
            value = jnp.dot(
                modes_ref[which * size:(which + 1) * size, :], weighted, preferred_element_type=jnp.float32
            )
            out[:, span, :] = value.astype(jnp.bfloat16).reshape(freqs, ROWS, ell)


def restore(stay, came, ratios, modes, parts, freqs):
    _, rows, ell = stay.shape
    vmem = pl.BlockSpec(memory_space=pltpu.VMEM)
    return pl.pallas_call(
        restore_kernel,
        in_specs=[vmem] * 4,
        out_specs=[vmem] * parts,
        out_shape=[jax.ShapeDtypeStruct((freqs, rows, ell), jnp.bfloat16)] * parts,
        compiler_params=pltpu.CompilerParams(vmem_limit_bytes=VMEM_LIMIT),
        cost_estimate=pl.CostEstimate(
            flops=2 * modes.size * rows // ROWS * ell, bytes_accessed=4 * stay.size, transcendentals=0
        ),
    )(stay, came, ratios, modes)


def gather_kernel(where, *refs, chunks):
    pieces, out, sems = refs[:-2], refs[-2], refs[-1]
    parts = len(pieces) // len(chunks)
    copies = []
    for c, (first, rows) in enumerate(chunks):
        for j in range(parts):
            n = c * parts + j
            copies.append(
                pltpu.make_async_copy(pieces[n], out.at[:, where[j], first:first + rows, :], sems.at[n])
            )
    for copy in copies:
        copy.start()
    for copy in copies:
        copy.wait()


def gather_pieces(where, pieces, chunks, shape):
    flat = [piece for group in pieces for piece in group]
    anywhere = pl.BlockSpec(memory_space=pl.ANY)
    return pl.pallas_call(
        functools.partial(gather_kernel, chunks=chunks),
        grid_spec=pltpu.PrefetchScalarGridSpec(
            num_scalar_prefetch=1,
            grid=(),
            in_specs=[anywhere] * len(flat),
            out_specs=anywhere,
            scratch_shapes=[pltpu.SemaphoreType.DMA((len(flat),))],
        ),
        out_shape=jax.ShapeDtypeStruct(shape, jnp.bfloat16),
        cost_estimate=pl.CostEstimate(flops=0, bytes_accessed=4 * len(flat) * flat[0].size, transcendentals=0),
    )(where, *flat)


def chunked(visibility, beam_transfer, tile_mask, first_block, eigen_modes, signal_noise, chunks):
    freqs, parts, _, base = visibility.shape
    _, freq_total, _, ell = beam_transfer.shape
    n_modes = eigen_modes.shape[2]
    base_tiles, ell_tiles = base // TILE, ell // TILE
    z, x, p = lax.axis_index("fm"), lax.axis_index("kl"), lax.axis_index("pol")
    order = jnp.stack([z ^ j for j in range(parts)]).astype(jnp.int32)
    swaps = [[(i, i ^ j) for i in range(parts)] for j in range(parts)]
    other = [(0, 1), (1, 0)]

    sends = [
        [
            lax.dynamic_slice(
                visibility, (0, z ^ j, first, 0), (freqs, 1, rows, base)
            ).reshape(freqs, rows, base)
            for j in range(parts)
        ]
        for first, rows in chunks
    ]
    block_ids = x * ell_tiles + jnp.arange(ell_tiles, dtype=jnp.int32)
    keep = tile_mask[0] * (first_block[0] <= block_ids).astype(jnp.int32)[None, :]
    where = jnp.concatenate([order, (x == p).astype(jnp.int32)[None], keep.reshape(-1)])
    near = eigen_modes[0].reshape(parts, freqs, n_modes)[order].reshape(freq_total, n_modes)
    eye = jnp.eye(ROWS, dtype=jnp.bfloat16)
    down = (near.T[:, None, :, None] * eye[None, :, None, :]).reshape(n_modes * ROWS, freq_total * ROWS)
    up = (near[:, None, :, None] * eye[None, :, None, :]).reshape(freq_total * ROWS, n_modes * ROWS)
    ratio = signal_noise[0] / (1.0 + signal_noise[0])
    ratios = jnp.broadcast_to(ratio[:, None, None], (n_modes, 1, ell))
    beam = beam_transfer.reshape(freq_total, base, ell)

    returned = []
    for send in sends:
        mine = [send[0]] + [lax.ppermute(send[j], "fm", swaps[j]) for j in range(1, parts)]
        others = [lax.ppermute(piece, "kl", other) for piece in mine]
        stay, leave = project(where, mine, others, beam, down, n_modes)
        came = lax.ppermute(leave, "pol", other)
        outs = restore(stay, came, ratios, up, parts, freqs)
        returned.append([outs[0]] + [lax.ppermute(outs[j], "fm", swaps[j]) for j in range(1, parts)])
    out_rows = sum(rows for _, rows in chunks)
    return gather_pieces(order, returned, chunks, (freqs, parts, out_rows, ell))


def plain(visibility, beam_transfer, tile_mask, first_block, eigen_modes, signal_noise):
    owned_modes, freq_total, base_half, ell_local = beam_transfer.shape
    base_tiles, ell_tiles = base_half // TILE, ell_local // TILE
    block_ids = lax.axis_index("kl") * ell_tiles + jnp.arange(ell_tiles, dtype=jnp.int32)
    inside = (first_block[:, None] <= block_ids[None, :]).astype(jnp.int32)
    keep_tiles = tile_mask * inside[:, None, :]
    shaped = beam_transfer.reshape(owned_modes, freq_total, base_tiles, TILE, ell_tiles, TILE)
    masked_beam = shaped * keep_tiles.astype(jnp.bfloat16)[:, None, :, None, :, None]
    masked_beam = masked_beam.reshape(owned_modes, freq_total, base_half, ell_local)
    arrived = lax.all_to_all(visibility, "fm", split_axis=1, concat_axis=0, tiled=True)
    partial_value = jnp.einsum(
        "fmrb,mfbl->fmrl",
        lax.all_gather(arrived, "kl", axis=2, tiled=True),
        masked_beam,
        preferred_element_type=jnp.float32,
    )
    sky_sum = lax.psum_scatter(
        partial_value.astype(jnp.bfloat16), "pol", scatter_dimension=2, tiled=True
    ).astype(jnp.float32)
    modes_float = eigen_modes.astype(jnp.float32)
    coeffs = jnp.einsum("mfk,fmrl->mkrl", modes_float, sky_sum, precision=lax.Precision.HIGHEST)
    ratios = signal_noise / (1.0 + signal_noise)
    weighted = (coeffs * ratios[:, :, None, None]).astype(jnp.bfloat16)
    filtered = jnp.einsum(
        "mfk,mkrl->fmrl", eigen_modes, weighted, preferred_element_type=jnp.float32
    ).astype(jnp.bfloat16)
    return lax.all_to_all(filtered, "fm", split_axis=0, concat_axis=1, tiled=True)


def per_device(*args, sizes):
    visibility, beam_transfer = args[0], args[1]
    freqs, modes, rows, _ = visibility.shape
    fits = (
        sizes["kl"] == 2
        and sizes["pol"] == 2
        and modes == sizes["fm"]
        and modes & (modes - 1) == 0
        and beam_transfer.shape[0] == 1
        and rows % ROWS == 0
        and freqs % STEP_F == 0
    )
    if not fits:
        return plain(*args)
    chunks = [(first, ROWS) for first in range(0, rows, ROWS)]
    return chunked(*args, chunks=chunks)


def solution(mesh):
    placed = (
        P(("group", "fm"), None, "kl", "pol"),
        P(("group", "fm"), None, "pol", "kl"),
        P("fm", "pol", "kl"),
        P("fm"),
        P(("group", "fm"), None, None),
        P(("group", "fm"), None),
    )
    return jax.shard_map(
        functools.partial(per_device, sizes=dict(mesh.shape)),
        mesh=mesh,
        in_specs=placed,
        out_specs=P(("group", "fm"), None, "pol", "kl"),
        check_vma=False,
    )
```

```python
import functools
import jax
import jax.numpy as jnp
from jax import lax
from jax.experimental import pallas as pl
from jax.experimental.pallas import tpu as pltpu
from jax.sharding import PartitionSpec as P

TILE = 128
WIDE = 256
ROWS = 16
STEP_F = 4
VMEM_LIMIT = 40 * 1024 * 1024


def after(value, *earlier):
    return lax.optimization_barrier((value, earlier))[0]


def spread_kernel(modes_ref, down_ref, up_ref):
    freq, n_modes = modes_ref.shape
    modes = modes_ref[...]

    def pick(shape, axis):
        big = lax.broadcasted_iota(jnp.int32, shape, axis) // ROWS
        small = lax.broadcasted_iota(jnp.int32, shape, 1 - axis)
        return jnp.where(big == small, 1.0, 0.0).astype(jnp.bfloat16)

    def lane(shape):
        rows = lax.broadcasted_iota(jnp.int32, shape, 0) % ROWS
        columns = lax.broadcasted_iota(jnp.int32, shape, 1) % ROWS
        return rows == columns

    def dot(a, b, dims):
        return lax.dot_general(a, b, (dims, ((), ())), preferred_element_type=jnp.float32)

    tall = dot(pick((n_modes * ROWS, n_modes), 0), modes, ((1,), (1,))).astype(jnp.bfloat16)
    value = dot(tall, pick((freq, freq * ROWS), 1), ((1,), (0,)))
    down_ref[...] = jnp.where(lane(value.shape), value, 0.0).astype(jnp.bfloat16)
    tall = dot(pick((freq * ROWS, freq), 0), modes, ((1,), (0,))).astype(jnp.bfloat16)
    value = dot(tall, pick((n_modes, n_modes * ROWS), 1), ((1,), (0,)))
    up_ref[...] = jnp.where(lane(value.shape), value, 0.0).astype(jnp.bfloat16)


def spread(modes):
    freq, n_modes = modes.shape
    vmem = pl.BlockSpec(memory_space=pltpu.VMEM)
    return pl.pallas_call(
        spread_kernel,
        in_specs=[vmem],
        out_specs=[vmem, vmem],
        out_shape=[
            jax.ShapeDtypeStruct((n_modes * ROWS, freq * ROWS), jnp.bfloat16),
            jax.ShapeDtypeStruct((freq * ROWS, n_modes * ROWS), jnp.bfloat16),
        ],
        compiler_params=pltpu.CompilerParams(vmem_limit_bytes=VMEM_LIMIT),
        cost_estimate=pl.CostEstimate(
            flops=2 * 256 * n_modes * freq * freq, bytes_accessed=4 * 256 * n_modes * freq, transcendentals=0
        ),
    )(modes)


def project_kernel(where, *refs, parts, freqs, rows):
    mine, others = refs[:parts], refs[parts:2 * parts]
    beam_ref, modes_ref, stay_ref, leave_ref, mask, sky, lines = refs[2 * parts:]
    piece, step = pl.program_id(0), pl.program_id(1)
    ell_tiles, _, base = mask.shape
    base_tiles, both = base // TILE, 2 * rows

    @pl.when((piece == 0) & (step == 0))
    def _():
        for b in range(base_tiles):
            for l in range(ell_tiles):
                kept = where[parts + 1 + b * ell_tiles + l].astype(jnp.float32)
                mask[l, :, b * TILE:(b + 1) * TILE] = jnp.full((ROWS, TILE), kept, jnp.float32).astype(jnp.bfloat16)

    for which in range(parts):

        @pl.when(piece == which)
        def _():
            for u in range(STEP_F):
                for start in range(0, both, ROWS):
                    from_ref, row = (mine[which], start) if start < rows else (others[which], start - rows)
                    value = from_ref[u, row:row + ROWS, :]
                    for l in range(ell_tiles):
                        lines[u, l, start:start + ROWS, :] = value * mask[l]

    first = where[piece] * freqs + step * STEP_F
    per = WIDE // TILE
    for u in range(STEP_F):
        for n in range(ell_tiles // per):
            value = jnp.dot(
                lines[u, n * per:(n + 1) * per].reshape(per * both, base),
                beam_ref[u, :, n * WIDE:(n + 1) * WIDE],
                preferred_element_type=jnp.float32,
            )
            for k in range(per):
                at = n * WIDE + k * TILE
                sky[first + u, :, at:at + TILE] = value[
                    k * both:(k + 1) * both, k * TILE:(k + 1) * TILE
                ].astype(jnp.bfloat16)

    @pl.when((piece == parts - 1) & (step == freqs // STEP_F - 1))
    def _():
        own = where[parts]
        for ref, low in ((stay_ref, (1 - own) * rows), (leave_ref, own * rows)):
            for g in range(rows // ROWS):
                start = pl.multiple_of(low + g * ROWS, ROWS)
                block = sky[:, pl.ds(start, ROWS), :].reshape(sky.shape[0] * ROWS, sky.shape[2])
                value = jnp.dot(modes_ref[...], block, preferred_element_type=jnp.float32)
                ref[:, g * ROWS:(g + 1) * ROWS, :] = value.astype(jnp.bfloat16).reshape(
                    ref.shape[0], ROWS, ref.shape[2]
                )


def project(where, mine, others, beam, modes, n_modes):
    parts = len(mine)
    freqs, rows, base = mine[0].shape
    ell = beam.shape[2]
    steps = freqs // STEP_F

    def block_of(which):
        def index(j, i, s):
            return (jnp.where(j == which, i, jnp.where(j < which, 0, steps - 1)), 0, 0)

        return pl.BlockSpec((STEP_F, rows, base), index)

    out = jax.ShapeDtypeStruct((n_modes, rows, ell), jnp.bfloat16)
    out_spec = pl.BlockSpec((n_modes, rows, ell), lambda j, i, s: (0, 0, 0))
    return pl.pallas_call(
        functools.partial(project_kernel, parts=parts, freqs=freqs, rows=rows),
        grid_spec=pltpu.PrefetchScalarGridSpec(
            num_scalar_prefetch=1,
            grid=(parts, steps),
            in_specs=[block_of(j) for j in range(parts)] * 2
            + [
                pl.BlockSpec((STEP_F, base, ell), lambda j, i, s: (s[j] * steps + i, 0, 0)),
                pl.BlockSpec(modes.shape, lambda j, i, s: (0, 0)),
            ],
            out_specs=[out_spec, out_spec],
            scratch_shapes=[
                pltpu.VMEM((ell // TILE, ROWS, base), jnp.bfloat16),
                pltpu.VMEM((parts * freqs, 2 * rows, ell), jnp.bfloat16),
                pltpu.VMEM((STEP_F, ell // TILE, 2 * rows, base), jnp.bfloat16),
            ],
        ),
        out_shape=[out, out],
        compiler_params=pltpu.CompilerParams(vmem_limit_bytes=VMEM_LIMIT),
        cost_estimate=pl.CostEstimate(
            flops=4 * parts * freqs * rows * base * ell,
            bytes_accessed=2 * beam.size + 4 * parts * mine[0].size,
            transcendentals=0,
        ),
    )(where, *mine, *others, beam, modes)


def restore_kernel(where, stay_ref, came_ref, ratio_ref, modes_ref, *outs):
    n_modes, rows, ell = stay_ref.shape
    size = outs[0].shape[0] * ROWS
    for g in range(rows // ROWS):
        span = slice(g * ROWS, (g + 1) * ROWS)
        total = stay_ref[:, span, :].astype(jnp.float32) + came_ref[:, span, :].astype(jnp.float32)
        weighted = (total * ratio_ref[...]).astype(jnp.bfloat16).reshape(n_modes * ROWS, ell)
        for which, out in enumerate(outs):
            start = pl.multiple_of(where[which] * size, size)
            value = jnp.dot(modes_ref[pl.ds(start, size), :], weighted, preferred_element_type=jnp.float32)
            out[:, span, :] = value.astype(jnp.bfloat16).reshape(out.shape[0], ROWS, ell)


def restore(where, stay, came, ratios, modes, parts, freqs):
    _, rows, ell = stay.shape
    vmem = pl.BlockSpec(memory_space=pltpu.VMEM)
    return pl.pallas_call(
        restore_kernel,
        grid_spec=pltpu.PrefetchScalarGridSpec(
            num_scalar_prefetch=1, grid=(), in_specs=[vmem] * 4, out_specs=[vmem] * parts
        ),
        out_shape=[jax.ShapeDtypeStruct((freqs, rows, ell), jnp.bfloat16)] * parts,
        compiler_params=pltpu.CompilerParams(vmem_limit_bytes=VMEM_LIMIT),
        cost_estimate=pl.CostEstimate(
            flops=2 * modes.size * rows // ROWS * ell, bytes_accessed=8 * stay.size, transcendentals=0
        ),
    )(where, stay, came, ratios, modes)


def place_kernel(where, *refs, parts):
    pieces, out = refs[:parts], refs[-1]
    for which in range(parts):

        @pl.when(pl.program_id(0) == which)
        def _():
            out[:, 0] = pieces[which][...]


def place(where, pieces, first, shape, into=None):
    parts = len(pieces)
    freqs, rows, ell = pieces[0].shape

    def block_of(which):
        def index(j, g, s):
            return (0, jnp.where(j == which, g, jnp.where(j < which, 0, rows // ROWS - 1)), 0)

        return pl.BlockSpec((freqs, ROWS, ell), index)

    extra = [] if into is None else [into]
    return pl.pallas_call(
        functools.partial(place_kernel, parts=parts),
        grid_spec=pltpu.PrefetchScalarGridSpec(
            num_scalar_prefetch=1,
            grid=(parts, rows // ROWS),
            in_specs=[block_of(j) for j in range(parts)] + [pl.BlockSpec(memory_space=pl.ANY)] * len(extra),
            out_specs=pl.BlockSpec((freqs, 1, ROWS, ell), lambda j, g, s: (0, s[j], first // ROWS + g, 0)),
        ),
        out_shape=jax.ShapeDtypeStruct(shape, jnp.bfloat16),
        input_output_aliases={parts + 1: 0} if extra else {},
        compiler_params=pltpu.CompilerParams(vmem_limit_bytes=VMEM_LIMIT),
        cost_estimate=pl.CostEstimate(flops=0, bytes_accessed=4 * parts * pieces[0].size, transcendentals=0),
    )(where, *pieces, *extra)


def chunked(visibility, beam_transfer, tile_mask, first_block, eigen_modes, signal_noise, chunks):
    freqs, parts, rows_all, base = visibility.shape
    _, freq_total, _, ell = beam_transfer.shape
    n_modes = eigen_modes.shape[2]
    ell_tiles = ell // TILE
    z, x, p = lax.axis_index("fm"), lax.axis_index("kl"), lax.axis_index("pol")
    other = [(0, 1), (1, 0)]

    def along_z(value, j):
        return lax.ppermute(value, "fm", [(i, i ^ j) for i in range(parts)])

    def along_x(value):
        return lax.ppermute(value, "kl", other)

    def cut(chunk, j):
        first, rows = chunk
        return lax.dynamic_slice(visibility, (0, z ^ j, first, 0), (freqs, 1, rows, base)).reshape(freqs, rows, base)

    order = jnp.stack([z ^ j for j in range(parts)]).astype(jnp.int32)
    block_ids = x * ell_tiles + jnp.arange(ell_tiles, dtype=jnp.int32)
    keep = tile_mask[0] * (first_block[0] <= block_ids).astype(jnp.int32)[None, :]
    where = jnp.concatenate([order, (x == p).astype(jnp.int32)[None], keep.reshape(-1)])
    down, up = spread(eigen_modes[0])
    ratio = signal_noise[0] / (1.0 + signal_noise[0])
    ratios = jnp.broadcast_to(ratio[:, None, None], (n_modes, 1, ell))
    beam = beam_transfer.reshape(freq_total, base, ell)
    shape = (freqs, parts, rows_all, ell)

    def filter_rows(mine, others):
        stay, leave = project(where, mine, others, beam, down, n_modes)
        came = lax.ppermute(leave, "pol", other)
        return leave, restore(where, stay, came, ratios, up, parts, freqs)

    a, b = [[cut(chunk, j) for j in range(parts)] for chunk in chunks]
    got_a, got_b = [a[0]] + [None] * 3, [b[0]] + [None] * 3
    side_a, side_b = [None] * 4, [None] * 4
    for j in (2, 3, 1):
        got_a[j] = along_z(a[j], j)
    got_b[2] = along_z(b[2], 2)
    side_a[0] = along_x(a[0])
    got_b[1] = along_z(after(b[1], got_a[1]), 1)
    side_b[0] = along_x(after(b[0], side_a[0]))
    side_a[1] = along_x(after(got_a[1], side_a[0]))
    got_b[3] = along_z(after(b[3], got_a[2]), 3)
    side_a[2] = along_x(after(got_a[2], side_b[0]))
    side_a[3] = along_x(after(got_a[3], side_a[1]))
    side_b[1] = along_x(after(got_b[1], side_a[2]))
    side_b[2] = along_x(after(got_b[2], side_a[3]))
    leave_a, outs_a = filter_rows(got_a, side_a)
    side_b[3] = along_x(after(got_b[3], outs_a[0]))
    back_a = [outs_a[0]] + [along_z(after(outs_a[j], got_b[3]), j) for j in range(1, parts)]
    leave_b, outs_b = filter_rows(got_b, side_b)
    back_b = [outs_b[0]] + [along_z(outs_b[j], j) for j in range(1, parts)]
    result = place(where, back_a, chunks[0][0], shape)
    return place(where, back_b, chunks[1][0], shape, into=result)


def plain(visibility, beam_transfer, tile_mask, first_block, eigen_modes, signal_noise):
    owned_modes, freq_total, base_half, ell_local = beam_transfer.shape
    base_tiles, ell_tiles = base_half // TILE, ell_local // TILE
    block_ids = lax.axis_index("kl") * ell_tiles + jnp.arange(ell_tiles, dtype=jnp.int32)
    inside = (first_block[:, None] <= block_ids[None, :]).astype(jnp.int32)
    keep_tiles = tile_mask * inside[:, None, :]
    shaped = beam_transfer.reshape(owned_modes, freq_total, base_tiles, TILE, ell_tiles, TILE)
    masked_beam = shaped * keep_tiles.astype(jnp.bfloat16)[:, None, :, None, :, None]
    masked_beam = masked_beam.reshape(owned_modes, freq_total, base_half, ell_local)
    arrived = lax.all_to_all(visibility, "fm", split_axis=1, concat_axis=0, tiled=True)
    partial_value = jnp.einsum(
        "fmrb,mfbl->fmrl",
        lax.all_gather(arrived, "kl", axis=2, tiled=True),
        masked_beam,
        preferred_element_type=jnp.float32,
    )
    sky_sum = lax.psum_scatter(
        partial_value.astype(jnp.bfloat16), "pol", scatter_dimension=2, tiled=True
    ).astype(jnp.float32)
    modes_float = eigen_modes.astype(jnp.float32)
    coeffs = jnp.einsum("mfk,fmrl->mkrl", modes_float, sky_sum, precision=lax.Precision.HIGHEST)
    ratios = signal_noise / (1.0 + signal_noise)
    weighted = (coeffs * ratios[:, :, None, None]).astype(jnp.bfloat16)
    filtered = jnp.einsum(
        "mfk,mkrl->fmrl", eigen_modes, weighted, preferred_element_type=jnp.float32
    ).astype(jnp.bfloat16)
    return lax.all_to_all(filtered, "fm", split_axis=0, concat_axis=1, tiled=True)


def per_device(*args, sizes):
    visibility, beam_transfer = args[0], args[1]
    freqs, modes, rows, _ = visibility.shape
    fits = (
        sizes["kl"] == 2
        and sizes["pol"] == 2
        and modes == sizes["fm"] == 4
        and beam_transfer.shape[0] == 1
        and rows % ROWS == 0
        and rows >= 2 * ROWS
        and freqs % STEP_F == 0
        and beam_transfer.shape[3] % WIDE == 0
    )
    if not fits:
        return plain(*args)
    return chunked(*args, chunks=[(0, ROWS), (ROWS, rows - ROWS)])


def solution(mesh):
    placed = (
        P(("group", "fm"), None, "kl", "pol"),
        P(("group", "fm"), None, "pol", "kl"),
        P("fm", "pol", "kl"),
        P("fm"),
        P(("group", "fm"), None, None),
        P(("group", "fm"), None),
    )
    return jax.shard_map(
        functools.partial(per_device, sizes=dict(mesh.shape)),
        mesh=mesh,
        in_specs=placed,
        out_specs=P(("group", "fm"), None, "pol", "kl"),
        check_vma=False,
    )
```

```python
import functools
import jax
import jax.numpy as jnp
from jax import lax
from jax.experimental import pallas as pl
from jax.experimental.pallas import tpu as pltpu
from jax.sharding import PartitionSpec as P

TILE = 128
PARTS = 4
WIDE = 256
ROWS = 16
STEP_F = 4
VMEM_LIMIT = 40 * 1024 * 1024


def spread_kernel(where, modes_ref, down_ref, up_ref, *, parts):
    freq, n_modes = modes_ref.shape
    modes = modes_ref[...]
    freqs = freq // parts

    def pick(shape, axis):
        big = lax.broadcasted_iota(jnp.int32, shape, axis) // ROWS
        small = lax.broadcasted_iota(jnp.int32, shape, 1 - axis)
        if freq in shape:
            piece, within = big // freqs, big % freqs
            big = within
            for j in range(parts):
                big = jnp.where(piece == j, where[j] * freqs + within, big)
        return jnp.where(big == small, 1.0, 0.0).astype(jnp.bfloat16)

    def lane(shape):
        rows = lax.broadcasted_iota(jnp.int32, shape, 0) % ROWS
        columns = lax.broadcasted_iota(jnp.int32, shape, 1) % ROWS
        return rows == columns

    def dot(a, b, dims):
        return lax.dot_general(a, b, (dims, ((), ())), preferred_element_type=jnp.float32)

    tall = dot(pick((n_modes * ROWS, n_modes), 0), modes, ((1,), (1,))).astype(jnp.bfloat16)
    value = dot(tall, pick((freq, freq * ROWS), 1), ((1,), (0,)))
    down_ref[...] = jnp.where(lane(value.shape), value, 0.0).astype(jnp.bfloat16)
    tall = dot(pick((freq * ROWS, freq), 0), modes, ((1,), (0,))).astype(jnp.bfloat16)
    value = dot(tall, pick((n_modes, n_modes * ROWS), 1), ((1,), (0,)))
    up_ref[...] = jnp.where(lane(value.shape), value, 0.0).astype(jnp.bfloat16)


def spread(where, modes, parts):
    freq, n_modes = modes.shape
    vmem = pl.BlockSpec(memory_space=pltpu.VMEM)
    return pl.pallas_call(
        functools.partial(spread_kernel, parts=parts),
        grid_spec=pltpu.PrefetchScalarGridSpec(
            num_scalar_prefetch=1, grid=(), in_specs=[vmem], out_specs=[vmem, vmem]
        ),
        out_shape=[
            jax.ShapeDtypeStruct((n_modes * ROWS, freq * ROWS), jnp.bfloat16),
            jax.ShapeDtypeStruct((freq * ROWS, n_modes * ROWS), jnp.bfloat16),
        ],
        compiler_params=pltpu.CompilerParams(vmem_limit_bytes=VMEM_LIMIT),
        cost_estimate=pl.CostEstimate(flops=1024, bytes_accessed=1024, transcendentals=0),
    )(where, modes)


def project_kernel(where, *refs, pieces, before, last, freqs, rows, step_f):
    count = len(pieces)
    mine, others, refs = refs[:count], refs[count:2 * count], refs[2 * count:]
    beam_ref, refs = refs[0], refs[1:]
    earlier, refs = (refs[0], refs[1:]) if before else (None, refs)
    if last:
        modes_ref, stay_ref, leave_ref, sky, mask, lines = refs
    else:
        sky, mask, lines = refs
    piece, step = pl.program_id(0), pl.program_id(1)
    ell_tiles, _, base = mask.shape
    base_tiles, both = base // TILE, 2 * rows

    @pl.when((piece == 0) & (step == 0))
    def _():
        for b in range(base_tiles):
            for l in range(ell_tiles):
                kept = where[PARTS + 1 + b * ell_tiles + l].astype(jnp.float32)
                mask[l, :, b * TILE:(b + 1) * TILE] = jnp.full((ROWS, TILE), kept, jnp.float32).astype(jnp.bfloat16)

    for which in range(count):

        @pl.when(piece == which)
        def _():
            for u in range(step_f):
                for start in range(0, both, ROWS):
                    from_ref, row = (mine[which], start) if start < rows else (others[which], start - rows)
                    value = from_ref[u, row:row + ROWS, :]
                    for l in range(ell_tiles):
                        lines[u, l, start:start + ROWS, :] = value * mask[l]

    first = piece * freqs + step * step_f
    per = WIDE // TILE
    for u in range(step_f):
        for n in range(ell_tiles // per):
            value = jnp.dot(
                lines[u, n * per:(n + 1) * per].reshape(per * both, base),
                beam_ref[u, :, n * WIDE:(n + 1) * WIDE],
                preferred_element_type=jnp.float32,
            )
            for k in range(per):
                at = n * WIDE + k * TILE
                sky[first + u, :, at:at + TILE] = value[
                    k * both:(k + 1) * both, k * TILE:(k + 1) * TILE
                ].astype(jnp.bfloat16)

    if not last:
        return

    @pl.when((piece == count - 1) & (step == freqs // step_f - 1))
    def _():
        own = where[PARTS]
        split = before * ROWS
        for ref, low in ((stay_ref, (1 - own) * rows), (leave_ref, own * rows)):
            for g in range(rows // ROWS):
                start = pl.multiple_of(low + g * ROWS, ROWS)
                value = jnp.zeros((modes_ref.shape[0], sky.shape[2]), jnp.float32)
                for part, low_f, high_f in ((earlier, 0, split), (sky, split, modes_ref.shape[1])):
                    if part is not None:
                        value += jnp.dot(
                            modes_ref[:, low_f:high_f],
                            part[:, pl.ds(start, ROWS), :].reshape(high_f - low_f, sky.shape[2]),
                            preferred_element_type=jnp.float32,
                        )
                ref[:, g * ROWS:(g + 1) * ROWS, :] = value.astype(jnp.bfloat16).reshape(
                    ref.shape[0], ROWS, ref.shape[2]
                )


def project(where, mine, others, beam, pieces, n_modes, earlier=None, modes=None):
    freqs, rows, base = mine[0].shape
    ell = beam.shape[2]
    step_f = STEP_F if len(pieces) > 1 else STEP_F // 2
    steps = freqs // step_f
    base_piece, last = pieces[0], modes is not None

    def block_of(which):
        def index(j, i, s):
            return (jnp.where(j == which, i, jnp.where(j < which, 0, steps - 1)), 0, 0)

        return pl.BlockSpec((step_f, rows, base), index)

    def whole(shape):
        return pl.BlockSpec(shape, lambda j, i, s: (0,) * len(shape))

    in_specs = [block_of(j) for j in range(len(pieces))] * 2
    in_specs += [pl.BlockSpec((step_f, base, ell), lambda j, i, s: (s[base_piece + j] * steps + i, 0, 0))]
    operands = [*mine, *others, beam]
    sky = (len(pieces) * freqs, 2 * rows, ell)
    scratch = [
        pltpu.VMEM((ell // TILE, ROWS, base), jnp.bfloat16),
        pltpu.VMEM((step_f, ell // TILE, 2 * rows, base), jnp.bfloat16),
    ]
    before = 0 if earlier is None else earlier.shape[0]
    if before:
        in_specs, operands = in_specs + [whole(earlier.shape)], operands + [earlier]
    if last:
        in_specs, operands = in_specs + [whole(modes.shape)], operands + [modes]
        scratch = [pltpu.VMEM(sky, jnp.bfloat16)] + scratch
        shapes = [(n_modes, rows, ell)] * 2
    else:
        shapes = [sky]
    return pl.pallas_call(
        functools.partial(
            project_kernel, pieces=pieces, before=before, last=last, freqs=freqs, rows=rows, step_f=step_f
        ),
        grid_spec=pltpu.PrefetchScalarGridSpec(
            num_scalar_prefetch=1,
            grid=(len(pieces), steps),
            in_specs=in_specs,
            out_specs=[whole(shape) for shape in shapes],
            scratch_shapes=scratch,
        ),
        out_shape=[jax.ShapeDtypeStruct(shape, jnp.bfloat16) for shape in shapes],
        compiler_params=pltpu.CompilerParams(vmem_limit_bytes=VMEM_LIMIT),
        cost_estimate=pl.CostEstimate(flops=1024, bytes_accessed=1024, transcendentals=0),
    )(where, *operands)


def restore_kernel(stay_ref, came_ref, ratio_ref, modes_ref, *outs):
    n_modes, rows, ell = stay_ref.shape
    size = outs[0].shape[0] * ROWS
    for g in range(rows // ROWS):
        span = slice(g * ROWS, (g + 1) * ROWS)
        total = stay_ref[:, span, :].astype(jnp.float32) + came_ref[:, span, :].astype(jnp.float32)
        weighted = (total * ratio_ref[...]).astype(jnp.bfloat16).reshape(n_modes * ROWS, ell)
        for which, out in enumerate(outs):
            value = jnp.dot(
                modes_ref[which * size:(which + 1) * size, :], weighted, preferred_element_type=jnp.float32
            )
            out[:, span, :] = value.astype(jnp.bfloat16).reshape(out.shape[0], ROWS, ell)


def restore(stay, came, ratios, modes, parts, freqs):
    _, rows, ell = stay.shape
    vmem = pl.BlockSpec(memory_space=pltpu.VMEM)
    return pl.pallas_call(
        restore_kernel,
        in_specs=[vmem] * 4,
        out_specs=[vmem] * parts,
        out_shape=[jax.ShapeDtypeStruct((freqs, rows, ell), jnp.bfloat16)] * parts,
        compiler_params=pltpu.CompilerParams(vmem_limit_bytes=VMEM_LIMIT),
        cost_estimate=pl.CostEstimate(flops=1024, bytes_accessed=1024, transcendentals=0),
    )(stay, came, ratios, modes)


def place_kernel(where, *refs, first):
    pieces, out, sems = refs[:PARTS], refs[-2], refs[-1]
    rows = pieces[0].shape[1]
    copies = [
        pltpu.make_async_copy(pieces[j], out.at[:, where[j], first:first + rows, :], sems.at[j])
        for j in range(PARTS)
    ]
    for copy in copies:
        copy.start()
    for copy in copies:
        copy.wait()


def place(where, pieces, first, shape, into=None):
    extra = [] if into is None else [into]
    anywhere = pl.BlockSpec(memory_space=pl.ANY)
    return pl.pallas_call(
        functools.partial(place_kernel, first=first),
        grid_spec=pltpu.PrefetchScalarGridSpec(
            num_scalar_prefetch=1,
            grid=(),
            in_specs=[pl.BlockSpec(memory_space=pltpu.VMEM)] * PARTS + [anywhere] * len(extra),
            out_specs=anywhere,
            scratch_shapes=[pltpu.SemaphoreType.DMA((PARTS,))],
        ),
        out_shape=jax.ShapeDtypeStruct(shape, jnp.bfloat16),
        input_output_aliases={PARTS + 1: 0} if extra else {},
        compiler_params=pltpu.CompilerParams(vmem_limit_bytes=VMEM_LIMIT),
        cost_estimate=pl.CostEstimate(flops=1024, bytes_accessed=1024, transcendentals=0),
    )(where, *pieces, *extra)


def chunked(visibility, beam_transfer, tile_mask, first_block, eigen_modes, signal_noise, chunks):
    freqs, parts, rows_all, base = visibility.shape
    _, freq_total, _, ell = beam_transfer.shape
    n_modes = eigen_modes.shape[2]
    ell_tiles = ell // TILE
    z, x, p = lax.axis_index("fm"), lax.axis_index("kl"), lax.axis_index("pol")
    other = [(0, 1), (1, 0)]

    def along_z(value, j):
        return lax.ppermute(value, "fm", [(i, i ^ j) for i in range(parts)])

    def along_x(value):
        return lax.ppermute(value, "kl", other)

    def cut(chunk, j):
        first, rows = chunk
        return lax.dynamic_slice(visibility, (0, z ^ j, first, 0), (freqs, 1, rows, base)).reshape(freqs, rows, base)

    order = jnp.stack([z ^ j for j in range(parts)]).astype(jnp.int32)
    block_ids = x * ell_tiles + jnp.arange(ell_tiles, dtype=jnp.int32)
    keep = tile_mask[0] * (first_block[0] <= block_ids).astype(jnp.int32)[None, :]
    where = jnp.concatenate([order, (x == p).astype(jnp.int32)[None], keep.reshape(-1)])
    down, up = spread(where, eigen_modes[0], parts)
    ratio = signal_noise[0] / (1.0 + signal_noise[0])
    ratios = jnp.broadcast_to(ratio[:, None, None], (n_modes, 1, ell))
    beam = beam_transfer.reshape(freq_total, base, ell)
    shape = (freqs, parts, rows_all, ell)

    a, b = [[cut(chunk, j) for j in range(parts)] for chunk in chunks]

    def half(mine, others, pieces, earlier=None, modes=None):
        return project(
            where, [mine[j] for j in pieces], [others[j] for j in pieces], beam, pieces, n_modes, earlier, modes
        )

    ga, gb, xa, xb, ba, bb = ({} for _ in range(6))
    ga[0], gb[0] = a[0], b[0]
    for j in (2, 3, 1):
        ga[j] = along_z(a[j], j)
    xa[0], xa[1], xb[0] = along_x(ga[0]), along_x(ga[1]), along_x(gb[0])
    ga, gb, xa, xb, b, where, beam, down, up = lax.optimization_barrier((ga, gb, xa, xb, b, where, beam, down, up))
    gb[2], gb[1] = along_z(b[2], 2), along_z(b[1], 1)
    xa[2], xa[3] = along_x(ga[2]), along_x(ga[3])
    xb[1] = along_x(gb[1])
    sky_a, = half(ga, xa, (0, 1))
    stay_a, leave_a = half(ga, xa, (2, 3), sky_a, down)
    gb, xb, b, stay_a, leave_a = lax.optimization_barrier((gb, xb, b, stay_a, leave_a))
    gb[3] = along_z(b[3], 3)
    xb[2] = along_x(gb[2])
    outs_a = restore(stay_a, lax.ppermute(leave_a, "pol", other), ratios, up, parts, freqs)
    sky_b, = half(gb, xb, (0, 1))
    gb, xb, outs_a, sky_b = lax.optimization_barrier((gb, xb, outs_a, sky_b))
    xb[3] = along_x(gb[3])
    ba = [outs_a[0]] + [along_z(outs_a[j], j) for j in range(1, parts)]
    stay_b, leave_b = half(gb, xb, (2, 3), sky_b, down)
    ba, stay_b, leave_b = lax.optimization_barrier((ba, stay_b, leave_b))
    outs_b = restore(stay_b, lax.ppermute(leave_b, "pol", other), ratios, up, parts, freqs)
    bb = [outs_b[0]] + [along_z(outs_b[j], j) for j in range(1, parts)]
    result = place(where, ba, chunks[0][0], shape)
    return place(where, bb, chunks[1][0], shape, into=result)


def plain(visibility, beam_transfer, tile_mask, first_block, eigen_modes, signal_noise):
    owned_modes, freq_total, base_half, ell_local = beam_transfer.shape
    base_tiles, ell_tiles = base_half // TILE, ell_local // TILE
    block_ids = lax.axis_index("kl") * ell_tiles + jnp.arange(ell_tiles, dtype=jnp.int32)
    inside = (first_block[:, None] <= block_ids[None, :]).astype(jnp.int32)
    keep_tiles = tile_mask * inside[:, None, :]
    shaped = beam_transfer.reshape(owned_modes, freq_total, base_tiles, TILE, ell_tiles, TILE)
    masked_beam = shaped * keep_tiles.astype(jnp.bfloat16)[:, None, :, None, :, None]
    masked_beam = masked_beam.reshape(owned_modes, freq_total, base_half, ell_local)
    arrived = lax.all_to_all(visibility, "fm", split_axis=1, concat_axis=0, tiled=True)
    partial_value = jnp.einsum(
        "fmrb,mfbl->fmrl",
        lax.all_gather(arrived, "kl", axis=2, tiled=True),
        masked_beam,
        preferred_element_type=jnp.float32,
    )
    sky_sum = lax.psum_scatter(
        partial_value.astype(jnp.bfloat16), "pol", scatter_dimension=2, tiled=True
    ).astype(jnp.float32)
    modes_float = eigen_modes.astype(jnp.float32)
    coeffs = jnp.einsum("mfk,fmrl->mkrl", modes_float, sky_sum, precision=lax.Precision.HIGHEST)
    ratios = signal_noise / (1.0 + signal_noise)
    weighted = (coeffs * ratios[:, :, None, None]).astype(jnp.bfloat16)
    filtered = jnp.einsum(
        "mfk,mkrl->fmrl", eigen_modes, weighted, preferred_element_type=jnp.float32
    ).astype(jnp.bfloat16)
    return lax.all_to_all(filtered, "fm", split_axis=0, concat_axis=1, tiled=True)


def per_device(*args, sizes):
    visibility, beam_transfer = args[0], args[1]
    freqs, modes, rows, _ = visibility.shape
    fits = (
        sizes["kl"] == 2
        and sizes["pol"] == 2
        and modes == sizes["fm"] == PARTS
        and beam_transfer.shape[0] == 1
        and rows % ROWS == 0
        and rows >= 2 * ROWS
        and freqs % STEP_F == 0
        and beam_transfer.shape[3] % WIDE == 0
    )
    if not fits:
        return plain(*args)
    return chunked(*args, chunks=[(0, ROWS), (ROWS, rows - ROWS)])


def solution(mesh):
    placed = (
        P(("group", "fm"), None, "kl", "pol"),
        P(("group", "fm"), None, "pol", "kl"),
        P("fm", "pol", "kl"),
        P("fm"),
        P(("group", "fm"), None, None),
        P(("group", "fm"), None),
    )
    return jax.shard_map(
        functools.partial(per_device, sizes=dict(mesh.shape)),
        mesh=mesh,
        in_specs=placed,
        out_specs=P(("group", "fm"), None, "pol", "kl"),
        check_vma=False,
    )
```

```python
import functools
import jax
import jax.numpy as jnp
from jax import lax
from jax.experimental import pallas as pl
from jax.experimental.pallas import tpu as pltpu
from jax.sharding import PartitionSpec as P

TILE = 128
PARTS = 4
ROWS = 16
VMEM_LIMIT = 24 * 1024 * 1024


def spread_kernel(where, modes_ref, down_ref, up_ref, *, parts):
    freq, n_modes = modes_ref.shape
    modes = modes_ref[...]
    freqs = freq // parts

    def pick(shape, axis):
        big = lax.broadcasted_iota(jnp.int32, shape, axis) // ROWS
        small = lax.broadcasted_iota(jnp.int32, shape, 1 - axis)
        if freq in shape:
            piece, within = big // freqs, big % freqs
            big = within
            for j in range(parts):
                big = jnp.where(piece == j, where[j] * freqs + within, big)
        return jnp.where(big == small, 1.0, 0.0).astype(jnp.bfloat16)

    def lane(shape):
        rows = lax.broadcasted_iota(jnp.int32, shape, 0) % ROWS
        columns = lax.broadcasted_iota(jnp.int32, shape, 1) % ROWS
        return rows == columns

    def dot(a, b, dims):
        return lax.dot_general(a, b, (dims, ((), ())), preferred_element_type=jnp.float32)

    tall = dot(pick((n_modes * ROWS, n_modes), 0), modes, ((1,), (1,))).astype(jnp.bfloat16)
    value = dot(tall, pick((freq, freq * ROWS), 1), ((1,), (0,)))
    down_ref[...] = jnp.where(lane(value.shape), value, 0.0).astype(jnp.bfloat16)
    tall = dot(pick((freq * ROWS, freq), 0), modes, ((1,), (0,))).astype(jnp.bfloat16)
    value = dot(tall, pick((n_modes, n_modes * ROWS), 1), ((1,), (0,)))
    up_ref[...] = jnp.where(lane(value.shape), value, 0.0).astype(jnp.bfloat16)


def spread(where, modes, parts):
    freq, n_modes = modes.shape
    vmem = pl.BlockSpec(memory_space=pltpu.VMEM)
    return pl.pallas_call(
        functools.partial(spread_kernel, parts=parts),
        grid_spec=pltpu.PrefetchScalarGridSpec(
            num_scalar_prefetch=1, grid=(), in_specs=[vmem], out_specs=[vmem, vmem]
        ),
        out_shape=[
            jax.ShapeDtypeStruct((n_modes * ROWS, freq * ROWS), jnp.bfloat16),
            jax.ShapeDtypeStruct((freq * ROWS, n_modes * ROWS), jnp.bfloat16),
        ],
        compiler_params=pltpu.CompilerParams(vmem_limit_bytes=VMEM_LIMIT),
        cost_estimate=pl.CostEstimate(flops=1024, bytes_accessed=1024, transcendentals=0),
    )(where, modes)


def hold_kernel(where, beam, held, mask, sems):
    freq, base, ell = held.shape
    ell_tiles, base_tiles = ell // TILE, base // TILE
    copies = [pltpu.make_async_copy(beam.at[f], held.at[f], sems.at[f]) for f in range(freq)]
    for copy in copies:
        copy.start()
    for b in range(base_tiles):
        for l in range(ell_tiles):
            kept = where[PARTS + 1 + b * ell_tiles + l].astype(jnp.float32)
            mask[b * TILE:(b + 1) * TILE, l * TILE:(l + 1) * TILE] = jnp.full(
                (TILE, TILE), kept, jnp.float32
            ).astype(jnp.bfloat16)
    for f, copy in enumerate(copies):
        copy.wait()
        held[f] = held[f] * mask[...]


def hold(where, beam):
    freq, base, ell = beam.shape
    return pl.pallas_call(
        hold_kernel,
        grid_spec=pltpu.PrefetchScalarGridSpec(
            num_scalar_prefetch=1,
            grid=(),
            in_specs=[pl.BlockSpec(memory_space=pl.ANY)],
            out_specs=pl.BlockSpec(memory_space=pltpu.VMEM),
            scratch_shapes=[pltpu.VMEM((base, ell), jnp.bfloat16), pltpu.SemaphoreType.DMA((freq,))],
        ),
        out_shape=pltpu.VMEM(beam.shape, beam.dtype),
        compiler_params=pltpu.CompilerParams(vmem_limit_bytes=VMEM_LIMIT),
        cost_estimate=pl.CostEstimate(flops=1024, bytes_accessed=1024, transcendentals=0),
    )(where, beam)


def project_kernel(where, mine, others, held, stay_ref, leave_ref, *, piece):
    freqs, rows, _ = mine.shape
    first = where[piece] * freqs
    own = where[PARTS] == 1
    for f in range(freqs):
        a, b = mine[f], others[f]
        lines = jnp.concatenate([jnp.where(own, a, b), jnp.where(own, b, a)], axis=0)
        value = jnp.dot(lines, held[first + f], preferred_element_type=jnp.float32).astype(jnp.bfloat16)
        stay_ref[f] = value[:rows]
        leave_ref[f] = value[rows:]


def project(where, mine, others, held, piece):
    freqs, rows, _ = mine.shape
    ell = held.shape[2]
    vmem = pl.BlockSpec(memory_space=pltpu.VMEM)
    return pl.pallas_call(
        functools.partial(project_kernel, piece=piece),
        grid_spec=pltpu.PrefetchScalarGridSpec(
            num_scalar_prefetch=1, grid=(), in_specs=[vmem] * 3, out_specs=[vmem] * 2
        ),
        out_shape=[jax.ShapeDtypeStruct((freqs, rows, ell), jnp.bfloat16)] * 2,
        compiler_params=pltpu.CompilerParams(vmem_limit_bytes=VMEM_LIMIT),
        cost_estimate=pl.CostEstimate(flops=1024, bytes_accessed=1024, transcendentals=0),
    )(where, mine, others, pltpu.with_memory_space_constraint(held, pltpu.VMEM))


def contract(modes, skies):
    block = jnp.concatenate([sky[...].reshape(sky.shape[0] * ROWS, sky.shape[2]) for sky in skies], axis=0)
    return jnp.dot(modes, block, preferred_element_type=jnp.float32)


def reduce_kernel(modes_ref, *refs):
    out = refs[-1]
    out[...] = contract(modes_ref[...], refs[:-1]).astype(jnp.bfloat16).reshape(out.shape)


def by_rows(count, ell, first=0):
    return pl.BlockSpec((count, ROWS, ell), lambda g: (0, g + first // ROWS, 0))


def fixed(shape):
    return pl.BlockSpec(shape, lambda g: (0,) * len(shape))


def sky_specs(skies, first):
    return [by_rows(sky.shape[0], sky.shape[2], first if n == 0 else 0) for n, sky in enumerate(skies)]


def reduce(modes, skies, first, n_modes):
    _, rows, ell = skies[-1].shape
    return pl.pallas_call(
        reduce_kernel,
        grid=(rows // ROWS,),
        in_specs=[fixed(modes.shape)] + sky_specs(skies, first),
        out_specs=by_rows(n_modes, ell),
        out_shape=jax.ShapeDtypeStruct((n_modes, rows, ell), jnp.bfloat16),
        compiler_params=pltpu.CompilerParams(vmem_limit_bytes=VMEM_LIMIT),
        cost_estimate=pl.CostEstimate(flops=1024, bytes_accessed=1024, transcendentals=0),
    )(modes, *skies)


def restore_kernel(down_ref, up_ref, ratio_ref, came_ref, *refs):
    skies, outs = refs[:-PARTS], refs[-PARTS:]
    n_modes, _, ell = came_ref.shape
    size = outs[0].shape[0] * ROWS
    total = contract(down_ref[...], skies).reshape(came_ref.shape) + came_ref[...].astype(jnp.float32)
    weighted = (total * ratio_ref[...]).astype(jnp.bfloat16).reshape(n_modes * ROWS, ell)
    for which, out in enumerate(outs):
        value = jnp.dot(up_ref[which * size:(which + 1) * size, :], weighted, preferred_element_type=jnp.float32)
        out[...] = value.astype(jnp.bfloat16).reshape(out.shape)


def restore(skies, first, came, ratios, down, up, freqs):
    n_modes, rows, ell = came.shape
    return pl.pallas_call(
        restore_kernel,
        grid=(rows // ROWS,),
        in_specs=[fixed(down.shape), fixed(up.shape), fixed(ratios.shape), by_rows(n_modes, ell)]
        + sky_specs(skies, first),
        out_specs=[by_rows(freqs, ell)] * PARTS,
        out_shape=[jax.ShapeDtypeStruct((freqs, rows, ell), jnp.bfloat16)] * PARTS,
        compiler_params=pltpu.CompilerParams(vmem_limit_bytes=VMEM_LIMIT),
        cost_estimate=pl.CostEstimate(flops=1024, bytes_accessed=1024, transcendentals=0),
    )(down, up, ratios, came, *skies)


def place_kernel(where, *refs, spots, first):
    count = len(spots)
    pieces, out, sems = refs[:count], refs[-2], refs[-1]
    rows = pieces[0].shape[1]
    copies = [
        pltpu.make_async_copy(pieces[n], out.at[:, where[j], first:first + rows, :], sems.at[n])
        for n, j in enumerate(spots)
    ]
    for copy in copies:
        copy.start()
    for copy in copies:
        copy.wait()


def place(where, pieces, spots, first, shape, into=None):
    count = len(spots)
    extra = [] if into is None else [into]
    anywhere = pl.BlockSpec(memory_space=pl.ANY)
    return pl.pallas_call(
        functools.partial(place_kernel, spots=spots, first=first),
        grid_spec=pltpu.PrefetchScalarGridSpec(
            num_scalar_prefetch=1,
            grid=(),
            in_specs=[pl.BlockSpec(memory_space=pltpu.VMEM)] * count + [anywhere] * len(extra),
            out_specs=anywhere,
            scratch_shapes=[pltpu.SemaphoreType.DMA((count,))],
        ),
        out_shape=jax.ShapeDtypeStruct(shape, jnp.bfloat16),
        input_output_aliases={count + 1: 0} if extra else {},
        compiler_params=pltpu.CompilerParams(vmem_limit_bytes=VMEM_LIMIT),
        cost_estimate=pl.CostEstimate(flops=1024, bytes_accessed=1024, transcendentals=0),
    )(where, *[pieces[j] for j in spots], *extra)


def staged(visibility, beam_transfer, tile_mask, first_block, eigen_modes, signal_noise):
    freqs, parts, rows_all, base = visibility.shape
    _, freq_total, _, ell = beam_transfer.shape
    n_modes = eigen_modes.shape[2]
    ell_tiles = ell // TILE
    z, x, p = lax.axis_index("fm"), lax.axis_index("kl"), lax.axis_index("pol")
    other = [(0, 1), (1, 0)]

    def along_z(value, j):
        return lax.ppermute(value, "fm", [(i, i ^ j) for i in range(parts)])

    def along_x(value):
        return lax.ppermute(value, "kl", other)

    def cut(j, first, rows):
        return lax.dynamic_slice(visibility, (0, z ^ j, first, 0), (freqs, 1, rows, base)).reshape(freqs, rows, base)

    order = jnp.stack([z ^ j for j in range(parts)]).astype(jnp.int32)
    block_ids = x * ell_tiles + jnp.arange(ell_tiles, dtype=jnp.int32)
    keep = tile_mask[0] * (first_block[0] <= block_ids).astype(jnp.int32)[None, :]
    where = jnp.concatenate([order, (x == p).astype(jnp.int32)[None], keep.reshape(-1)])
    down, up = spread(where, eigen_modes[0], parts)
    ratio = signal_noise[0] / (1.0 + signal_noise[0])
    ratios = jnp.broadcast_to(ratio[:, None, None], (n_modes, 1, ell))
    beam = beam_transfer.reshape(freq_total, base, ell)
    shape = (freqs, parts, rows_all, ell)

    fence = lax.optimization_barrier
    most = rows_all - ROWS
    a = [cut(j, 0, ROWS) for j in range(1, parts)]
    mine = cut(0, 0, rows_all)
    b = [cut(j, ROWS, most) for j in range(1, parts)]
    a = [along_z(a[j - 1], j) for j in (1, 2, 3)]
    others = along_x(mine)
    held = hold(where, beam)
    stay_own, leave_own = project(where, mine, others, held, 0)
    a, b, held, stay_own, leave_own, down, up = fence((a, b, held, stay_own, leave_own, down, up))
    b[0], b[1] = along_z(b[0], 1), along_z(b[1], 2)
    skies = [project(where, a[j - 1], along_x(a[j - 1]), held, j) for j in (1, 2, 3)]
    stay_a = [stay_own] + [stay for stay, _ in skies]
    gone = reduce(down, [leave_own] + [leave for _, leave in skies], 0, n_modes)
    b, held, stay_a, gone = fence((b, held, stay_a, gone))
    b[2] = along_z(b[2], 3)
    x_1, x_2 = along_x(b[0]), along_x(b[1])
    outs = restore(stay_a, 0, lax.ppermute(gone, "pol", other), ratios, down, up, freqs)
    stay_1, leave_1 = project(where, b[0], x_1, held, 1)
    b, x_2, held, outs, stay_1, leave_1 = fence((b, x_2, held, outs, stay_1, leave_1))
    back_a = [outs[0]] + [along_z(outs[j], j) for j in range(1, parts)]
    x_3 = along_x(b[2])
    stay_2, leave_2 = project(where, b[1], x_2, held, 2)
    stay_3, leave_3 = project(where, b[2], x_3, held, 3)
    gone = reduce(down, [leave_own, leave_1, leave_2, leave_3], ROWS, n_modes)
    back_a, stay_2, stay_3, gone = fence((back_a, stay_2, stay_3, gone))
    came = lax.ppermute(gone, "pol", other)
    outs = restore([stay_own, stay_1, stay_2, stay_3], ROWS, came, ratios, down, up, freqs)
    back_b = [outs[0]] + [along_z(outs[j], j) for j in range(1, parts)]
    result = place(where, back_a, (0, 1, 2, 3), 0, shape)
    result = place(where, back_b, (0, 1), ROWS, shape, into=result)
    return place(where, back_b, (2, 3), ROWS, shape, into=result)


def plain(visibility, beam_transfer, tile_mask, first_block, eigen_modes, signal_noise):
    owned_modes, freq_total, base_half, ell_local = beam_transfer.shape
    base_tiles, ell_tiles = base_half // TILE, ell_local // TILE
    block_ids = lax.axis_index("kl") * ell_tiles + jnp.arange(ell_tiles, dtype=jnp.int32)
    inside = (first_block[:, None] <= block_ids[None, :]).astype(jnp.int32)
    keep_tiles = tile_mask * inside[:, None, :]
    shaped = beam_transfer.reshape(owned_modes, freq_total, base_tiles, TILE, ell_tiles, TILE)
    masked_beam = shaped * keep_tiles.astype(jnp.bfloat16)[:, None, :, None, :, None]
    masked_beam = masked_beam.reshape(owned_modes, freq_total, base_half, ell_local)
    arrived = lax.all_to_all(visibility, "fm", split_axis=1, concat_axis=0, tiled=True)
    partial_value = jnp.einsum(
        "fmrb,mfbl->fmrl",
        lax.all_gather(arrived, "kl", axis=2, tiled=True),
        masked_beam,
        preferred_element_type=jnp.float32,
    )
    sky_sum = lax.psum_scatter(
        partial_value.astype(jnp.bfloat16), "pol", scatter_dimension=2, tiled=True
    ).astype(jnp.float32)
    modes_float = eigen_modes.astype(jnp.float32)
    coeffs = jnp.einsum("mfk,fmrl->mkrl", modes_float, sky_sum, precision=lax.Precision.HIGHEST)
    ratios = signal_noise / (1.0 + signal_noise)
    weighted = (coeffs * ratios[:, :, None, None]).astype(jnp.bfloat16)
    filtered = jnp.einsum(
        "mfk,mkrl->fmrl", eigen_modes, weighted, preferred_element_type=jnp.float32
    ).astype(jnp.bfloat16)
    return lax.all_to_all(filtered, "fm", split_axis=0, concat_axis=1, tiled=True)


def per_device(*args, sizes):
    visibility, beam_transfer = args[0], args[1]
    _, modes, rows, _ = visibility.shape
    fits = (
        sizes["kl"] == 2
        and sizes["pol"] == 2
        and modes == sizes["fm"] == PARTS
        and beam_transfer.shape[0] == 1
        and rows % ROWS == 0
        and rows > ROWS
    )
    if not fits:
        return plain(*args)
    return staged(*args)


def solution(mesh):
    placed = (
        P(("group", "fm"), None, "kl", "pol"),
        P(("group", "fm"), None, "pol", "kl"),
        P("fm", "pol", "kl"),
        P("fm"),
        P(("group", "fm"), None, None),
        P(("group", "fm"), None),
    )
    return jax.shard_map(
        functools.partial(per_device, sizes=dict(mesh.shape)),
        mesh=mesh,
        in_specs=placed,
        out_specs=P(("group", "fm"), None, "pol", "kl"),
        check_vma=False,
    )
```

```python
import functools
import jax
import jax.numpy as jnp
from jax import lax
from jax.experimental import pallas as pl
from jax.experimental.pallas import tpu as pltpu
from jax.sharding import PartitionSpec as P

TILE = 128
PARTS = 4
ROWS = 16
VMEM_LIMIT = 24 * 1024 * 1024


def hold_kernel(where, beam, modes_ref, held, down_ref, up_ref, mask, sems):
    freq, base, ell = held.shape
    n_modes = modes_ref.shape[1]
    ell_tiles, base_tiles, freqs = ell // TILE, base // TILE, freq // PARTS
    copies = [pltpu.make_async_copy(beam.at[f], held.at[f], sems.at[f]) for f in range(freq)]
    for copy in copies:
        copy.start()
    for b in range(base_tiles):
        for l in range(ell_tiles):
            kept = where[PARTS + 1 + b * ell_tiles + l].astype(jnp.float32)
            mask[b * TILE:(b + 1) * TILE, l * TILE:(l + 1) * TILE] = jnp.full(
                (TILE, TILE), kept, jnp.float32
            ).astype(jnp.bfloat16)
    modes = modes_ref[...]

    def pick(shape, axis):
        big = lax.broadcasted_iota(jnp.int32, shape, axis) // ROWS
        small = lax.broadcasted_iota(jnp.int32, shape, 1 - axis)
        if freq in shape:
            piece, within = big // freqs, big % freqs
            big = within
            for j in range(PARTS):
                big = jnp.where(piece == j, where[j] * freqs + within, big)
        return jnp.where(big == small, 1.0, 0.0).astype(jnp.bfloat16)

    def lane(shape):
        rows = lax.broadcasted_iota(jnp.int32, shape, 0) % ROWS
        columns = lax.broadcasted_iota(jnp.int32, shape, 1) % ROWS
        return rows == columns

    def dot(a, b, dims):
        return lax.dot_general(a, b, (dims, ((), ())), preferred_element_type=jnp.float32)

    tall = dot(pick((n_modes * ROWS, n_modes), 0), modes, ((1,), (1,))).astype(jnp.bfloat16)
    value = dot(tall, pick((freq, freq * ROWS), 1), ((1,), (0,)))
    down_ref[...] = jnp.where(lane(value.shape), value, 0.0).astype(jnp.bfloat16)
    tall = dot(pick((freq * ROWS, freq), 0), modes, ((1,), (0,))).astype(jnp.bfloat16)
    value = dot(tall, pick((n_modes, n_modes * ROWS), 1), ((1,), (0,)))
    up_ref[...] = jnp.where(lane(value.shape), value, 0.0).astype(jnp.bfloat16)
    for f, copy in enumerate(copies):
        copy.wait()
        held[f] = held[f] * mask[...]


def hold(where, beam, modes):
    freq, base, ell = beam.shape
    size, wide = freq * ROWS, modes.shape[1] * ROWS
    vmem = pl.BlockSpec(memory_space=pltpu.VMEM)
    return pl.pallas_call(
        hold_kernel,
        grid_spec=pltpu.PrefetchScalarGridSpec(
            num_scalar_prefetch=1,
            grid=(),
            in_specs=[pl.BlockSpec(memory_space=pl.ANY), vmem],
            out_specs=[vmem] * 3,
            scratch_shapes=[pltpu.VMEM((base, ell), jnp.bfloat16), pltpu.SemaphoreType.DMA((freq,))],
        ),
        out_shape=[
            pltpu.VMEM(beam.shape, beam.dtype),
            jax.ShapeDtypeStruct((wide, size), jnp.bfloat16),
            jax.ShapeDtypeStruct((size, wide), jnp.bfloat16),
        ],
        compiler_params=pltpu.CompilerParams(vmem_limit_bytes=VMEM_LIMIT),
        cost_estimate=pl.CostEstimate(flops=1024, bytes_accessed=1024, transcendentals=0),
    )(where, beam, modes)


def project_kernel(where, mine, others, held, stay_ref, leave_ref, *, piece):
    freqs, rows, _ = mine.shape
    first = where[piece] * freqs
    own = where[PARTS] == 1
    for f in range(freqs):
        a, b = mine[f], others[f]
        lines = jnp.concatenate([jnp.where(own, a, b), jnp.where(own, b, a)], axis=0)
        value = jnp.dot(lines, held[first + f], preferred_element_type=jnp.float32).astype(jnp.bfloat16)
        stay_ref[f] = value[:rows]
        leave_ref[f] = value[rows:]


def project(where, mine, others, held, piece):
    freqs, rows, _ = mine.shape
    ell = held.shape[2]
    vmem = pl.BlockSpec(memory_space=pltpu.VMEM)
    return pl.pallas_call(
        functools.partial(project_kernel, piece=piece),
        grid_spec=pltpu.PrefetchScalarGridSpec(
            num_scalar_prefetch=1, grid=(), in_specs=[vmem] * 3, out_specs=[vmem] * 2
        ),
        out_shape=[jax.ShapeDtypeStruct((freqs, rows, ell), jnp.bfloat16)] * 2,
        compiler_params=pltpu.CompilerParams(vmem_limit_bytes=VMEM_LIMIT),
        cost_estimate=pl.CostEstimate(flops=1024, bytes_accessed=1024, transcendentals=0),
    )(where, mine, others, pltpu.with_memory_space_constraint(held, pltpu.VMEM))


def contract(modes, skies):
    block = jnp.concatenate([sky[...].reshape(sky.shape[0] * ROWS, sky.shape[2]) for sky in skies], axis=0)
    return jnp.dot(modes, block, preferred_element_type=jnp.float32)


def reduce_kernel(modes_ref, *refs):
    out = refs[-1]
    out[...] = contract(modes_ref[...], refs[:-1]).astype(jnp.bfloat16).reshape(out.shape)


def by_rows(count, ell, first=0):
    return pl.BlockSpec((count, ROWS, ell), lambda g: (0, g + first // ROWS, 0))


def fixed(shape):
    return pl.BlockSpec(shape, lambda g: (0,) * len(shape))


def sky_specs(skies, first):
    return [by_rows(sky.shape[0], sky.shape[2], first if n == 0 else 0) for n, sky in enumerate(skies)]


def reduce(modes, skies, first, n_modes):
    _, rows, ell = skies[-1].shape
    return pl.pallas_call(
        reduce_kernel,
        grid=(rows // ROWS,),
        in_specs=[fixed(modes.shape)] + sky_specs(skies, first),
        out_specs=by_rows(n_modes, ell),
        out_shape=jax.ShapeDtypeStruct((n_modes, rows, ell), jnp.bfloat16),
        compiler_params=pltpu.CompilerParams(vmem_limit_bytes=VMEM_LIMIT),
        cost_estimate=pl.CostEstimate(flops=1024, bytes_accessed=1024, transcendentals=0),
    )(modes, *skies)


def restore_kernel(down_ref, up_ref, ratio_ref, came_ref, *refs):
    skies, outs = refs[:-PARTS], refs[-PARTS:]
    n_modes, _, ell = came_ref.shape
    size = outs[0].shape[0] * ROWS
    total = contract(down_ref[...], skies).reshape(came_ref.shape) + came_ref[...].astype(jnp.float32)
    weighted = (total * ratio_ref[...]).astype(jnp.bfloat16).reshape(n_modes * ROWS, ell)
    for which, out in enumerate(outs):
        value = jnp.dot(up_ref[which * size:(which + 1) * size, :], weighted, preferred_element_type=jnp.float32)
        out[...] = value.astype(jnp.bfloat16).reshape(out.shape)


def restore(skies, first, came, ratios, down, up, freqs):
    n_modes, rows, ell = came.shape
    return pl.pallas_call(
        restore_kernel,
        grid=(rows // ROWS,),
        in_specs=[fixed(down.shape), fixed(up.shape), fixed(ratios.shape), by_rows(n_modes, ell)]
        + sky_specs(skies, first),
        out_specs=[by_rows(freqs, ell)] * PARTS,
        out_shape=[jax.ShapeDtypeStruct((freqs, rows, ell), jnp.bfloat16)] * PARTS,
        compiler_params=pltpu.CompilerParams(vmem_limit_bytes=VMEM_LIMIT),
        cost_estimate=pl.CostEstimate(flops=1024, bytes_accessed=1024, transcendentals=0),
    )(down, up, ratios, came, *skies)


def place_kernel(where, *refs, spots, first):
    count = len(spots)
    pieces, out, sems = refs[:count], refs[-2], refs[-1]
    rows = pieces[0].shape[1]
    copies = [
        pltpu.make_async_copy(pieces[n], out.at[:, where[j], first:first + rows, :], sems.at[n])
        for n, j in enumerate(spots)
    ]
    for copy in copies:
        copy.start()
    for copy in copies:
        copy.wait()


def place(where, pieces, spots, first, shape, into=None):
    count = len(spots)
    extra = [] if into is None else [into]
    anywhere = pl.BlockSpec(memory_space=pl.ANY)
    return pl.pallas_call(
        functools.partial(place_kernel, spots=spots, first=first),
        grid_spec=pltpu.PrefetchScalarGridSpec(
            num_scalar_prefetch=1,
            grid=(),
            in_specs=[pl.BlockSpec(memory_space=pltpu.VMEM)] * count + [anywhere] * len(extra),
            out_specs=anywhere,
            scratch_shapes=[pltpu.SemaphoreType.DMA((count,))],
        ),
        out_shape=jax.ShapeDtypeStruct(shape, jnp.bfloat16),
        input_output_aliases={count + 1: 0} if extra else {},
        compiler_params=pltpu.CompilerParams(vmem_limit_bytes=VMEM_LIMIT),
        cost_estimate=pl.CostEstimate(flops=1024, bytes_accessed=1024, transcendentals=0),
    )(where, *[pieces[j] for j in spots], *extra)


def staged(visibility, beam_transfer, tile_mask, first_block, eigen_modes, signal_noise):
    freqs, parts, rows_all, base = visibility.shape
    _, freq_total, _, ell = beam_transfer.shape
    n_modes = eigen_modes.shape[2]
    ell_tiles = ell // TILE
    z, x, p = lax.axis_index("fm"), lax.axis_index("kl"), lax.axis_index("pol")
    other = [(0, 1), (1, 0)]

    def along_z(value, j):
        return lax.ppermute(value, "fm", [(i, i ^ j) for i in range(parts)])

    def along_x(value):
        return lax.ppermute(value, "kl", other)

    def cut(j, first, rows):
        return lax.dynamic_slice(visibility, (0, z ^ j, first, 0), (freqs, 1, rows, base)).reshape(freqs, rows, base)

    order = jnp.stack([z ^ j for j in range(parts)]).astype(jnp.int32)
    block_ids = x * ell_tiles + jnp.arange(ell_tiles, dtype=jnp.int32)
    keep = tile_mask[0] * (first_block[0] <= block_ids).astype(jnp.int32)[None, :]
    where = jnp.concatenate([order, (x == p).astype(jnp.int32)[None], keep.reshape(-1)])
    ratio = signal_noise[0] / (1.0 + signal_noise[0])
    ratios = jnp.broadcast_to(ratio[:, None, None], (n_modes, 1, ell))
    beam = beam_transfer.reshape(freq_total, base, ell)
    shape = (freqs, parts, rows_all, ell)

    fence = lax.optimization_barrier
    most = rows_all - ROWS
    a = {j: along_z(cut(j, 0, ROWS), j) for j in (3, 2, 1)}
    mine = [cut(0, 0, rows_all)[n:n + freqs // 2] for n in (0, freqs // 2)]
    others = [along_x(part) for part in mine]
    b = {j: cut(j, ROWS, most) for j in (1, 2, 3)}
    held, down, up = hold(where, beam, eigen_modes[0])
    (a[3], a[2], a[1]), b, others, down, up = fence(((a[3], a[2], a[1]), b, others, down, up))
    b[1], b[2] = along_z(b[1], 1), along_z(b[2], 2)
    stay_own, leave_own = project(where, jnp.concatenate(mine, axis=0), jnp.concatenate(others, axis=0), held, 0)
    skies = [project(where, a[j], along_x(a[j]), held, j) for j in (1, 2, 3)]
    stay_a = [stay_own] + [stay for stay, _ in skies]
    gone = reduce(down, [leave_own] + [leave for _, leave in skies], 0, n_modes)
    b, stay_a, gone = fence((b, stay_a, gone))
    b[3] = along_z(b[3], 3)
    x_1, x_2 = along_x(b[1]), along_x(b[2])
    outs = restore(stay_a, 0, lax.ppermute(gone, "pol", other), ratios, down, up, freqs)
    stay_1, leave_1 = project(where, b[1], x_1, held, 1)
    b, x_2, outs, stay_1, leave_1 = fence((b, x_2, outs, stay_1, leave_1))
    back_a = [outs[0]] + [along_z(outs[j], j) for j in range(1, parts)]
    x_3 = along_x(b[3])
    stay_2, leave_2 = project(where, b[2], x_2, held, 2)
    stay_3, leave_3 = project(where, b[3], x_3, held, 3)
    gone = reduce(down, [leave_own, leave_1, leave_2, leave_3], ROWS, n_modes)
    back_a, stay_2, stay_3, gone = fence((back_a, stay_2, stay_3, gone))
    came = lax.ppermute(gone, "pol", other)
    outs = restore([stay_own, stay_1, stay_2, stay_3], ROWS, came, ratios, down, up, freqs)
    back_b = [outs[0]] + [along_z(outs[j], j) for j in range(1, parts)]
    result = place(where, back_a, (0, 1, 2, 3), 0, shape)
    result = place(where, back_b, (0, 1), ROWS, shape, into=result)
    return place(where, back_b, (2, 3), ROWS, shape, into=result)


def plain(visibility, beam_transfer, tile_mask, first_block, eigen_modes, signal_noise):
    owned_modes, freq_total, base_half, ell_local = beam_transfer.shape
    base_tiles, ell_tiles = base_half // TILE, ell_local // TILE
    block_ids = lax.axis_index("kl") * ell_tiles + jnp.arange(ell_tiles, dtype=jnp.int32)
    inside = (first_block[:, None] <= block_ids[None, :]).astype(jnp.int32)
    keep_tiles = tile_mask * inside[:, None, :]
    shaped = beam_transfer.reshape(owned_modes, freq_total, base_tiles, TILE, ell_tiles, TILE)
    masked_beam = shaped * keep_tiles.astype(jnp.bfloat16)[:, None, :, None, :, None]
    masked_beam = masked_beam.reshape(owned_modes, freq_total, base_half, ell_local)
    arrived = lax.all_to_all(visibility, "fm", split_axis=1, concat_axis=0, tiled=True)
    partial_value = jnp.einsum(
        "fmrb,mfbl->fmrl",
        lax.all_gather(arrived, "kl", axis=2, tiled=True),
        masked_beam,
        preferred_element_type=jnp.float32,
    )
    sky_sum = lax.psum_scatter(
        partial_value.astype(jnp.bfloat16), "pol", scatter_dimension=2, tiled=True
    ).astype(jnp.float32)
    modes_float = eigen_modes.astype(jnp.float32)
    coeffs = jnp.einsum("mfk,fmrl->mkrl", modes_float, sky_sum, precision=lax.Precision.HIGHEST)
    ratios = signal_noise / (1.0 + signal_noise)
    weighted = (coeffs * ratios[:, :, None, None]).astype(jnp.bfloat16)
    filtered = jnp.einsum(
        "mfk,mkrl->fmrl", eigen_modes, weighted, preferred_element_type=jnp.float32
    ).astype(jnp.bfloat16)
    return lax.all_to_all(filtered, "fm", split_axis=0, concat_axis=1, tiled=True)


def per_device(*args, sizes):
    visibility, beam_transfer = args[0], args[1]
    _, modes, rows, _ = visibility.shape
    fits = (
        sizes["kl"] == 2
        and sizes["pol"] == 2
        and modes == sizes["fm"] == PARTS
        and beam_transfer.shape[0] == 1
        and rows % ROWS == 0
        and rows > ROWS
    )
    if not fits:
        return plain(*args)
    return staged(*args)


def solution(mesh):
    placed = (
        P(("group", "fm"), None, "kl", "pol"),
        P(("group", "fm"), None, "pol", "kl"),
        P("fm", "pol", "kl"),
        P("fm"),
        P(("group", "fm"), None, None),
        P(("group", "fm"), None),
    )
    return jax.shard_map(
        functools.partial(per_device, sizes=dict(mesh.shape)),
        mesh=mesh,
        in_specs=placed,
        out_specs=P(("group", "fm"), None, "pol", "kl"),
        check_vma=False,
    )
```

```python
import functools
import jax
import jax.numpy as jnp
from jax import lax
from jax.experimental import pallas as pl
from jax.experimental.pallas import tpu as pltpu
from jax.sharding import PartitionSpec as P

TILE = 128
PARTS = 4
ROWS = 16
VMEM_LIMIT = 24 * 1024 * 1024


def hold_kernel(where, tiles, starts, beam, modes_ref, held, down_ref, up_ref, mask, sems):
    freq, base, ell = held.shape
    n_modes = modes_ref.shape[1]
    ell_tiles, base_tiles, freqs = ell // TILE, base // TILE, freq // PARTS
    copies = [pltpu.make_async_copy(beam.at[f], held.at[f], sems.at[f]) for f in range(freq)]
    for copy in copies:
        copy.start()
    for b in range(base_tiles):
        for l in range(ell_tiles):
            kept = jnp.where(starts[0] <= where[PARTS + 1] + l, tiles[b, l], 0).astype(jnp.float32)
            mask[b * TILE:(b + 1) * TILE, l * TILE:(l + 1) * TILE] = jnp.full(
                (TILE, TILE), kept, jnp.float32
            ).astype(jnp.bfloat16)
    modes = modes_ref[...]

    def pick(shape, axis):
        big = lax.broadcasted_iota(jnp.int32, shape, axis) // ROWS
        small = lax.broadcasted_iota(jnp.int32, shape, 1 - axis)
        if freq in shape:
            piece, within = big // freqs, big % freqs
            big = within
            for j in range(PARTS):
                big = jnp.where(piece == j, where[j] * freqs + within, big)
        return jnp.where(big == small, 1.0, 0.0).astype(jnp.bfloat16)

    def lane(shape):
        rows = lax.broadcasted_iota(jnp.int32, shape, 0) % ROWS
        columns = lax.broadcasted_iota(jnp.int32, shape, 1) % ROWS
        return rows == columns

    def dot(a, b, dims):
        return lax.dot_general(a, b, (dims, ((), ())), preferred_element_type=jnp.float32)

    tall = dot(pick((n_modes * ROWS, n_modes), 0), modes, ((1,), (1,))).astype(jnp.bfloat16)
    value = dot(tall, pick((freq, freq * ROWS), 1), ((1,), (0,)))
    down_ref[...] = jnp.where(lane(value.shape), value, 0.0).astype(jnp.bfloat16)
    tall = dot(pick((freq * ROWS, freq), 0), modes, ((1,), (0,))).astype(jnp.bfloat16)
    value = dot(tall, pick((n_modes, n_modes * ROWS), 1), ((1,), (0,)))
    up_ref[...] = jnp.where(lane(value.shape), value, 0.0).astype(jnp.bfloat16)
    for f, copy in enumerate(copies):
        copy.wait()
        held[f] = held[f] * mask[...]


def hold(where, tiles, starts, beam, modes):
    freq, base, ell = beam.shape
    size, wide = freq * ROWS, modes.shape[1] * ROWS
    vmem = pl.BlockSpec(memory_space=pltpu.VMEM)
    return pl.pallas_call(
        hold_kernel,
        grid_spec=pltpu.PrefetchScalarGridSpec(
            num_scalar_prefetch=3,
            grid=(),
            in_specs=[pl.BlockSpec(memory_space=pl.ANY), vmem],
            out_specs=[vmem] * 3,
            scratch_shapes=[pltpu.VMEM((base, ell), jnp.bfloat16), pltpu.SemaphoreType.DMA((freq,))],
        ),
        out_shape=[
            pltpu.VMEM(beam.shape, beam.dtype),
            jax.ShapeDtypeStruct((wide, size), jnp.bfloat16),
            jax.ShapeDtypeStruct((size, wide), jnp.bfloat16),
        ],
        compiler_params=pltpu.CompilerParams(vmem_limit_bytes=VMEM_LIMIT),
        cost_estimate=pl.CostEstimate(flops=1024, bytes_accessed=1024, transcendentals=0),
    )(where, tiles, starts, beam, modes)


def project_kernel(where, mine, others, held, stay_ref, leave_ref, *, piece):
    freqs, rows, _ = mine.shape
    first = where[piece] * freqs
    own = where[PARTS] == 1
    for f in range(freqs):
        a, b = mine[f], others[f]
        lines = jnp.concatenate([jnp.where(own, a, b), jnp.where(own, b, a)], axis=0)
        value = jnp.dot(lines, held[first + f], preferred_element_type=jnp.float32).astype(jnp.bfloat16)
        stay_ref[f] = value[:rows]
        leave_ref[f] = value[rows:]


def project(where, mine, others, held, piece):
    freqs, rows, _ = mine.shape
    ell = held.shape[2]
    vmem = pl.BlockSpec(memory_space=pltpu.VMEM)
    return pl.pallas_call(
        functools.partial(project_kernel, piece=piece),
        grid_spec=pltpu.PrefetchScalarGridSpec(
            num_scalar_prefetch=1, grid=(), in_specs=[vmem] * 3, out_specs=[vmem] * 2
        ),
        out_shape=[jax.ShapeDtypeStruct((freqs, rows, ell), jnp.bfloat16)] * 2,
        compiler_params=pltpu.CompilerParams(vmem_limit_bytes=VMEM_LIMIT),
        cost_estimate=pl.CostEstimate(flops=1024, bytes_accessed=1024, transcendentals=0),
    )(where, mine, others, pltpu.with_memory_space_constraint(held, pltpu.VMEM))


def contract(modes, skies):
    block = jnp.concatenate([sky[...].reshape(sky.shape[0] * ROWS, sky.shape[2]) for sky in skies], axis=0)
    return jnp.dot(modes, block, preferred_element_type=jnp.float32)


def reduce_kernel(modes_ref, *refs):
    out = refs[-1]
    out[...] = contract(modes_ref[...], refs[:-1]).astype(out.dtype).reshape(out.shape)


def by_rows(count, ell, first=0):
    return pl.BlockSpec((count, ROWS, ell), lambda g: (0, g + first // ROWS, 0))


def fixed(shape):
    return pl.BlockSpec(shape, lambda g: (0,) * len(shape))


def sky_specs(skies, first):
    return [by_rows(sky.shape[0], sky.shape[2], first if n == 0 else 0) for n, sky in enumerate(skies)]


def reduce(modes, skies, first, n_modes, dtype=jnp.bfloat16):
    _, rows, ell = skies[-1].shape
    return pl.pallas_call(
        reduce_kernel,
        grid=(rows // ROWS,),
        in_specs=[fixed(modes.shape)] + sky_specs(skies, first),
        out_specs=by_rows(n_modes, ell),
        out_shape=jax.ShapeDtypeStruct((n_modes, rows, ell), dtype),
        compiler_params=pltpu.CompilerParams(vmem_limit_bytes=VMEM_LIMIT),
        cost_estimate=pl.CostEstimate(flops=1024, bytes_accessed=1024, transcendentals=0),
    )(modes, *skies)


def restore_kernel(up_ref, ratio_ref, kept_ref, came_ref, *outs, spots):
    n_modes, _, ell = came_ref.shape
    size = outs[0].shape[0] * ROWS
    total = kept_ref[...] + came_ref[...].astype(jnp.float32)
    weighted = (total * ratio_ref[...]).astype(jnp.bfloat16).reshape(n_modes * ROWS, ell)
    for which, out in zip(spots, outs):
        value = jnp.dot(up_ref[which * size:(which + 1) * size, :], weighted, preferred_element_type=jnp.float32)
        out[...] = value.astype(jnp.bfloat16).reshape(out.shape)


def restore(kept, came, ratios, up, freqs, spots):
    n_modes, rows, ell = came.shape
    return pl.pallas_call(
        functools.partial(restore_kernel, spots=spots),
        grid=(rows // ROWS,),
        in_specs=[fixed(up.shape), fixed(ratios.shape)] + [by_rows(n_modes, ell)] * 2,
        out_specs=[by_rows(freqs, ell)] * len(spots),
        out_shape=[jax.ShapeDtypeStruct((freqs, rows, ell), jnp.bfloat16)] * len(spots),
        compiler_params=pltpu.CompilerParams(vmem_limit_bytes=VMEM_LIMIT),
        cost_estimate=pl.CostEstimate(flops=1024, bytes_accessed=1024, transcendentals=0),
    )(up, ratios, kept, came)


def place_kernel(where, *refs, spots, first):
    count = len(spots)
    pieces, out, sems = refs[:count], refs[-2], refs[-1]
    rows = pieces[0].shape[1]
    copies = [
        pltpu.make_async_copy(pieces[n], out.at[:, where[j], first:first + rows, :], sems.at[n])
        for n, j in enumerate(spots)
    ]
    for copy in copies:
        copy.start()
    for copy in copies:
        copy.wait()


def place(where, pieces, spots, first, shape, into=None):
    count = len(spots)
    extra = [] if into is None else [into]
    anywhere = pl.BlockSpec(memory_space=pl.ANY)
    return pl.pallas_call(
        functools.partial(place_kernel, spots=spots, first=first),
        grid_spec=pltpu.PrefetchScalarGridSpec(
            num_scalar_prefetch=1,
            grid=(),
            in_specs=[pl.BlockSpec(memory_space=pltpu.VMEM)] * count + [anywhere] * len(extra),
            out_specs=anywhere,
            scratch_shapes=[pltpu.SemaphoreType.DMA((count,))],
        ),
        out_shape=jax.ShapeDtypeStruct(shape, jnp.bfloat16),
        input_output_aliases={count + 1: 0} if extra else {},
        compiler_params=pltpu.CompilerParams(vmem_limit_bytes=VMEM_LIMIT),
        cost_estimate=pl.CostEstimate(flops=1024, bytes_accessed=1024, transcendentals=0),
    )(where, *[pieces[j] for j in spots], *extra)


def staged(visibility, beam_transfer, tile_mask, first_block, eigen_modes, signal_noise):
    freqs, parts, rows_all, base = visibility.shape
    _, freq_total, _, ell = beam_transfer.shape
    n_modes = eigen_modes.shape[2]
    ell_tiles = ell // TILE
    z, x, p = lax.axis_index("fm"), lax.axis_index("kl"), lax.axis_index("pol")
    other = [(0, 1), (1, 0)]

    def along_z(value, j):
        return lax.ppermute(value, "fm", [(i, i ^ j) for i in range(parts)])

    def along_x(value):
        return lax.ppermute(value, "kl", other)

    def cut(j, first, rows):
        return lax.dynamic_slice(visibility, (0, z ^ j, first, 0), (freqs, 1, rows, base)).reshape(freqs, rows, base)

    index = jnp.arange(parts + 2, dtype=jnp.int32)
    where = jnp.where(
        index < parts, z ^ index, jnp.where(index == parts, (x == p).astype(jnp.int32), x * ell_tiles)
    ).astype(jnp.int32)
    ratio = signal_noise[0] / (1.0 + signal_noise[0])
    ratios = jnp.broadcast_to(ratio[:, None, None], (n_modes, 1, ell))
    beam = beam_transfer.reshape(freq_total, base, ell)
    shape = (freqs, parts, rows_all, ell)

    fence = lax.optimization_barrier
    most, half = rows_all - ROWS, freqs // 2
    a = {j: along_z(cut(j, 0, ROWS), j) for j in (3, 2, 1)}
    mine = [cut(0, 0, rows_all)[n:n + half] for n in (0, half)]
    others = [along_x(part) for part in mine]
    b = {j: cut(j, ROWS, most) for j in (1, 2, 3)}
    held, down, up = hold(where, tile_mask[0], first_block, beam, eigen_modes[0])
    (a[3], a[2], a[1]), b, others, down, up = fence(((a[3], a[2], a[1]), b, others, down, up))
    b[1], b[2] = along_z(b[1], 1), along_z(b[2], 2)
    stay_own, leave_own = project(where, jnp.concatenate(mine, axis=0), jnp.concatenate(others, axis=0), held, 0)
    skies = [project(where, a[j], along_x(a[j]), held, j) for j in (1, 2, 3)]
    stay_a = [stay_own] + [stay for stay, _ in skies]
    gone = reduce(down, [leave_own] + [leave for _, leave in skies], 0, n_modes)
    (b[2], b[1]), b[3], stay_a, gone = fence(((b[2], b[1]), b[3], stay_a, gone))
    x_2, x_1 = along_x(b[2]), along_x(b[1])
    b[3] = along_z(b[3], 3)
    kept = reduce(down, stay_a, 0, n_modes, jnp.float32)
    outs = restore(kept, lax.ppermute(gone, "pol", other), ratios, up, freqs, (0, 1, 2, 3))
    stay_1, leave_1 = project(where, b[1], x_1, held, 1)
    x_2, b, outs, stay_1, leave_1 = fence((x_2, b, outs, stay_1, leave_1))
    back_a = [outs[0]] + [along_z(outs[j], j) for j in range(1, parts)]
    x_3 = along_x(b[3])
    stay_2, leave_2 = project(where, b[2], x_2, held, 2)
    stay_3, leave_3 = project(where, b[3], x_3, held, 3)
    gone = reduce(down, [leave_own, leave_1, leave_2, leave_3], ROWS, n_modes)
    kept = reduce(down, [stay_own, stay_1, stay_2, stay_3], ROWS, n_modes, jnp.float32)
    (back_a[2], back_a[3], back_a[1]), back_a[0], kept, gone = fence(
        ((back_a[2], back_a[3], back_a[1]), back_a[0], kept, gone)
    )
    came = lax.ppermute(gone, "pol", other)
    outs = dict(zip((3, 2), restore(kept, came, ratios, up, freqs, (3, 2))))
    outs.update(zip((1, 0), restore(kept, came, ratios, up, freqs, (1, 0))))
    back_b = {j: along_z(outs[j], j) for j in (3, 2, 1)}
    back_b[0] = outs[0]
    result = place(where, back_a, (0, 1, 2, 3), 0, shape)
    result = place(where, back_b, (0,), ROWS, shape, into=result)
    return place(where, back_b, (3, 2, 1), ROWS, shape, into=result)


def plain(visibility, beam_transfer, tile_mask, first_block, eigen_modes, signal_noise):
    owned_modes, freq_total, base_half, ell_local = beam_transfer.shape
    base_tiles, ell_tiles = base_half // TILE, ell_local // TILE
    block_ids = lax.axis_index("kl") * ell_tiles + jnp.arange(ell_tiles, dtype=jnp.int32)
    inside = (first_block[:, None] <= block_ids[None, :]).astype(jnp.int32)
    keep_tiles = tile_mask * inside[:, None, :]
    shaped = beam_transfer.reshape(owned_modes, freq_total, base_tiles, TILE, ell_tiles, TILE)
    masked_beam = shaped * keep_tiles.astype(jnp.bfloat16)[:, None, :, None, :, None]
    masked_beam = masked_beam.reshape(owned_modes, freq_total, base_half, ell_local)
    arrived = lax.all_to_all(visibility, "fm", split_axis=1, concat_axis=0, tiled=True)
    partial_value = jnp.einsum(
        "fmrb,mfbl->fmrl",
        lax.all_gather(arrived, "kl", axis=2, tiled=True),
        masked_beam,
        preferred_element_type=jnp.float32,
    )
    sky_sum = lax.psum_scatter(
        partial_value.astype(jnp.bfloat16), "pol", scatter_dimension=2, tiled=True
    ).astype(jnp.float32)
    modes_float = eigen_modes.astype(jnp.float32)
    coeffs = jnp.einsum("mfk,fmrl->mkrl", modes_float, sky_sum, precision=lax.Precision.HIGHEST)
    ratios = signal_noise / (1.0 + signal_noise)
    weighted = (coeffs * ratios[:, :, None, None]).astype(jnp.bfloat16)
    filtered = jnp.einsum(
        "mfk,mkrl->fmrl", eigen_modes, weighted, preferred_element_type=jnp.float32
    ).astype(jnp.bfloat16)
    return lax.all_to_all(filtered, "fm", split_axis=0, concat_axis=1, tiled=True)


def per_device(*args, sizes):
    visibility, beam_transfer = args[0], args[1]
    _, modes, rows, _ = visibility.shape
    fits = (
        sizes["kl"] == 2
        and sizes["pol"] == 2
        and modes == sizes["fm"] == PARTS
        and beam_transfer.shape[0] == 1
        and rows % ROWS == 0
        and rows > ROWS
    )
    if not fits:
        return plain(*args)
    return staged(*args)


def solution(mesh):
    placed = (
        P(("group", "fm"), None, "kl", "pol"),
        P(("group", "fm"), None, "pol", "kl"),
        P("fm", "pol", "kl"),
        P("fm"),
        P(("group", "fm"), None, None),
        P(("group", "fm"), None),
    )
    return jax.shard_map(
        functools.partial(per_device, sizes=dict(mesh.shape)),
        mesh=mesh,
        in_specs=placed,
        out_specs=P(("group", "fm"), None, "pol", "kl"),
        check_vma=False,
    )
```

```python
import functools
import jax
import jax.numpy as jnp
from jax import lax
from jax.experimental import pallas as pl
from jax.experimental.pallas import tpu as pltpu
from jax.sharding import PartitionSpec as P

TILE = 128
PARTS = 4
ROWS = 16
VMEM_LIMIT = 24 * 1024 * 1024


def hold_kernel(where, tiles, starts, beam, modes_ref, held, down_ref, up_ref, mask, sems):
    freq, base, ell = held.shape
    n_modes = modes_ref.shape[1]
    ell_tiles, base_tiles, freqs = ell // TILE, base // TILE, freq // PARTS
    copies = [pltpu.make_async_copy(beam.at[f], held.at[f], sems.at[f]) for f in range(freq)]
    for copy in copies:
        copy.start()
    for b in range(base_tiles):
        for l in range(ell_tiles):
            kept = jnp.where(starts[0] <= where[PARTS + 1] + l, tiles[b, l], 0).astype(jnp.float32)
            mask[b * TILE:(b + 1) * TILE, l * TILE:(l + 1) * TILE] = jnp.full(
                (TILE, TILE), kept, jnp.float32
            ).astype(jnp.bfloat16)
    modes = modes_ref[...]

    def pick(shape, axis):
        big = lax.broadcasted_iota(jnp.int32, shape, axis) // ROWS
        small = lax.broadcasted_iota(jnp.int32, shape, 1 - axis)
        if freq in shape:
            piece, within = big // freqs, big % freqs
            big = within
            for j in range(PARTS):
                big = jnp.where(piece == j, where[j] * freqs + within, big)
        return jnp.where(big == small, 1.0, 0.0).astype(jnp.bfloat16)

    def lane(shape):
        rows = lax.broadcasted_iota(jnp.int32, shape, 0) % ROWS
        columns = lax.broadcasted_iota(jnp.int32, shape, 1) % ROWS
        return rows == columns

    def dot(a, b, dims):
        return lax.dot_general(a, b, (dims, ((), ())), preferred_element_type=jnp.float32)

    tall = dot(pick((n_modes * ROWS, n_modes), 0), modes, ((1,), (1,))).astype(jnp.bfloat16)
    value = dot(tall, pick((freq, freq * ROWS), 1), ((1,), (0,)))
    down_ref[...] = jnp.where(lane(value.shape), value, 0.0).astype(jnp.bfloat16)
    tall = dot(pick((freq * ROWS, freq), 0), modes, ((1,), (0,))).astype(jnp.bfloat16)
    value = dot(tall, pick((n_modes, n_modes * ROWS), 1), ((1,), (0,)))
    up_ref[...] = jnp.where(lane(value.shape), value, 0.0).astype(jnp.bfloat16)
    for f, copy in enumerate(copies):
        copy.wait()
        held[f] = held[f] * mask[...]


def hold(where, tiles, starts, beam, modes):
    freq, base, ell = beam.shape
    size, wide = freq * ROWS, modes.shape[1] * ROWS
    vmem = pl.BlockSpec(memory_space=pltpu.VMEM)
    return pl.pallas_call(
        hold_kernel,
        grid_spec=pltpu.PrefetchScalarGridSpec(
            num_scalar_prefetch=3,
            grid=(),
            in_specs=[pl.BlockSpec(memory_space=pl.ANY), vmem],
            out_specs=[vmem] * 3,
            scratch_shapes=[pltpu.VMEM((base, ell), jnp.bfloat16), pltpu.SemaphoreType.DMA((freq,))],
        ),
        out_shape=[
            pltpu.VMEM(beam.shape, beam.dtype),
            jax.ShapeDtypeStruct((wide, size), jnp.bfloat16),
            jax.ShapeDtypeStruct((size, wide), jnp.bfloat16),
        ],
        compiler_params=pltpu.CompilerParams(vmem_limit_bytes=VMEM_LIMIT),
        cost_estimate=pl.CostEstimate(flops=1024, bytes_accessed=1024, transcendentals=0),
    )(where, tiles, starts, beam, modes)


def project_kernel(where, *refs, piece, blocks):
    count = (len(refs) - 3) // 2
    mine, others = refs[:count], refs[count:2 * count]
    held, stay_ref, leave_ref = refs[2 * count:]
    freqs, rows, _ = stay_ref.shape
    first = where[piece] * freqs
    own = where[PARTS] == 1
    for f in range(freqs):
        a = jnp.concatenate([mine[n][k] for n, k in blocks[f]], axis=0)
        b = jnp.concatenate([others[n][k] for n, k in blocks[f]], axis=0)
        lines = jnp.concatenate([jnp.where(own, a, b), jnp.where(own, b, a)], axis=0)
        value = jnp.dot(lines, held[first + f], preferred_element_type=jnp.float32).astype(jnp.bfloat16)
        stay_ref[f] = value[:rows]
        leave_ref[f] = value[rows:]


def project(where, mine, others, held, piece, blocks):
    ell = held.shape[2]
    rows = sum(mine[n].shape[1] for n, _ in blocks[0])
    vmem = pl.BlockSpec(memory_space=pltpu.VMEM)
    return pl.pallas_call(
        functools.partial(project_kernel, piece=piece, blocks=blocks),
        grid_spec=pltpu.PrefetchScalarGridSpec(
            num_scalar_prefetch=1, grid=(), in_specs=[vmem] * (2 * len(mine) + 1), out_specs=[vmem] * 2
        ),
        out_shape=[jax.ShapeDtypeStruct((len(blocks), rows, ell), jnp.bfloat16)] * 2,
        compiler_params=pltpu.CompilerParams(vmem_limit_bytes=VMEM_LIMIT),
        cost_estimate=pl.CostEstimate(flops=1024, bytes_accessed=1024, transcendentals=0),
    )(where, *mine, *others, pltpu.with_memory_space_constraint(held, pltpu.VMEM))


def contract(modes, skies):
    block = jnp.concatenate([sky[...].reshape(sky.shape[0] * ROWS, sky.shape[2]) for sky in skies], axis=0)
    return jnp.dot(modes, block, preferred_element_type=jnp.float32)


def reduce_kernel(modes_ref, *refs):
    out = refs[-1]
    out[...] = contract(modes_ref[...], refs[:-1]).astype(out.dtype).reshape(out.shape)


def by_rows(count, ell, first=0):
    return pl.BlockSpec((count, ROWS, ell), lambda g: (0, g + first // ROWS, 0))


def fixed(shape):
    return pl.BlockSpec(shape, lambda g: (0,) * len(shape))


def sky_specs(skies, first):
    return [by_rows(sky.shape[0], sky.shape[2], low) for sky, low in zip(skies, first)]


def reduce(modes, skies, first, n_modes, dtype=jnp.bfloat16):
    _, rows, ell = skies[-1].shape
    return pl.pallas_call(
        reduce_kernel,
        grid=(rows // ROWS,),
        in_specs=[fixed(modes.shape)] + sky_specs(skies, first),
        out_specs=by_rows(n_modes, ell),
        out_shape=jax.ShapeDtypeStruct((n_modes, rows, ell), dtype),
        compiler_params=pltpu.CompilerParams(vmem_limit_bytes=VMEM_LIMIT),
        cost_estimate=pl.CostEstimate(flops=1024, bytes_accessed=1024, transcendentals=0),
    )(modes, *skies)


def restore_kernel(up_ref, ratio_ref, kept_ref, came_ref, *outs, spots):
    n_modes, _, ell = came_ref.shape
    freqs = up_ref.shape[0] // ROWS // PARTS
    total = kept_ref[...] + came_ref[...].astype(jnp.float32)
    weighted = (total * ratio_ref[...]).astype(jnp.bfloat16).reshape(n_modes * ROWS, ell)
    for (j, low, high), out in zip(spots, outs):
        modes = up_ref[(j * freqs + low) * ROWS:(j * freqs + high) * ROWS, :]
        value = jnp.dot(modes, weighted, preferred_element_type=jnp.float32)
        out[...] = value.astype(jnp.bfloat16).reshape(out.shape)


def restore(kept, came, ratios, up, spots):
    n_modes, rows, ell = came.shape
    return pl.pallas_call(
        functools.partial(restore_kernel, spots=spots),
        grid=(rows // ROWS,),
        in_specs=[fixed(up.shape), fixed(ratios.shape)] + [by_rows(n_modes, ell)] * 2,
        out_specs=[by_rows(high - low, ell) for _, low, high in spots],
        out_shape=[jax.ShapeDtypeStruct((high - low, rows, ell), jnp.bfloat16) for _, low, high in spots],
        compiler_params=pltpu.CompilerParams(vmem_limit_bytes=VMEM_LIMIT),
        cost_estimate=pl.CostEstimate(flops=1024, bytes_accessed=1024, transcendentals=0),
    )(up, ratios, kept, came)


def place_kernel(where, *refs, spots, first):
    count = len(spots)
    pieces, out, sems = refs[:count], refs[-2], refs[-1]
    rows = pieces[0].shape[1]
    copies = [
        pltpu.make_async_copy(pieces[n], out.at[low:high, where[j], first:first + rows, :], sems.at[n])
        for n, (j, low, high) in enumerate(spots)
    ]
    for copy in copies:
        copy.start()
    for copy in copies:
        copy.wait()


def place(where, pieces, spots, first, shape, into=None):
    count = len(spots)
    extra = [] if into is None else [into]
    anywhere = pl.BlockSpec(memory_space=pl.ANY)
    return pl.pallas_call(
        functools.partial(place_kernel, spots=spots, first=first),
        grid_spec=pltpu.PrefetchScalarGridSpec(
            num_scalar_prefetch=1,
            grid=(),
            in_specs=[pl.BlockSpec(memory_space=pltpu.VMEM)] * count + [anywhere] * len(extra),
            out_specs=anywhere,
            scratch_shapes=[pltpu.SemaphoreType.DMA((count,))],
        ),
        out_shape=jax.ShapeDtypeStruct(shape, jnp.bfloat16),
        input_output_aliases={count + 1: 0} if extra else {},
        compiler_params=pltpu.CompilerParams(vmem_limit_bytes=VMEM_LIMIT),
        cost_estimate=pl.CostEstimate(flops=1024, bytes_accessed=1024, transcendentals=0),
    )(where, *pieces, *extra)


def staged(visibility, beam_transfer, tile_mask, first_block, eigen_modes, signal_noise):
    freqs, parts, rows_all, base = visibility.shape
    _, freq_total, _, ell = beam_transfer.shape
    n_modes = eigen_modes.shape[2]
    ell_tiles = ell // TILE
    z, x, p = lax.axis_index("fm"), lax.axis_index("kl"), lax.axis_index("pol")
    other = [(0, 1), (1, 0)]

    def along_z(value, j):
        return lax.ppermute(value, "fm", [(i, i ^ j) for i in range(parts)])

    def along_x(value):
        return lax.ppermute(value, "kl", other)

    def cut(j, first, rows):
        return lax.dynamic_slice(visibility, (0, z ^ j, first, 0), (freqs, 1, rows, base)).reshape(freqs, rows, base)

    index = jnp.arange(parts + 2, dtype=jnp.int32)
    where = jnp.where(
        index < parts, z ^ index, jnp.where(index == parts, (x == p).astype(jnp.int32), x * ell_tiles)
    ).astype(jnp.int32)
    ratio = signal_noise[0] / (1.0 + signal_noise[0])
    ratios = jnp.broadcast_to(ratio[:, None, None], (n_modes, 1, ell))
    beam = beam_transfer.reshape(freq_total, base, ell)
    shape = (freqs, parts, rows_all, ell)

    fence = lax.optimization_barrier
    most, half = rows_all - ROWS, freqs // 2
    plain_blocks = [[(0, f)] for f in range(freqs)]
    own_blocks = [[(f // half, f % half)] for f in range(freqs)]
    near_blocks = [
        [(0, freqs + f) if f < half else (1, f - half), (1, half + f)] for f in range(freqs)
    ]
    groups = [cut(1, n * ROWS, ROWS) for n in range(3)]
    near_1 = jnp.concatenate([groups[0], groups[1][:half]], axis=0)
    near_2 = jnp.concatenate([groups[1][half:], groups[2]], axis=0)
    near_1 = along_z(near_1, 1)
    a_3, a_2 = along_z(cut(3, 0, ROWS), 3), along_z(cut(2, 0, ROWS), 2)
    mine = [cut(0, 0, rows_all)[n:n + half] for n in (0, half)]
    others = [along_x(part) for part in mine]
    b_2, b_3 = cut(2, ROWS, most), cut(3, ROWS, most)
    held, down, up = hold(where, tile_mask[0], first_block, beam, eigen_modes[0])
    a_3, a_2, near_1, near_2, b_2, b_3, others, down, up = fence(
        (a_3, a_2, near_1, near_2, b_2, b_3, others, down, up)
    )
    b_2, near_2 = along_z(b_2, 2), along_z(near_2, 1)
    own = project(where, mine, others, held, 0, own_blocks)
    x_near = along_x(near_1)
    skies = [own, project(where, [near_1], [x_near], held, 1, plain_blocks)]
    skies += [project(where, [part], [along_x(part)], held, j, plain_blocks) for j, part in ((2, a_2), (3, a_3))]
    gone = reduce(down, [leave for _, leave in skies], (0, 0, 0, 0), n_modes)
    stay_a = [stay for stay, _ in skies]
    b_2, near_2, b_3, stay_a, x_near, gone = fence((b_2, near_2, b_3, stay_a, x_near, gone))
    x_2, x_near_2 = along_x(b_2), along_x(near_2)
    b_3 = along_z(b_3, 3)
    kept = reduce(down, stay_a, (0, 0, 0, 0), n_modes, jnp.float32)
    spots_a = [(2, 0, freqs), (3, 0, half), (3, half, freqs), (1, 0, freqs), (0, 0, freqs)]
    outs = restore(kept, lax.ppermute(gone, "pol", other), ratios, up, spots_a)
    near = project(where, [near_1, near_2], [x_near, x_near_2], held, 1, near_blocks)
    x_2, b_2, b_3, outs, near = fence((x_2, b_2, b_3, outs, near))
    back_2, back_3, back_1 = along_z(outs[0], 2), along_z(outs[1], 3), along_z(outs[3], 1)
    x_3 = along_x(b_3)
    skies = [own, near]
    skies += [project(where, [part], [x], held, j, plain_blocks) for j, part, x in ((2, b_2, x_2), (3, b_3, x_3))]
    gone = reduce(down, [leave for _, leave in skies], (ROWS, 0, 0, 0), n_modes)
    kept = reduce(down, [stay for stay, _ in skies], (ROWS, 0, 0, 0), n_modes, jnp.float32)
    back_2, back_3, back_1, late, here, kept, gone = fence((back_2, back_3, back_1, outs[2], outs[4], kept, gone))
    late = along_z(late, 3)
    came = lax.ppermute(gone, "pol", other)
    spots_b = [(j, 0, freqs) for j in (1, 2, 3, 0)]
    outs = restore(kept, came, ratios, up, spots_b)
    outs, late = fence((outs, late))
    back = [along_z(outs[n], spots_b[n][0]) for n in range(3)]
    result = place(where, [back_2, back_3, late, back_1, here], spots_a, 0, shape)
    result = place(where, [outs[3], back[0]], [spots_b[3], spots_b[0]], ROWS, shape, into=result)
    return place(where, back[1:], spots_b[1:3], ROWS, shape, into=result)


def plain(visibility, beam_transfer, tile_mask, first_block, eigen_modes, signal_noise):
    owned_modes, freq_total, base_half, ell_local = beam_transfer.shape
    base_tiles, ell_tiles = base_half // TILE, ell_local // TILE
    block_ids = lax.axis_index("kl") * ell_tiles + jnp.arange(ell_tiles, dtype=jnp.int32)
    inside = (first_block[:, None] <= block_ids[None, :]).astype(jnp.int32)
    keep_tiles = tile_mask * inside[:, None, :]
    shaped = beam_transfer.reshape(owned_modes, freq_total, base_tiles, TILE, ell_tiles, TILE)
    masked_beam = shaped * keep_tiles.astype(jnp.bfloat16)[:, None, :, None, :, None]
    masked_beam = masked_beam.reshape(owned_modes, freq_total, base_half, ell_local)
    arrived = lax.all_to_all(visibility, "fm", split_axis=1, concat_axis=0, tiled=True)
    partial_value = jnp.einsum(
        "fmrb,mfbl->fmrl",
        lax.all_gather(arrived, "kl", axis=2, tiled=True),
        masked_beam,
        preferred_element_type=jnp.float32,
    )
    sky_sum = lax.psum_scatter(
        partial_value.astype(jnp.bfloat16), "pol", scatter_dimension=2, tiled=True
    ).astype(jnp.float32)
    modes_float = eigen_modes.astype(jnp.float32)
    coeffs = jnp.einsum("mfk,fmrl->mkrl", modes_float, sky_sum, precision=lax.Precision.HIGHEST)
    ratios = signal_noise / (1.0 + signal_noise)
    weighted = (coeffs * ratios[:, :, None, None]).astype(jnp.bfloat16)
    filtered = jnp.einsum(
        "mfk,mkrl->fmrl", eigen_modes, weighted, preferred_element_type=jnp.float32
    ).astype(jnp.bfloat16)
    return lax.all_to_all(filtered, "fm", split_axis=0, concat_axis=1, tiled=True)


def per_device(*args, sizes):
    visibility, beam_transfer = args[0], args[1]
    _, modes, rows, _ = visibility.shape
    fits = (
        sizes["kl"] == 2
        and sizes["pol"] == 2
        and modes == sizes["fm"] == PARTS
        and beam_transfer.shape[0] == 1
        and rows == 3 * ROWS
        and visibility.shape[0] % 2 == 0
    )
    if not fits:
        return plain(*args)
    return staged(*args)


def solution(mesh):
    placed = (
        P(("group", "fm"), None, "kl", "pol"),
        P(("group", "fm"), None, "pol", "kl"),
        P("fm", "pol", "kl"),
        P("fm"),
        P(("group", "fm"), None, None),
        P(("group", "fm"), None),
    )
    return jax.shard_map(
        functools.partial(per_device, sizes=dict(mesh.shape)),
        mesh=mesh,
        in_specs=placed,
        out_specs=P(("group", "fm"), None, "pol", "kl"),
        check_vma=False,
    )
```

```python
import functools
import jax
import jax.numpy as jnp
from jax import lax
from jax.experimental import pallas as pl
from jax.experimental.pallas import tpu as pltpu
from jax.sharding import PartitionSpec as P

TILE = 128
PARTS = 4
ROWS = 16
VMEM_LIMIT = 24 * 1024 * 1024


def hold_kernel(where, tiles, starts, beam, modes_ref, held, down_ref, up_ref, mask, sems):
    freq, base, ell = held.shape
    n_modes = modes_ref.shape[1]
    ell_tiles, base_tiles, freqs = ell // TILE, base // TILE, freq // PARTS
    copies = [pltpu.make_async_copy(beam.at[f], held.at[f], sems.at[f]) for f in range(freq)]
    for copy in copies:
        copy.start()
    for b in range(base_tiles):
        for l in range(ell_tiles):
            kept = jnp.where(starts[0] <= where[PARTS + 1] + l, tiles[b, l], 0).astype(jnp.float32)
            mask[b * TILE:(b + 1) * TILE, l * TILE:(l + 1) * TILE] = jnp.full(
                (TILE, TILE), kept, jnp.float32
            ).astype(jnp.bfloat16)
    modes = modes_ref[...]

    def pick(shape, axis):
        big = lax.broadcasted_iota(jnp.int32, shape, axis) // ROWS
        small = lax.broadcasted_iota(jnp.int32, shape, 1 - axis)
        if freq in shape:
            piece, within = big // freqs, big % freqs
            big = within
            for j in range(PARTS):
                big = jnp.where(piece == j, where[j] * freqs + within, big)
        return jnp.where(big == small, 1.0, 0.0).astype(jnp.bfloat16)

    def lane(shape):
        rows = lax.broadcasted_iota(jnp.int32, shape, 0) % ROWS
        columns = lax.broadcasted_iota(jnp.int32, shape, 1) % ROWS
        return rows == columns

    def dot(a, b, dims):
        return lax.dot_general(a, b, (dims, ((), ())), preferred_element_type=jnp.float32)

    tall = dot(pick((n_modes * ROWS, n_modes), 0), modes, ((1,), (1,))).astype(jnp.bfloat16)
    value = dot(tall, pick((freq, freq * ROWS), 1), ((1,), (0,)))
    down_ref[...] = jnp.where(lane(value.shape), value, 0.0).astype(jnp.bfloat16)
    tall = dot(pick((freq * ROWS, freq), 0), modes, ((1,), (0,))).astype(jnp.bfloat16)
    value = dot(tall, pick((n_modes, n_modes * ROWS), 1), ((1,), (0,)))
    up_ref[...] = jnp.where(lane(value.shape), value, 0.0).astype(jnp.bfloat16)
    for f, copy in enumerate(copies):
        copy.wait()
        held[f] = held[f] * mask[...]


def hold(where, tiles, starts, beam, modes):
    freq, base, ell = beam.shape
    size, wide = freq * ROWS, modes.shape[1] * ROWS
    vmem = pl.BlockSpec(memory_space=pltpu.VMEM)
    return pl.pallas_call(
        hold_kernel,
        grid_spec=pltpu.PrefetchScalarGridSpec(
            num_scalar_prefetch=3,
            grid=(),
            in_specs=[pl.BlockSpec(memory_space=pl.ANY), vmem],
            out_specs=[vmem] * 3,
            scratch_shapes=[pltpu.VMEM((base, ell), jnp.bfloat16), pltpu.SemaphoreType.DMA((freq,))],
        ),
        out_shape=[
            pltpu.VMEM(beam.shape, beam.dtype),
            jax.ShapeDtypeStruct((wide, size), jnp.bfloat16),
            jax.ShapeDtypeStruct((size, wide), jnp.bfloat16),
        ],
        compiler_params=pltpu.CompilerParams(vmem_limit_bytes=VMEM_LIMIT),
        cost_estimate=pl.CostEstimate(flops=1024, bytes_accessed=1024, transcendentals=0),
    )(where, tiles, starts, beam, modes)


def project_kernel(where, *refs, piece, blocks):
    count = (len(refs) - 3) // 2
    mine, others = refs[:count], refs[count:2 * count]
    held, stay_ref, leave_ref = refs[2 * count:]
    freqs, rows, _ = stay_ref.shape
    first = where[piece] * freqs
    own = where[PARTS] == 1
    for f in range(freqs):
        a = jnp.concatenate([mine[n][k] for n, k in blocks[f]], axis=0)
        b = jnp.concatenate([others[n][k] for n, k in blocks[f]], axis=0)
        lines = jnp.concatenate([jnp.where(own, a, b), jnp.where(own, b, a)], axis=0)
        value = jnp.dot(lines, held[first + f], preferred_element_type=jnp.float32).astype(jnp.bfloat16)
        stay_ref[f] = value[:rows]
        leave_ref[f] = value[rows:]


def project(where, mine, others, held, piece, blocks):
    ell = held.shape[2]
    rows = sum(mine[n].shape[1] for n, _ in blocks[0])
    vmem = pl.BlockSpec(memory_space=pltpu.VMEM)
    return pl.pallas_call(
        functools.partial(project_kernel, piece=piece, blocks=blocks),
        grid_spec=pltpu.PrefetchScalarGridSpec(
            num_scalar_prefetch=1, grid=(), in_specs=[vmem] * (2 * len(mine) + 1), out_specs=[vmem] * 2
        ),
        out_shape=[jax.ShapeDtypeStruct((len(blocks), rows, ell), jnp.bfloat16)] * 2,
        compiler_params=pltpu.CompilerParams(vmem_limit_bytes=VMEM_LIMIT),
        cost_estimate=pl.CostEstimate(flops=1024, bytes_accessed=1024, transcendentals=0),
    )(where, *mine, *others, pltpu.with_memory_space_constraint(held, pltpu.VMEM))


def contract(modes, skies):
    block = jnp.concatenate([sky[...].reshape(sky.shape[0] * ROWS, sky.shape[2]) for sky in skies], axis=0)
    return jnp.dot(modes, block, preferred_element_type=jnp.float32)


def reduce_kernel(modes_ref, *refs):
    out = refs[-1]
    out[...] = contract(modes_ref[...], refs[:-1]).astype(out.dtype).reshape(out.shape)


def by_rows(count, ell, first=0):
    return pl.BlockSpec((count, ROWS, ell), lambda g: (0, g + first // ROWS, 0))


def fixed(shape):
    return pl.BlockSpec(shape, lambda g: (0,) * len(shape))


def sky_specs(skies, first):
    return [by_rows(sky.shape[0], sky.shape[2], low) for sky, low in zip(skies, first)]


def reduce(modes, skies, first, n_modes, dtype=jnp.bfloat16):
    _, rows, ell = skies[-1].shape
    return pl.pallas_call(
        reduce_kernel,
        grid=(rows // ROWS,),
        in_specs=[fixed(modes.shape)] + sky_specs(skies, first),
        out_specs=by_rows(n_modes, ell),
        out_shape=jax.ShapeDtypeStruct((n_modes, rows, ell), dtype),
        compiler_params=pltpu.CompilerParams(vmem_limit_bytes=VMEM_LIMIT),
        cost_estimate=pl.CostEstimate(flops=1024, bytes_accessed=1024, transcendentals=0),
    )(modes, *skies)


def restore_kernel(up_ref, ratio_ref, kept_ref, came_ref, *outs, spots):
    n_modes, _, ell = came_ref.shape
    freqs = up_ref.shape[0] // ROWS // PARTS
    total = kept_ref[...] + came_ref[...].astype(jnp.float32)
    weighted = (total * ratio_ref[...]).astype(jnp.bfloat16).reshape(n_modes * ROWS, ell)
    for (j, low, high), out in zip(spots, outs):
        modes = up_ref[(j * freqs + low) * ROWS:(j * freqs + high) * ROWS, :]
        value = jnp.dot(modes, weighted, preferred_element_type=jnp.float32)
        out[...] = value.astype(jnp.bfloat16).reshape(out.shape)


def restore(kept, came, ratios, up, spots):
    n_modes, rows, ell = came.shape
    return pl.pallas_call(
        functools.partial(restore_kernel, spots=spots),
        grid=(rows // ROWS,),
        in_specs=[fixed(up.shape), fixed(ratios.shape)] + [by_rows(n_modes, ell)] * 2,
        out_specs=[by_rows(high - low, ell) for _, low, high in spots],
        out_shape=[jax.ShapeDtypeStruct((high - low, rows, ell), jnp.bfloat16) for _, low, high in spots],
        compiler_params=pltpu.CompilerParams(vmem_limit_bytes=VMEM_LIMIT),
        cost_estimate=pl.CostEstimate(flops=1024, bytes_accessed=1024, transcendentals=0),
    )(up, ratios, kept, came)


def place_kernel(where, *refs, spots, first):
    count = len(spots)
    pieces, out, sems = refs[:count], refs[-2], refs[-1]
    rows = pieces[0].shape[1]
    copies = [
        pltpu.make_async_copy(pieces[n], out.at[low:high, where[j], first:first + rows, :], sems.at[n])
        for n, (j, low, high) in enumerate(spots)
    ]
    for copy in copies:
        copy.start()
    for copy in copies:
        copy.wait()


def place(where, pieces, spots, first, shape, into=None):
    count = len(spots)
    extra = [] if into is None else [into]
    anywhere = pl.BlockSpec(memory_space=pl.ANY)
    return pl.pallas_call(
        functools.partial(place_kernel, spots=spots, first=first),
        grid_spec=pltpu.PrefetchScalarGridSpec(
            num_scalar_prefetch=1,
            grid=(),
            in_specs=[pl.BlockSpec(memory_space=pltpu.VMEM)] * count + [anywhere] * len(extra),
            out_specs=anywhere,
            scratch_shapes=[pltpu.SemaphoreType.DMA((count,))],
        ),
        out_shape=jax.ShapeDtypeStruct(shape, jnp.bfloat16),
        input_output_aliases={count + 1: 0} if extra else {},
        compiler_params=pltpu.CompilerParams(vmem_limit_bytes=VMEM_LIMIT),
        cost_estimate=pl.CostEstimate(flops=1024, bytes_accessed=1024, transcendentals=0),
    )(where, *pieces, *extra)


def staged(visibility, beam_transfer, tile_mask, first_block, eigen_modes, signal_noise):
    freqs, parts, rows_all, base = visibility.shape
    _, freq_total, _, ell = beam_transfer.shape
    n_modes = eigen_modes.shape[2]
    ell_tiles = ell // TILE
    z, x, p = lax.axis_index("fm"), lax.axis_index("kl"), lax.axis_index("pol")
    other = [(0, 1), (1, 0)]

    def along_z(value, j):
        return lax.ppermute(value, "fm", [(i, i ^ j) for i in range(parts)])

    def along_x(value):
        return lax.ppermute(value, "kl", other)

    def cut(j, first, rows):
        return lax.dynamic_slice(visibility, (0, z ^ j, first, 0), (freqs, 1, rows, base)).reshape(freqs, rows, base)

    index = jnp.arange(parts + 2, dtype=jnp.int32)
    where = jnp.where(
        index < parts, z ^ index, jnp.where(index == parts, (x == p).astype(jnp.int32), x * ell_tiles)
    ).astype(jnp.int32)
    ratio = signal_noise[0] / (1.0 + signal_noise[0])
    ratios = jnp.broadcast_to(ratio[:, None, None], (n_modes, 1, ell))
    beam = beam_transfer.reshape(freq_total, base, ell)
    shape = (freqs, parts, rows_all, ell)

    fence = lax.optimization_barrier
    most, half = rows_all - ROWS, freqs // 2
    blocks = [[(0, f)] for f in range(freqs)]
    halves = [[(f // half, f % half)] for f in range(freqs)]
    a = {j: along_z(cut(j, 0, ROWS), j) for j in (3, 2, 1)}
    mine = [cut(0, 0, rows_all)[n:n + half] for n in (0, half)]
    others = [along_x(part) for part in mine]
    b = {j: cut(j, ROWS, most) for j in (1, 2, 3)}
    held, down, up = hold(where, tile_mask[0], first_block, beam, eigen_modes[0])
    (a[3], a[2], a[1]), b, others, down, up = fence(((a[3], a[2], a[1]), b, others, down, up))
    b[1], b[2] = along_z(b[1], 1), along_z(b[2], 2)
    own = project(where, mine, others, held, 0, halves)
    skies = [own] + [project(where, [a[j]], [along_x(a[j])], held, j, blocks) for j in (1, 2, 3)]
    gone = reduce(down, [leave for _, leave in skies], (0, 0, 0, 0), n_modes)
    stay_a = [stay for stay, _ in skies]
    (b[2], b[1]), b[3], stay_a, gone = fence(((b[2], b[1]), b[3], stay_a, gone))
    x_2, x_1 = along_x(b[2]), along_x(b[1])
    b[3] = along_z(b[3], 3)
    kept = reduce(down, stay_a, (0, 0, 0, 0), n_modes, jnp.float32)
    spots = [(j, 0, freqs) for j in (1, 2, 3, 0)]
    outs = restore(kept, lax.ppermute(gone, "pol", other), ratios, up, spots)
    near = project(where, [b[1]], [x_1], held, 1, blocks)
    x_2, b, outs, near = fence((x_2, b, outs, near))
    first = {j: along_z(outs[j - 1], j) for j in (1, 2, 3)}
    first[0] = outs[3]
    x_3 = along_x(b[3])
    skies = [own, near] + [project(where, [b[j]], [x], held, j, blocks) for j, x in ((2, x_2), (3, x_3))]
    gone = reduce(down, [leave for _, leave in skies], (ROWS, 0, 0, 0), n_modes)
    kept = reduce(down, [stay for stay, _ in skies], (ROWS, 0, 0, 0), n_modes, jnp.float32)
    (first[2], first[3], first[1]), first[0], kept, gone = fence(
        ((first[2], first[3], first[1]), first[0], kept, gone)
    )
    outs = fence(restore(kept, lax.ppermute(gone, "pol", other), ratios, up, spots))
    back = [along_z(outs[j - 1], j) for j in (1, 2, 3)]
    result = place(where, [first[j] for j in (1, 2, 3, 0)], spots, 0, shape)
    result = place(where, [outs[3], back[0]], [spots[3], spots[0]], ROWS, shape, into=result)
    return place(where, back[1:], spots[1:3], ROWS, shape, into=result)


def plain(visibility, beam_transfer, tile_mask, first_block, eigen_modes, signal_noise):
    owned_modes, freq_total, base_half, ell_local = beam_transfer.shape
    base_tiles, ell_tiles = base_half // TILE, ell_local // TILE
    block_ids = lax.axis_index("kl") * ell_tiles + jnp.arange(ell_tiles, dtype=jnp.int32)
    inside = (first_block[:, None] <= block_ids[None, :]).astype(jnp.int32)
    keep_tiles = tile_mask * inside[:, None, :]
    shaped = beam_transfer.reshape(owned_modes, freq_total, base_tiles, TILE, ell_tiles, TILE)
    masked_beam = shaped * keep_tiles.astype(jnp.bfloat16)[:, None, :, None, :, None]
    masked_beam = masked_beam.reshape(owned_modes, freq_total, base_half, ell_local)
    arrived = lax.all_to_all(visibility, "fm", split_axis=1, concat_axis=0, tiled=True)
    partial_value = jnp.einsum(
        "fmrb,mfbl->fmrl",
        lax.all_gather(arrived, "kl", axis=2, tiled=True),
        masked_beam,
        preferred_element_type=jnp.float32,
    )
    sky_sum = lax.psum_scatter(
        partial_value.astype(jnp.bfloat16), "pol", scatter_dimension=2, tiled=True
    ).astype(jnp.float32)
    modes_float = eigen_modes.astype(jnp.float32)
    coeffs = jnp.einsum("mfk,fmrl->mkrl", modes_float, sky_sum, precision=lax.Precision.HIGHEST)
    ratios = signal_noise / (1.0 + signal_noise)
    weighted = (coeffs * ratios[:, :, None, None]).astype(jnp.bfloat16)
    filtered = jnp.einsum(
        "mfk,mkrl->fmrl", eigen_modes, weighted, preferred_element_type=jnp.float32
    ).astype(jnp.bfloat16)
    return lax.all_to_all(filtered, "fm", split_axis=0, concat_axis=1, tiled=True)


def per_device(*args, sizes):
    visibility, beam_transfer = args[0], args[1]
    _, modes, rows, _ = visibility.shape
    fits = (
        sizes["kl"] == 2
        and sizes["pol"] == 2
        and modes == sizes["fm"] == PARTS
        and beam_transfer.shape[0] == 1
        and rows == 3 * ROWS
        and visibility.shape[0] % 2 == 0
    )
    if not fits:
        return plain(*args)
    return staged(*args)


def solution(mesh):
    placed = (
        P(("group", "fm"), None, "kl", "pol"),
        P(("group", "fm"), None, "pol", "kl"),
        P("fm", "pol", "kl"),
        P("fm"),
        P(("group", "fm"), None, None),
        P(("group", "fm"), None),
    )
    return jax.shard_map(
        functools.partial(per_device, sizes=dict(mesh.shape)),
        mesh=mesh,
        in_specs=placed,
        out_specs=P(("group", "fm"), None, "pol", "kl"),
        check_vma=False,
    )
```

```python
import functools
import jax
import jax.numpy as jnp
from jax import lax
from jax.experimental import pallas as pl
from jax.experimental.pallas import tpu as pltpu
from jax.sharding import PartitionSpec as P

TILE = 128
PARTS = 4
ROWS = 16
VMEM_LIMIT = 24 * 1024 * 1024


def hold_kernel(where, tiles, starts, beam, modes_ref, held, down_ref, up_ref, mask, sems):
    freq, base, ell = held.shape
    n_modes = modes_ref.shape[1]
    ell_tiles, base_tiles, freqs = ell // TILE, base // TILE, freq // PARTS
    copies = [pltpu.make_async_copy(beam.at[f], held.at[f], sems.at[f]) for f in range(freq)]
    for copy in copies:
        copy.start()
    for b in range(base_tiles):
        for l in range(ell_tiles):
            kept = jnp.where(starts[0] <= where[PARTS + 1] + l, tiles[b, l], 0).astype(jnp.float32)
            mask[b * TILE:(b + 1) * TILE, l * TILE:(l + 1) * TILE] = jnp.full(
                (TILE, TILE), kept, jnp.float32
            ).astype(jnp.bfloat16)
    modes = modes_ref[...]

    def pick(shape, axis):
        big = lax.broadcasted_iota(jnp.int32, shape, axis) // ROWS
        small = lax.broadcasted_iota(jnp.int32, shape, 1 - axis)
        if freq in shape:
            piece, within = big // freqs, big % freqs
            big = within
            for j in range(PARTS):
                big = jnp.where(piece == j, where[j] * freqs + within, big)
        return jnp.where(big == small, 1.0, 0.0).astype(jnp.bfloat16)

    def lane(shape):
        rows = lax.broadcasted_iota(jnp.int32, shape, 0) % ROWS
        columns = lax.broadcasted_iota(jnp.int32, shape, 1) % ROWS
        return rows == columns

    def dot(a, b, dims):
        return lax.dot_general(a, b, (dims, ((), ())), preferred_element_type=jnp.float32)

    tall = dot(pick((n_modes * ROWS, n_modes), 0), modes, ((1,), (1,))).astype(jnp.bfloat16)
    value = dot(tall, pick((freq, freq * ROWS), 1), ((1,), (0,)))
    down_ref[...] = jnp.where(lane(value.shape), value, 0.0).astype(jnp.bfloat16)
    tall = dot(pick((freq * ROWS, freq), 0), modes, ((1,), (0,))).astype(jnp.bfloat16)
    value = dot(tall, pick((n_modes, n_modes * ROWS), 1), ((1,), (0,)))
    up_ref[...] = jnp.where(lane(value.shape), value, 0.0).astype(jnp.bfloat16)
    for f, copy in enumerate(copies):
        copy.wait()
        held[f] = held[f] * mask[...]


def hold(where, tiles, starts, beam, modes):
    freq, base, ell = beam.shape
    size, wide = freq * ROWS, modes.shape[1] * ROWS
    vmem = pl.BlockSpec(memory_space=pltpu.VMEM)
    return pl.pallas_call(
        hold_kernel,
        grid_spec=pltpu.PrefetchScalarGridSpec(
            num_scalar_prefetch=3,
            grid=(),
            in_specs=[pl.BlockSpec(memory_space=pl.ANY), vmem],
            out_specs=[vmem] * 3,
            scratch_shapes=[pltpu.VMEM((base, ell), jnp.bfloat16), pltpu.SemaphoreType.DMA((freq,))],
        ),
        out_shape=[
            pltpu.VMEM(beam.shape, beam.dtype),
            jax.ShapeDtypeStruct((wide, size), jnp.bfloat16),
            jax.ShapeDtypeStruct((size, wide), jnp.bfloat16),
        ],
        compiler_params=pltpu.CompilerParams(vmem_limit_bytes=VMEM_LIMIT),
        cost_estimate=pl.CostEstimate(flops=1024, bytes_accessed=1024, transcendentals=0),
    )(where, tiles, starts, beam, modes)


def project_kernel(where, *refs, piece, blocks):
    count = (len(refs) - 3) // 2
    mine, others = refs[:count], refs[count:2 * count]
    held, stay_ref, leave_ref = refs[2 * count:]
    freqs, rows, _ = stay_ref.shape
    first = where[piece] * freqs
    own = where[PARTS] == 1
    for f in range(freqs):
        a = jnp.concatenate([mine[n][k] for n, k in blocks[f]], axis=0)
        b = jnp.concatenate([others[n][k] for n, k in blocks[f]], axis=0)
        lines = jnp.concatenate([jnp.where(own, a, b), jnp.where(own, b, a)], axis=0)
        value = jnp.dot(lines, held[first + f], preferred_element_type=jnp.float32).astype(jnp.bfloat16)
        stay_ref[f] = value[:rows]
        leave_ref[f] = value[rows:]


def project(where, mine, others, held, piece, blocks):
    ell = held.shape[2]
    rows = sum(mine[n].shape[1] for n, _ in blocks[0])
    vmem = pl.BlockSpec(memory_space=pltpu.VMEM)
    return pl.pallas_call(
        functools.partial(project_kernel, piece=piece, blocks=blocks),
        grid_spec=pltpu.PrefetchScalarGridSpec(
            num_scalar_prefetch=1, grid=(), in_specs=[vmem] * (2 * len(mine) + 1), out_specs=[vmem] * 2
        ),
        out_shape=[jax.ShapeDtypeStruct((len(blocks), rows, ell), jnp.bfloat16)] * 2,
        compiler_params=pltpu.CompilerParams(vmem_limit_bytes=VMEM_LIMIT),
        cost_estimate=pl.CostEstimate(flops=1024, bytes_accessed=1024, transcendentals=0),
    )(where, *mine, *others, pltpu.with_memory_space_constraint(held, pltpu.VMEM))


def contract(modes, skies):
    block = jnp.concatenate([sky[...].reshape(sky.shape[0] * ROWS, sky.shape[2]) for sky in skies], axis=0)
    return jnp.dot(modes, block, preferred_element_type=jnp.float32)


def reduce_kernel(modes_ref, *refs):
    out = refs[-1]
    out[...] = contract(modes_ref[...], refs[:-1]).astype(out.dtype).reshape(out.shape)


def by_rows(count, ell, first=0):
    return pl.BlockSpec((count, ROWS, ell), lambda g: (0, g + first // ROWS, 0))


def fixed(shape):
    return pl.BlockSpec(shape, lambda g: (0,) * len(shape))


def sky_specs(skies, first):
    return [by_rows(sky.shape[0], sky.shape[2], low) for sky, low in zip(skies, first)]


def reduce(modes, skies, first, n_modes, dtype=jnp.bfloat16):
    _, rows, ell = skies[-1].shape
    return pl.pallas_call(
        reduce_kernel,
        grid=(rows // ROWS,),
        in_specs=[fixed(modes.shape)] + sky_specs(skies, first),
        out_specs=by_rows(n_modes, ell),
        out_shape=jax.ShapeDtypeStruct((n_modes, rows, ell), dtype),
        compiler_params=pltpu.CompilerParams(vmem_limit_bytes=VMEM_LIMIT),
        cost_estimate=pl.CostEstimate(flops=1024, bytes_accessed=1024, transcendentals=0),
    )(modes, *skies)


def restore_kernel(up_ref, ratio_ref, kept_ref, came_ref, *outs, spots):
    n_modes, _, ell = came_ref.shape
    freqs = up_ref.shape[0] // ROWS // PARTS
    total = kept_ref[...] + came_ref[...].astype(jnp.float32)
    weighted = (total * ratio_ref[...]).astype(jnp.bfloat16).reshape(n_modes * ROWS, ell)
    for (j, low, high), out in zip(spots, outs):
        modes = up_ref[(j * freqs + low) * ROWS:(j * freqs + high) * ROWS, :]
        value = jnp.dot(modes, weighted, preferred_element_type=jnp.float32)
        out[...] = value.astype(jnp.bfloat16).reshape(out.shape)


def restore(kept, came, ratios, up, spots):
    n_modes, rows, ell = came.shape
    return pl.pallas_call(
        functools.partial(restore_kernel, spots=spots),
        grid=(rows // ROWS,),
        in_specs=[fixed(up.shape), fixed(ratios.shape)] + [by_rows(n_modes, ell)] * 2,
        out_specs=[by_rows(high - low, ell) for _, low, high in spots],
        out_shape=[jax.ShapeDtypeStruct((high - low, rows, ell), jnp.bfloat16) for _, low, high in spots],
        compiler_params=pltpu.CompilerParams(vmem_limit_bytes=VMEM_LIMIT),
        cost_estimate=pl.CostEstimate(flops=1024, bytes_accessed=1024, transcendentals=0),
    )(up, ratios, kept, came)


def place_kernel(where, *refs, spots, first):
    count = len(spots)
    pieces, out, sems = refs[:count], refs[-2], refs[-1]
    rows = pieces[0].shape[1]
    copies = [
        pltpu.make_async_copy(pieces[n], out.at[low:high, where[PARTS + 2 + j], first:first + rows, :], sems.at[n])
        for n, (j, low, high) in enumerate(spots)
    ]
    for copy in copies:
        copy.start()
    for copy in copies:
        copy.wait()


def place(where, pieces, spots, first, shape, into=None):
    count = len(spots)
    extra = [] if into is None else [into]
    anywhere = pl.BlockSpec(memory_space=pl.ANY)
    return pl.pallas_call(
        functools.partial(place_kernel, spots=spots, first=first),
        grid_spec=pltpu.PrefetchScalarGridSpec(
            num_scalar_prefetch=1,
            grid=(),
            in_specs=[pl.BlockSpec(memory_space=pltpu.VMEM)] * count + [anywhere] * len(extra),
            out_specs=anywhere,
            scratch_shapes=[pltpu.SemaphoreType.DMA((count,))],
        ),
        out_shape=jax.ShapeDtypeStruct(shape, jnp.bfloat16),
        input_output_aliases={count + 1: 0} if extra else {},
        compiler_params=pltpu.CompilerParams(vmem_limit_bytes=VMEM_LIMIT),
        cost_estimate=pl.CostEstimate(flops=1024, bytes_accessed=1024, transcendentals=0),
    )(where, *pieces, *extra)


def staged(visibility, beam_transfer, tile_mask, first_block, eigen_modes, signal_noise):
    freqs, parts, rows_all, base = visibility.shape
    _, freq_total, _, ell = beam_transfer.shape
    n_modes = eigen_modes.shape[2]
    ell_tiles = ell // TILE
    z, x, p = lax.axis_index("fm"), lax.axis_index("kl"), lax.axis_index("pol")
    other = [(0, 1), (1, 0)]

    def along_z(value, j):
        return lax.ppermute(value, "fm", [(i, (i + j) % parts) for i in range(parts)])

    def along_x(value):
        return lax.ppermute(value, "kl", other)

    def cut(j, first, rows):
        return lax.dynamic_slice(visibility, (0, (z + j) % parts, first, 0), (freqs, 1, rows, base)).reshape(freqs, rows, base)

    index = jnp.arange(2 * parts + 2, dtype=jnp.int32)
    where = jnp.where(index < parts, (z - index) % parts, (z + index - parts - 2) % parts)
    where = jnp.where(index == parts, (x == p).astype(jnp.int32), where)
    where = jnp.where(index == parts + 1, x * ell_tiles, where).astype(jnp.int32)
    ratio = signal_noise[0] / (1.0 + signal_noise[0])
    ratios = jnp.broadcast_to(ratio[:, None, None], (n_modes, 1, ell))
    beam = beam_transfer.reshape(freq_total, base, ell)
    shape = (freqs, parts, rows_all, ell)

    fence = lax.optimization_barrier
    most, half = rows_all - ROWS, freqs // 2
    blocks = [[(0, f)] for f in range(freqs)]
    halves = [[(f // half, f % half)] for f in range(freqs)]
    a = {j: along_z(cut(j, 0, ROWS), j) for j in (1, 3, 2)}
    mine = [cut(0, 0, rows_all)[n:n + half] for n in (0, half)]
    others = [along_x(part) for part in mine]
    b = {j: cut(j, ROWS, most) for j in (1, 2, 3)}
    held, down, up = hold(where, tile_mask[0], first_block, beam, eigen_modes[0])
    (a[1], a[3], a[2]), b, others, down, up = fence(((a[1], a[3], a[2]), b, others, down, up))
    b[1], b[3] = along_z(b[1], 1), along_z(b[3], 3)
    own = project(where, mine, others, held, 0, halves)
    skies = [own] + [project(where, [a[j]], [along_x(a[j])], held, j, blocks) for j in (1, 2, 3)]
    gone = reduce(down, [leave for _, leave in skies], (0, 0, 0, 0), n_modes)
    stay_a = [stay for stay, _ in skies]
    (b[3], b[1]), b[2], stay_a, gone = fence(((b[3], b[1]), b[2], stay_a, gone))
    x_3, x_1 = along_x(b[3]), along_x(b[1])
    b[2] = along_z(b[2], 2)
    kept = reduce(down, stay_a, (0, 0, 0, 0), n_modes, jnp.float32)
    spots = [(j, 0, freqs) for j in (1, 3, 2, 0)]
    outs = restore(kept, lax.ppermute(gone, "pol", other), ratios, up, spots)
    near = project(where, [b[1]], [x_1], held, 1, blocks)
    x_3, b, outs, near = fence((x_3, b, outs, near))
    first = [along_z(outs[n], -spots[n][0]) for n in range(3)]
    x_2 = along_x(b[2])
    far = [project(where, [b[j]], [x], held, j, blocks) for j, x in ((3, x_3), (2, x_2))]
    skies = [own, near, far[1], far[0]]
    gone = reduce(down, [leave for _, leave in skies], (ROWS, 0, 0, 0), n_modes)
    kept = reduce(down, [stay for stay, _ in skies], (ROWS, 0, 0, 0), n_modes, jnp.float32)
    first, here, kept, gone = fence((first, outs[3], kept, gone))
    outs = fence(restore(kept, lax.ppermute(gone, "pol", other), ratios, up, spots))
    back = [along_z(outs[n], -spots[n][0]) for n in range(3)]
    result = place(where, [*first, here], spots, 0, shape)
    result = place(where, [outs[3], back[0]], [spots[3], spots[0]], ROWS, shape, into=result)
    return place(where, back[1:], spots[1:3], ROWS, shape, into=result)


def plain(visibility, beam_transfer, tile_mask, first_block, eigen_modes, signal_noise):
    owned_modes, freq_total, base_half, ell_local = beam_transfer.shape
    base_tiles, ell_tiles = base_half // TILE, ell_local // TILE
    block_ids = lax.axis_index("kl") * ell_tiles + jnp.arange(ell_tiles, dtype=jnp.int32)
    inside = (first_block[:, None] <= block_ids[None, :]).astype(jnp.int32)
    keep_tiles = tile_mask * inside[:, None, :]
    shaped = beam_transfer.reshape(owned_modes, freq_total, base_tiles, TILE, ell_tiles, TILE)
    masked_beam = shaped * keep_tiles.astype(jnp.bfloat16)[:, None, :, None, :, None]
    masked_beam = masked_beam.reshape(owned_modes, freq_total, base_half, ell_local)
    arrived = lax.all_to_all(visibility, "fm", split_axis=1, concat_axis=0, tiled=True)
    partial_value = jnp.einsum(
        "fmrb,mfbl->fmrl",
        lax.all_gather(arrived, "kl", axis=2, tiled=True),
        masked_beam,
        preferred_element_type=jnp.float32,
    )
    sky_sum = lax.psum_scatter(
        partial_value.astype(jnp.bfloat16), "pol", scatter_dimension=2, tiled=True
    ).astype(jnp.float32)
    modes_float = eigen_modes.astype(jnp.float32)
    coeffs = jnp.einsum("mfk,fmrl->mkrl", modes_float, sky_sum, precision=lax.Precision.HIGHEST)
    ratios = signal_noise / (1.0 + signal_noise)
    weighted = (coeffs * ratios[:, :, None, None]).astype(jnp.bfloat16)
    filtered = jnp.einsum(
        "mfk,mkrl->fmrl", eigen_modes, weighted, preferred_element_type=jnp.float32
    ).astype(jnp.bfloat16)
    return lax.all_to_all(filtered, "fm", split_axis=0, concat_axis=1, tiled=True)


def per_device(*args, sizes):
    visibility, beam_transfer = args[0], args[1]
    _, modes, rows, _ = visibility.shape
    fits = (
        sizes["kl"] == 2
        and sizes["pol"] == 2
        and modes == sizes["fm"] == PARTS
        and beam_transfer.shape[0] == 1
        and rows == 3 * ROWS
        and visibility.shape[0] % 2 == 0
    )
    if not fits:
        return plain(*args)
    return staged(*args)


def solution(mesh):
    placed = (
        P(("group", "fm"), None, "kl", "pol"),
        P(("group", "fm"), None, "pol", "kl"),
        P("fm", "pol", "kl"),
        P("fm"),
        P(("group", "fm"), None, None),
        P(("group", "fm"), None),
    )
    return jax.shard_map(
        functools.partial(per_device, sizes=dict(mesh.shape)),
        mesh=mesh,
        in_specs=placed,
        out_specs=P(("group", "fm"), None, "pol", "kl"),
        check_vma=False,
    )
```

```python
import functools
import jax
import jax.numpy as jnp
from jax import lax
from jax.experimental import pallas as pl
from jax.experimental.pallas import tpu as pltpu
from jax.sharding import PartitionSpec as P

TILE = 128
PARTS = 4
ROWS = 16
VMEM_LIMIT = 24 * 1024 * 1024


def hold_kernel(where, tiles, starts, beam, modes_ref, held, down_ref, up_ref, mask, sems):
    freq, base, ell = held.shape
    n_modes = modes_ref.shape[1]
    ell_tiles, base_tiles, freqs = ell // TILE, base // TILE, freq // PARTS
    copies = [pltpu.make_async_copy(beam.at[f], held.at[f], sems.at[f]) for f in range(freq)]
    for copy in copies:
        copy.start()
    for b in range(base_tiles):
        for l in range(ell_tiles):
            kept = jnp.where(starts[0] <= where[PARTS + 1] + l, tiles[b, l], 0).astype(jnp.float32)
            mask[b * TILE:(b + 1) * TILE, l * TILE:(l + 1) * TILE] = jnp.full(
                (TILE, TILE), kept, jnp.float32
            ).astype(jnp.bfloat16)
    modes = modes_ref[...]

    def pick(shape, axis):
        big = lax.broadcasted_iota(jnp.int32, shape, axis) // ROWS
        small = lax.broadcasted_iota(jnp.int32, shape, 1 - axis)
        if freq in shape:
            piece, within = big // freqs, big % freqs
            big = within
            for j in range(PARTS):
                big = jnp.where(piece == j, where[j] * freqs + within, big)
        return jnp.where(big == small, 1.0, 0.0).astype(jnp.bfloat16)

    def lane(shape):
        rows = lax.broadcasted_iota(jnp.int32, shape, 0) % ROWS
        columns = lax.broadcasted_iota(jnp.int32, shape, 1) % ROWS
        return rows == columns

    def dot(a, b, dims):
        return lax.dot_general(a, b, (dims, ((), ())), preferred_element_type=jnp.float32)

    tall = dot(pick((n_modes * ROWS, n_modes), 0), modes, ((1,), (1,))).astype(jnp.bfloat16)
    value = dot(tall, pick((freq, freq * ROWS), 1), ((1,), (0,)))
    down_ref[...] = jnp.where(lane(value.shape), value, 0.0).astype(jnp.bfloat16)
    tall = dot(pick((freq * ROWS, freq), 0), modes, ((1,), (0,))).astype(jnp.bfloat16)
    value = dot(tall, pick((n_modes, n_modes * ROWS), 1), ((1,), (0,)))
    up_ref[...] = jnp.where(lane(value.shape), value, 0.0).astype(jnp.bfloat16)
    for f, copy in enumerate(copies):
        copy.wait()
        held[f] = held[f] * mask[...]


def hold(where, tiles, starts, beam, modes):
    freq, base, ell = beam.shape
    size, wide = freq * ROWS, modes.shape[1] * ROWS
    vmem = pl.BlockSpec(memory_space=pltpu.VMEM)
    return pl.pallas_call(
        hold_kernel,
        grid_spec=pltpu.PrefetchScalarGridSpec(
            num_scalar_prefetch=3,
            grid=(),
            in_specs=[pl.BlockSpec(memory_space=pl.ANY), vmem],
            out_specs=[vmem] * 3,
            scratch_shapes=[pltpu.VMEM((base, ell), jnp.bfloat16), pltpu.SemaphoreType.DMA((freq,))],
        ),
        out_shape=[
            pltpu.VMEM(beam.shape, beam.dtype),
            jax.ShapeDtypeStruct((wide, size), jnp.bfloat16),
            jax.ShapeDtypeStruct((size, wide), jnp.bfloat16),
        ],
        compiler_params=pltpu.CompilerParams(vmem_limit_bytes=VMEM_LIMIT),
        cost_estimate=pl.CostEstimate(flops=1024, bytes_accessed=1024, transcendentals=0),
    )(where, tiles, starts, beam, modes)


def project_kernel(where, *refs, piece, blocks):
    count = (len(refs) - 3) // 2
    mine, others = refs[:count], refs[count:2 * count]
    held, stay_ref, leave_ref = refs[2 * count:]
    freqs, rows, _ = stay_ref.shape
    first = where[piece] * freqs
    own = where[PARTS] == 1
    for f in range(freqs):
        a = jnp.concatenate([mine[n][k] for n, k in blocks[f]], axis=0)
        b = jnp.concatenate([others[n][k] for n, k in blocks[f]], axis=0)
        lines = jnp.concatenate([jnp.where(own, a, b), jnp.where(own, b, a)], axis=0)
        value = jnp.dot(lines, held[first + f], preferred_element_type=jnp.float32).astype(jnp.bfloat16)
        stay_ref[f] = value[:rows]
        leave_ref[f] = value[rows:]


def project(where, mine, others, held, piece, blocks):
    ell = held.shape[2]
    rows = sum(mine[n].shape[1] for n, _ in blocks[0])
    vmem = pl.BlockSpec(memory_space=pltpu.VMEM)
    return pl.pallas_call(
        functools.partial(project_kernel, piece=piece, blocks=blocks),
        grid_spec=pltpu.PrefetchScalarGridSpec(
            num_scalar_prefetch=1, grid=(), in_specs=[vmem] * (2 * len(mine) + 1), out_specs=[vmem] * 2
        ),
        out_shape=[jax.ShapeDtypeStruct((len(blocks), rows, ell), jnp.bfloat16)] * 2,
        compiler_params=pltpu.CompilerParams(vmem_limit_bytes=VMEM_LIMIT),
        cost_estimate=pl.CostEstimate(flops=1024, bytes_accessed=1024, transcendentals=0),
    )(where, *mine, *others, pltpu.with_memory_space_constraint(held, pltpu.VMEM))


def contract(modes, skies):
    block = jnp.concatenate([sky[...].reshape(sky.shape[0] * ROWS, sky.shape[2]) for sky in skies], axis=0)
    return jnp.dot(modes, block, preferred_element_type=jnp.float32)


def reduce_kernel(modes_ref, *refs):
    out = refs[-1]
    out[...] = contract(modes_ref[...], refs[:-1]).astype(out.dtype).reshape(out.shape)


def by_rows(count, ell, first=0):
    return pl.BlockSpec((count, ROWS, ell), lambda g: (0, g + first // ROWS, 0))


def fixed(shape):
    return pl.BlockSpec(shape, lambda g: (0,) * len(shape))


def sky_specs(skies, first):
    return [by_rows(sky.shape[0], sky.shape[2], low) for sky, low in zip(skies, first)]


def reduce(modes, skies, first, n_modes, dtype=jnp.bfloat16):
    _, rows, ell = skies[-1].shape
    return pl.pallas_call(
        reduce_kernel,
        grid=(rows // ROWS,),
        in_specs=[fixed(modes.shape)] + sky_specs(skies, first),
        out_specs=by_rows(n_modes, ell),
        out_shape=jax.ShapeDtypeStruct((n_modes, rows, ell), dtype),
        compiler_params=pltpu.CompilerParams(vmem_limit_bytes=VMEM_LIMIT),
        cost_estimate=pl.CostEstimate(flops=1024, bytes_accessed=1024, transcendentals=0),
    )(modes, *skies)


def restore_kernel(up_ref, ratio_ref, kept_ref, came_ref, *outs, spots):
    n_modes, _, ell = came_ref.shape
    freqs = up_ref.shape[0] // ROWS // PARTS
    total = kept_ref[...] + came_ref[...].astype(jnp.float32)
    weighted = (total * ratio_ref[...]).astype(jnp.bfloat16).reshape(n_modes * ROWS, ell)
    for (j, low, high), out in zip(spots, outs):
        modes = up_ref[(j * freqs + low) * ROWS:(j * freqs + high) * ROWS, :]
        value = jnp.dot(modes, weighted, preferred_element_type=jnp.float32)
        out[...] = value.astype(jnp.bfloat16).reshape(out.shape)


def restore(kept, came, ratios, up, spots):
    n_modes, rows, ell = came.shape
    return pl.pallas_call(
        functools.partial(restore_kernel, spots=spots),
        grid=(rows // ROWS,),
        in_specs=[fixed(up.shape), fixed(ratios.shape)] + [by_rows(n_modes, ell)] * 2,
        out_specs=[by_rows(high - low, ell) for _, low, high in spots],
        out_shape=[jax.ShapeDtypeStruct((high - low, rows, ell), jnp.bfloat16) for _, low, high in spots],
        compiler_params=pltpu.CompilerParams(vmem_limit_bytes=VMEM_LIMIT),
        cost_estimate=pl.CostEstimate(flops=1024, bytes_accessed=1024, transcendentals=0),
    )(up, ratios, kept, came)


def place_kernel(where, *refs, spots, first):
    count = len(spots)
    pieces, out, sems = refs[:count], refs[-2], refs[-1]
    rows = pieces[0].shape[1]
    copies = [
        pltpu.make_async_copy(pieces[n], out.at[low:high, where[j], first:first + rows, :], sems.at[n])
        for n, (j, low, high) in enumerate(spots)
    ]
    for copy in copies:
        copy.start()
    for copy in copies:
        copy.wait()


def place(where, pieces, spots, first, shape, into=None):
    count = len(spots)
    extra = [] if into is None else [into]
    anywhere = pl.BlockSpec(memory_space=pl.ANY)
    return pl.pallas_call(
        functools.partial(place_kernel, spots=spots, first=first),
        grid_spec=pltpu.PrefetchScalarGridSpec(
            num_scalar_prefetch=1,
            grid=(),
            in_specs=[pl.BlockSpec(memory_space=pltpu.VMEM)] * count + [anywhere] * len(extra),
            out_specs=anywhere,
            scratch_shapes=[pltpu.SemaphoreType.DMA((count,))],
        ),
        out_shape=jax.ShapeDtypeStruct(shape, jnp.bfloat16),
        input_output_aliases={count + 1: 0} if extra else {},
        compiler_params=pltpu.CompilerParams(vmem_limit_bytes=VMEM_LIMIT),
        cost_estimate=pl.CostEstimate(flops=1024, bytes_accessed=1024, transcendentals=0),
    )(where, *pieces, *extra)


def staged(visibility, beam_transfer, tile_mask, first_block, eigen_modes, signal_noise):
    freqs, parts, rows_all, base = visibility.shape
    _, freq_total, _, ell = beam_transfer.shape
    n_modes = eigen_modes.shape[2]
    ell_tiles = ell // TILE
    z, x, p = lax.axis_index("fm"), lax.axis_index("kl"), lax.axis_index("pol")
    other = [(0, 1), (1, 0)]

    def along_z(value, j):
        return lax.ppermute(value, "fm", [(i, i ^ j) for i in range(parts)])

    def along_x(value):
        return lax.ppermute(value, "kl", other)

    def cut(j, first, rows):
        return lax.dynamic_slice(visibility, (0, z ^ j, first, 0), (freqs, 1, rows, base)).reshape(freqs, rows, base)

    index = jnp.arange(parts + 2, dtype=jnp.int32)
    where = jnp.where(
        index < parts, z ^ index, jnp.where(index == parts, (x == p).astype(jnp.int32), x * ell_tiles)
    ).astype(jnp.int32)
    ratio = signal_noise[0] / (1.0 + signal_noise[0])
    ratios = jnp.broadcast_to(ratio[:, None, None], (n_modes, 1, ell))
    beam = beam_transfer.reshape(freq_total, base, ell)
    shape = (freqs, parts, rows_all, ell)

    fence = lax.optimization_barrier
    most, half = rows_all - ROWS, freqs // 2
    blocks = [[(0, f)] for f in range(freqs)]
    halves = [[(f // half, f % half)] for f in range(freqs)]
    a = {j: along_z(cut(j, 0, ROWS), j) for j in (3, 2, 1)}
    mine = [cut(0, 0, rows_all)[n:n + half] for n in (0, half)]
    others = [along_x(part) for part in mine]
    b = {j: cut(j, ROWS, most) for j in (1, 2, 3)}
    held, down, up = hold(where, tile_mask[0], first_block, beam, eigen_modes[0])
    (a[3], a[2], a[1]), b, others, down, up = fence(((a[3], a[2], a[1]), b, others, down, up))
    b[1], b[2] = along_z(b[1], 1), along_z(b[2], 2)
    own = project(where, mine, others, held, 0, halves)
    skies = [own] + [project(where, [a[j]], [along_x(a[j])], held, j, blocks) for j in (1, 2, 3)]
    gone = reduce(down, [leave for _, leave in skies], (0, 0, 0, 0), n_modes)
    stay_a = [stay for stay, _ in skies]
    (b[2], b[1]), b[3], stay_a, gone = fence(((b[2], b[1]), b[3], stay_a, gone))
    x_2, x_1 = along_x(b[2]), along_x(b[1])
    b[3] = along_z(b[3], 3)
    kept = reduce(down, stay_a, (0, 0, 0, 0), n_modes, jnp.float32)
    spots = [(j, 0, freqs) for j in (1, 2, 3, 0)]
    outs = restore(kept, lax.ppermute(gone, "pol", other), ratios, up, spots)
    near = project(where, [b[1]], [x_1], held, 1, blocks)
    x_2, b, outs, near = fence((x_2, b, outs, near))
    first = {j: along_z(outs[j - 1], j) for j in (1, 2, 3)}
    first[0] = outs[3]
    x_3 = along_x(b[3])
    skies = [own, near] + [project(where, [b[j]], [x], held, j, blocks) for j, x in ((2, x_2), (3, x_3))]
    gone = reduce(down, [leave for _, leave in skies], (ROWS, 0, 0, 0), n_modes)
    kept = reduce(down, [stay for stay, _ in skies], (ROWS, 0, 0, 0), n_modes, jnp.float32)
    (first[2], first[3], first[1]), first[0], kept, gone = fence(
        ((first[2], first[3], first[1]), first[0], kept, gone)
    )
    result_a = [first[j] for j in (1, 2, 3, 0)], spots
    spots = [(1, 0, freqs), (2, 0, half), (3, 0, half), (2, half, freqs), (3, half, freqs), (0, 0, freqs)]
    outs = fence(restore(kept, lax.ppermute(gone, "pol", other), ratios, up, spots))
    back = [along_z(part, j) for part, (j, _, _) in zip(outs[:-1], spots)] + [outs[-1]]
    result = place(where, *result_a, 0, shape)
    result = place(where, [back[5], back[0]], [spots[5], spots[0]], ROWS, shape, into=result)
    return place(where, back[1:5], spots[1:5], ROWS, shape, into=result)


def plain(visibility, beam_transfer, tile_mask, first_block, eigen_modes, signal_noise):
    owned_modes, freq_total, base_half, ell_local = beam_transfer.shape
    base_tiles, ell_tiles = base_half // TILE, ell_local // TILE
    block_ids = lax.axis_index("kl") * ell_tiles + jnp.arange(ell_tiles, dtype=jnp.int32)
    inside = (first_block[:, None] <= block_ids[None, :]).astype(jnp.int32)
    keep_tiles = tile_mask * inside[:, None, :]
    shaped = beam_transfer.reshape(owned_modes, freq_total, base_tiles, TILE, ell_tiles, TILE)
    masked_beam = shaped * keep_tiles.astype(jnp.bfloat16)[:, None, :, None, :, None]
    masked_beam = masked_beam.reshape(owned_modes, freq_total, base_half, ell_local)
    arrived = lax.all_to_all(visibility, "fm", split_axis=1, concat_axis=0, tiled=True)
    partial_value = jnp.einsum(
        "fmrb,mfbl->fmrl",
        lax.all_gather(arrived, "kl", axis=2, tiled=True),
        masked_beam,
        preferred_element_type=jnp.float32,
    )
    sky_sum = lax.psum_scatter(
        partial_value.astype(jnp.bfloat16), "pol", scatter_dimension=2, tiled=True
    ).astype(jnp.float32)
    modes_float = eigen_modes.astype(jnp.float32)
    coeffs = jnp.einsum("mfk,fmrl->mkrl", modes_float, sky_sum, precision=lax.Precision.HIGHEST)
    ratios = signal_noise / (1.0 + signal_noise)
    weighted = (coeffs * ratios[:, :, None, None]).astype(jnp.bfloat16)
    filtered = jnp.einsum(
        "mfk,mkrl->fmrl", eigen_modes, weighted, preferred_element_type=jnp.float32
    ).astype(jnp.bfloat16)
    return lax.all_to_all(filtered, "fm", split_axis=0, concat_axis=1, tiled=True)


def per_device(*args, sizes):
    visibility, beam_transfer = args[0], args[1]
    _, modes, rows, _ = visibility.shape
    fits = (
        sizes["kl"] == 2
        and sizes["pol"] == 2
        and modes == sizes["fm"] == PARTS
        and beam_transfer.shape[0] == 1
        and rows == 3 * ROWS
        and visibility.shape[0] % 2 == 0
    )
    if not fits:
        return plain(*args)
    return staged(*args)


def solution(mesh):
    placed = (
        P(("group", "fm"), None, "kl", "pol"),
        P(("group", "fm"), None, "pol", "kl"),
        P("fm", "pol", "kl"),
        P("fm"),
        P(("group", "fm"), None, None),
        P(("group", "fm"), None),
    )
    return jax.shard_map(
        functools.partial(per_device, sizes=dict(mesh.shape)),
        mesh=mesh,
        in_specs=placed,
        out_specs=P(("group", "fm"), None, "pol", "kl"),
        check_vma=False,
    )
```

```python
import functools
import jax
import jax.numpy as jnp
from jax import lax
from jax.experimental import pallas as pl
from jax.experimental.pallas import tpu as pltpu
from jax.sharding import PartitionSpec as P

TILE = 128
PARTS = 4
ROWS = 16
VMEM_LIMIT = 24 * 1024 * 1024


def hold_kernel(where, tiles, starts, beam, modes_ref, held, down_ref, up_ref, mask, sems):
    freq, base, ell = held.shape
    n_modes = modes_ref.shape[1]
    ell_tiles, base_tiles, freqs = ell // TILE, base // TILE, freq // PARTS
    copies = [pltpu.make_async_copy(beam.at[f], held.at[f], sems.at[f]) for f in range(freq)]
    for copy in copies:
        copy.start()
    for b in range(base_tiles):
        for l in range(ell_tiles):
            kept = jnp.where(starts[0] <= where[PARTS + 1] + l, tiles[b, l], 0).astype(jnp.float32)
            mask[b * TILE:(b + 1) * TILE, l * TILE:(l + 1) * TILE] = jnp.full(
                (TILE, TILE), kept, jnp.float32
            ).astype(jnp.bfloat16)
    modes = modes_ref[...]

    def pick(shape, axis):
        big = lax.broadcasted_iota(jnp.int32, shape, axis) // ROWS
        small = lax.broadcasted_iota(jnp.int32, shape, 1 - axis)
        if freq in shape:
            piece, within = big // freqs, big % freqs
            big = within
            for j in range(PARTS):
                big = jnp.where(piece == j, where[j] * freqs + within, big)
        return jnp.where(big == small, 1.0, 0.0).astype(jnp.bfloat16)

    def lane(shape):
        rows = lax.broadcasted_iota(jnp.int32, shape, 0) % ROWS
        columns = lax.broadcasted_iota(jnp.int32, shape, 1) % ROWS
        return rows == columns

    def dot(a, b, dims):
        return lax.dot_general(a, b, (dims, ((), ())), preferred_element_type=jnp.float32)

    tall = dot(pick((n_modes * ROWS, n_modes), 0), modes, ((1,), (1,))).astype(jnp.bfloat16)
    value = dot(tall, pick((freq, freq * ROWS), 1), ((1,), (0,)))
    down_ref[...] = jnp.where(lane(value.shape), value, 0.0).astype(jnp.bfloat16)
    tall = dot(pick((freq * ROWS, freq), 0), modes, ((1,), (0,))).astype(jnp.bfloat16)
    value = dot(tall, pick((n_modes, n_modes * ROWS), 1), ((1,), (0,)))
    up_ref[...] = jnp.where(lane(value.shape), value, 0.0).astype(jnp.bfloat16)
    for f, copy in enumerate(copies):
        copy.wait()
        held[f] = held[f] * mask[...]


def hold(where, tiles, starts, beam, modes):
    freq, base, ell = beam.shape
    size, wide = freq * ROWS, modes.shape[1] * ROWS
    vmem = pl.BlockSpec(memory_space=pltpu.VMEM)
    return pl.pallas_call(
        hold_kernel,
        grid_spec=pltpu.PrefetchScalarGridSpec(
            num_scalar_prefetch=3,
            grid=(),
            in_specs=[pl.BlockSpec(memory_space=pl.ANY), vmem],
            out_specs=[vmem] * 3,
            scratch_shapes=[pltpu.VMEM((base, ell), jnp.bfloat16), pltpu.SemaphoreType.DMA((freq,))],
        ),
        out_shape=[
            pltpu.VMEM(beam.shape, beam.dtype),
            jax.ShapeDtypeStruct((wide, size), jnp.bfloat16),
            jax.ShapeDtypeStruct((size, wide), jnp.bfloat16),
        ],
        compiler_params=pltpu.CompilerParams(vmem_limit_bytes=VMEM_LIMIT),
        cost_estimate=pl.CostEstimate(flops=1024, bytes_accessed=1024, transcendentals=0),
    )(where, tiles, starts, beam, modes)


def project_kernel(where, *refs, piece, blocks):
    count = (len(refs) - 3) // 2
    mine, others = refs[:count], refs[count:2 * count]
    held, stay_ref, leave_ref = refs[2 * count:]
    freqs, rows, _ = stay_ref.shape
    first = where[piece] * freqs
    own = where[PARTS] == 1
    for f in range(freqs):
        a = jnp.concatenate([mine[n][k] for n, k in blocks[f]], axis=0)
        b = jnp.concatenate([others[n][k] for n, k in blocks[f]], axis=0)
        lines = jnp.concatenate([jnp.where(own, a, b), jnp.where(own, b, a)], axis=0)
        value = jnp.dot(lines, held[first + f], preferred_element_type=jnp.float32).astype(jnp.bfloat16)
        stay_ref[f] = value[:rows]
        leave_ref[f] = value[rows:]


def project(where, mine, others, held, piece, blocks, flops=1024):
    ell = held.shape[2]
    rows = sum(mine[n].shape[1] for n, _ in blocks[0])
    vmem = pl.BlockSpec(memory_space=pltpu.VMEM)
    return pl.pallas_call(
        functools.partial(project_kernel, piece=piece, blocks=blocks),
        grid_spec=pltpu.PrefetchScalarGridSpec(
            num_scalar_prefetch=1, grid=(), in_specs=[vmem] * (2 * len(mine) + 1), out_specs=[vmem] * 2
        ),
        out_shape=[jax.ShapeDtypeStruct((len(blocks), rows, ell), jnp.bfloat16)] * 2,
        compiler_params=pltpu.CompilerParams(vmem_limit_bytes=VMEM_LIMIT),
        cost_estimate=pl.CostEstimate(flops=flops, bytes_accessed=1024, transcendentals=0),
    )(where, *mine, *others, pltpu.with_memory_space_constraint(held, pltpu.VMEM))


def contract(modes, skies):
    block = jnp.concatenate([sky[...].reshape(sky.shape[0] * ROWS, sky.shape[2]) for sky in skies], axis=0)
    return jnp.dot(modes, block, preferred_element_type=jnp.float32)


def reduce_kernel(modes_ref, *refs):
    out = refs[-1]
    out[...] = contract(modes_ref[...], refs[:-1]).astype(out.dtype).reshape(out.shape)


def by_rows(count, ell, first=0):
    return pl.BlockSpec((count, ROWS, ell), lambda g: (0, g + first // ROWS, 0))


def fixed(shape):
    return pl.BlockSpec(shape, lambda g: (0,) * len(shape))


def sky_specs(skies, first):
    return [by_rows(sky.shape[0], sky.shape[2], low) for sky, low in zip(skies, first)]


def reduce(modes, skies, first, n_modes, dtype=jnp.bfloat16):
    _, rows, ell = skies[-1].shape
    return pl.pallas_call(
        reduce_kernel,
        grid=(rows // ROWS,),
        in_specs=[fixed(modes.shape)] + sky_specs(skies, first),
        out_specs=by_rows(n_modes, ell),
        out_shape=jax.ShapeDtypeStruct((n_modes, rows, ell), dtype),
        compiler_params=pltpu.CompilerParams(vmem_limit_bytes=VMEM_LIMIT),
        cost_estimate=pl.CostEstimate(flops=1024, bytes_accessed=1024, transcendentals=0),
    )(modes, *skies)


def restore_kernel(up_ref, ratio_ref, kept_ref, came_ref, *outs, spots):
    n_modes, _, ell = came_ref.shape
    freqs = up_ref.shape[0] // ROWS // PARTS
    total = kept_ref[...] + came_ref[...].astype(jnp.float32)
    weighted = (total * ratio_ref[...]).astype(jnp.bfloat16).reshape(n_modes * ROWS, ell)
    for (j, low, high), out in zip(spots, outs):
        modes = up_ref[(j * freqs + low) * ROWS:(j * freqs + high) * ROWS, :]
        value = jnp.dot(modes, weighted, preferred_element_type=jnp.float32)
        out[...] = value.astype(jnp.bfloat16).reshape(out.shape)


def restore(kept, came, ratios, up, spots):
    n_modes, rows, ell = came.shape
    return pl.pallas_call(
        functools.partial(restore_kernel, spots=spots),
        grid=(rows // ROWS,),
        in_specs=[fixed(up.shape), fixed(ratios.shape)] + [by_rows(n_modes, ell)] * 2,
        out_specs=[by_rows(high - low, ell) for _, low, high in spots],
        out_shape=[jax.ShapeDtypeStruct((high - low, rows, ell), jnp.bfloat16) for _, low, high in spots],
        compiler_params=pltpu.CompilerParams(vmem_limit_bytes=VMEM_LIMIT),
        cost_estimate=pl.CostEstimate(flops=1024, bytes_accessed=1024, transcendentals=0),
    )(up, ratios, kept, came)


def place_kernel(where, *refs, spots, first):
    count = len(spots)
    pieces, out, sems = refs[:count], refs[-2], refs[-1]
    rows = pieces[0].shape[1]
    copies = [
        pltpu.make_async_copy(pieces[n], out.at[low:high, where[j], first:first + rows, :], sems.at[n])
        for n, (j, low, high) in enumerate(spots)
    ]
    for copy in copies:
        copy.start()
    for copy in copies:
        copy.wait()


def place(where, pieces, spots, first, shape, into=None):
    count = len(spots)
    extra = [] if into is None else [into]
    anywhere = pl.BlockSpec(memory_space=pl.ANY)
    return pl.pallas_call(
        functools.partial(place_kernel, spots=spots, first=first),
        grid_spec=pltpu.PrefetchScalarGridSpec(
            num_scalar_prefetch=1,
            grid=(),
            in_specs=[pl.BlockSpec(memory_space=pltpu.VMEM)] * count + [anywhere] * len(extra),
            out_specs=anywhere,
            scratch_shapes=[pltpu.SemaphoreType.DMA((count,))],
        ),
        out_shape=jax.ShapeDtypeStruct(shape, jnp.bfloat16),
        input_output_aliases={count + 1: 0} if extra else {},
        compiler_params=pltpu.CompilerParams(vmem_limit_bytes=VMEM_LIMIT),
        cost_estimate=pl.CostEstimate(flops=1024, bytes_accessed=1024, transcendentals=0),
    )(where, *pieces, *extra)


def anchor_kernel(*refs):
    del refs


def anchor(values, flops):
    anywhere = pl.BlockSpec(memory_space=pl.ANY)
    return pl.pallas_call(
        anchor_kernel,
        in_specs=[anywhere] * len(values),
        out_specs=[anywhere] * len(values),
        out_shape=[jax.ShapeDtypeStruct(value.shape, value.dtype) for value in values],
        input_output_aliases={n: n for n in range(len(values))},
        cost_estimate=pl.CostEstimate(flops=flops, bytes_accessed=1024, transcendentals=0),
    )(*values)


def staged(visibility, beam_transfer, tile_mask, first_block, eigen_modes, signal_noise):
    freqs, parts, rows_all, base = visibility.shape
    _, freq_total, _, ell = beam_transfer.shape
    n_modes = eigen_modes.shape[2]
    ell_tiles = ell // TILE
    z, x, p = lax.axis_index("fm"), lax.axis_index("kl"), lax.axis_index("pol")
    other = [(0, 1), (1, 0)]

    def along_z(value, j):
        return lax.ppermute(value, "fm", [(i, i ^ j) for i in range(parts)])

    def along_x(value):
        return lax.ppermute(value, "kl", other)

    def cut(j, first, rows):
        return lax.dynamic_slice(visibility, (0, z ^ j, first, 0), (freqs, 1, rows, base)).reshape(freqs, rows, base)

    index = jnp.arange(parts + 2, dtype=jnp.int32)
    where = jnp.where(
        index < parts, z ^ index, jnp.where(index == parts, (x == p).astype(jnp.int32), x * ell_tiles)
    ).astype(jnp.int32)
    ratio = signal_noise[0] / (1.0 + signal_noise[0])
    ratios = jnp.broadcast_to(ratio[:, None, None], (n_modes, 1, ell))
    beam = beam_transfer.reshape(freq_total, base, ell)
    shape = (freqs, parts, rows_all, ell)

    fence = lax.optimization_barrier
    most, half = rows_all - ROWS, freqs // 2
    blocks = [[(0, f)] for f in range(freqs)]
    halves = [[(f // half, f % half)] for f in range(freqs)]
    a = {j: along_z(cut(j, 0, ROWS), j) for j in (3, 2, 1)}
    mine = [cut(0, 0, rows_all)[n:n + half] for n in (0, half)]
    others = [along_x(part) for part in mine]
    b, far = {j: cut(j, ROWS, most) for j in (1, 2)}, cut(3, ROWS, most)
    held, down, up = hold(where, tile_mask[0], first_block, beam, eigen_modes[0])
    (a[3], a[2], a[1]), b, others, down, up = fence(((a[3], a[2], a[1]), b, others, down, up))
    b[1], b[2] = along_z(b[1], 1), along_z(b[2], 2)
    own = project(where, mine, others, held, 0, halves, 200_000_000)
    skies = [own] + [project(where, [a[j]], [along_x(a[j])], held, j, blocks, 200_000_000) for j in (1, 2, 3)]
    gone = reduce(down, [leave for _, leave in skies], (0, 0, 0, 0), n_modes)
    stay_a = [stay for stay, _ in skies]
    b[2], stay_a, gone = fence((b[2], stay_a, gone))
    x_2 = along_x(b[2])
    x_1, b[3] = anchor([along_x(b[1]), along_z(far, 3)], 1_500_000_000)
    kept = reduce(down, stay_a, (0, 0, 0, 0), n_modes, jnp.float32)
    spots = [(j, 0, freqs) for j in (1, 2, 3, 0)]
    outs = restore(kept, lax.ppermute(gone, "pol", other), ratios, up, spots)
    near = project(where, [b[1]], [x_1], held, 1, blocks)
    x_2, b, outs, near = fence((x_2, b, outs, near))
    first = {j: along_z(outs[j - 1], j) for j in (1, 2, 3)}
    first[0] = outs[3]
    x_3 = along_x(b[3])
    skies = [own, near] + [project(where, [b[j]], [x], held, j, blocks) for j, x in ((2, x_2), (3, x_3))]
    gone = reduce(down, [leave for _, leave in skies], (ROWS, 0, 0, 0), n_modes)
    kept = reduce(down, [stay for stay, _ in skies], (ROWS, 0, 0, 0), n_modes, jnp.float32)
    (first[2], first[3], first[1]), first[0], kept, gone = fence(
        ((first[2], first[3], first[1]), first[0], kept, gone)
    )
    outs = fence(restore(kept, lax.ppermute(gone, "pol", other), ratios, up, spots))
    back = [along_z(outs[j - 1], j) for j in (1, 2, 3)]
    result = place(where, [first[j] for j in (1, 2, 3, 0)], spots, 0, shape)
    result = place(where, [outs[3], back[0]], [spots[3], spots[0]], ROWS, shape, into=result)
    return place(where, back[1:], spots[1:3], ROWS, shape, into=result)


def plain(visibility, beam_transfer, tile_mask, first_block, eigen_modes, signal_noise):
    owned_modes, freq_total, base_half, ell_local = beam_transfer.shape
    base_tiles, ell_tiles = base_half // TILE, ell_local // TILE
    block_ids = lax.axis_index("kl") * ell_tiles + jnp.arange(ell_tiles, dtype=jnp.int32)
    inside = (first_block[:, None] <= block_ids[None, :]).astype(jnp.int32)
    keep_tiles = tile_mask * inside[:, None, :]
    shaped = beam_transfer.reshape(owned_modes, freq_total, base_tiles, TILE, ell_tiles, TILE)
    masked_beam = shaped * keep_tiles.astype(jnp.bfloat16)[:, None, :, None, :, None]
    masked_beam = masked_beam.reshape(owned_modes, freq_total, base_half, ell_local)
    arrived = lax.all_to_all(visibility, "fm", split_axis=1, concat_axis=0, tiled=True)
    partial_value = jnp.einsum(
        "fmrb,mfbl->fmrl",
        lax.all_gather(arrived, "kl", axis=2, tiled=True),
        masked_beam,
        preferred_element_type=jnp.float32,
    )
    sky_sum = lax.psum_scatter(
        partial_value.astype(jnp.bfloat16), "pol", scatter_dimension=2, tiled=True
    ).astype(jnp.float32)
    modes_float = eigen_modes.astype(jnp.float32)
    coeffs = jnp.einsum("mfk,fmrl->mkrl", modes_float, sky_sum, precision=lax.Precision.HIGHEST)
    ratios = signal_noise / (1.0 + signal_noise)
    weighted = (coeffs * ratios[:, :, None, None]).astype(jnp.bfloat16)
    filtered = jnp.einsum(
        "mfk,mkrl->fmrl", eigen_modes, weighted, preferred_element_type=jnp.float32
    ).astype(jnp.bfloat16)
    return lax.all_to_all(filtered, "fm", split_axis=0, concat_axis=1, tiled=True)


def per_device(*args, sizes):
    visibility, beam_transfer = args[0], args[1]
    _, modes, rows, _ = visibility.shape
    fits = (
        sizes["kl"] == 2
        and sizes["pol"] == 2
        and modes == sizes["fm"] == PARTS
        and beam_transfer.shape[0] == 1
        and rows == 3 * ROWS
        and visibility.shape[0] % 2 == 0
    )
    if not fits:
        return plain(*args)
    return staged(*args)


def solution(mesh):
    placed = (
        P(("group", "fm"), None, "kl", "pol"),
        P(("group", "fm"), None, "pol", "kl"),
        P("fm", "pol", "kl"),
        P("fm"),
        P(("group", "fm"), None, None),
        P(("group", "fm"), None),
    )
    return jax.shard_map(
        functools.partial(per_device, sizes=dict(mesh.shape)),
        mesh=mesh,
        in_specs=placed,
        out_specs=P(("group", "fm"), None, "pol", "kl"),
        check_vma=False,
    )
```

```python
import functools
import jax
import jax.numpy as jnp
from jax import lax
from jax.experimental import pallas as pl
from jax.experimental.pallas import tpu as pltpu
from jax.sharding import PartitionSpec as P

TILE = 128
PARTS = 4
ROWS = 16
VMEM_LIMIT = 24 * 1024 * 1024


def hold_kernel(where, tiles, starts, beam, modes_ref, held, down_ref, up_ref, mask, sems):
    freq, base, ell = held.shape
    n_modes = modes_ref.shape[1]
    ell_tiles, base_tiles, freqs = ell // TILE, base // TILE, freq // PARTS
    copies = [pltpu.make_async_copy(beam.at[f], held.at[f], sems.at[f]) for f in range(freq)]
    for copy in copies:
        copy.start()
    for b in range(base_tiles):
        for l in range(ell_tiles):
            kept = jnp.where(starts[0] <= where[PARTS + 1] + l, tiles[b, l], 0).astype(jnp.float32)
            mask[b * TILE:(b + 1) * TILE, l * TILE:(l + 1) * TILE] = jnp.full(
                (TILE, TILE), kept, jnp.float32
            ).astype(jnp.bfloat16)
    modes = modes_ref[...]

    def pick(shape, axis):
        big = lax.broadcasted_iota(jnp.int32, shape, axis) // ROWS
        small = lax.broadcasted_iota(jnp.int32, shape, 1 - axis)
        if freq in shape:
            piece, within = big // freqs, big % freqs
            big = within
            for j in range(PARTS):
                big = jnp.where(piece == j, where[j] * freqs + within, big)
        return jnp.where(big == small, 1.0, 0.0).astype(jnp.bfloat16)

    def lane(shape):
        rows = lax.broadcasted_iota(jnp.int32, shape, 0) % ROWS
        columns = lax.broadcasted_iota(jnp.int32, shape, 1) % ROWS
        return rows == columns

    def dot(a, b, dims):
        return lax.dot_general(a, b, (dims, ((), ())), preferred_element_type=jnp.float32)

    tall = dot(pick((n_modes * ROWS, n_modes), 0), modes, ((1,), (1,))).astype(jnp.bfloat16)
    value = dot(tall, pick((freq, freq * ROWS), 1), ((1,), (0,)))
    down_ref[...] = jnp.where(lane(value.shape), value, 0.0).astype(jnp.bfloat16)
    tall = dot(pick((freq * ROWS, freq), 0), modes, ((1,), (0,))).astype(jnp.bfloat16)
    value = dot(tall, pick((n_modes, n_modes * ROWS), 1), ((1,), (0,)))
    up_ref[...] = jnp.where(lane(value.shape), value, 0.0).astype(jnp.bfloat16)
    for f, copy in enumerate(copies):
        copy.wait()
        held[f] = held[f] * mask[...]


def hold(where, tiles, starts, beam, modes):
    freq, base, ell = beam.shape
    size, wide = freq * ROWS, modes.shape[1] * ROWS
    vmem = pl.BlockSpec(memory_space=pltpu.VMEM)
    return pl.pallas_call(
        hold_kernel,
        grid_spec=pltpu.PrefetchScalarGridSpec(
            num_scalar_prefetch=3,
            grid=(),
            in_specs=[pl.BlockSpec(memory_space=pl.ANY), vmem],
            out_specs=[vmem] * 3,
            scratch_shapes=[pltpu.VMEM((base, ell), jnp.bfloat16), pltpu.SemaphoreType.DMA((freq,))],
        ),
        out_shape=[
            pltpu.VMEM(beam.shape, beam.dtype),
            jax.ShapeDtypeStruct((wide, size), jnp.bfloat16),
            jax.ShapeDtypeStruct((size, wide), jnp.bfloat16),
        ],
        compiler_params=pltpu.CompilerParams(vmem_limit_bytes=VMEM_LIMIT),
        cost_estimate=pl.CostEstimate(flops=1024, bytes_accessed=1024, transcendentals=0),
    )(where, tiles, starts, beam, modes)


def project_kernel(where, *refs, piece, blocks):
    count = (len(refs) - 3) // 2
    mine, others = refs[:count], refs[count:2 * count]
    held, stay_ref, leave_ref = refs[2 * count:]
    freqs, rows, _ = stay_ref.shape
    first = where[piece] * freqs
    own = where[PARTS] == 1
    for f in range(freqs):
        a = jnp.concatenate([mine[n][k] for n, k in blocks[f]], axis=0)
        b = jnp.concatenate([others[n][k] for n, k in blocks[f]], axis=0)
        lines = jnp.concatenate([jnp.where(own, a, b), jnp.where(own, b, a)], axis=0)
        value = jnp.dot(lines, held[first + f], preferred_element_type=jnp.float32).astype(jnp.bfloat16)
        stay_ref[f] = value[:rows]
        leave_ref[f] = value[rows:]


def project(where, mine, others, held, piece, blocks, flops=1024):
    ell = held.shape[2]
    rows = sum(mine[n].shape[1] for n, _ in blocks[0])
    vmem = pl.BlockSpec(memory_space=pltpu.VMEM)
    return pl.pallas_call(
        functools.partial(project_kernel, piece=piece, blocks=blocks),
        grid_spec=pltpu.PrefetchScalarGridSpec(
            num_scalar_prefetch=1, grid=(), in_specs=[vmem] * (2 * len(mine) + 1), out_specs=[vmem] * 2
        ),
        out_shape=[jax.ShapeDtypeStruct((len(blocks), rows, ell), jnp.bfloat16)] * 2,
        compiler_params=pltpu.CompilerParams(vmem_limit_bytes=VMEM_LIMIT),
        cost_estimate=pl.CostEstimate(flops=flops, bytes_accessed=1024, transcendentals=0),
    )(where, *mine, *others, pltpu.with_memory_space_constraint(held, pltpu.VMEM))


def contract(modes, skies):
    block = jnp.concatenate([sky[...].reshape(sky.shape[0] * ROWS, sky.shape[2]) for sky in skies], axis=0)
    return jnp.dot(modes, block, preferred_element_type=jnp.float32)


def reduce_kernel(modes_ref, *refs):
    out = refs[-1]
    out[...] = contract(modes_ref[...], refs[:-1]).astype(out.dtype).reshape(out.shape)


def by_rows(count, ell, first=0):
    return pl.BlockSpec((count, ROWS, ell), lambda g: (0, g + first // ROWS, 0))


def fixed(shape):
    return pl.BlockSpec(shape, lambda g: (0,) * len(shape))


def sky_specs(skies, first):
    return [by_rows(sky.shape[0], sky.shape[2], low) for sky, low in zip(skies, first)]


def reduce(modes, skies, first, n_modes, dtype=jnp.bfloat16):
    _, rows, ell = skies[-1].shape
    return pl.pallas_call(
        reduce_kernel,
        grid=(rows // ROWS,),
        in_specs=[fixed(modes.shape)] + sky_specs(skies, first),
        out_specs=by_rows(n_modes, ell),
        out_shape=jax.ShapeDtypeStruct((n_modes, rows, ell), dtype),
        compiler_params=pltpu.CompilerParams(vmem_limit_bytes=VMEM_LIMIT),
        cost_estimate=pl.CostEstimate(flops=1024, bytes_accessed=1024, transcendentals=0),
    )(modes, *skies)


def restore_kernel(up_ref, ratio_ref, kept_ref, came_ref, *outs, spots):
    n_modes, _, ell = came_ref.shape
    freqs = up_ref.shape[0] // ROWS // PARTS
    total = kept_ref[...] + came_ref[...].astype(jnp.float32)
    weighted = (total * ratio_ref[...]).astype(jnp.bfloat16).reshape(n_modes * ROWS, ell)
    for (j, low, high), out in zip(spots, outs):
        modes = up_ref[(j * freqs + low) * ROWS:(j * freqs + high) * ROWS, :]
        value = jnp.dot(modes, weighted, preferred_element_type=jnp.float32)
        out[...] = value.astype(jnp.bfloat16).reshape(out.shape)


def restore(kept, came, ratios, up, spots):
    n_modes, rows, ell = came.shape
    return pl.pallas_call(
        functools.partial(restore_kernel, spots=spots),
        grid=(rows // ROWS,),
        in_specs=[fixed(up.shape), fixed(ratios.shape)] + [by_rows(n_modes, ell)] * 2,
        out_specs=[by_rows(high - low, ell) for _, low, high in spots],
        out_shape=[jax.ShapeDtypeStruct((high - low, rows, ell), jnp.bfloat16) for _, low, high in spots],
        compiler_params=pltpu.CompilerParams(vmem_limit_bytes=VMEM_LIMIT),
        cost_estimate=pl.CostEstimate(flops=1024, bytes_accessed=1024, transcendentals=0),
    )(up, ratios, kept, came)


def place_kernel(where, *refs, spots, first):
    count = len(spots)
    pieces, out, sems = refs[:count], refs[-2], refs[-1]
    rows = pieces[0].shape[1]
    copies = [
        pltpu.make_async_copy(pieces[n], out.at[low:high, where[j], first:first + rows, :], sems.at[n])
        for n, (j, low, high) in enumerate(spots)
    ]
    for copy in copies:
        copy.start()
    for copy in copies:
        copy.wait()


def place(where, pieces, spots, first, shape, into=None):
    count = len(spots)
    extra = [] if into is None else [into]
    anywhere = pl.BlockSpec(memory_space=pl.ANY)
    return pl.pallas_call(
        functools.partial(place_kernel, spots=spots, first=first),
        grid_spec=pltpu.PrefetchScalarGridSpec(
            num_scalar_prefetch=1,
            grid=(),
            in_specs=[pl.BlockSpec(memory_space=pltpu.VMEM)] * count + [anywhere] * len(extra),
            out_specs=anywhere,
            scratch_shapes=[pltpu.SemaphoreType.DMA((count,))],
        ),
        out_shape=jax.ShapeDtypeStruct(shape, jnp.bfloat16),
        input_output_aliases={count + 1: 0} if extra else {},
        compiler_params=pltpu.CompilerParams(vmem_limit_bytes=VMEM_LIMIT),
        cost_estimate=pl.CostEstimate(flops=1024, bytes_accessed=1024, transcendentals=0),
    )(where, *pieces, *extra)


def anchor_kernel(*refs):
    del refs


def anchor(values, flops):
    anywhere = pl.BlockSpec(memory_space=pl.ANY)
    return pl.pallas_call(
        anchor_kernel,
        in_specs=[anywhere] * len(values),
        out_specs=[anywhere] * len(values),
        out_shape=[jax.ShapeDtypeStruct(value.shape, value.dtype) for value in values],
        input_output_aliases={n: n for n in range(len(values))},
        compiler_params=pltpu.CompilerParams(vmem_limit_bytes=1024 * 1024),
        cost_estimate=pl.CostEstimate(flops=flops, bytes_accessed=1024, transcendentals=0),
    )(*values)


def staged(visibility, beam_transfer, tile_mask, first_block, eigen_modes, signal_noise):
    freqs, parts, rows_all, base = visibility.shape
    _, freq_total, _, ell = beam_transfer.shape
    n_modes = eigen_modes.shape[2]
    ell_tiles = ell // TILE
    z, x, p = lax.axis_index("fm"), lax.axis_index("kl"), lax.axis_index("pol")
    other = [(0, 1), (1, 0)]

    def along_z(value, j):
        return lax.ppermute(value, "fm", [(i, i ^ j) for i in range(parts)])

    def along_x(value):
        return lax.ppermute(value, "kl", other)

    def cut(j, first, rows):
        return lax.dynamic_slice(visibility, (0, z ^ j, first, 0), (freqs, 1, rows, base)).reshape(freqs, rows, base)

    index = jnp.arange(parts + 2, dtype=jnp.int32)
    where = jnp.where(
        index < parts, z ^ index, jnp.where(index == parts, (x == p).astype(jnp.int32), x * ell_tiles)
    ).astype(jnp.int32)
    ratio = signal_noise[0] / (1.0 + signal_noise[0])
    ratios = jnp.broadcast_to(ratio[:, None, None], (n_modes, 1, ell))
    beam = beam_transfer.reshape(freq_total, base, ell)
    shape = (freqs, parts, rows_all, ell)

    fence = lax.optimization_barrier
    most, half = rows_all - ROWS, freqs // 2
    blocks = [[(0, f)] for f in range(freqs)]
    halves = [[(f // half, f % half)] for f in range(freqs)]
    a = {j: along_z(cut(j, 0, ROWS), j) for j in (3, 2, 1)}
    mine = [cut(0, 0, rows_all)[n:n + half] for n in (0, half)]
    others = [along_x(part) for part in mine]
    b = {j: cut(j, ROWS, most) for j in (1, 2, 3)}
    held, down, up = hold(where, tile_mask[0], first_block, beam, eigen_modes[0])
    (a[1], a[2], a[3]), b, others, down, up = fence(((a[1], a[2], a[3]), b, others, down, up))
    b[1], b[3] = along_z(b[1], 1), along_z(b[3], 3)
    own = project(where, mine, others, held, 0, halves, 200_000_000)
    skies = [own] + [project(where, [a[j]], [along_x(a[j])], held, j, blocks, 200_000_000) for j in (1, 2, 3)]
    gone = reduce(down, [leave for _, leave in skies], (0, 0, 0, 0), n_modes)
    stay_a = [stay for stay, _ in skies]
    b[3], stay_a, gone = fence((b[3], stay_a, gone))
    x_3 = along_x(b[3])
    x_1, b[2] = anchor([along_x(b[1]), along_z(b[2], 2)], 1_500_000_000)
    kept = reduce(down, stay_a, (0, 0, 0, 0), n_modes, jnp.float32)
    spots = [(j, 0, freqs) for j in (1, 2, 3, 0)]
    outs = restore(kept, lax.ppermute(gone, "pol", other), ratios, up, spots)
    near = project(where, [b[1]], [x_1], held, 1, blocks)
    x_3, b, outs, near = fence((x_3, b, outs, near))
    first = {j: along_z(outs[j - 1], j) for j in (1, 2, 3)}
    first[0] = outs[3]
    x_2 = along_x(b[2])
    last = project(where, [b[3]], [x_3], held, 3, blocks)
    skies = [own, near, project(where, [b[2]], [x_2], held, 2, blocks), last]
    gone = reduce(down, [leave for _, leave in skies], (ROWS, 0, 0, 0), n_modes)
    kept = reduce(down, [stay for stay, _ in skies], (ROWS, 0, 0, 0), n_modes, jnp.float32)
    (first[2], first[3], first[1]), first[0], kept, gone = fence(
        ((first[2], first[3], first[1]), first[0], kept, gone)
    )
    outs = fence(restore(kept, lax.ppermute(gone, "pol", other), ratios, up, spots))
    back = [along_z(outs[j - 1], j) for j in (1, 2, 3)]
    result = place(where, [first[j] for j in (1, 2, 3, 0)], spots, 0, shape)
    result = place(where, [outs[3], back[0]], [spots[3], spots[0]], ROWS, shape, into=result)
    return place(where, back[1:], spots[1:3], ROWS, shape, into=result)


def plain(visibility, beam_transfer, tile_mask, first_block, eigen_modes, signal_noise):
    owned_modes, freq_total, base_half, ell_local = beam_transfer.shape
    base_tiles, ell_tiles = base_half // TILE, ell_local // TILE
    block_ids = lax.axis_index("kl") * ell_tiles + jnp.arange(ell_tiles, dtype=jnp.int32)
    inside = (first_block[:, None] <= block_ids[None, :]).astype(jnp.int32)
    keep_tiles = tile_mask * inside[:, None, :]
    shaped = beam_transfer.reshape(owned_modes, freq_total, base_tiles, TILE, ell_tiles, TILE)
    masked_beam = shaped * keep_tiles.astype(jnp.bfloat16)[:, None, :, None, :, None]
    masked_beam = masked_beam.reshape(owned_modes, freq_total, base_half, ell_local)
    arrived = lax.all_to_all(visibility, "fm", split_axis=1, concat_axis=0, tiled=True)
    partial_value = jnp.einsum(
        "fmrb,mfbl->fmrl",
        lax.all_gather(arrived, "kl", axis=2, tiled=True),
        masked_beam,
        preferred_element_type=jnp.float32,
    )
    sky_sum = lax.psum_scatter(
        partial_value.astype(jnp.bfloat16), "pol", scatter_dimension=2, tiled=True
    ).astype(jnp.float32)
    modes_float = eigen_modes.astype(jnp.float32)
    coeffs = jnp.einsum("mfk,fmrl->mkrl", modes_float, sky_sum, precision=lax.Precision.HIGHEST)
    ratios = signal_noise / (1.0 + signal_noise)
    weighted = (coeffs * ratios[:, :, None, None]).astype(jnp.bfloat16)
    filtered = jnp.einsum(
        "mfk,mkrl->fmrl", eigen_modes, weighted, preferred_element_type=jnp.float32
    ).astype(jnp.bfloat16)
    return lax.all_to_all(filtered, "fm", split_axis=0, concat_axis=1, tiled=True)


def per_device(*args, sizes):
    visibility, beam_transfer = args[0], args[1]
    _, modes, rows, _ = visibility.shape
    fits = (
        sizes["kl"] == 2
        and sizes["pol"] == 2
        and modes == sizes["fm"] == PARTS
        and beam_transfer.shape[0] == 1
        and rows == 3 * ROWS
        and visibility.shape[0] % 2 == 0
    )
    if not fits:
        return plain(*args)
    return staged(*args)


def solution(mesh):
    placed = (
        P(("group", "fm"), None, "kl", "pol"),
        P(("group", "fm"), None, "pol", "kl"),
        P("fm", "pol", "kl"),
        P("fm"),
        P(("group", "fm"), None, None),
        P(("group", "fm"), None),
    )
    return jax.shard_map(
        functools.partial(per_device, sizes=dict(mesh.shape)),
        mesh=mesh,
        in_specs=placed,
        out_specs=P(("group", "fm"), None, "pol", "kl"),
        check_vma=False,
    )
```

```python
import functools
import jax
import jax.numpy as jnp
from jax import lax
from jax.experimental import pallas as pl
from jax.experimental.pallas import tpu as pltpu
from jax.sharding import PartitionSpec as P

TILE = 128
PARTS = 4
ROWS = 16
VMEM_LIMIT = 24 * 1024 * 1024


def hold_kernel(where, tiles, starts, beam, modes_ref, held, down_ref, up_ref, mask, sems):
    freq, base, ell = held.shape
    n_modes = modes_ref.shape[1]
    ell_tiles, base_tiles, freqs = ell // TILE, base // TILE, freq // PARTS
    copies = [pltpu.make_async_copy(beam.at[f], held.at[f], sems.at[f]) for f in range(freq)]
    for copy in copies:
        copy.start()
    for b in range(base_tiles):
        for l in range(ell_tiles):
            kept = jnp.where(starts[0] <= where[PARTS + 1] + l, tiles[b, l], 0).astype(jnp.float32)
            mask[b * TILE:(b + 1) * TILE, l * TILE:(l + 1) * TILE] = jnp.full(
                (TILE, TILE), kept, jnp.float32
            ).astype(jnp.bfloat16)
    modes = modes_ref[...]

    def pick(shape, axis):
        big = lax.broadcasted_iota(jnp.int32, shape, axis) // ROWS
        small = lax.broadcasted_iota(jnp.int32, shape, 1 - axis)
        if freq in shape:
            piece, within = big // freqs, big % freqs
            big = within
            for j in range(PARTS):
                big = jnp.where(piece == j, where[j] * freqs + within, big)
        return jnp.where(big == small, 1.0, 0.0).astype(jnp.bfloat16)

    def lane(shape):
        rows = lax.broadcasted_iota(jnp.int32, shape, 0) % ROWS
        columns = lax.broadcasted_iota(jnp.int32, shape, 1) % ROWS
        return rows == columns

    def dot(a, b, dims):
        return lax.dot_general(a, b, (dims, ((), ())), preferred_element_type=jnp.float32)

    tall = dot(pick((n_modes * ROWS, n_modes), 0), modes, ((1,), (1,))).astype(jnp.bfloat16)
    value = dot(tall, pick((freq, freq * ROWS), 1), ((1,), (0,)))
    down_ref[...] = jnp.where(lane(value.shape), value, 0.0).astype(jnp.bfloat16)
    tall = dot(pick((freq * ROWS, freq), 0), modes, ((1,), (0,))).astype(jnp.bfloat16)
    value = dot(tall, pick((n_modes, n_modes * ROWS), 1), ((1,), (0,)))
    up_ref[...] = jnp.where(lane(value.shape), value, 0.0).astype(jnp.bfloat16)
    for f, copy in enumerate(copies):
        copy.wait()
        held[f] = held[f] * mask[...]


def hold(where, tiles, starts, beam, modes):
    freq, base, ell = beam.shape
    size, wide = freq * ROWS, modes.shape[1] * ROWS
    vmem = pl.BlockSpec(memory_space=pltpu.VMEM)
    return pl.pallas_call(
        hold_kernel,
        grid_spec=pltpu.PrefetchScalarGridSpec(
            num_scalar_prefetch=3,
            grid=(),
            in_specs=[pl.BlockSpec(memory_space=pl.ANY), vmem],
            out_specs=[vmem] * 3,
            scratch_shapes=[pltpu.VMEM((base, ell), jnp.bfloat16), pltpu.SemaphoreType.DMA((freq,))],
        ),
        out_shape=[
            pltpu.VMEM(beam.shape, beam.dtype),
            jax.ShapeDtypeStruct((wide, size), jnp.bfloat16),
            jax.ShapeDtypeStruct((size, wide), jnp.bfloat16),
        ],
        compiler_params=pltpu.CompilerParams(vmem_limit_bytes=VMEM_LIMIT),
        cost_estimate=pl.CostEstimate(flops=1024, bytes_accessed=1024, transcendentals=0),
    )(where, tiles, starts, beam, modes)


def project_kernel(where, *refs, piece, blocks):
    count = (len(refs) - 3) // 2
    mine, others = refs[:count], refs[count:2 * count]
    held, stay_ref, leave_ref = refs[2 * count:]
    freqs, rows, _ = stay_ref.shape
    first = where[piece] * freqs
    own = where[PARTS] == 1
    for f in range(freqs):
        a = jnp.concatenate([mine[n][k] for n, k in blocks[f]], axis=0)
        b = jnp.concatenate([others[n][k] for n, k in blocks[f]], axis=0)
        lines = jnp.concatenate([jnp.where(own, a, b), jnp.where(own, b, a)], axis=0)
        value = jnp.dot(lines, held[first + f], preferred_element_type=jnp.float32).astype(jnp.bfloat16)
        stay_ref[f] = value[:rows]
        leave_ref[f] = value[rows:]


def project(where, mine, others, held, piece, blocks, flops=1024):
    ell = held.shape[2]
    rows = sum(mine[n].shape[1] for n, _ in blocks[0])
    vmem = pl.BlockSpec(memory_space=pltpu.VMEM)
    return pl.pallas_call(
        functools.partial(project_kernel, piece=piece, blocks=blocks),
        grid_spec=pltpu.PrefetchScalarGridSpec(
            num_scalar_prefetch=1, grid=(), in_specs=[vmem] * (2 * len(mine) + 1), out_specs=[vmem] * 2
        ),
        out_shape=[jax.ShapeDtypeStruct((len(blocks), rows, ell), jnp.bfloat16)] * 2,
        compiler_params=pltpu.CompilerParams(vmem_limit_bytes=VMEM_LIMIT),
        cost_estimate=pl.CostEstimate(flops=flops, bytes_accessed=1024, transcendentals=0),
    )(where, *mine, *others, pltpu.with_memory_space_constraint(held, pltpu.VMEM))


def contract(modes, skies):
    block = jnp.concatenate([sky[...].reshape(sky.shape[0] * ROWS, sky.shape[2]) for sky in skies], axis=0)
    return jnp.dot(modes, block, preferred_element_type=jnp.float32)


def reduce_kernel(modes_ref, *refs):
    out = refs[-1]
    out[...] = contract(modes_ref[...], refs[:-1]).astype(out.dtype).reshape(out.shape)


def by_rows(count, ell, first=0):
    return pl.BlockSpec((count, ROWS, ell), lambda g: (0, g + first // ROWS, 0))


def fixed(shape):
    return pl.BlockSpec(shape, lambda g: (0,) * len(shape))


def sky_specs(skies, first):
    return [by_rows(sky.shape[0], sky.shape[2], low) for sky, low in zip(skies, first)]


def reduce(modes, skies, first, n_modes, dtype=jnp.bfloat16):
    _, rows, ell = skies[-1].shape
    return pl.pallas_call(
        reduce_kernel,
        grid=(rows // ROWS,),
        in_specs=[fixed(modes.shape)] + sky_specs(skies, first),
        out_specs=by_rows(n_modes, ell),
        out_shape=jax.ShapeDtypeStruct((n_modes, rows, ell), dtype),
        compiler_params=pltpu.CompilerParams(vmem_limit_bytes=VMEM_LIMIT),
        cost_estimate=pl.CostEstimate(flops=1024, bytes_accessed=1024, transcendentals=0),
    )(modes, *skies)


def restore_kernel(up_ref, ratio_ref, kept_ref, came_ref, *outs, spots):
    n_modes, _, ell = came_ref.shape
    freqs = up_ref.shape[0] // ROWS // PARTS
    total = kept_ref[...] + came_ref[...].astype(jnp.float32)
    weighted = (total * ratio_ref[...]).astype(jnp.bfloat16).reshape(n_modes * ROWS, ell)
    for (j, low, high), out in zip(spots, outs):
        modes = up_ref[(j * freqs + low) * ROWS:(j * freqs + high) * ROWS, :]
        value = jnp.dot(modes, weighted, preferred_element_type=jnp.float32)
        out[...] = value.astype(jnp.bfloat16).reshape(out.shape)


def restore(kept, came, ratios, up, spots):
    n_modes, rows, ell = came.shape
    return pl.pallas_call(
        functools.partial(restore_kernel, spots=spots),
        grid=(rows // ROWS,),
        in_specs=[fixed(up.shape), fixed(ratios.shape)] + [by_rows(n_modes, ell)] * 2,
        out_specs=[by_rows(high - low, ell) for _, low, high in spots],
        out_shape=[jax.ShapeDtypeStruct((high - low, rows, ell), jnp.bfloat16) for _, low, high in spots],
        compiler_params=pltpu.CompilerParams(vmem_limit_bytes=VMEM_LIMIT),
        cost_estimate=pl.CostEstimate(flops=1024, bytes_accessed=1024, transcendentals=0),
    )(up, ratios, kept, came)


def place_kernel(where, *refs, spots, first):
    count = len(spots)
    pieces, out, sems = refs[:count], refs[-2], refs[-1]
    rows = pieces[0].shape[1]
    copies = [
        pltpu.make_async_copy(pieces[n], out.at[low:high, where[j], first:first + rows, :], sems.at[n])
        for n, (j, low, high) in enumerate(spots)
    ]
    for copy in copies:
        copy.start()
    for copy in copies:
        copy.wait()


def place(where, pieces, spots, first, shape, into=None):
    count = len(spots)
    extra = [] if into is None else [into]
    anywhere = pl.BlockSpec(memory_space=pl.ANY)
    return pl.pallas_call(
        functools.partial(place_kernel, spots=spots, first=first),
        grid_spec=pltpu.PrefetchScalarGridSpec(
            num_scalar_prefetch=1,
            grid=(),
            in_specs=[pl.BlockSpec(memory_space=pltpu.VMEM)] * count + [anywhere] * len(extra),
            out_specs=anywhere,
            scratch_shapes=[pltpu.SemaphoreType.DMA((count,))],
        ),
        out_shape=jax.ShapeDtypeStruct(shape, jnp.bfloat16),
        input_output_aliases={count + 1: 0} if extra else {},
        compiler_params=pltpu.CompilerParams(vmem_limit_bytes=VMEM_LIMIT),
        cost_estimate=pl.CostEstimate(flops=1024, bytes_accessed=1024, transcendentals=0),
    )(where, *pieces, *extra)


def anchor_kernel(*refs):
    del refs


def anchor(values, flops):
    anywhere = pl.BlockSpec(memory_space=pl.ANY)
    return pl.pallas_call(
        anchor_kernel,
        in_specs=[anywhere] * len(values),
        out_specs=[anywhere] * len(values),
        out_shape=[jax.ShapeDtypeStruct(value.shape, value.dtype) for value in values],
        input_output_aliases={n: n for n in range(len(values))},
        compiler_params=pltpu.CompilerParams(vmem_limit_bytes=1024 * 1024),
        cost_estimate=pl.CostEstimate(flops=flops, bytes_accessed=1024, transcendentals=0),
    )(*values)


def staged(visibility, beam_transfer, tile_mask, first_block, eigen_modes, signal_noise):
    freqs, parts, rows_all, base = visibility.shape
    _, freq_total, _, ell = beam_transfer.shape
    n_modes = eigen_modes.shape[2]
    ell_tiles = ell // TILE
    z, x, p = lax.axis_index("fm"), lax.axis_index("kl"), lax.axis_index("pol")
    other = [(0, 1), (1, 0)]

    def along_z(value, j):
        return lax.ppermute(value, "fm", [(i, i ^ j) for i in range(parts)])

    def along_x(value):
        return lax.ppermute(value, "kl", other)

    def cut(j, first, rows):
        return lax.dynamic_slice(visibility, (0, z ^ j, first, 0), (freqs, 1, rows, base)).reshape(freqs, rows, base)

    index = jnp.arange(parts + 2, dtype=jnp.int32)
    where = jnp.where(
        index < parts, z ^ index, jnp.where(index == parts, (x == p).astype(jnp.int32), x * ell_tiles)
    ).astype(jnp.int32)
    ratio = signal_noise[0] / (1.0 + signal_noise[0])
    ratios = jnp.broadcast_to(ratio[:, None, None], (n_modes, 1, ell))
    beam = beam_transfer.reshape(freq_total, base, ell)
    shape = (freqs, parts, rows_all, ell)

    fence = lax.optimization_barrier
    most, half = rows_all - ROWS, freqs // 2
    blocks = [[(0, f)] for f in range(freqs)]
    halves = [[(f // half, f % half)] for f in range(freqs)]
    a = {j: along_z(cut(j, 0, ROWS), j) for j in (3, 2, 1)}
    mine = [cut(0, 0, rows_all)[n:n + half] for n in (0, half)]
    others = [along_x(part) for part in mine]
    b = {j: cut(j, ROWS, most) for j in (1, 2, 3)}
    held, down, up = hold(where, tile_mask[0], first_block, beam, eigen_modes[0])
    (a[3], a[2], a[1]), b, others, down, up = fence(((a[3], a[2], a[1]), b, others, down, up))
    b[1], b[2] = along_z(b[1], 1), along_z(b[2], 2)
    own = project(where, mine, others, held, 0, halves, 400_000_000)
    skies = [own] + [project(where, [a[j]], [along_x(a[j])], held, j, blocks, 400_000_000) for j in (1, 2, 3)]
    gone = reduce(down, [leave for _, leave in skies], (0, 0, 0, 0), n_modes)
    stay_a = [stay for stay, _ in skies]
    b[2], b[3], stay_a, gone = fence((b[2], b[3], stay_a, gone))
    x_2 = along_x(b[2])
    x_1, = anchor([along_x(b[1])], 2_500_000_000)
    b[3] = along_z(b[3], 3)
    kept = reduce(down, stay_a, (0, 0, 0, 0), n_modes, jnp.float32)
    spots = [(j, 0, freqs) for j in (1, 2, 3, 0)]
    outs = restore(kept, lax.ppermute(gone, "pol", other), ratios, up, spots)
    near = project(where, [b[1]], [x_1], held, 1, blocks)
    x_2, b, outs, near = fence((x_2, b, outs, near))
    first = {j: along_z(outs[j - 1], j) for j in (1, 2, 3)}
    first[0] = outs[3]
    x_3 = along_x(b[3])
    skies = [own, near] + [project(where, [b[j]], [x], held, j, blocks) for j, x in ((2, x_2), (3, x_3))]
    gone = reduce(down, [leave for _, leave in skies], (ROWS, 0, 0, 0), n_modes)
    kept = reduce(down, [stay for stay, _ in skies], (ROWS, 0, 0, 0), n_modes, jnp.float32)
    (first[2], first[3], first[1]), first[0], kept, gone = fence(
        ((first[2], first[3], first[1]), first[0], kept, gone)
    )
    outs = fence(restore(kept, lax.ppermute(gone, "pol", other), ratios, up, spots))
    back = [along_z(outs[j - 1], j) for j in (1, 2, 3)]
    result = place(where, [first[j] for j in (1, 2, 3, 0)], spots, 0, shape)
    result = place(where, [outs[3], back[0]], [spots[3], spots[0]], ROWS, shape, into=result)
    return place(where, back[1:], spots[1:3], ROWS, shape, into=result)


def plain(visibility, beam_transfer, tile_mask, first_block, eigen_modes, signal_noise):
    owned_modes, freq_total, base_half, ell_local = beam_transfer.shape
    base_tiles, ell_tiles = base_half // TILE, ell_local // TILE
    block_ids = lax.axis_index("kl") * ell_tiles + jnp.arange(ell_tiles, dtype=jnp.int32)
    inside = (first_block[:, None] <= block_ids[None, :]).astype(jnp.int32)
    keep_tiles = tile_mask * inside[:, None, :]
    shaped = beam_transfer.reshape(owned_modes, freq_total, base_tiles, TILE, ell_tiles, TILE)
    masked_beam = shaped * keep_tiles.astype(jnp.bfloat16)[:, None, :, None, :, None]
    masked_beam = masked_beam.reshape(owned_modes, freq_total, base_half, ell_local)
    arrived = lax.all_to_all(visibility, "fm", split_axis=1, concat_axis=0, tiled=True)
    partial_value = jnp.einsum(
        "fmrb,mfbl->fmrl",
        lax.all_gather(arrived, "kl", axis=2, tiled=True),
        masked_beam,
        preferred_element_type=jnp.float32,
    )
    sky_sum = lax.psum_scatter(
        partial_value.astype(jnp.bfloat16), "pol", scatter_dimension=2, tiled=True
    ).astype(jnp.float32)
    modes_float = eigen_modes.astype(jnp.float32)
    coeffs = jnp.einsum("mfk,fmrl->mkrl", modes_float, sky_sum, precision=lax.Precision.HIGHEST)
    ratios = signal_noise / (1.0 + signal_noise)
    weighted = (coeffs * ratios[:, :, None, None]).astype(jnp.bfloat16)
    filtered = jnp.einsum(
        "mfk,mkrl->fmrl", eigen_modes, weighted, preferred_element_type=jnp.float32
    ).astype(jnp.bfloat16)
    return lax.all_to_all(filtered, "fm", split_axis=0, concat_axis=1, tiled=True)


def per_device(*args, sizes):
    visibility, beam_transfer = args[0], args[1]
    _, modes, rows, _ = visibility.shape
    fits = (
        sizes["kl"] == 2
        and sizes["pol"] == 2
        and modes == sizes["fm"] == PARTS
        and beam_transfer.shape[0] == 1
        and rows == 3 * ROWS
        and visibility.shape[0] % 2 == 0
    )
    if not fits:
        return plain(*args)
    return staged(*args)


def solution(mesh):
    placed = (
        P(("group", "fm"), None, "kl", "pol"),
        P(("group", "fm"), None, "pol", "kl"),
        P("fm", "pol", "kl"),
        P("fm"),
        P(("group", "fm"), None, None),
        P(("group", "fm"), None),
    )
    return jax.shard_map(
        functools.partial(per_device, sizes=dict(mesh.shape)),
        mesh=mesh,
        in_specs=placed,
        out_specs=P(("group", "fm"), None, "pol", "kl"),
        check_vma=False,
    )
```

```python
import functools
import jax
import jax.numpy as jnp
from jax import lax
from jax.experimental import pallas as pl
from jax.experimental.pallas import tpu as pltpu
from jax.sharding import PartitionSpec as P

TILE = 128
PARTS = 4
ROWS = 16
VMEM_LIMIT = 24 * 1024 * 1024


def hold_kernel(where, tiles, starts, beam, modes_ref, held, down_ref, up_ref, mask, sems):
    freq, base, ell = held.shape
    n_modes = modes_ref.shape[1]
    ell_tiles, base_tiles, freqs = ell // TILE, base // TILE, freq // PARTS
    copies = [pltpu.make_async_copy(beam.at[f], held.at[f], sems.at[f]) for f in range(freq)]
    for copy in copies:
        copy.start()
    for b in range(base_tiles):
        for l in range(ell_tiles):
            kept = jnp.where(starts[0] <= where[PARTS + 1] + l, tiles[b, l], 0).astype(jnp.float32)
            mask[b * TILE:(b + 1) * TILE, l * TILE:(l + 1) * TILE] = jnp.full(
                (TILE, TILE), kept, jnp.float32
            ).astype(jnp.bfloat16)
    modes = modes_ref[...]

    def pick(shape, axis):
        big = lax.broadcasted_iota(jnp.int32, shape, axis) // ROWS
        small = lax.broadcasted_iota(jnp.int32, shape, 1 - axis)
        if freq in shape:
            piece, within = big // freqs, big % freqs
            big = within
            for j in range(PARTS):
                big = jnp.where(piece == j, where[j] * freqs + within, big)
        return jnp.where(big == small, 1.0, 0.0).astype(jnp.bfloat16)

    def lane(shape):
        rows = lax.broadcasted_iota(jnp.int32, shape, 0) % ROWS
        columns = lax.broadcasted_iota(jnp.int32, shape, 1) % ROWS
        return rows == columns

    def dot(a, b, dims):
        return lax.dot_general(a, b, (dims, ((), ())), preferred_element_type=jnp.float32)

    tall = dot(pick((n_modes * ROWS, n_modes), 0), modes, ((1,), (1,))).astype(jnp.bfloat16)
    value = dot(tall, pick((freq, freq * ROWS), 1), ((1,), (0,)))
    down_ref[...] = jnp.where(lane(value.shape), value, 0.0).astype(jnp.bfloat16)
    tall = dot(pick((freq * ROWS, freq), 0), modes, ((1,), (0,))).astype(jnp.bfloat16)
    value = dot(tall, pick((n_modes, n_modes * ROWS), 1), ((1,), (0,)))
    up_ref[...] = jnp.where(lane(value.shape), value, 0.0).astype(jnp.bfloat16)
    for f, copy in enumerate(copies):
        copy.wait()
        held[f] = held[f] * mask[...]


def hold(where, tiles, starts, beam, modes):
    freq, base, ell = beam.shape
    size, wide = freq * ROWS, modes.shape[1] * ROWS
    vmem = pl.BlockSpec(memory_space=pltpu.VMEM)
    return pl.pallas_call(
        hold_kernel,
        grid_spec=pltpu.PrefetchScalarGridSpec(
            num_scalar_prefetch=3,
            grid=(),
            in_specs=[pl.BlockSpec(memory_space=pl.ANY), vmem],
            out_specs=[vmem] * 3,
            scratch_shapes=[pltpu.VMEM((base, ell), jnp.bfloat16), pltpu.SemaphoreType.DMA((freq,))],
        ),
        out_shape=[
            pltpu.VMEM(beam.shape, beam.dtype),
            jax.ShapeDtypeStruct((wide, size), jnp.bfloat16),
            jax.ShapeDtypeStruct((size, wide), jnp.bfloat16),
        ],
        compiler_params=pltpu.CompilerParams(vmem_limit_bytes=VMEM_LIMIT),
        cost_estimate=pl.CostEstimate(flops=1024, bytes_accessed=1024, transcendentals=0),
    )(where, tiles, starts, beam, modes)


def project_kernel(where, *refs, piece, blocks):
    count = (len(refs) - 3) // 2
    mine, others = refs[:count], refs[count:2 * count]
    held, stay_ref, leave_ref = refs[2 * count:]
    freqs, rows, _ = stay_ref.shape
    first = where[piece] * freqs
    own = where[PARTS] == 1
    for f in range(freqs):
        a = jnp.concatenate([mine[n][k] for n, k in blocks[f]], axis=0)
        b = jnp.concatenate([others[n][k] for n, k in blocks[f]], axis=0)
        lines = jnp.concatenate([jnp.where(own, a, b), jnp.where(own, b, a)], axis=0)
        value = jnp.dot(lines, held[first + f], preferred_element_type=jnp.float32).astype(jnp.bfloat16)
        stay_ref[f] = value[:rows]
        leave_ref[f] = value[rows:]


def project(where, mine, others, held, piece, blocks, flops=1024):
    ell = held.shape[2]
    rows = sum(mine[n].shape[1] for n, _ in blocks[0])
    vmem = pl.BlockSpec(memory_space=pltpu.VMEM)
    return pl.pallas_call(
        functools.partial(project_kernel, piece=piece, blocks=blocks),
        grid_spec=pltpu.PrefetchScalarGridSpec(
            num_scalar_prefetch=1, grid=(), in_specs=[vmem] * (2 * len(mine) + 1), out_specs=[vmem] * 2
        ),
        out_shape=[jax.ShapeDtypeStruct((len(blocks), rows, ell), jnp.bfloat16)] * 2,
        compiler_params=pltpu.CompilerParams(vmem_limit_bytes=VMEM_LIMIT),
        cost_estimate=pl.CostEstimate(flops=flops, bytes_accessed=1024, transcendentals=0),
    )(where, *mine, *others, pltpu.with_memory_space_constraint(held, pltpu.VMEM))


def contract(modes, skies):
    block = jnp.concatenate([sky[...].reshape(sky.shape[0] * ROWS, sky.shape[2]) for sky in skies], axis=0)
    return jnp.dot(modes, block, preferred_element_type=jnp.float32)


def reduce_kernel(modes_ref, *refs):
    out = refs[-1]
    out[...] = contract(modes_ref[...], refs[:-1]).astype(out.dtype).reshape(out.shape)


def by_rows(count, ell, first=0):
    return pl.BlockSpec((count, ROWS, ell), lambda g: (0, g + first // ROWS, 0))


def fixed(shape):
    return pl.BlockSpec(shape, lambda g: (0,) * len(shape))


def sky_specs(skies, first):
    return [by_rows(sky.shape[0], sky.shape[2], low) for sky, low in zip(skies, first)]


def reduce(modes, skies, first, n_modes, dtype=jnp.bfloat16):
    _, rows, ell = skies[-1].shape
    return pl.pallas_call(
        reduce_kernel,
        grid=(rows // ROWS,),
        in_specs=[fixed(modes.shape)] + sky_specs(skies, first),
        out_specs=by_rows(n_modes, ell),
        out_shape=jax.ShapeDtypeStruct((n_modes, rows, ell), dtype),
        compiler_params=pltpu.CompilerParams(vmem_limit_bytes=VMEM_LIMIT),
        cost_estimate=pl.CostEstimate(flops=1024, bytes_accessed=1024, transcendentals=0),
    )(modes, *skies)


def restore_kernel(up_ref, ratio_ref, kept_ref, came_ref, *outs, spots):
    n_modes, _, ell = came_ref.shape
    freqs = up_ref.shape[0] // ROWS // PARTS
    total = kept_ref[...] + came_ref[...].astype(jnp.float32)
    weighted = (total * ratio_ref[...]).astype(jnp.bfloat16).reshape(n_modes * ROWS, ell)
    for (j, low, high), out in zip(spots, outs):
        modes = up_ref[(j * freqs + low) * ROWS:(j * freqs + high) * ROWS, :]
        value = jnp.dot(modes, weighted, preferred_element_type=jnp.float32)
        out[...] = value.astype(jnp.bfloat16).reshape(out.shape)


def restore(kept, came, ratios, up, spots):
    n_modes, rows, ell = came.shape
    return pl.pallas_call(
        functools.partial(restore_kernel, spots=spots),
        grid=(rows // ROWS,),
        in_specs=[fixed(up.shape), fixed(ratios.shape)] + [by_rows(n_modes, ell)] * 2,
        out_specs=[by_rows(high - low, ell) for _, low, high in spots],
        out_shape=[jax.ShapeDtypeStruct((high - low, rows, ell), jnp.bfloat16) for _, low, high in spots],
        compiler_params=pltpu.CompilerParams(vmem_limit_bytes=VMEM_LIMIT),
        cost_estimate=pl.CostEstimate(flops=1024, bytes_accessed=1024, transcendentals=0),
    )(up, ratios, kept, came)


def place_kernel(where, *refs, spots, first):
    count = len(spots)
    pieces, out, sems = refs[:count], refs[-2], refs[-1]
    rows = pieces[0].shape[1]
    copies = [
        pltpu.make_async_copy(pieces[n], out.at[low:high, where[j], first:first + rows, :], sems.at[n])
        for n, (j, low, high) in enumerate(spots)
    ]
    for copy in copies:
        copy.start()
    for copy in copies:
        copy.wait()


def place(where, pieces, spots, first, shape, into=None):
    count = len(spots)
    extra = [] if into is None else [into]
    anywhere = pl.BlockSpec(memory_space=pl.ANY)
    return pl.pallas_call(
        functools.partial(place_kernel, spots=spots, first=first),
        grid_spec=pltpu.PrefetchScalarGridSpec(
            num_scalar_prefetch=1,
            grid=(),
            in_specs=[pl.BlockSpec(memory_space=pltpu.VMEM)] * count + [anywhere] * len(extra),
            out_specs=anywhere,
            scratch_shapes=[pltpu.SemaphoreType.DMA((count,))],
        ),
        out_shape=jax.ShapeDtypeStruct(shape, jnp.bfloat16),
        input_output_aliases={count + 1: 0} if extra else {},
        compiler_params=pltpu.CompilerParams(vmem_limit_bytes=VMEM_LIMIT),
        cost_estimate=pl.CostEstimate(flops=1024, bytes_accessed=1024, transcendentals=0),
    )(where, *pieces, *extra)


def anchor_kernel(*refs):
    del refs


def anchor(values, flops):
    anywhere = pl.BlockSpec(memory_space=pl.ANY)
    return pl.pallas_call(
        anchor_kernel,
        in_specs=[anywhere] * len(values),
        out_specs=[anywhere] * len(values),
        out_shape=[jax.ShapeDtypeStruct(value.shape, value.dtype) for value in values],
        input_output_aliases={n: n for n in range(len(values))},
        compiler_params=pltpu.CompilerParams(vmem_limit_bytes=1024 * 1024),
        cost_estimate=pl.CostEstimate(flops=flops, bytes_accessed=1024, transcendentals=0),
    )(*values)


def staged(visibility, beam_transfer, tile_mask, first_block, eigen_modes, signal_noise):
    freqs, parts, rows_all, base = visibility.shape
    _, freq_total, _, ell = beam_transfer.shape
    n_modes = eigen_modes.shape[2]
    ell_tiles = ell // TILE
    z, x, p = lax.axis_index("fm"), lax.axis_index("kl"), lax.axis_index("pol")
    other = [(0, 1), (1, 0)]

    def along_z(value, j):
        return lax.ppermute(value, "fm", [(i, i ^ j) for i in range(parts)])

    def along_x(value):
        return lax.ppermute(value, "kl", other)

    def cut(j, first, rows):
        return lax.dynamic_slice(visibility, (0, z ^ j, first, 0), (freqs, 1, rows, base)).reshape(freqs, rows, base)

    index = jnp.arange(parts + 2, dtype=jnp.int32)
    where = jnp.where(
        index < parts, z ^ index, jnp.where(index == parts, (x == p).astype(jnp.int32), x * ell_tiles)
    ).astype(jnp.int32)
    ratio = signal_noise[0] / (1.0 + signal_noise[0])
    ratios = jnp.broadcast_to(ratio[:, None, None], (n_modes, 1, ell))
    beam = beam_transfer.reshape(freq_total, base, ell)
    shape = (freqs, parts, rows_all, ell)

    fence = lax.optimization_barrier
    most, half = rows_all - ROWS, freqs // 2
    blocks = [[(0, f)] for f in range(freqs)]
    halves = [[(f // half, f % half)] for f in range(freqs)]
    a = {j: along_z(cut(j, 0, ROWS), j) for j in (3, 2, 1)}
    mine = [cut(0, 0, rows_all)[n:n + half] for n in (0, half)]
    others = [along_x(part) for part in mine]
    b = {j: cut(j, ROWS, most) for j in (1, 2, 3)}
    held, down, up = hold(where, tile_mask[0], first_block, beam, eigen_modes[0])
    (a[3], a[2], a[1]), b, others, down, up = fence(((a[3], a[2], a[1]), b, others, down, up))
    b[1], b[2] = along_z(b[1], 1), along_z(b[2], 2)
    own = project(where, mine, others, held, 0, halves, 200_000_000)
    skies = [own] + [project(where, [a[j]], [along_x(a[j])], held, j, blocks, 200_000_000) for j in (1, 2, 3)]
    gone = reduce(down, [leave for _, leave in skies], (0, 0, 0, 0), n_modes)
    stay_a = [stay for stay, _ in skies]
    b[2], b[3], stay_a, gone = fence((b[2], b[3], stay_a, gone))
    x_2 = along_x(b[2])
    x_1, = anchor([along_x(b[1])], 1_500_000_000)
    b[3] = along_z(b[3], 3)
    kept = reduce(down, stay_a, (0, 0, 0, 0), n_modes, jnp.float32)
    spots = [(j, 0, freqs) for j in (1, 2, 3, 0)]
    outs = restore(kept, lax.ppermute(gone, "pol", other), ratios, up, spots)
    near = project(where, [b[1]], [x_1], held, 1, blocks)
    x_2, b, outs, near = fence((x_2, b, outs, near))
    first = {j: along_z(outs[j - 1], j) for j in (1, 2, 3)}
    first[0] = outs[3]
    x_3 = along_x(b[3])
    skies = [own, near] + [project(where, [b[j]], [x], held, j, blocks) for j, x in ((2, x_2), (3, x_3))]
    gone = reduce(down, [leave for _, leave in skies], (ROWS, 0, 0, 0), n_modes)
    kept = reduce(down, [stay for stay, _ in skies], (ROWS, 0, 0, 0), n_modes, jnp.float32)
    (first[2], first[3], first[1]), first[0], kept, gone = fence(
        ((first[2], first[3], first[1]), first[0], kept, gone)
    )
    outs = fence(restore(kept, lax.ppermute(gone, "pol", other), ratios, up, spots))
    back = [along_z(outs[j - 1], j) for j in (1, 2, 3)]
    result = place(where, [first[j] for j in (1, 2, 3, 0)], spots, 0, shape)
    result = place(where, [outs[3], back[0]], [spots[3], spots[0]], ROWS, shape, into=result)
    return place(where, back[1:], spots[1:3], ROWS, shape, into=result)


def plain(visibility, beam_transfer, tile_mask, first_block, eigen_modes, signal_noise):
    owned_modes, freq_total, base_half, ell_local = beam_transfer.shape
    base_tiles, ell_tiles = base_half // TILE, ell_local // TILE
    block_ids = lax.axis_index("kl") * ell_tiles + jnp.arange(ell_tiles, dtype=jnp.int32)
    inside = (first_block[:, None] <= block_ids[None, :]).astype(jnp.int32)
    keep_tiles = tile_mask * inside[:, None, :]
    shaped = beam_transfer.reshape(owned_modes, freq_total, base_tiles, TILE, ell_tiles, TILE)
    masked_beam = shaped * keep_tiles.astype(jnp.bfloat16)[:, None, :, None, :, None]
    masked_beam = masked_beam.reshape(owned_modes, freq_total, base_half, ell_local)
    arrived = lax.all_to_all(visibility, "fm", split_axis=1, concat_axis=0, tiled=True)
    partial_value = jnp.einsum(
        "fmrb,mfbl->fmrl",
        lax.all_gather(arrived, "kl", axis=2, tiled=True),
        masked_beam,
        preferred_element_type=jnp.float32,
    )
    sky_sum = lax.psum_scatter(
        partial_value.astype(jnp.bfloat16), "pol", scatter_dimension=2, tiled=True
    ).astype(jnp.float32)
    modes_float = eigen_modes.astype(jnp.float32)
    coeffs = jnp.einsum("mfk,fmrl->mkrl", modes_float, sky_sum, precision=lax.Precision.HIGHEST)
    ratios = signal_noise / (1.0 + signal_noise)
    weighted = (coeffs * ratios[:, :, None, None]).astype(jnp.bfloat16)
    filtered = jnp.einsum(
        "mfk,mkrl->fmrl", eigen_modes, weighted, preferred_element_type=jnp.float32
    ).astype(jnp.bfloat16)
    return lax.all_to_all(filtered, "fm", split_axis=0, concat_axis=1, tiled=True)


def per_device(*args, sizes):
    visibility, beam_transfer = args[0], args[1]
    _, modes, rows, _ = visibility.shape
    fits = (
        sizes["kl"] == 2
        and sizes["pol"] == 2
        and modes == sizes["fm"] == PARTS
        and beam_transfer.shape[0] == 1
        and rows == 3 * ROWS
        and visibility.shape[0] % 2 == 0
    )
    if not fits:
        return plain(*args)
    return staged(*args)


def solution(mesh):
    placed = (
        P(("group", "fm"), None, "kl", "pol"),
        P(("group", "fm"), None, "pol", "kl"),
        P("fm", "pol", "kl"),
        P("fm"),
        P(("group", "fm"), None, None),
        P(("group", "fm"), None),
    )
    return jax.shard_map(
        functools.partial(per_device, sizes=dict(mesh.shape)),
        mesh=mesh,
        in_specs=placed,
        out_specs=P(("group", "fm"), None, "pol", "kl"),
        check_vma=False,
    )
```

```python
import functools
import jax
import jax.numpy as jnp
from jax import lax
from jax.experimental import pallas as pl
from jax.experimental.pallas import tpu as pltpu
from jax.sharding import PartitionSpec as P

TILE = 128
PARTS = 4
ROWS = 16
VMEM_LIMIT = 24 * 1024 * 1024


def hold_kernel(where, tiles, starts, beam, modes_ref, held, down_ref, up_ref, mask, sems):
    freq, base, ell = held.shape
    n_modes = modes_ref.shape[1]
    ell_tiles, base_tiles, freqs = ell // TILE, base // TILE, freq // PARTS
    copies = [pltpu.make_async_copy(beam.at[f], held.at[f], sems.at[f]) for f in range(freq)]
    for copy in copies:
        copy.start()
    for b in range(base_tiles):
        for l in range(ell_tiles):
            kept = jnp.where(starts[0] <= where[PARTS + 1] + l, tiles[b, l], 0).astype(jnp.float32)
            mask[b * TILE:(b + 1) * TILE, l * TILE:(l + 1) * TILE] = jnp.full(
                (TILE, TILE), kept, jnp.float32
            ).astype(jnp.bfloat16)
    modes = modes_ref[...]

    def pick(shape, axis):
        big = lax.broadcasted_iota(jnp.int32, shape, axis) // ROWS
        small = lax.broadcasted_iota(jnp.int32, shape, 1 - axis)
        if freq in shape:
            piece, within = big // freqs, big % freqs
            big = within
            for j in range(PARTS):
                big = jnp.where(piece == j, where[j] * freqs + within, big)
        return jnp.where(big == small, 1.0, 0.0).astype(jnp.bfloat16)

    def lane(shape):
        rows = lax.broadcasted_iota(jnp.int32, shape, 0) % ROWS
        columns = lax.broadcasted_iota(jnp.int32, shape, 1) % ROWS
        return rows == columns

    def dot(a, b, dims):
        return lax.dot_general(a, b, (dims, ((), ())), preferred_element_type=jnp.float32)

    tall = dot(pick((n_modes * ROWS, n_modes), 0), modes, ((1,), (1,))).astype(jnp.bfloat16)
    value = dot(tall, pick((freq, freq * ROWS), 1), ((1,), (0,)))
    down_ref[...] = jnp.where(lane(value.shape), value, 0.0).astype(jnp.bfloat16)
    tall = dot(pick((freq * ROWS, freq), 0), modes, ((1,), (0,))).astype(jnp.bfloat16)
    value = dot(tall, pick((n_modes, n_modes * ROWS), 1), ((1,), (0,)))
    up_ref[...] = jnp.where(lane(value.shape), value, 0.0).astype(jnp.bfloat16)
    for f, copy in enumerate(copies):
        copy.wait()
        held[f] = held[f] * mask[...]


def hold(where, tiles, starts, beam, modes):
    freq, base, ell = beam.shape
    size, wide = freq * ROWS, modes.shape[1] * ROWS
    vmem = pl.BlockSpec(memory_space=pltpu.VMEM)
    return pl.pallas_call(
        hold_kernel,
        grid_spec=pltpu.PrefetchScalarGridSpec(
            num_scalar_prefetch=3,
            grid=(),
            in_specs=[pl.BlockSpec(memory_space=pl.ANY), vmem],
            out_specs=[vmem] * 3,
            scratch_shapes=[pltpu.VMEM((base, ell), jnp.bfloat16), pltpu.SemaphoreType.DMA((freq,))],
        ),
        out_shape=[
            pltpu.VMEM(beam.shape, beam.dtype),
            jax.ShapeDtypeStruct((wide, size), jnp.bfloat16),
            jax.ShapeDtypeStruct((size, wide), jnp.bfloat16),
        ],
        compiler_params=pltpu.CompilerParams(vmem_limit_bytes=VMEM_LIMIT),
        cost_estimate=pl.CostEstimate(flops=1024, bytes_accessed=1024, transcendentals=0),
    )(where, tiles, starts, beam, modes)


def project_kernel(where, *refs, piece, blocks):
    count = (len(refs) - 3) // 2
    mine, others = refs[:count], refs[count:2 * count]
    held, stay_ref, leave_ref = refs[2 * count:]
    freqs, rows, _ = stay_ref.shape
    first = where[piece] * freqs
    own = where[PARTS] == 1
    for f in range(freqs):
        a = jnp.concatenate([mine[n][k] for n, k in blocks[f]], axis=0)
        b = jnp.concatenate([others[n][k] for n, k in blocks[f]], axis=0)
        lines = jnp.concatenate([jnp.where(own, a, b), jnp.where(own, b, a)], axis=0)
        value = jnp.dot(lines, held[first + f], preferred_element_type=jnp.float32).astype(jnp.bfloat16)
        stay_ref[f] = value[:rows]
        leave_ref[f] = value[rows:]


def project(where, mine, others, held, piece, blocks, flops=1024):
    ell = held.shape[2]
    rows = sum(mine[n].shape[1] for n, _ in blocks[0])
    vmem = pl.BlockSpec(memory_space=pltpu.VMEM)
    return pl.pallas_call(
        functools.partial(project_kernel, piece=piece, blocks=blocks),
        grid_spec=pltpu.PrefetchScalarGridSpec(
            num_scalar_prefetch=1, grid=(), in_specs=[vmem] * (2 * len(mine) + 1), out_specs=[vmem] * 2
        ),
        out_shape=[jax.ShapeDtypeStruct((len(blocks), rows, ell), jnp.bfloat16)] * 2,
        compiler_params=pltpu.CompilerParams(vmem_limit_bytes=VMEM_LIMIT),
        cost_estimate=pl.CostEstimate(flops=flops, bytes_accessed=1024, transcendentals=0),
    )(where, *mine, *others, pltpu.with_memory_space_constraint(held, pltpu.VMEM))


def contract(modes, skies):
    block = jnp.concatenate([sky[...].reshape(sky.shape[0] * ROWS, sky.shape[2]) for sky in skies], axis=0)
    return jnp.dot(modes, block, preferred_element_type=jnp.float32)


def reduce_kernel(modes_ref, *refs):
    out = refs[-1]
    out[...] = contract(modes_ref[...], refs[:-1]).astype(out.dtype).reshape(out.shape)


def by_rows(count, ell, first=0):
    return pl.BlockSpec((count, ROWS, ell), lambda g: (0, g + first // ROWS, 0))


def fixed(shape):
    return pl.BlockSpec(shape, lambda g: (0,) * len(shape))


def sky_specs(skies, first):
    return [by_rows(sky.shape[0], sky.shape[2], low) for sky, low in zip(skies, first)]


def reduce(modes, skies, first, n_modes, dtype=jnp.bfloat16):
    _, rows, ell = skies[-1].shape
    return pl.pallas_call(
        reduce_kernel,
        grid=(rows // ROWS,),
        in_specs=[fixed(modes.shape)] + sky_specs(skies, first),
        out_specs=by_rows(n_modes, ell),
        out_shape=jax.ShapeDtypeStruct((n_modes, rows, ell), dtype),
        compiler_params=pltpu.CompilerParams(vmem_limit_bytes=VMEM_LIMIT),
        cost_estimate=pl.CostEstimate(flops=1024, bytes_accessed=1024, transcendentals=0),
    )(modes, *skies)


def restore_kernel(up_ref, ratio_ref, kept_ref, came_ref, *outs, spots):
    n_modes, _, ell = came_ref.shape
    freqs = up_ref.shape[0] // ROWS // PARTS
    total = kept_ref[...] + came_ref[...].astype(jnp.float32)
    weighted = (total * ratio_ref[...]).astype(jnp.bfloat16).reshape(n_modes * ROWS, ell)
    for (j, low, high), out in zip(spots, outs):
        modes = up_ref[(j * freqs + low) * ROWS:(j * freqs + high) * ROWS, :]
        value = jnp.dot(modes, weighted, preferred_element_type=jnp.float32)
        out[...] = value.astype(jnp.bfloat16).reshape(out.shape)


def restore(kept, came, ratios, up, spots):
    n_modes, rows, ell = came.shape
    return pl.pallas_call(
        functools.partial(restore_kernel, spots=spots),
        grid=(rows // ROWS,),
        in_specs=[fixed(up.shape), fixed(ratios.shape)] + [by_rows(n_modes, ell)] * 2,
        out_specs=[by_rows(high - low, ell) for _, low, high in spots],
        out_shape=[jax.ShapeDtypeStruct((high - low, rows, ell), jnp.bfloat16) for _, low, high in spots],
        compiler_params=pltpu.CompilerParams(vmem_limit_bytes=VMEM_LIMIT),
        cost_estimate=pl.CostEstimate(flops=1024, bytes_accessed=1024, transcendentals=0),
    )(up, ratios, kept, came)


def place_kernel(where, *refs, spots, first):
    count = len(spots)
    pieces, out, sems = refs[:count], refs[-2], refs[-1]
    rows = pieces[0].shape[1]
    copies = [
        pltpu.make_async_copy(pieces[n], out.at[low:high, where[j], first:first + rows, :], sems.at[n])
        for n, (j, low, high) in enumerate(spots)
    ]
    for copy in copies:
        copy.start()
    for copy in copies:
        copy.wait()


def place(where, pieces, spots, first, shape, into=None):
    count = len(spots)
    extra = [] if into is None else [into]
    anywhere = pl.BlockSpec(memory_space=pl.ANY)
    return pl.pallas_call(
        functools.partial(place_kernel, spots=spots, first=first),
        grid_spec=pltpu.PrefetchScalarGridSpec(
            num_scalar_prefetch=1,
            grid=(),
            in_specs=[pl.BlockSpec(memory_space=pltpu.VMEM)] * count + [anywhere] * len(extra),
            out_specs=anywhere,
            scratch_shapes=[pltpu.SemaphoreType.DMA((count,))],
        ),
        out_shape=jax.ShapeDtypeStruct(shape, jnp.bfloat16),
        input_output_aliases={count + 1: 0} if extra else {},
        compiler_params=pltpu.CompilerParams(vmem_limit_bytes=VMEM_LIMIT),
        cost_estimate=pl.CostEstimate(flops=1024, bytes_accessed=1024, transcendentals=0),
    )(where, *pieces, *extra)


def anchor_kernel(*refs):
    del refs


def anchor(values, flops):
    anywhere = pl.BlockSpec(memory_space=pl.ANY)
    return pl.pallas_call(
        anchor_kernel,
        in_specs=[anywhere] * len(values),
        out_specs=[anywhere] * len(values),
        out_shape=[jax.ShapeDtypeStruct(value.shape, value.dtype) for value in values],
        input_output_aliases={n: n for n in range(len(values))},
        compiler_params=pltpu.CompilerParams(vmem_limit_bytes=1024 * 1024),
        cost_estimate=pl.CostEstimate(flops=flops, bytes_accessed=1024, transcendentals=0),
    )(*values)


def staged(visibility, beam_transfer, tile_mask, first_block, eigen_modes, signal_noise):
    freqs, parts, rows_all, base = visibility.shape
    _, freq_total, _, ell = beam_transfer.shape
    n_modes = eigen_modes.shape[2]
    ell_tiles = ell // TILE
    z, x, p = lax.axis_index("fm"), lax.axis_index("kl"), lax.axis_index("pol")
    other = [(0, 1), (1, 0)]

    def along_z(value, j):
        return lax.ppermute(value, "fm", [(i, i ^ j) for i in range(parts)])

    def along_x(value):
        return lax.ppermute(value, "kl", other)

    def cut(j, first, rows):
        return lax.dynamic_slice(visibility, (0, z ^ j, first, 0), (freqs, 1, rows, base)).reshape(freqs, rows, base)

    index = jnp.arange(parts + 2, dtype=jnp.int32)
    where = jnp.where(
        index < parts, z ^ index, jnp.where(index == parts, (x == p).astype(jnp.int32), x * ell_tiles)
    ).astype(jnp.int32)
    ratio = signal_noise[0] / (1.0 + signal_noise[0])
    ratios = jnp.broadcast_to(ratio[:, None, None], (n_modes, 1, ell))
    beam = beam_transfer.reshape(freq_total, base, ell)
    shape = (freqs, parts, rows_all, ell)

    fence = lax.optimization_barrier
    most, half = rows_all - ROWS, freqs // 2
    blocks = [[(0, f)] for f in range(freqs)]
    halves = [[(f // half, f % half)] for f in range(freqs)]
    a = {j: along_z(cut(j, 0, ROWS), j) for j in (3, 2, 1)}
    mine = [cut(0, 0, rows_all)[n:n + half] for n in (0, half)]
    others = [along_x(part) for part in mine]
    b = {j: cut(j, ROWS, most) for j in (1, 2, 3)}
    held, down, up = hold(where, tile_mask[0], first_block, beam, eigen_modes[0])
    (a[3], a[2], a[1]), b, others, down, up = fence(((a[3], a[2], a[1]), b, others, down, up))
    b[1], b[2] = along_z(b[1], 1), along_z(b[2], 2)
    own = project(where, mine, others, held, 0, halves, 400_000_000)
    skies = [own] + [project(where, [a[j]], [along_x(a[j])], held, j, blocks, 400_000_000) for j in (1, 2, 3)]
    gone = reduce(down, [leave for _, leave in skies], (0, 0, 0, 0), n_modes)
    stay_a = [stay for stay, _ in skies]
    b[2], b[3], stay_a, gone = fence((b[2], b[3], stay_a, gone))
    x_2 = along_x(b[2])
    x_1, = anchor([along_x(b[1])], 2_500_000_000)
    b[3] = along_z(b[3], 3)
    kept = reduce(down, stay_a, (0, 0, 0, 0), n_modes, jnp.float32)
    spots = [(j, 0, freqs) for j in (1, 2, 3, 0)]
    outs = restore(kept, lax.ppermute(gone, "pol", other), ratios, up, spots)
    near = project(where, [b[1]], [x_1], held, 1, blocks)
    x_2, b, outs, near = fence((x_2, b, outs, near))
    first = {j: along_z(outs[j - 1], j) for j in (1, 2, 3)}
    first[0] = outs[3]
    x_3 = along_x(b[3])
    skies = [own, near] + [project(where, [b[j]], [x], held, j, blocks) for j, x in ((2, x_2), (3, x_3))]
    gone = reduce(down, [leave for _, leave in skies], (ROWS, 0, 0, 0), n_modes)
    stays = [stay for stay, _ in skies]
    first[2], first[1], here, stays, gone = fence((first[2], first[1], first[0], stays, gone))
    came = lax.ppermute(gone, "pol", other)
    kept = reduce(down, stays, (ROWS, 0, 0, 0), n_modes, jnp.float32)
    first[3], = anchor([first[3]], 20_000_000_000)
    outs, first[3] = fence((restore(kept, came, ratios, up, spots), first[3]))
    first[0] = here
    back = [along_z(outs[j - 1], j) for j in (1, 2, 3)]
    result = place(where, [first[j] for j in (1, 2, 3, 0)], spots, 0, shape)
    result = place(where, [outs[3], back[0]], [spots[3], spots[0]], ROWS, shape, into=result)
    return place(where, back[1:], spots[1:3], ROWS, shape, into=result)


def plain(visibility, beam_transfer, tile_mask, first_block, eigen_modes, signal_noise):
    owned_modes, freq_total, base_half, ell_local = beam_transfer.shape
    base_tiles, ell_tiles = base_half // TILE, ell_local // TILE
    block_ids = lax.axis_index("kl") * ell_tiles + jnp.arange(ell_tiles, dtype=jnp.int32)
    inside = (first_block[:, None] <= block_ids[None, :]).astype(jnp.int32)
    keep_tiles = tile_mask * inside[:, None, :]
    shaped = beam_transfer.reshape(owned_modes, freq_total, base_tiles, TILE, ell_tiles, TILE)
    masked_beam = shaped * keep_tiles.astype(jnp.bfloat16)[:, None, :, None, :, None]
    masked_beam = masked_beam.reshape(owned_modes, freq_total, base_half, ell_local)
    arrived = lax.all_to_all(visibility, "fm", split_axis=1, concat_axis=0, tiled=True)
    partial_value = jnp.einsum(
        "fmrb,mfbl->fmrl",
        lax.all_gather(arrived, "kl", axis=2, tiled=True),
        masked_beam,
        preferred_element_type=jnp.float32,
    )
    sky_sum = lax.psum_scatter(
        partial_value.astype(jnp.bfloat16), "pol", scatter_dimension=2, tiled=True
    ).astype(jnp.float32)
    modes_float = eigen_modes.astype(jnp.float32)
    coeffs = jnp.einsum("mfk,fmrl->mkrl", modes_float, sky_sum, precision=lax.Precision.HIGHEST)
    ratios = signal_noise / (1.0 + signal_noise)
    weighted = (coeffs * ratios[:, :, None, None]).astype(jnp.bfloat16)
    filtered = jnp.einsum(
        "mfk,mkrl->fmrl", eigen_modes, weighted, preferred_element_type=jnp.float32
    ).astype(jnp.bfloat16)
    return lax.all_to_all(filtered, "fm", split_axis=0, concat_axis=1, tiled=True)


def per_device(*args, sizes):
    visibility, beam_transfer = args[0], args[1]
    _, modes, rows, _ = visibility.shape
    fits = (
        sizes["kl"] == 2
        and sizes["pol"] == 2
        and modes == sizes["fm"] == PARTS
        and beam_transfer.shape[0] == 1
        and rows == 3 * ROWS
        and visibility.shape[0] % 2 == 0
    )
    if not fits:
        return plain(*args)
    return staged(*args)


def solution(mesh):
    placed = (
        P(("group", "fm"), None, "kl", "pol"),
        P(("group", "fm"), None, "pol", "kl"),
        P("fm", "pol", "kl"),
        P("fm"),
        P(("group", "fm"), None, None),
        P(("group", "fm"), None),
    )
    return jax.shard_map(
        functools.partial(per_device, sizes=dict(mesh.shape)),
        mesh=mesh,
        in_specs=placed,
        out_specs=P(("group", "fm"), None, "pol", "kl"),
        check_vma=False,
    )
```

```python
import functools
import jax
import jax.numpy as jnp
from jax import lax
from jax.experimental import pallas as pl
from jax.experimental.pallas import tpu as pltpu
from jax.sharding import PartitionSpec as P

TILE = 128
PARTS = 4
ROWS = 16
VMEM_LIMIT = 24 * 1024 * 1024


def hold_kernel(where, tiles, starts, beam, modes_ref, held, down_ref, up_ref, mask, sems):
    freq, base, ell = held.shape
    n_modes = modes_ref.shape[1]
    ell_tiles, base_tiles, freqs = ell // TILE, base // TILE, freq // PARTS
    copies = [pltpu.make_async_copy(beam.at[f], held.at[f], sems.at[f]) for f in range(freq)]
    for copy in copies:
        copy.start()
    for b in range(base_tiles):
        for l in range(ell_tiles):
            kept = jnp.where(starts[0] <= where[PARTS + 1] + l, tiles[b, l], 0).astype(jnp.float32)
            mask[b * TILE:(b + 1) * TILE, l * TILE:(l + 1) * TILE] = jnp.full(
                (TILE, TILE), kept, jnp.float32
            ).astype(jnp.bfloat16)
    modes = modes_ref[...]

    def pick(shape, axis):
        big = lax.broadcasted_iota(jnp.int32, shape, axis) // ROWS
        small = lax.broadcasted_iota(jnp.int32, shape, 1 - axis)
        if freq in shape:
            piece, within = big // freqs, big % freqs
            big = within
            for j in range(PARTS):
                big = jnp.where(piece == j, where[j] * freqs + within, big)
        return jnp.where(big == small, 1.0, 0.0).astype(jnp.bfloat16)

    def lane(shape):
        rows = lax.broadcasted_iota(jnp.int32, shape, 0) % ROWS
        columns = lax.broadcasted_iota(jnp.int32, shape, 1) % ROWS
        return rows == columns

    def dot(a, b, dims):
        return lax.dot_general(a, b, (dims, ((), ())), preferred_element_type=jnp.float32)

    tall = dot(pick((n_modes * ROWS, n_modes), 0), modes, ((1,), (1,))).astype(jnp.bfloat16)
    value = dot(tall, pick((freq, freq * ROWS), 1), ((1,), (0,)))
    down_ref[...] = jnp.where(lane(value.shape), value, 0.0).astype(jnp.bfloat16)
    tall = dot(pick((freq * ROWS, freq), 0), modes, ((1,), (0,))).astype(jnp.bfloat16)
    value = dot(tall, pick((n_modes, n_modes * ROWS), 1), ((1,), (0,)))
    up_ref[...] = jnp.where(lane(value.shape), value, 0.0).astype(jnp.bfloat16)
    for f, copy in enumerate(copies):
        copy.wait()
        held[f] = held[f] * mask[...]


def hold(where, tiles, starts, beam, modes):
    freq, base, ell = beam.shape
    size, wide = freq * ROWS, modes.shape[1] * ROWS
    vmem = pl.BlockSpec(memory_space=pltpu.VMEM)
    return pl.pallas_call(
        hold_kernel,
        grid_spec=pltpu.PrefetchScalarGridSpec(
            num_scalar_prefetch=3,
            grid=(),
            in_specs=[pl.BlockSpec(memory_space=pl.ANY), vmem],
            out_specs=[vmem] * 3,
            scratch_shapes=[pltpu.VMEM((base, ell), jnp.bfloat16), pltpu.SemaphoreType.DMA((freq,))],
        ),
        out_shape=[
            pltpu.VMEM(beam.shape, beam.dtype),
            jax.ShapeDtypeStruct((wide, size), jnp.bfloat16),
            jax.ShapeDtypeStruct((size, wide), jnp.bfloat16),
        ],
        compiler_params=pltpu.CompilerParams(vmem_limit_bytes=VMEM_LIMIT),
        cost_estimate=pl.CostEstimate(flops=1024, bytes_accessed=1024, transcendentals=0),
    )(where, tiles, starts, beam, modes)


def project_kernel(where, *refs, piece, blocks):
    count = (len(refs) - 3) // 2
    mine, others = refs[:count], refs[count:2 * count]
    held, stay_ref, leave_ref = refs[2 * count:]
    freqs, rows, _ = stay_ref.shape
    first = where[piece] * freqs
    own = where[PARTS] == 1
    for f in range(freqs):
        a = jnp.concatenate([mine[n][k] for n, k in blocks[f]], axis=0)
        b = jnp.concatenate([others[n][k] for n, k in blocks[f]], axis=0)
        lines = jnp.concatenate([jnp.where(own, a, b), jnp.where(own, b, a)], axis=0)
        value = jnp.dot(lines, held[first + f], preferred_element_type=jnp.float32).astype(jnp.bfloat16)
        stay_ref[f] = value[:rows]
        leave_ref[f] = value[rows:]


def project(where, mine, others, held, piece, blocks, flops=1024):
    ell = held.shape[2]
    rows = sum(mine[n].shape[1] for n, _ in blocks[0])
    vmem = pl.BlockSpec(memory_space=pltpu.VMEM)
    return pl.pallas_call(
        functools.partial(project_kernel, piece=piece, blocks=blocks),
        grid_spec=pltpu.PrefetchScalarGridSpec(
            num_scalar_prefetch=1, grid=(), in_specs=[vmem] * (2 * len(mine) + 1), out_specs=[vmem] * 2
        ),
        out_shape=[jax.ShapeDtypeStruct((len(blocks), rows, ell), jnp.bfloat16)] * 2,
        compiler_params=pltpu.CompilerParams(vmem_limit_bytes=VMEM_LIMIT),
        cost_estimate=pl.CostEstimate(flops=flops, bytes_accessed=1024, transcendentals=0),
    )(where, *mine, *others, pltpu.with_memory_space_constraint(held, pltpu.VMEM))


def contract(modes, skies):
    block = jnp.concatenate([sky[...].reshape(sky.shape[0] * ROWS, sky.shape[2]) for sky in skies], axis=0)
    return jnp.dot(modes, block, preferred_element_type=jnp.float32)


def reduce_kernel(modes_ref, *refs):
    out = refs[-1]
    out[...] = contract(modes_ref[...], refs[:-1]).astype(out.dtype).reshape(out.shape)


def by_rows(count, ell, first=0):
    return pl.BlockSpec((count, ROWS, ell), lambda g: (0, g + first // ROWS, 0))


def fixed(shape):
    return pl.BlockSpec(shape, lambda g: (0,) * len(shape))


def sky_specs(skies, first):
    return [by_rows(sky.shape[0], sky.shape[2], low) for sky, low in zip(skies, first)]


def reduce(modes, skies, first, n_modes, dtype=jnp.bfloat16):
    _, rows, ell = skies[-1].shape
    return pl.pallas_call(
        reduce_kernel,
        grid=(rows // ROWS,),
        in_specs=[fixed(modes.shape)] + sky_specs(skies, first),
        out_specs=by_rows(n_modes, ell),
        out_shape=jax.ShapeDtypeStruct((n_modes, rows, ell), dtype),
        compiler_params=pltpu.CompilerParams(vmem_limit_bytes=VMEM_LIMIT),
        cost_estimate=pl.CostEstimate(flops=1024, bytes_accessed=1024, transcendentals=0),
    )(modes, *skies)


def restore_kernel(up_ref, ratio_ref, kept_ref, came_ref, *outs, spots):
    n_modes, _, ell = came_ref.shape
    freqs = up_ref.shape[0] // ROWS // PARTS
    total = kept_ref[...] + came_ref[...].astype(jnp.float32)
    weighted = (total * ratio_ref[...]).astype(jnp.bfloat16).reshape(n_modes * ROWS, ell)
    for (j, low, high), out in zip(spots, outs):
        modes = up_ref[(j * freqs + low) * ROWS:(j * freqs + high) * ROWS, :]
        value = jnp.dot(modes, weighted, preferred_element_type=jnp.float32)
        out[...] = value.astype(jnp.bfloat16).reshape(out.shape)


def restore(kept, came, ratios, up, spots):
    n_modes, rows, ell = came.shape
    return pl.pallas_call(
        functools.partial(restore_kernel, spots=spots),
        grid=(rows // ROWS,),
        in_specs=[fixed(up.shape), fixed(ratios.shape)] + [by_rows(n_modes, ell)] * 2,
        out_specs=[by_rows(high - low, ell) for _, low, high in spots],
        out_shape=[jax.ShapeDtypeStruct((high - low, rows, ell), jnp.bfloat16) for _, low, high in spots],
        compiler_params=pltpu.CompilerParams(vmem_limit_bytes=VMEM_LIMIT),
        cost_estimate=pl.CostEstimate(flops=1024, bytes_accessed=1024, transcendentals=0),
    )(up, ratios, kept, came)


def place_kernel(where, *refs, spots, first):
    count = len(spots)
    pieces, out, sems = refs[:count], refs[-2], refs[-1]
    rows = pieces[0].shape[1]
    copies = [
        pltpu.make_async_copy(pieces[n], out.at[low:high, where[j], first:first + rows, :], sems.at[n])
        for n, (j, low, high) in enumerate(spots)
    ]
    for copy in copies:
        copy.start()
    for copy in copies:
        copy.wait()


def place(where, pieces, spots, first, shape, into=None):
    count = len(spots)
    extra = [] if into is None else [into]
    anywhere = pl.BlockSpec(memory_space=pl.ANY)
    return pl.pallas_call(
        functools.partial(place_kernel, spots=spots, first=first),
        grid_spec=pltpu.PrefetchScalarGridSpec(
            num_scalar_prefetch=1,
            grid=(),
            in_specs=[pl.BlockSpec(memory_space=pltpu.VMEM)] * count + [anywhere] * len(extra),
            out_specs=anywhere,
            scratch_shapes=[pltpu.SemaphoreType.DMA((count,))],
        ),
        out_shape=jax.ShapeDtypeStruct(shape, jnp.bfloat16),
        input_output_aliases={count + 1: 0} if extra else {},
        compiler_params=pltpu.CompilerParams(vmem_limit_bytes=VMEM_LIMIT),
        cost_estimate=pl.CostEstimate(flops=1024, bytes_accessed=1024, transcendentals=0),
    )(where, *pieces, *extra)


def anchor_kernel(*refs):
    del refs


def anchor(values, flops):
    anywhere = pl.BlockSpec(memory_space=pl.ANY)
    return pl.pallas_call(
        anchor_kernel,
        in_specs=[anywhere] * len(values),
        out_specs=[anywhere] * len(values),
        out_shape=[jax.ShapeDtypeStruct(value.shape, value.dtype) for value in values],
        input_output_aliases={n: n for n in range(len(values))},
        compiler_params=pltpu.CompilerParams(vmem_limit_bytes=1024 * 1024),
        cost_estimate=pl.CostEstimate(flops=flops, bytes_accessed=1024, transcendentals=0),
    )(*values)


def staged(visibility, beam_transfer, tile_mask, first_block, eigen_modes, signal_noise):
    freqs, parts, rows_all, base = visibility.shape
    _, freq_total, _, ell = beam_transfer.shape
    n_modes = eigen_modes.shape[2]
    ell_tiles = ell // TILE
    z, x, p = lax.axis_index("fm"), lax.axis_index("kl"), lax.axis_index("pol")
    other = [(0, 1), (1, 0)]

    def along_z(value, j):
        return lax.ppermute(value, "fm", [(i, i ^ j) for i in range(parts)])

    def along_x(value):
        return lax.ppermute(value, "kl", other)

    def cut(j, first, rows):
        return lax.dynamic_slice(visibility, (0, z ^ j, first, 0), (freqs, 1, rows, base)).reshape(freqs, rows, base)

    index = jnp.arange(parts + 2, dtype=jnp.int32)
    where = jnp.where(
        index < parts, z ^ index, jnp.where(index == parts, (x == p).astype(jnp.int32), x * ell_tiles)
    ).astype(jnp.int32)
    ratio = signal_noise[0] / (1.0 + signal_noise[0])
    ratios = jnp.broadcast_to(ratio[:, None, None], (n_modes, 1, ell))
    beam = beam_transfer.reshape(freq_total, base, ell)
    shape = (freqs, parts, rows_all, ell)

    fence = lax.optimization_barrier
    most, half = rows_all - ROWS, freqs // 2
    blocks = [[(0, f)] for f in range(freqs)]
    halves = [[(f // half, f % half)] for f in range(freqs)]
    a = {j: along_z(cut(j, 0, ROWS), j) for j in (3, 2, 1)}
    mine = [cut(0, 0, rows_all)[n:n + half] for n in (0, half)]
    others = [along_x(part) for part in mine]
    b = {j: cut(j, ROWS, most) for j in (1, 2, 3)}
    held, down, up = hold(where, tile_mask[0], first_block, beam, eigen_modes[0])
    (a[3], a[2], a[1]), b, others, down, up = fence(((a[3], a[2], a[1]), b, others, down, up))
    b[1], b[2] = along_z(b[1], 1), along_z(b[2], 2)
    own = project(where, mine, others, held, 0, halves, 400_000_000)
    skies = [own] + [project(where, [a[j]], [along_x(a[j])], held, j, blocks, 400_000_000) for j in (1, 2, 3)]
    gone = reduce(down, [leave for _, leave in skies], (0, 0, 0, 0), n_modes)
    stay_a = [stay for stay, _ in skies]
    b[2], b[3], stay_a, gone = fence((b[2], b[3], stay_a, gone))
    x_2 = along_x(b[2])
    x_1, = anchor([along_x(b[1])], 2_500_000_000)
    b[3] = along_z(b[3], 3)
    kept = reduce(down, stay_a, (0, 0, 0, 0), n_modes, jnp.float32)
    spots = [(j, 0, freqs) for j in (1, 2, 3, 0)]
    outs = restore(kept, lax.ppermute(gone, "pol", other), ratios, up, spots)
    near = project(where, [b[1]], [x_1], held, 1, blocks)
    x_2, b, outs, near = fence((x_2, b, outs, near))
    first = {j: along_z(outs[j - 1], j) for j in (1, 2, 3)}
    first[0] = outs[3]
    x_3 = along_x(b[3])
    skies = [own, near] + [project(where, [b[j]], [x], held, j, blocks) for j, x in ((2, x_2), (3, x_3))]
    gone = reduce(down, [leave for _, leave in skies], (ROWS, 0, 0, 0), n_modes)
    stays = [stay for stay, _ in skies]
    first[2], first[1], here, stays, gone = fence((first[2], first[1], first[0], stays, gone))
    came = lax.ppermute(gone, "pol", other)
    kept = reduce(down, stays, (ROWS, 0, 0, 0), n_modes, jnp.float32)
    first[3], = anchor([first[3]], 20_000_000_000)
    outs, first[3] = fence((restore(kept, came, ratios, up, spots), first[3]))
    first[0] = here
    back = [along_z(outs[j - 1], j) for j in (3, 1, 2)]
    result = place(where, [first[j] for j in (1, 2, 3, 0)], spots, 0, shape)
    result = place(where, [outs[3]], [spots[3]], ROWS, shape, into=result)
    return place(where, back, [spots[2], spots[0], spots[1]], ROWS, shape, into=result)


def plain(visibility, beam_transfer, tile_mask, first_block, eigen_modes, signal_noise):
    owned_modes, freq_total, base_half, ell_local = beam_transfer.shape
    base_tiles, ell_tiles = base_half // TILE, ell_local // TILE
    block_ids = lax.axis_index("kl") * ell_tiles + jnp.arange(ell_tiles, dtype=jnp.int32)
    inside = (first_block[:, None] <= block_ids[None, :]).astype(jnp.int32)
    keep_tiles = tile_mask * inside[:, None, :]
    shaped = beam_transfer.reshape(owned_modes, freq_total, base_tiles, TILE, ell_tiles, TILE)
    masked_beam = shaped * keep_tiles.astype(jnp.bfloat16)[:, None, :, None, :, None]
    masked_beam = masked_beam.reshape(owned_modes, freq_total, base_half, ell_local)
    arrived = lax.all_to_all(visibility, "fm", split_axis=1, concat_axis=0, tiled=True)
    partial_value = jnp.einsum(
        "fmrb,mfbl->fmrl",
        lax.all_gather(arrived, "kl", axis=2, tiled=True),
        masked_beam,
        preferred_element_type=jnp.float32,
    )
    sky_sum = lax.psum_scatter(
        partial_value.astype(jnp.bfloat16), "pol", scatter_dimension=2, tiled=True
    ).astype(jnp.float32)
    modes_float = eigen_modes.astype(jnp.float32)
    coeffs = jnp.einsum("mfk,fmrl->mkrl", modes_float, sky_sum, precision=lax.Precision.HIGHEST)
    ratios = signal_noise / (1.0 + signal_noise)
    weighted = (coeffs * ratios[:, :, None, None]).astype(jnp.bfloat16)
    filtered = jnp.einsum(
        "mfk,mkrl->fmrl", eigen_modes, weighted, preferred_element_type=jnp.float32
    ).astype(jnp.bfloat16)
    return lax.all_to_all(filtered, "fm", split_axis=0, concat_axis=1, tiled=True)


def per_device(*args, sizes):
    visibility, beam_transfer = args[0], args[1]
    _, modes, rows, _ = visibility.shape
    fits = (
        sizes["kl"] == 2
        and sizes["pol"] == 2
        and modes == sizes["fm"] == PARTS
        and beam_transfer.shape[0] == 1
        and rows == 3 * ROWS
        and visibility.shape[0] % 2 == 0
    )
    if not fits:
        return plain(*args)
    return staged(*args)


def solution(mesh):
    placed = (
        P(("group", "fm"), None, "kl", "pol"),
        P(("group", "fm"), None, "pol", "kl"),
        P("fm", "pol", "kl"),
        P("fm"),
        P(("group", "fm"), None, None),
        P(("group", "fm"), None),
    )
    return jax.shard_map(
        functools.partial(per_device, sizes=dict(mesh.shape)),
        mesh=mesh,
        in_specs=placed,
        out_specs=P(("group", "fm"), None, "pol", "kl"),
        check_vma=False,
    )
```

```python
import functools
import jax
import jax.numpy as jnp
from jax import lax
from jax.experimental import pallas as pl
from jax.experimental.pallas import tpu as pltpu
from jax.sharding import PartitionSpec as P

TILE = 128
PARTS = 4
ROWS = 16
VMEM_LIMIT = 24 * 1024 * 1024


def hold_kernel(where, tiles, starts, beam, modes_ref, held, down_ref, up_ref, mask, sems):
    freq, base, ell = held.shape
    n_modes = modes_ref.shape[1]
    ell_tiles, base_tiles, freqs = ell // TILE, base // TILE, freq // PARTS
    copies = [pltpu.make_async_copy(beam.at[f], held.at[f], sems.at[f]) for f in range(freq)]
    for copy in copies:
        copy.start()
    for b in range(base_tiles):
        for l in range(ell_tiles):
            kept = jnp.where(starts[0] <= where[PARTS + 1] + l, tiles[b, l], 0).astype(jnp.float32)
            mask[b * TILE:(b + 1) * TILE, l * TILE:(l + 1) * TILE] = jnp.full(
                (TILE, TILE), kept, jnp.float32
            ).astype(jnp.bfloat16)
    modes = modes_ref[...]

    def pick(shape, axis):
        big = lax.broadcasted_iota(jnp.int32, shape, axis) // ROWS
        small = lax.broadcasted_iota(jnp.int32, shape, 1 - axis)
        if freq in shape:
            piece, within = big // freqs, big % freqs
            big = within
            for j in range(PARTS):
                big = jnp.where(piece == j, where[j] * freqs + within, big)
        return jnp.where(big == small, 1.0, 0.0).astype(jnp.bfloat16)

    def lane(shape):
        rows = lax.broadcasted_iota(jnp.int32, shape, 0) % ROWS
        columns = lax.broadcasted_iota(jnp.int32, shape, 1) % ROWS
        return rows == columns

    def dot(a, b, dims):
        return lax.dot_general(a, b, (dims, ((), ())), preferred_element_type=jnp.float32)

    tall = dot(pick((n_modes * ROWS, n_modes), 0), modes, ((1,), (1,))).astype(jnp.bfloat16)
    value = dot(tall, pick((freq, freq * ROWS), 1), ((1,), (0,)))
    down_ref[...] = jnp.where(lane(value.shape), value, 0.0).astype(jnp.bfloat16)
    tall = dot(pick((freq * ROWS, freq), 0), modes, ((1,), (0,))).astype(jnp.bfloat16)
    value = dot(tall, pick((n_modes, n_modes * ROWS), 1), ((1,), (0,)))
    up_ref[...] = jnp.where(lane(value.shape), value, 0.0).astype(jnp.bfloat16)
    for f, copy in enumerate(copies):
        copy.wait()
        held[f] = held[f] * mask[...]


def hold(where, tiles, starts, beam, modes):
    freq, base, ell = beam.shape
    size, wide = freq * ROWS, modes.shape[1] * ROWS
    vmem = pl.BlockSpec(memory_space=pltpu.VMEM)
    return pl.pallas_call(
        hold_kernel,
        grid_spec=pltpu.PrefetchScalarGridSpec(
            num_scalar_prefetch=3,
            grid=(),
            in_specs=[pl.BlockSpec(memory_space=pl.ANY), vmem],
            out_specs=[vmem] * 3,
            scratch_shapes=[pltpu.VMEM((base, ell), jnp.bfloat16), pltpu.SemaphoreType.DMA((freq,))],
        ),
        out_shape=[
            pltpu.VMEM(beam.shape, beam.dtype),
            jax.ShapeDtypeStruct((wide, size), jnp.bfloat16),
            jax.ShapeDtypeStruct((size, wide), jnp.bfloat16),
        ],
        compiler_params=pltpu.CompilerParams(vmem_limit_bytes=VMEM_LIMIT),
        cost_estimate=pl.CostEstimate(flops=1024, bytes_accessed=1024, transcendentals=0),
    )(where, tiles, starts, beam, modes)


def project_kernel(where, *refs, piece, blocks):
    count = (len(refs) - 3) // 2
    mine, others = refs[:count], refs[count:2 * count]
    held, stay_ref, leave_ref = refs[2 * count:]
    freqs, rows, _ = stay_ref.shape
    first = where[piece] * freqs
    own = where[PARTS] == 1
    for f in range(freqs):
        a = jnp.concatenate([mine[n][k] for n, k in blocks[f]], axis=0)
        b = jnp.concatenate([others[n][k] for n, k in blocks[f]], axis=0)
        lines = jnp.concatenate([jnp.where(own, a, b), jnp.where(own, b, a)], axis=0)
        value = jnp.dot(lines, held[first + f], preferred_element_type=jnp.float32).astype(jnp.bfloat16)
        stay_ref[f] = value[:rows]
        leave_ref[f] = value[rows:]


def project(where, mine, others, held, piece, blocks, flops=1024):
    ell = held.shape[2]
    rows = sum(mine[n].shape[1] for n, _ in blocks[0])
    vmem = pl.BlockSpec(memory_space=pltpu.VMEM)
    return pl.pallas_call(
        functools.partial(project_kernel, piece=piece, blocks=blocks),
        grid_spec=pltpu.PrefetchScalarGridSpec(
            num_scalar_prefetch=1, grid=(), in_specs=[vmem] * (2 * len(mine) + 1), out_specs=[vmem] * 2
        ),
        out_shape=[jax.ShapeDtypeStruct((len(blocks), rows, ell), jnp.bfloat16)] * 2,
        compiler_params=pltpu.CompilerParams(vmem_limit_bytes=VMEM_LIMIT),
        cost_estimate=pl.CostEstimate(flops=flops, bytes_accessed=1024, transcendentals=0),
    )(where, *mine, *others, pltpu.with_memory_space_constraint(held, pltpu.VMEM))


def contract(modes, skies):
    block = jnp.concatenate([sky[...].reshape(sky.shape[0] * ROWS, sky.shape[2]) for sky in skies], axis=0)
    return jnp.dot(modes, block, preferred_element_type=jnp.float32)


def reduce_kernel(modes_ref, *refs):
    out = refs[-1]
    out[...] = contract(modes_ref[...], refs[:-1]).astype(out.dtype).reshape(out.shape)


def by_rows(count, ell, first=0):
    return pl.BlockSpec((count, ROWS, ell), lambda g: (0, g + first // ROWS, 0))


def fixed(shape):
    return pl.BlockSpec(shape, lambda g: (0,) * len(shape))


def sky_specs(skies, first):
    return [by_rows(sky.shape[0], sky.shape[2], low) for sky, low in zip(skies, first)]


def reduce(modes, skies, first, n_modes, dtype=jnp.bfloat16):
    _, rows, ell = skies[-1].shape
    return pl.pallas_call(
        reduce_kernel,
        grid=(rows // ROWS,),
        in_specs=[fixed(modes.shape)] + sky_specs(skies, first),
        out_specs=by_rows(n_modes, ell),
        out_shape=jax.ShapeDtypeStruct((n_modes, rows, ell), dtype),
        compiler_params=pltpu.CompilerParams(vmem_limit_bytes=VMEM_LIMIT),
        cost_estimate=pl.CostEstimate(flops=1024, bytes_accessed=1024, transcendentals=0),
    )(modes, *skies)


def restore_kernel(up_ref, ratio_ref, kept_ref, came_ref, *outs, spots):
    n_modes, _, ell = came_ref.shape
    freqs = up_ref.shape[0] // ROWS // PARTS
    total = kept_ref[...] + came_ref[...].astype(jnp.float32)
    weighted = (total * ratio_ref[...]).astype(jnp.bfloat16).reshape(n_modes * ROWS, ell)
    for (j, low, high), out in zip(spots, outs):
        modes = up_ref[(j * freqs + low) * ROWS:(j * freqs + high) * ROWS, :]
        value = jnp.dot(modes, weighted, preferred_element_type=jnp.float32)
        out[...] = value.astype(jnp.bfloat16).reshape(out.shape)


def restore(kept, came, ratios, up, spots):
    n_modes, rows, ell = came.shape
    return pl.pallas_call(
        functools.partial(restore_kernel, spots=spots),
        grid=(rows // ROWS,),
        in_specs=[fixed(up.shape), fixed(ratios.shape)] + [by_rows(n_modes, ell)] * 2,
        out_specs=[by_rows(high - low, ell) for _, low, high in spots],
        out_shape=[jax.ShapeDtypeStruct((high - low, rows, ell), jnp.bfloat16) for _, low, high in spots],
        compiler_params=pltpu.CompilerParams(vmem_limit_bytes=VMEM_LIMIT),
        cost_estimate=pl.CostEstimate(flops=1024, bytes_accessed=1024, transcendentals=0),
    )(up, ratios, kept, came)


def place_kernel(where, *refs, spots, first):
    count = len(spots)
    pieces, out, sems = refs[:count], refs[-2], refs[-1]
    rows = pieces[0].shape[1]
    copies = [
        pltpu.make_async_copy(pieces[n], out.at[low:high, where[j], first:first + rows, :], sems.at[n])
        for n, (j, low, high) in enumerate(spots)
    ]
    for copy in copies:
        copy.start()
    for copy in copies:
        copy.wait()


def place(where, pieces, spots, first, shape, into=None):
    count = len(spots)
    extra = [] if into is None else [into]
    anywhere = pl.BlockSpec(memory_space=pl.ANY)
    return pl.pallas_call(
        functools.partial(place_kernel, spots=spots, first=first),
        grid_spec=pltpu.PrefetchScalarGridSpec(
            num_scalar_prefetch=1,
            grid=(),
            in_specs=[pl.BlockSpec(memory_space=pltpu.VMEM)] * count + [anywhere] * len(extra),
            out_specs=anywhere,
            scratch_shapes=[pltpu.SemaphoreType.DMA((count,))],
        ),
        out_shape=jax.ShapeDtypeStruct(shape, jnp.bfloat16),
        input_output_aliases={count + 1: 0} if extra else {},
        compiler_params=pltpu.CompilerParams(vmem_limit_bytes=VMEM_LIMIT),
        cost_estimate=pl.CostEstimate(flops=1024, bytes_accessed=1024, transcendentals=0),
    )(where, *pieces, *extra)


def anchor_kernel(*refs):
    del refs


def anchor(values, flops):
    anywhere = pl.BlockSpec(memory_space=pl.ANY)
    return pl.pallas_call(
        anchor_kernel,
        in_specs=[anywhere] * len(values),
        out_specs=[anywhere] * len(values),
        out_shape=[jax.ShapeDtypeStruct(value.shape, value.dtype) for value in values],
        input_output_aliases={n: n for n in range(len(values))},
        compiler_params=pltpu.CompilerParams(vmem_limit_bytes=1024 * 1024),
        cost_estimate=pl.CostEstimate(flops=flops, bytes_accessed=1024, transcendentals=0),
    )(*values)


def staged(visibility, beam_transfer, tile_mask, first_block, eigen_modes, signal_noise):
    freqs, parts, rows_all, base = visibility.shape
    _, freq_total, _, ell = beam_transfer.shape
    n_modes = eigen_modes.shape[2]
    ell_tiles = ell // TILE
    z, x, p = lax.axis_index("fm"), lax.axis_index("kl"), lax.axis_index("pol")
    other = [(0, 1), (1, 0)]

    def along_z(value, j):
        return lax.ppermute(value, "fm", [(i, i ^ j) for i in range(parts)])

    def along_x(value):
        return lax.ppermute(value, "kl", other)

    def cut(j, first, rows):
        return lax.dynamic_slice(visibility, (0, z ^ j, first, 0), (freqs, 1, rows, base)).reshape(freqs, rows, base)

    index = jnp.arange(parts + 2, dtype=jnp.int32)
    where = jnp.where(
        index < parts, z ^ index, jnp.where(index == parts, (x == p).astype(jnp.int32), x * ell_tiles)
    ).astype(jnp.int32)
    ratio = signal_noise[0] / (1.0 + signal_noise[0])
    ratios = jnp.broadcast_to(ratio[:, None, None], (n_modes, 1, ell))
    beam = beam_transfer.reshape(freq_total, base, ell)
    shape = (freqs, parts, rows_all, ell)

    fence = lax.optimization_barrier
    most, half = rows_all - ROWS, freqs // 2
    blocks = [[(0, f)] for f in range(freqs)]
    halves = [[(f // half, f % half)] for f in range(freqs)]
    a = {j: along_z(cut(j, 0, ROWS), j) for j in (3, 2, 1)}
    mine = [cut(0, 0, rows_all)[n:n + half] for n in (0, half)]
    others = [along_x(part) for part in mine]
    b = {j: cut(j, ROWS, most) for j in (1, 2, 3)}
    held, down, up = hold(where, tile_mask[0], first_block, beam, eigen_modes[0])
    (a[3], a[2], a[1]), b, others, down, up = fence(((a[3], a[2], a[1]), b, others, down, up))
    b[1], b[2] = along_z(b[1], 1), along_z(b[2], 2)
    own = project(where, mine, others, held, 0, halves, 400_000_000)
    skies = [own] + [project(where, [a[j]], [along_x(a[j])], held, j, blocks, 400_000_000) for j in (1, 2, 3)]
    gone = reduce(down, [leave for _, leave in skies], (0, 0, 0, 0), n_modes)
    stay_a = [stay for stay, _ in skies]
    b[2], b[3], stay_a, gone = fence((b[2], b[3], stay_a, gone))
    x_2 = along_x(b[2])
    x_1, = anchor([along_x(b[1])], 2_500_000_000)
    b[3] = along_z(b[3], 3)
    kept = reduce(down, stay_a, (0, 0, 0, 0), n_modes, jnp.float32)
    spots = [(j, 0, freqs) for j in (1, 2, 3, 0)]
    outs = restore(kept, lax.ppermute(gone, "pol", other), ratios, up, spots)
    near = project(where, [b[1]], [x_1], held, 1, blocks)
    x_2, b, outs, near = fence((x_2, b, outs, near))
    first = {j: along_z(outs[j - 1], j) for j in (1, 2, 3)}
    first[0] = outs[3]
    x_3 = along_x(b[3])
    skies = [own, near] + [project(where, [b[j]], [x], held, j, blocks) for j, x in ((2, x_2), (3, x_3))]
    gone = reduce(down, [leave for _, leave in skies], (ROWS, 0, 0, 0), n_modes)
    stays = [stay for stay, _ in skies]
    first[2], first[1], here, stays, gone = fence((first[2], first[1], first[0], stays, gone))
    came = lax.ppermute(gone, "pol", other)
    kept = reduce(down, stays, (ROWS, 0, 0, 0), n_modes, jnp.float32)
    first[3], = anchor([first[3]], 20_000_000_000)
    outs, first[3] = fence((restore(kept, came, ratios, up, spots), first[3]))
    first[0] = here
    back = [along_z(outs[j - 1], j) for j in (1, 3, 2)]
    result = place(where, [first[j] for j in (1, 2, 3, 0)], spots, 0, shape)
    result = place(where, [outs[3]], [spots[3]], ROWS, shape, into=result)
    return place(where, back, [spots[0], spots[2], spots[1]], ROWS, shape, into=result)


def plain(visibility, beam_transfer, tile_mask, first_block, eigen_modes, signal_noise):
    owned_modes, freq_total, base_half, ell_local = beam_transfer.shape
    base_tiles, ell_tiles = base_half // TILE, ell_local // TILE
    block_ids = lax.axis_index("kl") * ell_tiles + jnp.arange(ell_tiles, dtype=jnp.int32)
    inside = (first_block[:, None] <= block_ids[None, :]).astype(jnp.int32)
    keep_tiles = tile_mask * inside[:, None, :]
    shaped = beam_transfer.reshape(owned_modes, freq_total, base_tiles, TILE, ell_tiles, TILE)
    masked_beam = shaped * keep_tiles.astype(jnp.bfloat16)[:, None, :, None, :, None]
    masked_beam = masked_beam.reshape(owned_modes, freq_total, base_half, ell_local)
    arrived = lax.all_to_all(visibility, "fm", split_axis=1, concat_axis=0, tiled=True)
    partial_value = jnp.einsum(
        "fmrb,mfbl->fmrl",
        lax.all_gather(arrived, "kl", axis=2, tiled=True),
        masked_beam,
        preferred_element_type=jnp.float32,
    )
    sky_sum = lax.psum_scatter(
        partial_value.astype(jnp.bfloat16), "pol", scatter_dimension=2, tiled=True
    ).astype(jnp.float32)
    modes_float = eigen_modes.astype(jnp.float32)
    coeffs = jnp.einsum("mfk,fmrl->mkrl", modes_float, sky_sum, precision=lax.Precision.HIGHEST)
    ratios = signal_noise / (1.0 + signal_noise)
    weighted = (coeffs * ratios[:, :, None, None]).astype(jnp.bfloat16)
    filtered = jnp.einsum(
        "mfk,mkrl->fmrl", eigen_modes, weighted, preferred_element_type=jnp.float32
    ).astype(jnp.bfloat16)
    return lax.all_to_all(filtered, "fm", split_axis=0, concat_axis=1, tiled=True)


def per_device(*args, sizes):
    visibility, beam_transfer = args[0], args[1]
    _, modes, rows, _ = visibility.shape
    fits = (
        sizes["kl"] == 2
        and sizes["pol"] == 2
        and modes == sizes["fm"] == PARTS
        and beam_transfer.shape[0] == 1
        and rows == 3 * ROWS
        and visibility.shape[0] % 2 == 0
    )
    if not fits:
        return plain(*args)
    return staged(*args)


def solution(mesh):
    placed = (
        P(("group", "fm"), None, "kl", "pol"),
        P(("group", "fm"), None, "pol", "kl"),
        P("fm", "pol", "kl"),
        P("fm"),
        P(("group", "fm"), None, None),
        P(("group", "fm"), None),
    )
    return jax.shard_map(
        functools.partial(per_device, sizes=dict(mesh.shape)),
        mesh=mesh,
        in_specs=placed,
        out_specs=P(("group", "fm"), None, "pol", "kl"),
        check_vma=False,
    )
```

```python
import functools
import jax
import jax.numpy as jnp
from jax import lax
from jax.experimental import pallas as pl
from jax.experimental.pallas import tpu as pltpu
from jax.sharding import PartitionSpec as P

TILE = 128
PARTS = 4
ROWS = 16
VMEM_LIMIT = 24 * 1024 * 1024


def hold_kernel(where, tiles, starts, beam, modes_ref, held, down_ref, up_ref, mask, sems):
    freq, base, ell = held.shape
    n_modes = modes_ref.shape[1]
    ell_tiles, base_tiles, freqs = ell // TILE, base // TILE, freq // PARTS
    copies = [pltpu.make_async_copy(beam.at[f], held.at[f], sems.at[f]) for f in range(freq)]
    for copy in copies:
        copy.start()
    for b in range(base_tiles):
        for l in range(ell_tiles):
            kept = jnp.where(starts[0] <= where[PARTS + 1] + l, tiles[b, l], 0).astype(jnp.float32)
            mask[b * TILE:(b + 1) * TILE, l * TILE:(l + 1) * TILE] = jnp.full(
                (TILE, TILE), kept, jnp.float32
            ).astype(jnp.bfloat16)
    modes = modes_ref[...]

    def pick(shape, axis, orders=0):
        big = lax.broadcasted_iota(jnp.int32, shape, axis) // ROWS
        small = lax.broadcasted_iota(jnp.int32, shape, 1 - axis)
        if freq in shape:
            piece, within = big // freqs, big % freqs
            big = within
            for j in range(PARTS):
                big = jnp.where(piece == j, where[orders + j] * freqs + within, big)
        return jnp.where(big == small, 1.0, 0.0).astype(jnp.bfloat16)

    def lane(shape):
        rows = lax.broadcasted_iota(jnp.int32, shape, 0) % ROWS
        columns = lax.broadcasted_iota(jnp.int32, shape, 1) % ROWS
        return rows == columns

    def dot(a, b, dims):
        return lax.dot_general(a, b, (dims, ((), ())), preferred_element_type=jnp.float32)

    tall = dot(pick((n_modes * ROWS, n_modes), 0), modes, ((1,), (1,))).astype(jnp.bfloat16)
    value = dot(tall, pick((freq, freq * ROWS), 1), ((1,), (0,)))
    down_ref[...] = jnp.where(lane(value.shape), value, 0.0).astype(jnp.bfloat16)
    tall = dot(pick((freq * ROWS, freq), 0, PARTS + 2), modes, ((1,), (0,))).astype(jnp.bfloat16)
    value = dot(tall, pick((n_modes, n_modes * ROWS), 1), ((1,), (0,)))
    up_ref[...] = jnp.where(lane(value.shape), value, 0.0).astype(jnp.bfloat16)
    for f, copy in enumerate(copies):
        copy.wait()
        held[f] = held[f] * mask[...]


def hold(where, tiles, starts, beam, modes):
    freq, base, ell = beam.shape
    size, wide = freq * ROWS, modes.shape[1] * ROWS
    vmem = pl.BlockSpec(memory_space=pltpu.VMEM)
    return pl.pallas_call(
        hold_kernel,
        grid_spec=pltpu.PrefetchScalarGridSpec(
            num_scalar_prefetch=3,
            grid=(),
            in_specs=[pl.BlockSpec(memory_space=pl.ANY), vmem],
            out_specs=[vmem] * 3,
            scratch_shapes=[pltpu.VMEM((base, ell), jnp.bfloat16), pltpu.SemaphoreType.DMA((freq,))],
        ),
        out_shape=[
            pltpu.VMEM(beam.shape, beam.dtype),
            jax.ShapeDtypeStruct((wide, size), jnp.bfloat16),
            jax.ShapeDtypeStruct((size, wide), jnp.bfloat16),
        ],
        compiler_params=pltpu.CompilerParams(vmem_limit_bytes=VMEM_LIMIT),
        cost_estimate=pl.CostEstimate(flops=1024, bytes_accessed=1024, transcendentals=0),
    )(where, tiles, starts, beam, modes)


def project_kernel(where, *refs, piece, blocks):
    count = (len(refs) - 3) // 2
    mine, others = refs[:count], refs[count:2 * count]
    held, stay_ref, leave_ref = refs[2 * count:]
    freqs, rows, _ = stay_ref.shape
    first = where[piece] * freqs
    own = where[PARTS] == 1
    for f in range(freqs):
        a = jnp.concatenate([mine[n][k] for n, k in blocks[f]], axis=0)
        b = jnp.concatenate([others[n][k] for n, k in blocks[f]], axis=0)
        lines = jnp.concatenate([jnp.where(own, a, b), jnp.where(own, b, a)], axis=0)
        value = jnp.dot(lines, held[first + f], preferred_element_type=jnp.float32).astype(jnp.bfloat16)
        stay_ref[f] = value[:rows]
        leave_ref[f] = value[rows:]


def project(where, mine, others, held, piece, blocks, flops=1024):
    ell = held.shape[2]
    rows = sum(mine[n].shape[1] for n, _ in blocks[0])
    vmem = pl.BlockSpec(memory_space=pltpu.VMEM)
    return pl.pallas_call(
        functools.partial(project_kernel, piece=piece, blocks=blocks),
        grid_spec=pltpu.PrefetchScalarGridSpec(
            num_scalar_prefetch=1, grid=(), in_specs=[vmem] * (2 * len(mine) + 1), out_specs=[vmem] * 2
        ),
        out_shape=[jax.ShapeDtypeStruct((len(blocks), rows, ell), jnp.bfloat16)] * 2,
        compiler_params=pltpu.CompilerParams(vmem_limit_bytes=VMEM_LIMIT),
        cost_estimate=pl.CostEstimate(flops=flops, bytes_accessed=1024, transcendentals=0),
    )(where, *mine, *others, pltpu.with_memory_space_constraint(held, pltpu.VMEM))


def contract(modes, skies):
    block = jnp.concatenate([sky[...].reshape(sky.shape[0] * ROWS, sky.shape[2]) for sky in skies], axis=0)
    return jnp.dot(modes, block, preferred_element_type=jnp.float32)


def reduce_kernel(modes_ref, *refs):
    out = refs[-1]
    out[...] = contract(modes_ref[...], refs[:-1]).astype(out.dtype).reshape(out.shape)


def by_rows(count, ell, first=0):
    return pl.BlockSpec((count, ROWS, ell), lambda g: (0, g + first // ROWS, 0))


def fixed(shape):
    return pl.BlockSpec(shape, lambda g: (0,) * len(shape))


def sky_specs(skies, first):
    return [by_rows(sky.shape[0], sky.shape[2], low) for sky, low in zip(skies, first)]


def reduce(modes, skies, first, n_modes, dtype=jnp.bfloat16):
    _, rows, ell = skies[-1].shape
    return pl.pallas_call(
        reduce_kernel,
        grid=(rows // ROWS,),
        in_specs=[fixed(modes.shape)] + sky_specs(skies, first),
        out_specs=by_rows(n_modes, ell),
        out_shape=jax.ShapeDtypeStruct((n_modes, rows, ell), dtype),
        compiler_params=pltpu.CompilerParams(vmem_limit_bytes=VMEM_LIMIT),
        cost_estimate=pl.CostEstimate(flops=1024, bytes_accessed=1024, transcendentals=0),
    )(modes, *skies)


def restore_kernel(up_ref, ratio_ref, kept_ref, came_ref, *outs, spots):
    n_modes, _, ell = came_ref.shape
    freqs = up_ref.shape[0] // ROWS // PARTS
    total = kept_ref[...] + came_ref[...].astype(jnp.float32)
    weighted = (total * ratio_ref[...]).astype(jnp.bfloat16).reshape(n_modes * ROWS, ell)
    for (j, low, high), out in zip(spots, outs):
        modes = up_ref[(j * freqs + low) * ROWS:(j * freqs + high) * ROWS, :]
        value = jnp.dot(modes, weighted, preferred_element_type=jnp.float32)
        out[...] = value.astype(jnp.bfloat16).reshape(out.shape)


def restore(kept, came, ratios, up, spots):
    n_modes, rows, ell = came.shape
    return pl.pallas_call(
        functools.partial(restore_kernel, spots=spots),
        grid=(rows // ROWS,),
        in_specs=[fixed(up.shape), fixed(ratios.shape)] + [by_rows(n_modes, ell)] * 2,
        out_specs=[by_rows(high - low, ell) for _, low, high in spots],
        out_shape=[jax.ShapeDtypeStruct((high - low, rows, ell), jnp.bfloat16) for _, low, high in spots],
        compiler_params=pltpu.CompilerParams(vmem_limit_bytes=VMEM_LIMIT),
        cost_estimate=pl.CostEstimate(flops=1024, bytes_accessed=1024, transcendentals=0),
    )(up, ratios, kept, came)


def place_kernel(where, *refs, spots, first):
    count = len(spots)
    pieces, out, sems = refs[:count], refs[-2], refs[-1]
    rows = pieces[0].shape[1]
    copies = [
        pltpu.make_async_copy(pieces[n], out.at[low:high, where[PARTS + 2 + j], first:first + rows, :], sems.at[n])
        for n, (j, low, high) in enumerate(spots)
    ]
    for copy in copies:
        copy.start()
    for copy in copies:
        copy.wait()


def place(where, pieces, spots, first, shape, into=None):
    count = len(spots)
    extra = [] if into is None else [into]
    anywhere = pl.BlockSpec(memory_space=pl.ANY)
    return pl.pallas_call(
        functools.partial(place_kernel, spots=spots, first=first),
        grid_spec=pltpu.PrefetchScalarGridSpec(
            num_scalar_prefetch=1,
            grid=(),
            in_specs=[pl.BlockSpec(memory_space=pltpu.VMEM)] * count + [anywhere] * len(extra),
            out_specs=anywhere,
            scratch_shapes=[pltpu.SemaphoreType.DMA((count,))],
        ),
        out_shape=jax.ShapeDtypeStruct(shape, jnp.bfloat16),
        input_output_aliases={count + 1: 0} if extra else {},
        compiler_params=pltpu.CompilerParams(vmem_limit_bytes=VMEM_LIMIT),
        cost_estimate=pl.CostEstimate(flops=1024, bytes_accessed=1024, transcendentals=0),
    )(where, *pieces, *extra)


def anchor_kernel(*refs):
    del refs


def anchor(values, flops):
    anywhere = pl.BlockSpec(memory_space=pl.ANY)
    return pl.pallas_call(
        anchor_kernel,
        in_specs=[anywhere] * len(values),
        out_specs=[anywhere] * len(values),
        out_shape=[jax.ShapeDtypeStruct(value.shape, value.dtype) for value in values],
        input_output_aliases={n: n for n in range(len(values))},
        compiler_params=pltpu.CompilerParams(vmem_limit_bytes=1024 * 1024),
        cost_estimate=pl.CostEstimate(flops=flops, bytes_accessed=1024, transcendentals=0),
    )(*values)


def staged(visibility, beam_transfer, tile_mask, first_block, eigen_modes, signal_noise):
    freqs, parts, rows_all, base = visibility.shape
    _, freq_total, _, ell = beam_transfer.shape
    n_modes = eigen_modes.shape[2]
    ell_tiles = ell // TILE
    z, x, p = lax.axis_index("fm"), lax.axis_index("kl"), lax.axis_index("pol")
    other = [(0, 1), (1, 0)]

    def shift_z(value, j):
        return lax.ppermute(value, "fm", [(i, (i + j) % parts) for i in range(parts)])

    def swap_z(value, j):
        return lax.ppermute(value, "fm", [(i, i ^ j) for i in range(parts)])

    def along_x(value):
        return lax.ppermute(value, "kl", other)

    def cut(j, first, rows):
        return lax.dynamic_slice(visibility, (0, (z + j) % parts, first, 0), (freqs, 1, rows, base)).reshape(freqs, rows, base)

    index = jnp.arange(2 * parts + 2, dtype=jnp.int32)
    where = jnp.where(index < parts, (z - index) % parts, z ^ (index - parts - 2))
    where = jnp.where(index == parts, (x == p).astype(jnp.int32), where)
    where = jnp.where(index == parts + 1, x * ell_tiles, where).astype(jnp.int32)
    ratio = signal_noise[0] / (1.0 + signal_noise[0])
    ratios = jnp.broadcast_to(ratio[:, None, None], (n_modes, 1, ell))
    beam = beam_transfer.reshape(freq_total, base, ell)
    shape = (freqs, parts, rows_all, ell)

    fence = lax.optimization_barrier
    most, half = rows_all - ROWS, freqs // 2
    blocks = [[(0, f)] for f in range(freqs)]
    halves = [[(f // half, f % half)] for f in range(freqs)]
    a = {j: shift_z(cut(j, 0, ROWS), j) for j in (1, 3, 2)}
    mine = [cut(0, 0, rows_all)[n:n + half] for n in (0, half)]
    others = [along_x(part) for part in mine]
    b = {j: cut(j, ROWS, most) for j in (1, 2, 3)}
    held, down, up = hold(where, tile_mask[0], first_block, beam, eigen_modes[0])
    (a[1], a[3], a[2]), b, others, down, up = fence(((a[1], a[3], a[2]), b, others, down, up))
    b[1], b[3] = shift_z(b[1], 1), shift_z(b[3], 3)
    own = project(where, mine, others, held, 0, halves, 400_000_000)
    skies = [own] + [project(where, [a[j]], [along_x(a[j])], held, j, blocks, 400_000_000) for j in (1, 2, 3)]
    gone = reduce(down, [leave for _, leave in skies], (0, 0, 0, 0), n_modes)
    stay_a = [stay for stay, _ in skies]
    b[3], b[2], stay_a, gone = fence((b[3], b[2], stay_a, gone))
    x_3 = along_x(b[3])
    x_1, = anchor([along_x(b[1])], 2_500_000_000)
    b[2] = shift_z(b[2], 2)
    kept = reduce(down, stay_a, (0, 0, 0, 0), n_modes, jnp.float32)
    spots = [(j, 0, freqs) for j in (1, 2, 3, 0)]
    outs = restore(kept, lax.ppermute(gone, "pol", other), ratios, up, spots)
    near = project(where, [b[1]], [x_1], held, 1, blocks)
    x_3, b, outs, near = fence((x_3, b, outs, near))
    first = {j: swap_z(outs[j - 1], j) for j in (1, 2, 3)}
    first[0] = outs[3]
    x_2 = along_x(b[2])
    last = project(where, [b[3]], [x_3], held, 3, blocks)
    skies = [own, near, project(where, [b[2]], [x_2], held, 2, blocks), last]
    gone = reduce(down, [leave for _, leave in skies], (ROWS, 0, 0, 0), n_modes)
    stays = [stay for stay, _ in skies]
    first[2], first[1], here, stays, gone = fence((first[2], first[1], first[0], stays, gone))
    came = lax.ppermute(gone, "pol", other)
    kept = reduce(down, stays, (ROWS, 0, 0, 0), n_modes, jnp.float32)
    first[3], = anchor([first[3]], 20_000_000_000)
    outs, first[3] = fence((restore(kept, came, ratios, up, spots), first[3]))
    first[0] = here
    back = [swap_z(outs[j - 1], j) for j in (1, 2, 3)]
    result = place(where, [first[j] for j in (1, 2, 3, 0)], spots, 0, shape)
    result = place(where, [outs[3], back[0]], [spots[3], spots[0]], ROWS, shape, into=result)
    return place(where, back[1:], spots[1:3], ROWS, shape, into=result)


def plain(visibility, beam_transfer, tile_mask, first_block, eigen_modes, signal_noise):
    owned_modes, freq_total, base_half, ell_local = beam_transfer.shape
    base_tiles, ell_tiles = base_half // TILE, ell_local // TILE
    block_ids = lax.axis_index("kl") * ell_tiles + jnp.arange(ell_tiles, dtype=jnp.int32)
    inside = (first_block[:, None] <= block_ids[None, :]).astype(jnp.int32)
    keep_tiles = tile_mask * inside[:, None, :]
    shaped = beam_transfer.reshape(owned_modes, freq_total, base_tiles, TILE, ell_tiles, TILE)
    masked_beam = shaped * keep_tiles.astype(jnp.bfloat16)[:, None, :, None, :, None]
    masked_beam = masked_beam.reshape(owned_modes, freq_total, base_half, ell_local)
    arrived = lax.all_to_all(visibility, "fm", split_axis=1, concat_axis=0, tiled=True)
    partial_value = jnp.einsum(
        "fmrb,mfbl->fmrl",
        lax.all_gather(arrived, "kl", axis=2, tiled=True),
        masked_beam,
        preferred_element_type=jnp.float32,
    )
    sky_sum = lax.psum_scatter(
        partial_value.astype(jnp.bfloat16), "pol", scatter_dimension=2, tiled=True
    ).astype(jnp.float32)
    modes_float = eigen_modes.astype(jnp.float32)
    coeffs = jnp.einsum("mfk,fmrl->mkrl", modes_float, sky_sum, precision=lax.Precision.HIGHEST)
    ratios = signal_noise / (1.0 + signal_noise)
    weighted = (coeffs * ratios[:, :, None, None]).astype(jnp.bfloat16)
    filtered = jnp.einsum(
        "mfk,mkrl->fmrl", eigen_modes, weighted, preferred_element_type=jnp.float32
    ).astype(jnp.bfloat16)
    return lax.all_to_all(filtered, "fm", split_axis=0, concat_axis=1, tiled=True)


def per_device(*args, sizes):
    visibility, beam_transfer = args[0], args[1]
    _, modes, rows, _ = visibility.shape
    fits = (
        sizes["kl"] == 2
        and sizes["pol"] == 2
        and modes == sizes["fm"] == PARTS
        and beam_transfer.shape[0] == 1
        and rows == 3 * ROWS
        and visibility.shape[0] % 2 == 0
    )
    if not fits:
        return plain(*args)
    return staged(*args)


def solution(mesh):
    placed = (
        P(("group", "fm"), None, "kl", "pol"),
        P(("group", "fm"), None, "pol", "kl"),
        P("fm", "pol", "kl"),
        P("fm"),
        P(("group", "fm"), None, None),
        P(("group", "fm"), None),
    )
    return jax.shard_map(
        functools.partial(per_device, sizes=dict(mesh.shape)),
        mesh=mesh,
        in_specs=placed,
        out_specs=P(("group", "fm"), None, "pol", "kl"),
        check_vma=False,
    )
```

```python
import functools
import jax
import jax.numpy as jnp
from jax import lax
from jax.experimental import pallas as pl
from jax.experimental.pallas import tpu as pltpu
from jax.sharding import PartitionSpec as P

TILE = 128
PARTS = 4
ROWS = 16
VMEM_LIMIT = 24 * 1024 * 1024


def hold_kernel(where, tiles, starts, beam, modes_ref, held, down_ref, up_ref, mask, sems):
    freq, base, ell = held.shape
    n_modes = modes_ref.shape[1]
    ell_tiles, base_tiles, freqs = ell // TILE, base // TILE, freq // PARTS
    copies = [pltpu.make_async_copy(beam.at[f], held.at[f], sems.at[f]) for f in range(freq)]
    for copy in copies:
        copy.start()
    for b in range(base_tiles):
        for l in range(ell_tiles):
            kept = jnp.where(starts[0] <= where[PARTS + 1] + l, tiles[b, l], 0).astype(jnp.float32)
            mask[b * TILE:(b + 1) * TILE, l * TILE:(l + 1) * TILE] = jnp.full(
                (TILE, TILE), kept, jnp.float32
            ).astype(jnp.bfloat16)
    modes = modes_ref[...]

    def pick(shape, axis, orders=0):
        big = lax.broadcasted_iota(jnp.int32, shape, axis) // ROWS
        small = lax.broadcasted_iota(jnp.int32, shape, 1 - axis)
        if freq in shape:
            piece, within = big // freqs, big % freqs
            big = within
            for j in range(PARTS):
                big = jnp.where(piece == j, where[orders + j] * freqs + within, big)
        return jnp.where(big == small, 1.0, 0.0).astype(jnp.bfloat16)

    def lane(shape):
        rows = lax.broadcasted_iota(jnp.int32, shape, 0) % ROWS
        columns = lax.broadcasted_iota(jnp.int32, shape, 1) % ROWS
        return rows == columns

    def dot(a, b, dims):
        return lax.dot_general(a, b, (dims, ((), ())), preferred_element_type=jnp.float32)

    tall = dot(pick((n_modes * ROWS, n_modes), 0), modes, ((1,), (1,))).astype(jnp.bfloat16)
    value = dot(tall, pick((freq, freq * ROWS), 1), ((1,), (0,)))
    down_ref[...] = jnp.where(lane(value.shape), value, 0.0).astype(jnp.bfloat16)
    tall = dot(pick((freq * ROWS, freq), 0, PARTS + 2), modes, ((1,), (0,))).astype(jnp.bfloat16)
    value = dot(tall, pick((n_modes, n_modes * ROWS), 1), ((1,), (0,)))
    up_ref[...] = jnp.where(lane(value.shape), value, 0.0).astype(jnp.bfloat16)
    for f, copy in enumerate(copies):
        copy.wait()
        held[f] = held[f] * mask[...]


def hold(where, tiles, starts, beam, modes):
    freq, base, ell = beam.shape
    size, wide = freq * ROWS, modes.shape[1] * ROWS
    vmem = pl.BlockSpec(memory_space=pltpu.VMEM)
    return pl.pallas_call(
        hold_kernel,
        grid_spec=pltpu.PrefetchScalarGridSpec(
            num_scalar_prefetch=3,
            grid=(),
            in_specs=[pl.BlockSpec(memory_space=pl.ANY), vmem],
            out_specs=[vmem] * 3,
            scratch_shapes=[pltpu.VMEM((base, ell), jnp.bfloat16), pltpu.SemaphoreType.DMA((freq,))],
        ),
        out_shape=[
            pltpu.VMEM(beam.shape, beam.dtype),
            jax.ShapeDtypeStruct((wide, size), jnp.bfloat16),
            jax.ShapeDtypeStruct((size, wide), jnp.bfloat16),
        ],
        compiler_params=pltpu.CompilerParams(vmem_limit_bytes=VMEM_LIMIT),
        cost_estimate=pl.CostEstimate(flops=1024, bytes_accessed=1024, transcendentals=0),
    )(where, tiles, starts, beam, modes)


def project_kernel(where, *refs, piece, blocks):
    count = (len(refs) - 3) // 2
    mine, others = refs[:count], refs[count:2 * count]
    held, stay_ref, leave_ref = refs[2 * count:]
    freqs, rows, _ = stay_ref.shape
    first = where[piece] * freqs
    own = where[PARTS] == 1
    for f in range(freqs):
        a = jnp.concatenate([mine[n][k] for n, k in blocks[f]], axis=0)
        b = jnp.concatenate([others[n][k] for n, k in blocks[f]], axis=0)
        lines = jnp.concatenate([jnp.where(own, a, b), jnp.where(own, b, a)], axis=0)
        value = jnp.dot(lines, held[first + f], preferred_element_type=jnp.float32).astype(jnp.bfloat16)
        stay_ref[f] = value[:rows]
        leave_ref[f] = value[rows:]


def project(where, mine, others, held, piece, blocks, flops=1024):
    ell = held.shape[2]
    rows = sum(mine[n].shape[1] for n, _ in blocks[0])
    vmem = pl.BlockSpec(memory_space=pltpu.VMEM)
    return pl.pallas_call(
        functools.partial(project_kernel, piece=piece, blocks=blocks),
        grid_spec=pltpu.PrefetchScalarGridSpec(
            num_scalar_prefetch=1, grid=(), in_specs=[vmem] * (2 * len(mine) + 1), out_specs=[vmem] * 2
        ),
        out_shape=[jax.ShapeDtypeStruct((len(blocks), rows, ell), jnp.bfloat16)] * 2,
        compiler_params=pltpu.CompilerParams(vmem_limit_bytes=VMEM_LIMIT),
        cost_estimate=pl.CostEstimate(flops=flops, bytes_accessed=1024, transcendentals=0),
    )(where, *mine, *others, pltpu.with_memory_space_constraint(held, pltpu.VMEM))


def contract(modes, skies):
    block = jnp.concatenate([sky[...].reshape(sky.shape[0] * ROWS, sky.shape[2]) for sky in skies], axis=0)
    return jnp.dot(modes, block, preferred_element_type=jnp.float32)


def reduce_kernel(modes_ref, *refs):
    out = refs[-1]
    out[...] = contract(modes_ref[...], refs[:-1]).astype(out.dtype).reshape(out.shape)


def by_rows(count, ell, first=0):
    return pl.BlockSpec((count, ROWS, ell), lambda g: (0, g + first // ROWS, 0))


def fixed(shape):
    return pl.BlockSpec(shape, lambda g: (0,) * len(shape))


def sky_specs(skies, first):
    return [by_rows(sky.shape[0], sky.shape[2], low) for sky, low in zip(skies, first)]


def reduce(modes, skies, first, n_modes, dtype=jnp.bfloat16):
    _, rows, ell = skies[-1].shape
    return pl.pallas_call(
        reduce_kernel,
        grid=(rows // ROWS,),
        in_specs=[fixed(modes.shape)] + sky_specs(skies, first),
        out_specs=by_rows(n_modes, ell),
        out_shape=jax.ShapeDtypeStruct((n_modes, rows, ell), dtype),
        compiler_params=pltpu.CompilerParams(vmem_limit_bytes=VMEM_LIMIT),
        cost_estimate=pl.CostEstimate(flops=1024, bytes_accessed=1024, transcendentals=0),
    )(modes, *skies)


def restore_kernel(up_ref, ratio_ref, kept_ref, came_ref, *outs, spots):
    n_modes, _, ell = came_ref.shape
    freqs = up_ref.shape[0] // ROWS // PARTS
    total = kept_ref[...] + came_ref[...].astype(jnp.float32)
    weighted = (total * ratio_ref[...]).astype(jnp.bfloat16).reshape(n_modes * ROWS, ell)
    for (j, low, high), out in zip(spots, outs):
        modes = up_ref[(j * freqs + low) * ROWS:(j * freqs + high) * ROWS, :]
        value = jnp.dot(modes, weighted, preferred_element_type=jnp.float32)
        out[...] = value.astype(jnp.bfloat16).reshape(out.shape)


def restore(kept, came, ratios, up, spots):
    n_modes, rows, ell = came.shape
    return pl.pallas_call(
        functools.partial(restore_kernel, spots=spots),
        grid=(rows // ROWS,),
        in_specs=[fixed(up.shape), fixed(ratios.shape)] + [by_rows(n_modes, ell)] * 2,
        out_specs=[by_rows(high - low, ell) for _, low, high in spots],
        out_shape=[jax.ShapeDtypeStruct((high - low, rows, ell), jnp.bfloat16) for _, low, high in spots],
        compiler_params=pltpu.CompilerParams(vmem_limit_bytes=VMEM_LIMIT),
        cost_estimate=pl.CostEstimate(flops=1024, bytes_accessed=1024, transcendentals=0),
    )(up, ratios, kept, came)


def place_kernel(where, *refs, spots, first):
    count = len(spots)
    pieces, out, sems = refs[:count], refs[-2], refs[-1]
    rows = pieces[0].shape[1]
    copies = [
        pltpu.make_async_copy(pieces[n], out.at[low:high, where[PARTS + 2 + j], first:first + rows, :], sems.at[n])
        for n, (j, low, high) in enumerate(spots)
    ]
    for copy in copies:
        copy.start()
    for copy in copies:
        copy.wait()


def place(where, pieces, spots, first, shape, into=None):
    count = len(spots)
    extra = [] if into is None else [into]
    anywhere = pl.BlockSpec(memory_space=pl.ANY)
    return pl.pallas_call(
        functools.partial(place_kernel, spots=spots, first=first),
        grid_spec=pltpu.PrefetchScalarGridSpec(
            num_scalar_prefetch=1,
            grid=(),
            in_specs=[pl.BlockSpec(memory_space=pltpu.VMEM)] * count + [anywhere] * len(extra),
            out_specs=anywhere,
            scratch_shapes=[pltpu.SemaphoreType.DMA((count,))],
        ),
        out_shape=jax.ShapeDtypeStruct(shape, jnp.bfloat16),
        input_output_aliases={count + 1: 0} if extra else {},
        compiler_params=pltpu.CompilerParams(vmem_limit_bytes=VMEM_LIMIT),
        cost_estimate=pl.CostEstimate(flops=1024, bytes_accessed=1024, transcendentals=0),
    )(where, *pieces, *extra)


def anchor_kernel(*refs):
    del refs


def anchor(values, flops):
    anywhere = pl.BlockSpec(memory_space=pl.ANY)
    return pl.pallas_call(
        anchor_kernel,
        in_specs=[anywhere] * len(values),
        out_specs=[anywhere] * len(values),
        out_shape=[jax.ShapeDtypeStruct(value.shape, value.dtype) for value in values],
        input_output_aliases={n: n for n in range(len(values))},
        compiler_params=pltpu.CompilerParams(vmem_limit_bytes=1024 * 1024),
        cost_estimate=pl.CostEstimate(flops=flops, bytes_accessed=1024, transcendentals=0),
    )(*values)


def staged(visibility, beam_transfer, tile_mask, first_block, eigen_modes, signal_noise):
    freqs, parts, rows_all, base = visibility.shape
    _, freq_total, _, ell = beam_transfer.shape
    n_modes = eigen_modes.shape[2]
    ell_tiles = ell // TILE
    z, x, p = lax.axis_index("fm"), lax.axis_index("kl"), lax.axis_index("pol")
    other = [(0, 1), (1, 0)]

    def shift_z(value, j):
        return lax.ppermute(value, "fm", [(i, (i + j) % parts) for i in range(parts)])

    def swap_z(value, j):
        return lax.ppermute(value, "fm", [(i, i ^ j) for i in range(parts)])

    def along_x(value):
        return lax.ppermute(value, "kl", other)

    def cut(j, first, rows):
        return lax.dynamic_slice(visibility, (0, (z + j) % parts, first, 0), (freqs, 1, rows, base)).reshape(freqs, rows, base)

    index = jnp.arange(2 * parts + 2, dtype=jnp.int32)
    where = jnp.where(index < parts, (z - index) % parts, z ^ (index - parts - 2))
    where = jnp.where(index == parts, (x == p).astype(jnp.int32), where)
    where = jnp.where(index == parts + 1, x * ell_tiles, where).astype(jnp.int32)
    ratio = signal_noise[0] / (1.0 + signal_noise[0])
    ratios = jnp.broadcast_to(ratio[:, None, None], (n_modes, 1, ell))
    beam = beam_transfer.reshape(freq_total, base, ell)
    shape = (freqs, parts, rows_all, ell)

    fence = lax.optimization_barrier
    most, half = rows_all - ROWS, freqs // 2
    blocks = [[(0, f)] for f in range(freqs)]
    halves = [[(f // half, f % half)] for f in range(freqs)]
    a = {j: shift_z(cut(j, 0, ROWS), j) for j in (1, 3, 2)}
    mine = [cut(0, 0, rows_all)[n:n + half] for n in (0, half)]
    others = [along_x(part) for part in mine]
    b = {j: cut(j, ROWS, most) for j in (1, 2, 3)}
    held, down, up = hold(where, tile_mask[0], first_block, beam, eigen_modes[0])
    (a[1], a[3], a[2]), b, others, down, up = fence(((a[1], a[3], a[2]), b, others, down, up))
    b[1], b[3] = shift_z(b[1], 1), shift_z(b[3], 3)
    own = project(where, mine, others, held, 0, halves, 400_000_000)
    skies = [own] + [project(where, [a[j]], [along_x(a[j])], held, j, blocks, 400_000_000) for j in (1, 2, 3)]
    gone = reduce(down, [leave for _, leave in skies], (0, 0, 0, 0), n_modes)
    stay_a = [stay for stay, _ in skies]
    b[3], b[2], stay_a, gone = fence((b[3], b[2], stay_a, gone))
    x_3 = along_x(b[3])
    x_1, = anchor([along_x(b[1])], 2_500_000_000)
    b[2] = shift_z(b[2], 2)
    kept = reduce(down, stay_a, (0, 0, 0, 0), n_modes, jnp.float32)
    spots = [(j, 0, freqs) for j in (1, 2, 3, 0)]
    outs = restore(kept, lax.ppermute(gone, "pol", other), ratios, up, spots)
    near = project(where, [b[1]], [x_1], held, 1, blocks)
    x_3, b, outs, near = fence((x_3, b, outs, near))
    first = {j: swap_z(outs[j - 1], j) for j in (1, 2, 3)}
    first[0] = outs[3]
    x_2 = along_x(b[2])
    last = project(where, [b[3]], [x_3], held, 3, blocks)
    skies = [own, near, project(where, [b[2]], [x_2], held, 2, blocks), last]
    gone = reduce(down, [leave for _, leave in skies], (ROWS, 0, 0, 0), n_modes)
    stays = [stay for stay, _ in skies]
    here, stays, gone = fence((first[0], stays, gone))
    came = lax.ppermute(gone, "pol", other)
    kept = reduce(down, stays, (ROWS, 0, 0, 0), n_modes, jnp.float32)
    first[3], first[2], first[1], kept = fence((first[3], first[2], first[1], kept))
    first[3], first[2], first[1] = anchor([first[3], first[2], first[1]], 7_500_000_000)
    outs, first[3], first[2], first[1] = fence((restore(kept, came, ratios, up, spots), first[3], first[2], first[1]))
    first[0] = here
    back = [swap_z(outs[j - 1], j) for j in (1, 2, 3)]
    result = place(where, [first[j] for j in (1, 2, 3, 0)], spots, 0, shape)
    result = place(where, [outs[3], back[0]], [spots[3], spots[0]], ROWS, shape, into=result)
    return place(where, back[1:], spots[1:3], ROWS, shape, into=result)


def plain(visibility, beam_transfer, tile_mask, first_block, eigen_modes, signal_noise):
    owned_modes, freq_total, base_half, ell_local = beam_transfer.shape
    base_tiles, ell_tiles = base_half // TILE, ell_local // TILE
    block_ids = lax.axis_index("kl") * ell_tiles + jnp.arange(ell_tiles, dtype=jnp.int32)
    inside = (first_block[:, None] <= block_ids[None, :]).astype(jnp.int32)
    keep_tiles = tile_mask * inside[:, None, :]
    shaped = beam_transfer.reshape(owned_modes, freq_total, base_tiles, TILE, ell_tiles, TILE)
    masked_beam = shaped * keep_tiles.astype(jnp.bfloat16)[:, None, :, None, :, None]
    masked_beam = masked_beam.reshape(owned_modes, freq_total, base_half, ell_local)
    arrived = lax.all_to_all(visibility, "fm", split_axis=1, concat_axis=0, tiled=True)
    partial_value = jnp.einsum(
        "fmrb,mfbl->fmrl",
        lax.all_gather(arrived, "kl", axis=2, tiled=True),
        masked_beam,
        preferred_element_type=jnp.float32,
    )
    sky_sum = lax.psum_scatter(
        partial_value.astype(jnp.bfloat16), "pol", scatter_dimension=2, tiled=True
    ).astype(jnp.float32)
    modes_float = eigen_modes.astype(jnp.float32)
    coeffs = jnp.einsum("mfk,fmrl->mkrl", modes_float, sky_sum, precision=lax.Precision.HIGHEST)
    ratios = signal_noise / (1.0 + signal_noise)
    weighted = (coeffs * ratios[:, :, None, None]).astype(jnp.bfloat16)
    filtered = jnp.einsum(
        "mfk,mkrl->fmrl", eigen_modes, weighted, preferred_element_type=jnp.float32
    ).astype(jnp.bfloat16)
    return lax.all_to_all(filtered, "fm", split_axis=0, concat_axis=1, tiled=True)


def per_device(*args, sizes):
    visibility, beam_transfer = args[0], args[1]
    _, modes, rows, _ = visibility.shape
    fits = (
        sizes["kl"] == 2
        and sizes["pol"] == 2
        and modes == sizes["fm"] == PARTS
        and beam_transfer.shape[0] == 1
        and rows == 3 * ROWS
        and visibility.shape[0] % 2 == 0
    )
    if not fits:
        return plain(*args)
    return staged(*args)


def solution(mesh):
    placed = (
        P(("group", "fm"), None, "kl", "pol"),
        P(("group", "fm"), None, "pol", "kl"),
        P("fm", "pol", "kl"),
        P("fm"),
        P(("group", "fm"), None, None),
        P(("group", "fm"), None),
    )
    return jax.shard_map(
        functools.partial(per_device, sizes=dict(mesh.shape)),
        mesh=mesh,
        in_specs=placed,
        out_specs=P(("group", "fm"), None, "pol", "kl"),
        check_vma=False,
    )
```

```python
import functools
import jax
import jax.numpy as jnp
from jax import lax
from jax.experimental import pallas as pl
from jax.experimental.pallas import tpu as pltpu
from jax.sharding import PartitionSpec as P

TILE = 128
PARTS = 4
ROWS = 16
VMEM_LIMIT = 24 * 1024 * 1024


def hold_kernel(where, tiles, starts, beam, modes_ref, held, down_ref, up_ref, mask, sems):
    freq, base, ell = held.shape
    n_modes = modes_ref.shape[1]
    ell_tiles, base_tiles, freqs = ell // TILE, base // TILE, freq // PARTS
    copies = [pltpu.make_async_copy(beam.at[f], held.at[f], sems.at[f]) for f in range(freq)]
    for copy in copies:
        copy.start()
    for b in range(base_tiles):
        for l in range(ell_tiles):
            kept = jnp.where(starts[0] <= where[PARTS + 1] + l, tiles[b, l], 0).astype(jnp.float32)
            mask[b * TILE:(b + 1) * TILE, l * TILE:(l + 1) * TILE] = jnp.full(
                (TILE, TILE), kept, jnp.float32
            ).astype(jnp.bfloat16)
    modes = modes_ref[...]

    def pick(shape, axis, orders=0):
        big = lax.broadcasted_iota(jnp.int32, shape, axis) // ROWS
        small = lax.broadcasted_iota(jnp.int32, shape, 1 - axis)
        if freq in shape:
            piece, within = big // freqs, big % freqs
            big = within
            for j in range(PARTS):
                big = jnp.where(piece == j, where[orders + j] * freqs + within, big)
        return jnp.where(big == small, 1.0, 0.0).astype(jnp.bfloat16)

    def lane(shape):
        rows = lax.broadcasted_iota(jnp.int32, shape, 0) % ROWS
        columns = lax.broadcasted_iota(jnp.int32, shape, 1) % ROWS
        return rows == columns

    def dot(a, b, dims):
        return lax.dot_general(a, b, (dims, ((), ())), preferred_element_type=jnp.float32)

    tall = dot(pick((n_modes * ROWS, n_modes), 0), modes, ((1,), (1,))).astype(jnp.bfloat16)
    value = dot(tall, pick((freq, freq * ROWS), 1), ((1,), (0,)))
    down_ref[...] = jnp.where(lane(value.shape), value, 0.0).astype(jnp.bfloat16)
    tall = dot(pick((freq * ROWS, freq), 0, PARTS + 2), modes, ((1,), (0,))).astype(jnp.bfloat16)
    value = dot(tall, pick((n_modes, n_modes * ROWS), 1), ((1,), (0,)))
    up_ref[...] = jnp.where(lane(value.shape), value, 0.0).astype(jnp.bfloat16)
    for f, copy in enumerate(copies):
        copy.wait()
        held[f] = held[f] * mask[...]


def hold(where, tiles, starts, beam, modes):
    freq, base, ell = beam.shape
    size, wide = freq * ROWS, modes.shape[1] * ROWS
    vmem = pl.BlockSpec(memory_space=pltpu.VMEM)
    return pl.pallas_call(
        hold_kernel,
        grid_spec=pltpu.PrefetchScalarGridSpec(
            num_scalar_prefetch=3,
            grid=(),
            in_specs=[pl.BlockSpec(memory_space=pl.ANY), vmem],
            out_specs=[vmem] * 3,
            scratch_shapes=[pltpu.VMEM((base, ell), jnp.bfloat16), pltpu.SemaphoreType.DMA((freq,))],
        ),
        out_shape=[
            pltpu.VMEM(beam.shape, beam.dtype),
            jax.ShapeDtypeStruct((wide, size), jnp.bfloat16),
            jax.ShapeDtypeStruct((size, wide), jnp.bfloat16),
        ],
        compiler_params=pltpu.CompilerParams(vmem_limit_bytes=VMEM_LIMIT),
        cost_estimate=pl.CostEstimate(flops=1024, bytes_accessed=1024, transcendentals=0),
    )(where, tiles, starts, beam, modes)


def project_kernel(where, *refs, piece, blocks):
    count = (len(refs) - 3) // 2
    mine, others = refs[:count], refs[count:2 * count]
    held, stay_ref, leave_ref = refs[2 * count:]
    freqs, rows, _ = stay_ref.shape
    first = where[piece] * freqs
    own = where[PARTS] == 1
    for f in range(freqs):
        a = jnp.concatenate([mine[n][k] for n, k in blocks[f]], axis=0)
        b = jnp.concatenate([others[n][k] for n, k in blocks[f]], axis=0)
        lines = jnp.concatenate([jnp.where(own, a, b), jnp.where(own, b, a)], axis=0)
        value = jnp.dot(lines, held[first + f], preferred_element_type=jnp.float32).astype(jnp.bfloat16)
        stay_ref[f] = value[:rows]
        leave_ref[f] = value[rows:]


def project(where, mine, others, held, piece, blocks, flops=1024):
    ell = held.shape[2]
    rows = sum(mine[n].shape[1] for n, _ in blocks[0])
    vmem = pl.BlockSpec(memory_space=pltpu.VMEM)
    return pl.pallas_call(
        functools.partial(project_kernel, piece=piece, blocks=blocks),
        grid_spec=pltpu.PrefetchScalarGridSpec(
            num_scalar_prefetch=1, grid=(), in_specs=[vmem] * (2 * len(mine) + 1), out_specs=[vmem] * 2
        ),
        out_shape=[jax.ShapeDtypeStruct((len(blocks), rows, ell), jnp.bfloat16)] * 2,
        compiler_params=pltpu.CompilerParams(vmem_limit_bytes=VMEM_LIMIT),
        cost_estimate=pl.CostEstimate(flops=flops, bytes_accessed=1024, transcendentals=0),
    )(where, *mine, *others, pltpu.with_memory_space_constraint(held, pltpu.VMEM))


def contract(modes, skies):
    block = jnp.concatenate([sky[...].reshape(sky.shape[0] * ROWS, sky.shape[2]) for sky in skies], axis=0)
    return jnp.dot(modes, block, preferred_element_type=jnp.float32)


def reduce_kernel(modes_ref, *refs):
    out = refs[-1]
    out[...] = contract(modes_ref[...], refs[:-1]).astype(out.dtype).reshape(out.shape)


def by_rows(count, ell, first=0):
    return pl.BlockSpec((count, ROWS, ell), lambda g: (0, g + first // ROWS, 0))


def fixed(shape):
    return pl.BlockSpec(shape, lambda g: (0,) * len(shape))


def sky_specs(skies, first):
    return [by_rows(sky.shape[0], sky.shape[2], low) for sky, low in zip(skies, first)]


def reduce(modes, skies, first, n_modes, dtype=jnp.bfloat16):
    _, rows, ell = skies[-1].shape
    return pl.pallas_call(
        reduce_kernel,
        grid=(rows // ROWS,),
        in_specs=[fixed(modes.shape)] + sky_specs(skies, first),
        out_specs=by_rows(n_modes, ell),
        out_shape=jax.ShapeDtypeStruct((n_modes, rows, ell), dtype),
        compiler_params=pltpu.CompilerParams(vmem_limit_bytes=VMEM_LIMIT),
        cost_estimate=pl.CostEstimate(flops=1024, bytes_accessed=1024, transcendentals=0),
    )(modes, *skies)


def restore_kernel(up_ref, ratio_ref, kept_ref, came_ref, *outs, spots):
    n_modes, _, ell = came_ref.shape
    freqs = up_ref.shape[0] // ROWS // PARTS
    total = kept_ref[...] + came_ref[...].astype(jnp.float32)
    weighted = (total * ratio_ref[...]).astype(jnp.bfloat16).reshape(n_modes * ROWS, ell)
    for (j, low, high), out in zip(spots, outs):
        modes = up_ref[(j * freqs + low) * ROWS:(j * freqs + high) * ROWS, :]
        value = jnp.dot(modes, weighted, preferred_element_type=jnp.float32)
        out[...] = value.astype(jnp.bfloat16).reshape(out.shape)


def restore(kept, came, ratios, up, spots):
    n_modes, rows, ell = came.shape
    return pl.pallas_call(
        functools.partial(restore_kernel, spots=spots),
        grid=(rows // ROWS,),
        in_specs=[fixed(up.shape), fixed(ratios.shape)] + [by_rows(n_modes, ell)] * 2,
        out_specs=[by_rows(high - low, ell) for _, low, high in spots],
        out_shape=[jax.ShapeDtypeStruct((high - low, rows, ell), jnp.bfloat16) for _, low, high in spots],
        compiler_params=pltpu.CompilerParams(vmem_limit_bytes=VMEM_LIMIT),
        cost_estimate=pl.CostEstimate(flops=1024, bytes_accessed=1024, transcendentals=0),
    )(up, ratios, kept, came)


def place_kernel(where, *refs, spots, first):
    count = len(spots)
    pieces, out, sems = refs[:count], refs[-2], refs[-1]
    rows = pieces[0].shape[1]
    copies = [
        pltpu.make_async_copy(pieces[n], out.at[low:high, where[PARTS + 2 + j], first:first + rows, :], sems.at[n])
        for n, (j, low, high) in enumerate(spots)
    ]
    for copy in copies:
        copy.start()
    for copy in copies:
        copy.wait()


def place(where, pieces, spots, first, shape, into=None):
    count = len(spots)
    extra = [] if into is None else [into]
    anywhere = pl.BlockSpec(memory_space=pl.ANY)
    return pl.pallas_call(
        functools.partial(place_kernel, spots=spots, first=first),
        grid_spec=pltpu.PrefetchScalarGridSpec(
            num_scalar_prefetch=1,
            grid=(),
            in_specs=[pl.BlockSpec(memory_space=pltpu.VMEM)] * count + [anywhere] * len(extra),
            out_specs=anywhere,
            scratch_shapes=[pltpu.SemaphoreType.DMA((count,))],
        ),
        out_shape=jax.ShapeDtypeStruct(shape, jnp.bfloat16),
        input_output_aliases={count + 1: 0} if extra else {},
        compiler_params=pltpu.CompilerParams(vmem_limit_bytes=VMEM_LIMIT),
        cost_estimate=pl.CostEstimate(flops=1024, bytes_accessed=1024, transcendentals=0),
    )(where, *pieces, *extra)


def anchor_kernel(*refs):
    del refs


def anchor(values, flops):
    anywhere = pl.BlockSpec(memory_space=pl.ANY)
    return pl.pallas_call(
        anchor_kernel,
        in_specs=[anywhere] * len(values),
        out_specs=[anywhere] * len(values),
        out_shape=[jax.ShapeDtypeStruct(value.shape, value.dtype) for value in values],
        input_output_aliases={n: n for n in range(len(values))},
        compiler_params=pltpu.CompilerParams(vmem_limit_bytes=1024 * 1024),
        cost_estimate=pl.CostEstimate(flops=flops, bytes_accessed=1024, transcendentals=0),
    )(*values)


def staged(visibility, beam_transfer, tile_mask, first_block, eigen_modes, signal_noise):
    freqs, parts, rows_all, base = visibility.shape
    _, freq_total, _, ell = beam_transfer.shape
    n_modes = eigen_modes.shape[2]
    ell_tiles = ell // TILE
    z, x, p = lax.axis_index("fm"), lax.axis_index("kl"), lax.axis_index("pol")
    other = [(0, 1), (1, 0)]

    def shift_z(value, j):
        return lax.ppermute(value, "fm", [(i, (i + j) % parts) for i in range(parts)])

    def swap_z(value, j):
        return lax.ppermute(value, "fm", [(i, i ^ j) for i in range(parts)])

    def along_x(value):
        return lax.ppermute(value, "kl", other)

    def cut(j, first, rows):
        return lax.dynamic_slice(visibility, (0, (z + j) % parts, first, 0), (freqs, 1, rows, base)).reshape(freqs, rows, base)

    index = jnp.arange(2 * parts + 2, dtype=jnp.int32)
    where = jnp.where(index < parts, (z - index) % parts, z ^ (index - parts - 2))
    where = jnp.where(index == parts, (x == p).astype(jnp.int32), where)
    where = jnp.where(index == parts + 1, x * ell_tiles, where).astype(jnp.int32)
    ratio = signal_noise[0] / (1.0 + signal_noise[0])
    ratios = jnp.broadcast_to(ratio[:, None, None], (n_modes, 1, ell))
    beam = beam_transfer.reshape(freq_total, base, ell)
    shape = (freqs, parts, rows_all, ell)

    fence = lax.optimization_barrier
    most, half = rows_all - ROWS, freqs // 2
    blocks = [[(0, f)] for f in range(freqs)]
    halves = [[(f // half, f % half)] for f in range(freqs)]
    a = {j: shift_z(cut(j, 0, ROWS), j) for j in (1, 3, 2)}
    mine = [cut(0, 0, rows_all)[n:n + half] for n in (0, half)]
    others = [along_x(part) for part in mine]
    b = {j: cut(j, ROWS, most) for j in (1, 2, 3)}
    held, down, up = hold(where, tile_mask[0], first_block, beam, eigen_modes[0])
    (a[1], a[3], a[2]), b, others, down, up = fence(((a[1], a[3], a[2]), b, others, down, up))
    b[1], b[3] = shift_z(b[1], 1), shift_z(b[3], 3)
    own = project(where, mine, others, held, 0, halves, 400_000_000)
    skies = [own] + [project(where, [a[j]], [along_x(a[j])], held, j, blocks, 400_000_000) for j in (1, 2, 3)]
    gone = reduce(down, [leave for _, leave in skies], (0, 0, 0, 0), n_modes)
    stay_a = [stay for stay, _ in skies]
    b[3], b[2], stay_a, gone = fence((b[3], b[2], stay_a, gone))
    x_3 = along_x(b[3])
    x_1, = anchor([along_x(b[1])], 2_500_000_000)
    b[2], = anchor([shift_z(b[2], 2)], 2_000_000_000)
    kept = reduce(down, stay_a, (0, 0, 0, 0), n_modes, jnp.float32)
    spots = [(j, 0, freqs) for j in (1, 2, 3, 0)]
    outs = restore(kept, lax.ppermute(gone, "pol", other), ratios, up, spots)
    near = project(where, [b[1]], [x_1], held, 1, blocks)
    x_3, b, outs, near = fence((x_3, b, outs, near))
    first = {j: swap_z(outs[j - 1], j) for j in (1, 2, 3)}
    first[0] = outs[3]
    x_2 = along_x(b[2])
    last = project(where, [b[3]], [x_3], held, 3, blocks)
    skies = [own, near, project(where, [b[2]], [x_2], held, 2, blocks), last]
    gone = reduce(down, [leave for _, leave in skies], (ROWS, 0, 0, 0), n_modes)
    stays = [stay for stay, _ in skies]
    here, stays, gone = fence((first[0], stays, gone))
    came = lax.ppermute(gone, "pol", other)
    kept = reduce(down, stays, (ROWS, 0, 0, 0), n_modes, jnp.float32)
    first[3], first[2], first[1], kept = fence((first[3], first[2], first[1], kept))
    first[3], first[2], first[1] = anchor([first[3], first[2], first[1]], 7_500_000_000)
    outs, first[3], first[2], first[1] = fence((restore(kept, came, ratios, up, spots), first[3], first[2], first[1]))
    first[0] = here
    back = [swap_z(outs[j - 1], j) for j in (1, 2, 3)]
    result = place(where, [first[j] for j in (1, 2, 3, 0)], spots, 0, shape)
    result = place(where, [outs[3], back[0]], [spots[3], spots[0]], ROWS, shape, into=result)
    return place(where, back[1:], spots[1:3], ROWS, shape, into=result)


def plain(visibility, beam_transfer, tile_mask, first_block, eigen_modes, signal_noise):
    owned_modes, freq_total, base_half, ell_local = beam_transfer.shape
    base_tiles, ell_tiles = base_half // TILE, ell_local // TILE
    block_ids = lax.axis_index("kl") * ell_tiles + jnp.arange(ell_tiles, dtype=jnp.int32)
    inside = (first_block[:, None] <= block_ids[None, :]).astype(jnp.int32)
    keep_tiles = tile_mask * inside[:, None, :]
    shaped = beam_transfer.reshape(owned_modes, freq_total, base_tiles, TILE, ell_tiles, TILE)
    masked_beam = shaped * keep_tiles.astype(jnp.bfloat16)[:, None, :, None, :, None]
    masked_beam = masked_beam.reshape(owned_modes, freq_total, base_half, ell_local)
    arrived = lax.all_to_all(visibility, "fm", split_axis=1, concat_axis=0, tiled=True)
    partial_value = jnp.einsum(
        "fmrb,mfbl->fmrl",
        lax.all_gather(arrived, "kl", axis=2, tiled=True),
        masked_beam,
        preferred_element_type=jnp.float32,
    )
    sky_sum = lax.psum_scatter(
        partial_value.astype(jnp.bfloat16), "pol", scatter_dimension=2, tiled=True
    ).astype(jnp.float32)
    modes_float = eigen_modes.astype(jnp.float32)
    coeffs = jnp.einsum("mfk,fmrl->mkrl", modes_float, sky_sum, precision=lax.Precision.HIGHEST)
    ratios = signal_noise / (1.0 + signal_noise)
    weighted = (coeffs * ratios[:, :, None, None]).astype(jnp.bfloat16)
    filtered = jnp.einsum(
        "mfk,mkrl->fmrl", eigen_modes, weighted, preferred_element_type=jnp.float32
    ).astype(jnp.bfloat16)
    return lax.all_to_all(filtered, "fm", split_axis=0, concat_axis=1, tiled=True)


def per_device(*args, sizes):
    visibility, beam_transfer = args[0], args[1]
    _, modes, rows, _ = visibility.shape
    fits = (
        sizes["kl"] == 2
        and sizes["pol"] == 2
        and modes == sizes["fm"] == PARTS
        and beam_transfer.shape[0] == 1
        and rows == 3 * ROWS
        and visibility.shape[0] % 2 == 0
    )
    if not fits:
        return plain(*args)
    return staged(*args)


def solution(mesh):
    placed = (
        P(("group", "fm"), None, "kl", "pol"),
        P(("group", "fm"), None, "pol", "kl"),
        P("fm", "pol", "kl"),
        P("fm"),
        P(("group", "fm"), None, None),
        P(("group", "fm"), None),
    )
    return jax.shard_map(
        functools.partial(per_device, sizes=dict(mesh.shape)),
        mesh=mesh,
        in_specs=placed,
        out_specs=P(("group", "fm"), None, "pol", "kl"),
        check_vma=False,
    )
```

```python
import functools
import jax
import jax.numpy as jnp
from jax import lax
from jax.experimental import pallas as pl
from jax.experimental.pallas import tpu as pltpu
from jax.sharding import PartitionSpec as P

TILE = 128
PARTS = 4
ROWS = 16
VMEM_LIMIT = 24 * 1024 * 1024


def hold_kernel(where, tiles, starts, beam, modes_ref, held, down_ref, up_ref, mask, sems):
    freq, base, ell = held.shape
    n_modes = modes_ref.shape[1]
    ell_tiles, base_tiles, freqs = ell // TILE, base // TILE, freq // PARTS
    copies = [pltpu.make_async_copy(beam.at[f], held.at[f], sems.at[f]) for f in range(freq)]
    for copy in copies:
        copy.start()
    for b in range(base_tiles):
        for l in range(ell_tiles):
            kept = jnp.where(starts[0] <= where[PARTS + 1] + l, tiles[b, l], 0).astype(jnp.float32)
            mask[b * TILE:(b + 1) * TILE, l * TILE:(l + 1) * TILE] = jnp.full(
                (TILE, TILE), kept, jnp.float32
            ).astype(jnp.bfloat16)
    modes = modes_ref[...]

    def pick(shape, axis, orders=0):
        big = lax.broadcasted_iota(jnp.int32, shape, axis) // ROWS
        small = lax.broadcasted_iota(jnp.int32, shape, 1 - axis)
        if freq in shape:
            piece, within = big // freqs, big % freqs
            big = within
            for j in range(PARTS):
                big = jnp.where(piece == j, where[orders + j] * freqs + within, big)
        return jnp.where(big == small, 1.0, 0.0).astype(jnp.bfloat16)

    def lane(shape):
        rows = lax.broadcasted_iota(jnp.int32, shape, 0) % ROWS
        columns = lax.broadcasted_iota(jnp.int32, shape, 1) % ROWS
        return rows == columns

    def dot(a, b, dims):
        return lax.dot_general(a, b, (dims, ((), ())), preferred_element_type=jnp.float32)

    tall = dot(pick((n_modes * ROWS, n_modes), 0), modes, ((1,), (1,))).astype(jnp.bfloat16)
    value = dot(tall, pick((freq, freq * ROWS), 1), ((1,), (0,)))
    down_ref[...] = jnp.where(lane(value.shape), value, 0.0).astype(jnp.bfloat16)
    tall = dot(pick((freq * ROWS, freq), 0, PARTS + 2), modes, ((1,), (0,))).astype(jnp.bfloat16)
    value = dot(tall, pick((n_modes, n_modes * ROWS), 1), ((1,), (0,)))
    up_ref[...] = jnp.where(lane(value.shape), value, 0.0).astype(jnp.bfloat16)
    for f, copy in enumerate(copies):
        copy.wait()
        held[f] = held[f] * mask[...]


def hold(where, tiles, starts, beam, modes):
    freq, base, ell = beam.shape
    size, wide = freq * ROWS, modes.shape[1] * ROWS
    vmem = pl.BlockSpec(memory_space=pltpu.VMEM)
    return pl.pallas_call(
        hold_kernel,
        grid_spec=pltpu.PrefetchScalarGridSpec(
            num_scalar_prefetch=3,
            grid=(),
            in_specs=[pl.BlockSpec(memory_space=pl.ANY), vmem],
            out_specs=[vmem] * 3,
            scratch_shapes=[pltpu.VMEM((base, ell), jnp.bfloat16), pltpu.SemaphoreType.DMA((freq,))],
        ),
        out_shape=[
            pltpu.VMEM(beam.shape, beam.dtype),
            jax.ShapeDtypeStruct((wide, size), jnp.bfloat16),
            jax.ShapeDtypeStruct((size, wide), jnp.bfloat16),
        ],
        compiler_params=pltpu.CompilerParams(vmem_limit_bytes=VMEM_LIMIT),
        cost_estimate=pl.CostEstimate(flops=1024, bytes_accessed=1024, transcendentals=0),
    )(where, tiles, starts, beam, modes)


def project_kernel(where, *refs, piece, blocks):
    count = (len(refs) - 3) // 2
    mine, others = refs[:count], refs[count:2 * count]
    held, stay_ref, leave_ref = refs[2 * count:]
    freqs, rows, _ = stay_ref.shape
    first = where[piece] * freqs
    own = where[PARTS] == 1
    for f in range(freqs):
        a = jnp.concatenate([mine[n][k] for n, k in blocks[f]], axis=0)
        b = jnp.concatenate([others[n][k] for n, k in blocks[f]], axis=0)
        lines = jnp.concatenate([jnp.where(own, a, b), jnp.where(own, b, a)], axis=0)
        value = jnp.dot(lines, held[first + f], preferred_element_type=jnp.float32).astype(jnp.bfloat16)
        stay_ref[f] = value[:rows]
        leave_ref[f] = value[rows:]


def project(where, mine, others, held, piece, blocks, flops=1024):
    ell = held.shape[2]
    rows = sum(mine[n].shape[1] for n, _ in blocks[0])
    vmem = pl.BlockSpec(memory_space=pltpu.VMEM)
    return pl.pallas_call(
        functools.partial(project_kernel, piece=piece, blocks=blocks),
        grid_spec=pltpu.PrefetchScalarGridSpec(
            num_scalar_prefetch=1, grid=(), in_specs=[vmem] * (2 * len(mine) + 1), out_specs=[vmem] * 2
        ),
        out_shape=[jax.ShapeDtypeStruct((len(blocks), rows, ell), jnp.bfloat16)] * 2,
        compiler_params=pltpu.CompilerParams(vmem_limit_bytes=VMEM_LIMIT),
        cost_estimate=pl.CostEstimate(flops=flops, bytes_accessed=1024, transcendentals=0),
    )(where, *mine, *others, pltpu.with_memory_space_constraint(held, pltpu.VMEM))


def contract(modes, skies):
    block = jnp.concatenate([sky[...].reshape(sky.shape[0] * ROWS, sky.shape[2]) for sky in skies], axis=0)
    return jnp.dot(modes, block, preferred_element_type=jnp.float32)


def reduce_kernel(modes_ref, *refs):
    out = refs[-1]
    out[...] = contract(modes_ref[...], refs[:-1]).astype(out.dtype).reshape(out.shape)


def by_rows(count, ell, first=0):
    return pl.BlockSpec((count, ROWS, ell), lambda g, *_: (0, g + first // ROWS, 0))


def fixed(shape):
    return pl.BlockSpec(shape, lambda g, *_: (0,) * len(shape))


def sky_specs(skies, first):
    return [by_rows(sky.shape[0], sky.shape[2], low) for sky, low in zip(skies, first)]


def reduce(modes, skies, first, n_modes, dtype=jnp.bfloat16):
    _, rows, ell = skies[-1].shape
    return pl.pallas_call(
        reduce_kernel,
        grid=(rows // ROWS,),
        in_specs=[fixed(modes.shape)] + sky_specs(skies, first),
        out_specs=by_rows(n_modes, ell),
        out_shape=jax.ShapeDtypeStruct((n_modes, rows, ell), dtype),
        compiler_params=pltpu.CompilerParams(vmem_limit_bytes=VMEM_LIMIT),
        cost_estimate=pl.CostEstimate(flops=1024, bytes_accessed=1024, transcendentals=0),
    )(modes, *skies)


def restore_kernel(where, up_ref, ratio_ref, kept_ref, came_ref, *outs, spots, shifted):
    n_modes, _, ell = came_ref.shape
    freqs = up_ref.shape[0] // ROWS // PARTS
    total = kept_ref[...] + came_ref[...].astype(jnp.float32)
    weighted = (total * ratio_ref[...]).astype(jnp.bfloat16).reshape(n_modes * ROWS, ell)
    size = freqs * ROWS
    for j, out in zip(spots, outs):
        piece = where[2 * PARTS + 2 + j] if shifted else j
        modes = up_ref[pl.ds(pl.multiple_of(piece * size, size), size), :]
        value = jnp.dot(modes, weighted, preferred_element_type=jnp.float32)
        out[...] = value.astype(jnp.bfloat16).reshape(out.shape)


def restore(where, kept, came, ratios, up, spots, shifted):
    n_modes, rows, ell = came.shape
    freqs = up.shape[0] // ROWS // PARTS
    return pl.pallas_call(
        functools.partial(restore_kernel, spots=spots, shifted=shifted),
        grid_spec=pltpu.PrefetchScalarGridSpec(
            num_scalar_prefetch=1,
            grid=(rows // ROWS,),
            in_specs=[fixed(up.shape), fixed(ratios.shape)] + [by_rows(n_modes, ell)] * 2,
            out_specs=[by_rows(freqs, ell)] * len(spots),
        ),
        out_shape=[jax.ShapeDtypeStruct((freqs, rows, ell), jnp.bfloat16)] * len(spots),
        compiler_params=pltpu.CompilerParams(vmem_limit_bytes=VMEM_LIMIT),
        cost_estimate=pl.CostEstimate(flops=1024, bytes_accessed=1024, transcendentals=0),
    )(where, up, ratios, kept, came)


def place_kernel(where, *refs, spots, first, shifted):
    count = len(spots)
    pieces, out, sems = refs[:count], refs[-2], refs[-1]
    rows = pieces[0].shape[1]
    copies = [
        pltpu.make_async_copy(pieces[n], out.at[:, where[j if shifted else PARTS + 2 + j], first:first + rows, :], sems.at[n])
        for n, j in enumerate(spots)
    ]
    for copy in copies:
        copy.start()
    for copy in copies:
        copy.wait()


def place(where, pieces, spots, first, shape, shifted, into=None):
    count = len(spots)
    extra = [] if into is None else [into]
    anywhere = pl.BlockSpec(memory_space=pl.ANY)
    return pl.pallas_call(
        functools.partial(place_kernel, spots=spots, first=first, shifted=shifted),
        grid_spec=pltpu.PrefetchScalarGridSpec(
            num_scalar_prefetch=1,
            grid=(),
            in_specs=[pl.BlockSpec(memory_space=pltpu.VMEM)] * count + [anywhere] * len(extra),
            out_specs=anywhere,
            scratch_shapes=[pltpu.SemaphoreType.DMA((count,))],
        ),
        out_shape=jax.ShapeDtypeStruct(shape, jnp.bfloat16),
        input_output_aliases={count + 1: 0} if extra else {},
        compiler_params=pltpu.CompilerParams(vmem_limit_bytes=VMEM_LIMIT),
        cost_estimate=pl.CostEstimate(flops=1024, bytes_accessed=1024, transcendentals=0),
    )(where, *pieces, *extra)


def anchor_kernel(*refs):
    del refs


def anchor(values, flops):
    anywhere = pl.BlockSpec(memory_space=pl.ANY)
    return pl.pallas_call(
        anchor_kernel,
        in_specs=[anywhere] * len(values),
        out_specs=[anywhere] * len(values),
        out_shape=[jax.ShapeDtypeStruct(value.shape, value.dtype) for value in values],
        input_output_aliases={n: n for n in range(len(values))},
        compiler_params=pltpu.CompilerParams(vmem_limit_bytes=1024 * 1024),
        cost_estimate=pl.CostEstimate(flops=flops, bytes_accessed=1024, transcendentals=0),
    )(*values)


def staged(visibility, beam_transfer, tile_mask, first_block, eigen_modes, signal_noise):
    freqs, parts, rows_all, base = visibility.shape
    _, freq_total, _, ell = beam_transfer.shape
    n_modes = eigen_modes.shape[2]
    ell_tiles = ell // TILE
    z, x, p = lax.axis_index("fm"), lax.axis_index("kl"), lax.axis_index("pol")
    other = [(0, 1), (1, 0)]

    def shift_z(value, j):
        return lax.ppermute(value, "fm", [(i, (i + j) % parts) for i in range(parts)])

    def swap_z(value, j):
        return lax.ppermute(value, "fm", [(i, i ^ j) for i in range(parts)])

    def along_x(value):
        return lax.ppermute(value, "kl", other)

    def cut(j, first, rows):
        return lax.dynamic_slice(visibility, (0, (z + j) % parts, first, 0), (freqs, 1, rows, base)).reshape(freqs, rows, base)

    index = jnp.arange(3 * parts + 2, dtype=jnp.int32)
    where = jnp.where(index < parts, (z - index) % parts, z ^ (index - parts - 2))
    where = jnp.where(index < 2 * parts + 2, where, z ^ ((z + index - 2 * parts - 2) % parts))
    where = jnp.where(index == parts, (x == p).astype(jnp.int32), where)
    where = jnp.where(index == parts + 1, x * ell_tiles, where).astype(jnp.int32)
    ratio = signal_noise[0] / (1.0 + signal_noise[0])
    ratios = jnp.broadcast_to(ratio[:, None, None], (n_modes, 1, ell))
    beam = beam_transfer.reshape(freq_total, base, ell)
    shape = (freqs, parts, rows_all, ell)

    fence = lax.optimization_barrier
    most, half = rows_all - ROWS, freqs // 2
    blocks = [[(0, f)] for f in range(freqs)]
    halves = [[(f // half, f % half)] for f in range(freqs)]
    a = {j: shift_z(cut(j, 0, ROWS), j) for j in (1, 3, 2)}
    mine = [cut(0, 0, rows_all)[n:n + half] for n in (0, half)]
    others = [along_x(part) for part in mine]
    b = {j: cut(j, ROWS, most) for j in (1, 2, 3)}
    held, down, up = hold(where, tile_mask[0], first_block, beam, eigen_modes[0])
    (a[1], a[3], a[2]), b, others, down, up = fence(((a[1], a[3], a[2]), b, others, down, up))
    b[1], b[3] = shift_z(b[1], 1), shift_z(b[3], 3)
    own = project(where, mine, others, held, 0, halves, 400_000_000)
    skies = [own] + [project(where, [a[j]], [along_x(a[j])], held, j, blocks, 400_000_000) for j in (1, 2, 3)]
    gone = reduce(down, [leave for _, leave in skies], (0, 0, 0, 0), n_modes)
    stay_a = [stay for stay, _ in skies]
    b[3], b[2], stay_a, gone = fence((b[3], b[2], stay_a, gone))
    x_3 = along_x(b[3])
    x_1, = anchor([along_x(b[1])], 2_500_000_000)
    b[2] = shift_z(b[2], 2)
    kept = reduce(down, stay_a, (0, 0, 0, 0), n_modes, jnp.float32)
    spots = [1, 2, 3, 0]
    outs = restore(where, kept, lax.ppermute(gone, "pol", other), ratios, up, spots, False)
    near = project(where, [b[1]], [x_1], held, 1, blocks)
    x_3, b, outs, near = fence((x_3, b, outs, near))
    first = {j: swap_z(outs[j - 1], j) for j in (1, 2, 3)}
    first[0] = outs[3]
    x_2 = along_x(b[2])
    last = project(where, [b[3]], [x_3], held, 3, blocks)
    skies = [own, near, project(where, [b[2]], [x_2], held, 2, blocks), last]
    gone = reduce(down, [leave for _, leave in skies], (ROWS, 0, 0, 0), n_modes)
    stays = [stay for stay, _ in skies]
    here, stays, gone = fence((first[0], stays, gone))
    came = lax.ppermute(gone, "pol", other)
    kept = reduce(down, stays, (ROWS, 0, 0, 0), n_modes, jnp.float32)
    first[3], first[2], first[1], kept = fence((first[3], first[2], first[1], kept))
    first[3], first[2], first[1] = anchor([first[3], first[2], first[1]], 7_500_000_000)
    outs, first[3], first[2], first[1] = fence((restore(where, kept, came, ratios, up, spots, True), first[3], first[2], first[1]))
    first[0] = here
    back = [shift_z(outs[j - 1], j) for j in (1, 2, 3)]
    result = place(where, [first[j] for j in spots], spots, 0, shape, False)
    result = place(where, [outs[3], back[0]], [0, 1], ROWS, shape, True, into=result)
    return place(where, back[1:], [2, 3], ROWS, shape, True, into=result)


def plain(visibility, beam_transfer, tile_mask, first_block, eigen_modes, signal_noise):
    owned_modes, freq_total, base_half, ell_local = beam_transfer.shape
    base_tiles, ell_tiles = base_half // TILE, ell_local // TILE
    block_ids = lax.axis_index("kl") * ell_tiles + jnp.arange(ell_tiles, dtype=jnp.int32)
    inside = (first_block[:, None] <= block_ids[None, :]).astype(jnp.int32)
    keep_tiles = tile_mask * inside[:, None, :]
    shaped = beam_transfer.reshape(owned_modes, freq_total, base_tiles, TILE, ell_tiles, TILE)
    masked_beam = shaped * keep_tiles.astype(jnp.bfloat16)[:, None, :, None, :, None]
    masked_beam = masked_beam.reshape(owned_modes, freq_total, base_half, ell_local)
    arrived = lax.all_to_all(visibility, "fm", split_axis=1, concat_axis=0, tiled=True)
    partial_value = jnp.einsum(
        "fmrb,mfbl->fmrl",
        lax.all_gather(arrived, "kl", axis=2, tiled=True),
        masked_beam,
        preferred_element_type=jnp.float32,
    )
    sky_sum = lax.psum_scatter(
        partial_value.astype(jnp.bfloat16), "pol", scatter_dimension=2, tiled=True
    ).astype(jnp.float32)
    modes_float = eigen_modes.astype(jnp.float32)
    coeffs = jnp.einsum("mfk,fmrl->mkrl", modes_float, sky_sum, precision=lax.Precision.HIGHEST)
    ratios = signal_noise / (1.0 + signal_noise)
    weighted = (coeffs * ratios[:, :, None, None]).astype(jnp.bfloat16)
    filtered = jnp.einsum(
        "mfk,mkrl->fmrl", eigen_modes, weighted, preferred_element_type=jnp.float32
    ).astype(jnp.bfloat16)
    return lax.all_to_all(filtered, "fm", split_axis=0, concat_axis=1, tiled=True)


def per_device(*args, sizes):
    visibility, beam_transfer = args[0], args[1]
    _, modes, rows, _ = visibility.shape
    fits = (
        sizes["kl"] == 2
        and sizes["pol"] == 2
        and modes == sizes["fm"] == PARTS
        and beam_transfer.shape[0] == 1
        and rows == 3 * ROWS
        and visibility.shape[0] % 2 == 0
    )
    if not fits:
        return plain(*args)
    return staged(*args)


def solution(mesh):
    placed = (
        P(("group", "fm"), None, "kl", "pol"),
        P(("group", "fm"), None, "pol", "kl"),
        P("fm", "pol", "kl"),
        P("fm"),
        P(("group", "fm"), None, None),
        P(("group", "fm"), None),
    )
    return jax.shard_map(
        functools.partial(per_device, sizes=dict(mesh.shape)),
        mesh=mesh,
        in_specs=placed,
        out_specs=P(("group", "fm"), None, "pol", "kl"),
        check_vma=False,
    )
```

```python
import functools
import jax
import jax.numpy as jnp
from jax import lax
from jax.experimental import pallas as pl
from jax.experimental.pallas import tpu as pltpu
from jax.sharding import PartitionSpec as P

TILE = 128
PARTS = 4
ROWS = 16
VMEM_LIMIT = 24 * 1024 * 1024


def hold_kernel(where, tiles, starts, beam, modes_ref, held, down_ref, up_ref, mask, sems):
    freq, base, ell = held.shape
    n_modes = modes_ref.shape[1]
    ell_tiles, base_tiles, freqs = ell // TILE, base // TILE, freq // PARTS
    copies = [pltpu.make_async_copy(beam.at[f], held.at[f], sems.at[f]) for f in range(freq)]
    for copy in copies:
        copy.start()
    for b in range(base_tiles):
        for l in range(ell_tiles):
            kept = jnp.where(starts[0] <= where[PARTS + 1] + l, tiles[b, l], 0).astype(jnp.float32)
            mask[b * TILE:(b + 1) * TILE, l * TILE:(l + 1) * TILE] = jnp.full(
                (TILE, TILE), kept, jnp.float32
            ).astype(jnp.bfloat16)
    modes = modes_ref[...]

    def pick(shape, axis, orders=0):
        big = lax.broadcasted_iota(jnp.int32, shape, axis) // ROWS
        small = lax.broadcasted_iota(jnp.int32, shape, 1 - axis)
        if freq in shape:
            piece, within = big // freqs, big % freqs
            big = within
            for j in range(PARTS):
                big = jnp.where(piece == j, where[orders + j] * freqs + within, big)
        return jnp.where(big == small, 1.0, 0.0).astype(jnp.bfloat16)

    def lane(shape):
        rows = lax.broadcasted_iota(jnp.int32, shape, 0) % ROWS
        columns = lax.broadcasted_iota(jnp.int32, shape, 1) % ROWS
        return rows == columns

    def dot(a, b, dims):
        return lax.dot_general(a, b, (dims, ((), ())), preferred_element_type=jnp.float32)

    tall = dot(pick((n_modes * ROWS, n_modes), 0), modes, ((1,), (1,))).astype(jnp.bfloat16)
    value = dot(tall, pick((freq, freq * ROWS), 1), ((1,), (0,)))
    down_ref[...] = jnp.where(lane(value.shape), value, 0.0).astype(jnp.bfloat16)
    tall = dot(pick((freq * ROWS, freq), 0, PARTS + 2), modes, ((1,), (0,))).astype(jnp.bfloat16)
    value = dot(tall, pick((n_modes, n_modes * ROWS), 1), ((1,), (0,)))
    up_ref[...] = jnp.where(lane(value.shape), value, 0.0).astype(jnp.bfloat16)
    for f, copy in enumerate(copies):
        copy.wait()
        held[f] = held[f] * mask[...]


def hold(where, tiles, starts, beam, modes):
    freq, base, ell = beam.shape
    size, wide = freq * ROWS, modes.shape[1] * ROWS
    vmem = pl.BlockSpec(memory_space=pltpu.VMEM)
    return pl.pallas_call(
        hold_kernel,
        grid_spec=pltpu.PrefetchScalarGridSpec(
            num_scalar_prefetch=3,
            grid=(),
            in_specs=[pl.BlockSpec(memory_space=pl.ANY), vmem],
            out_specs=[vmem] * 3,
            scratch_shapes=[pltpu.VMEM((base, ell), jnp.bfloat16), pltpu.SemaphoreType.DMA((freq,))],
        ),
        out_shape=[
            pltpu.VMEM(beam.shape, beam.dtype),
            jax.ShapeDtypeStruct((wide, size), jnp.bfloat16),
            jax.ShapeDtypeStruct((size, wide), jnp.bfloat16),
        ],
        compiler_params=pltpu.CompilerParams(vmem_limit_bytes=VMEM_LIMIT),
        cost_estimate=pl.CostEstimate(flops=1024, bytes_accessed=1024, transcendentals=0),
    )(where, tiles, starts, beam, modes)


def project_kernel(where, *refs, piece, blocks):
    count = (len(refs) - 3) // 2
    mine, others = refs[:count], refs[count:2 * count]
    held, stay_ref, leave_ref = refs[2 * count:]
    freqs, rows, _ = stay_ref.shape
    first = where[piece] * freqs
    own = where[PARTS] == 1
    for f in range(freqs):
        a = jnp.concatenate([mine[n][k] for n, k in blocks[f]], axis=0)
        b = jnp.concatenate([others[n][k] for n, k in blocks[f]], axis=0)
        lines = jnp.concatenate([jnp.where(own, a, b), jnp.where(own, b, a)], axis=0)
        value = jnp.dot(lines, held[first + f], preferred_element_type=jnp.float32).astype(jnp.bfloat16)
        stay_ref[f] = value[:rows]
        leave_ref[f] = value[rows:]


def project(where, mine, others, held, piece, blocks, flops=1024):
    ell = held.shape[2]
    rows = sum(mine[n].shape[1] for n, _ in blocks[0])
    vmem = pl.BlockSpec(memory_space=pltpu.VMEM)
    return pl.pallas_call(
        functools.partial(project_kernel, piece=piece, blocks=blocks),
        grid_spec=pltpu.PrefetchScalarGridSpec(
            num_scalar_prefetch=1, grid=(), in_specs=[vmem] * (2 * len(mine) + 1), out_specs=[vmem] * 2
        ),
        out_shape=[jax.ShapeDtypeStruct((len(blocks), rows, ell), jnp.bfloat16)] * 2,
        compiler_params=pltpu.CompilerParams(vmem_limit_bytes=VMEM_LIMIT),
        cost_estimate=pl.CostEstimate(flops=flops, bytes_accessed=1024, transcendentals=0),
    )(where, *mine, *others, pltpu.with_memory_space_constraint(held, pltpu.VMEM))


def contract(modes, skies):
    block = jnp.concatenate([sky[...].reshape(sky.shape[0] * ROWS, sky.shape[2]) for sky in skies], axis=0)
    return jnp.dot(modes, block, preferred_element_type=jnp.float32)


def reduce_kernel(modes_ref, *refs):
    out = refs[-1]
    out[...] = contract(modes_ref[...], refs[:-1]).astype(out.dtype).reshape(out.shape)


def by_rows(count, ell, first=0):
    return pl.BlockSpec((count, ROWS, ell), lambda g: (0, g + first // ROWS, 0))


def fixed(shape):
    return pl.BlockSpec(shape, lambda g: (0,) * len(shape))


def sky_specs(skies, first):
    return [by_rows(sky.shape[0], sky.shape[2], low) for sky, low in zip(skies, first)]


def reduce(modes, skies, first, n_modes, dtype=jnp.bfloat16):
    _, rows, ell = skies[-1].shape
    return pl.pallas_call(
        reduce_kernel,
        grid=(rows // ROWS,),
        in_specs=[fixed(modes.shape)] + sky_specs(skies, first),
        out_specs=by_rows(n_modes, ell),
        out_shape=jax.ShapeDtypeStruct((n_modes, rows, ell), dtype),
        compiler_params=pltpu.CompilerParams(vmem_limit_bytes=VMEM_LIMIT),
        cost_estimate=pl.CostEstimate(flops=1024, bytes_accessed=1024, transcendentals=0),
    )(modes, *skies)


def restore_kernel(up_ref, ratio_ref, kept_ref, came_ref, *outs, spots):
    n_modes, _, ell = came_ref.shape
    freqs = up_ref.shape[0] // ROWS // PARTS
    total = kept_ref[...] + came_ref[...].astype(jnp.float32)
    weighted = (total * ratio_ref[...]).astype(jnp.bfloat16).reshape(n_modes * ROWS, ell)
    for (j, low, high), out in zip(spots, outs):
        modes = up_ref[(j * freqs + low) * ROWS:(j * freqs + high) * ROWS, :]
        value = jnp.dot(modes, weighted, preferred_element_type=jnp.float32)
        out[...] = value.astype(jnp.bfloat16).reshape(out.shape)


def restore(kept, came, ratios, up, spots):
    n_modes, rows, ell = came.shape
    return pl.pallas_call(
        functools.partial(restore_kernel, spots=spots),
        grid=(rows // ROWS,),
        in_specs=[fixed(up.shape), fixed(ratios.shape)] + [by_rows(n_modes, ell)] * 2,
        out_specs=[by_rows(high - low, ell) for _, low, high in spots],
        out_shape=[jax.ShapeDtypeStruct((high - low, rows, ell), jnp.bfloat16) for _, low, high in spots],
        compiler_params=pltpu.CompilerParams(vmem_limit_bytes=VMEM_LIMIT),
        cost_estimate=pl.CostEstimate(flops=1024, bytes_accessed=1024, transcendentals=0),
    )(up, ratios, kept, came)


def place_kernel(where, *refs, spots, first):
    count = len(spots)
    pieces, out, sems = refs[:count], refs[-2], refs[-1]
    rows = pieces[0].shape[1]
    copies = [
        pltpu.make_async_copy(pieces[n], out.at[low:high, where[PARTS + 2 + j], first:first + rows, :], sems.at[n])
        for n, (j, low, high) in enumerate(spots)
    ]
    for copy in copies:
        copy.start()
    for copy in copies:
        copy.wait()


def place(where, pieces, spots, first, shape, into=None):
    count = len(spots)
    extra = [] if into is None else [into]
    anywhere = pl.BlockSpec(memory_space=pl.ANY)
    return pl.pallas_call(
        functools.partial(place_kernel, spots=spots, first=first),
        grid_spec=pltpu.PrefetchScalarGridSpec(
            num_scalar_prefetch=1,
            grid=(),
            in_specs=[pl.BlockSpec(memory_space=pltpu.VMEM)] * count + [anywhere] * len(extra),
            out_specs=anywhere,
            scratch_shapes=[pltpu.SemaphoreType.DMA((count,))],
        ),
        out_shape=jax.ShapeDtypeStruct(shape, jnp.bfloat16),
        input_output_aliases={count + 1: 0} if extra else {},
        compiler_params=pltpu.CompilerParams(vmem_limit_bytes=VMEM_LIMIT),
        cost_estimate=pl.CostEstimate(flops=1024, bytes_accessed=1024, transcendentals=0),
    )(where, *pieces, *extra)


def anchor_kernel(*refs):
    del refs


def anchor(values, flops):
    anywhere = pl.BlockSpec(memory_space=pl.ANY)
    return pl.pallas_call(
        anchor_kernel,
        in_specs=[anywhere] * len(values),
        out_specs=[anywhere] * len(values),
        out_shape=[jax.ShapeDtypeStruct(value.shape, value.dtype) for value in values],
        input_output_aliases={n: n for n in range(len(values))},
        compiler_params=pltpu.CompilerParams(vmem_limit_bytes=1024 * 1024),
        cost_estimate=pl.CostEstimate(flops=flops, bytes_accessed=1024, transcendentals=0),
    )(*values)


def staged(visibility, beam_transfer, tile_mask, first_block, eigen_modes, signal_noise):
    freqs, parts, rows_all, base = visibility.shape
    _, freq_total, _, ell = beam_transfer.shape
    n_modes = eigen_modes.shape[2]
    ell_tiles = ell // TILE
    z, x, p = lax.axis_index("fm"), lax.axis_index("kl"), lax.axis_index("pol")
    other = [(0, 1), (1, 0)]

    def shift_z(value, j):
        return lax.ppermute(value, "fm", [(i, (i + j) % parts) for i in range(parts)])

    def swap_z(value, j):
        return lax.ppermute(value, "fm", [(i, i ^ j) for i in range(parts)])

    def along_x(value):
        return lax.ppermute(value, "kl", other)

    def cut(j, first, rows):
        return lax.dynamic_slice(visibility, (0, (z + j) % parts, first, 0), (freqs, 1, rows, base)).reshape(freqs, rows, base)

    index = jnp.arange(2 * parts + 2, dtype=jnp.int32)
    where = jnp.where(index < parts, (z - index) % parts, z ^ (index - parts - 2))
    where = jnp.where(index == parts, (x == p).astype(jnp.int32), where)
    where = jnp.where(index == parts + 1, x * ell_tiles, where).astype(jnp.int32)
    ratio = signal_noise[0] / (1.0 + signal_noise[0])
    ratios = jnp.broadcast_to(ratio[:, None, None], (n_modes, 1, ell))
    beam = beam_transfer.reshape(freq_total, base, ell)
    shape = (freqs, parts, rows_all, ell)

    fence = lax.optimization_barrier
    most, half = rows_all - ROWS, freqs // 2
    blocks = [[(0, f)] for f in range(freqs)]
    halves = [[(f // half, f % half)] for f in range(freqs)]
    a = {j: shift_z(cut(j, 0, ROWS), j) for j in (1, 3, 2)}
    mine = [cut(0, 0, rows_all)[n:n + half] for n in (0, half)]
    others = [along_x(part) for part in mine]
    b = {j: cut(j, ROWS, most) for j in (1, 2, 3)}
    held, down, up = hold(where, tile_mask[0], first_block, beam, eigen_modes[0])
    (a[1], a[3], a[2]), b, others, down, up = fence(((a[1], a[3], a[2]), b, others, down, up))
    b[1], b[3] = shift_z(b[1], 1), shift_z(b[3], 3)
    own = project(where, mine, others, held, 0, halves, 400_000_000)
    skies = [own] + [project(where, [a[j]], [along_x(a[j])], held, j, blocks, 400_000_000) for j in (1, 2, 3)]
    gone = reduce(down, [leave for _, leave in skies], (0, 0, 0, 0), n_modes)
    stay_a = [stay for stay, _ in skies]
    b[3], b[2], stay_a, gone = fence((b[3], b[2], stay_a, gone))
    x_3 = along_x(b[3])
    x_1, = anchor([along_x(b[1])], 2_500_000_000)
    b[2] = shift_z(b[2], 2)
    kept = reduce(down, stay_a, (0, 0, 0, 0), n_modes, jnp.float32)
    spots = [(j, 0, freqs) for j in (1, 2, 3, 0)]
    outs = restore(kept, lax.ppermute(gone, "pol", other), ratios, up, spots)
    near = project(where, [b[1]], [x_1], held, 1, blocks)
    x_3, b, outs, near = fence((x_3, b, outs, near))
    first = {j: swap_z(outs[j - 1], j) for j in (1, 2, 3)}
    first[0] = outs[3]
    x_2 = along_x(b[2])
    last = project(where, [b[3]], [x_3], held, 3, blocks)
    skies = [own, near, project(where, [b[2]], [x_2], held, 2, blocks), last]
    gone = reduce(down, [leave for _, leave in skies], (ROWS, 0, 0, 0), n_modes)
    stays = [stay for stay, _ in skies]
    here, stays, gone = fence((first[0], stays, gone))
    came = lax.ppermute(gone, "pol", other)
    kept = reduce(down, stays, (ROWS, 0, 0, 0), n_modes, jnp.float32)
    first[3], first[2], first[1], kept = fence((first[3], first[2], first[1], kept))
    first[3], first[2], first[1] = anchor([first[3], first[2], first[1]], 7_500_000_000)
    outs, first[3], first[2], first[1] = fence((restore(kept, came, ratios, up, spots), first[3], first[2], first[1]))
    first[0] = here
    back = [swap_z(outs[j - 1], j) for j in (2, 3, 1)]
    result = place(where, [first[j] for j in (1, 2, 3, 0)], spots, 0, shape)
    result = place(where, [outs[3]], [spots[3]], ROWS, shape, into=result)
    return place(where, back, [spots[1], spots[2], spots[0]], ROWS, shape, into=result)


def plain(visibility, beam_transfer, tile_mask, first_block, eigen_modes, signal_noise):
    owned_modes, freq_total, base_half, ell_local = beam_transfer.shape
    base_tiles, ell_tiles = base_half // TILE, ell_local // TILE
    block_ids = lax.axis_index("kl") * ell_tiles + jnp.arange(ell_tiles, dtype=jnp.int32)
    inside = (first_block[:, None] <= block_ids[None, :]).astype(jnp.int32)
    keep_tiles = tile_mask * inside[:, None, :]
    shaped = beam_transfer.reshape(owned_modes, freq_total, base_tiles, TILE, ell_tiles, TILE)
    masked_beam = shaped * keep_tiles.astype(jnp.bfloat16)[:, None, :, None, :, None]
    masked_beam = masked_beam.reshape(owned_modes, freq_total, base_half, ell_local)
    arrived = lax.all_to_all(visibility, "fm", split_axis=1, concat_axis=0, tiled=True)
    partial_value = jnp.einsum(
        "fmrb,mfbl->fmrl",
        lax.all_gather(arrived, "kl", axis=2, tiled=True),
        masked_beam,
        preferred_element_type=jnp.float32,
    )
    sky_sum = lax.psum_scatter(
        partial_value.astype(jnp.bfloat16), "pol", scatter_dimension=2, tiled=True
    ).astype(jnp.float32)
    modes_float = eigen_modes.astype(jnp.float32)
    coeffs = jnp.einsum("mfk,fmrl->mkrl", modes_float, sky_sum, precision=lax.Precision.HIGHEST)
    ratios = signal_noise / (1.0 + signal_noise)
    weighted = (coeffs * ratios[:, :, None, None]).astype(jnp.bfloat16)
    filtered = jnp.einsum(
        "mfk,mkrl->fmrl", eigen_modes, weighted, preferred_element_type=jnp.float32
    ).astype(jnp.bfloat16)
    return lax.all_to_all(filtered, "fm", split_axis=0, concat_axis=1, tiled=True)


def per_device(*args, sizes):
    visibility, beam_transfer = args[0], args[1]
    _, modes, rows, _ = visibility.shape
    fits = (
        sizes["kl"] == 2
        and sizes["pol"] == 2
        and modes == sizes["fm"] == PARTS
        and beam_transfer.shape[0] == 1
        and rows == 3 * ROWS
        and visibility.shape[0] % 2 == 0
    )
    if not fits:
        return plain(*args)
    return staged(*args)


def solution(mesh):
    placed = (
        P(("group", "fm"), None, "kl", "pol"),
        P(("group", "fm"), None, "pol", "kl"),
        P("fm", "pol", "kl"),
        P("fm"),
        P(("group", "fm"), None, None),
        P(("group", "fm"), None),
    )
    return jax.shard_map(
        functools.partial(per_device, sizes=dict(mesh.shape)),
        mesh=mesh,
        in_specs=placed,
        out_specs=P(("group", "fm"), None, "pol", "kl"),
        check_vma=False,
    )
```

```python
import functools
import jax
import jax.numpy as jnp
from jax import lax
from jax.experimental import pallas as pl
from jax.experimental.pallas import tpu as pltpu
from jax.sharding import PartitionSpec as P

TILE = 128
PARTS = 4
ROWS = 16
VMEM_LIMIT = 24 * 1024 * 1024


def hold_kernel(where, tiles, starts, beam, modes_ref, held, down_ref, up_ref, mask, sems):
    freq, base, ell = held.shape
    n_modes = modes_ref.shape[1]
    ell_tiles, base_tiles, freqs = ell // TILE, base // TILE, freq // PARTS
    copies = [pltpu.make_async_copy(beam.at[f], held.at[f], sems.at[f]) for f in range(freq)]
    for copy in copies:
        copy.start()
    for b in range(base_tiles):
        for l in range(ell_tiles):
            kept = jnp.where(starts[0] <= where[PARTS + 1] + l, tiles[b, l], 0).astype(jnp.float32)
            mask[b * TILE:(b + 1) * TILE, l * TILE:(l + 1) * TILE] = jnp.full(
                (TILE, TILE), kept, jnp.float32
            ).astype(jnp.bfloat16)
    modes = modes_ref[...]

    def pick(shape, axis, orders=0):
        big = lax.broadcasted_iota(jnp.int32, shape, axis) // ROWS
        small = lax.broadcasted_iota(jnp.int32, shape, 1 - axis)
        if freq in shape:
            piece, within = big // freqs, big % freqs
            big = within
            for j in range(PARTS):
                big = jnp.where(piece == j, where[orders + j] * freqs + within, big)
        return jnp.where(big == small, 1.0, 0.0).astype(jnp.bfloat16)

    def lane(shape):
        rows = lax.broadcasted_iota(jnp.int32, shape, 0) % ROWS
        columns = lax.broadcasted_iota(jnp.int32, shape, 1) % ROWS
        return rows == columns

    def dot(a, b, dims):
        return lax.dot_general(a, b, (dims, ((), ())), preferred_element_type=jnp.float32)

    tall = dot(pick((n_modes * ROWS, n_modes), 0), modes, ((1,), (1,))).astype(jnp.bfloat16)
    value = dot(tall, pick((freq, freq * ROWS), 1), ((1,), (0,)))
    down_ref[...] = jnp.where(lane(value.shape), value, 0.0).astype(jnp.bfloat16)
    tall = dot(pick((freq * ROWS, freq), 0, PARTS + 2), modes, ((1,), (0,))).astype(jnp.bfloat16)
    value = dot(tall, pick((n_modes, n_modes * ROWS), 1), ((1,), (0,)))
    up_ref[...] = jnp.where(lane(value.shape), value, 0.0).astype(jnp.bfloat16)
    for f, copy in enumerate(copies):
        copy.wait()
        held[f] = held[f] * mask[...]


def hold(where, tiles, starts, beam, modes):
    freq, base, ell = beam.shape
    size, wide = freq * ROWS, modes.shape[1] * ROWS
    vmem = pl.BlockSpec(memory_space=pltpu.VMEM)
    return pl.pallas_call(
        hold_kernel,
        grid_spec=pltpu.PrefetchScalarGridSpec(
            num_scalar_prefetch=3,
            grid=(),
            in_specs=[pl.BlockSpec(memory_space=pl.ANY), vmem],
            out_specs=[vmem] * 3,
            scratch_shapes=[pltpu.VMEM((base, ell), jnp.bfloat16), pltpu.SemaphoreType.DMA((freq,))],
        ),
        out_shape=[
            pltpu.VMEM(beam.shape, beam.dtype),
            jax.ShapeDtypeStruct((wide, size), jnp.bfloat16),
            jax.ShapeDtypeStruct((size, wide), jnp.bfloat16),
        ],
        compiler_params=pltpu.CompilerParams(vmem_limit_bytes=VMEM_LIMIT),
        cost_estimate=pl.CostEstimate(flops=1024, bytes_accessed=1024, transcendentals=0),
    )(where, tiles, starts, beam, modes)


def project_kernel(where, *refs, piece, blocks):
    count = (len(refs) - 3) // 2
    mine, others = refs[:count], refs[count:2 * count]
    held, stay_ref, leave_ref = refs[2 * count:]
    freqs, rows, _ = stay_ref.shape
    first = where[piece] * freqs
    own = where[PARTS] == 1
    for f in range(freqs):
        a = jnp.concatenate([mine[n][k] for n, k in blocks[f]], axis=0)
        b = jnp.concatenate([others[n][k] for n, k in blocks[f]], axis=0)
        lines = jnp.concatenate([jnp.where(own, a, b), jnp.where(own, b, a)], axis=0)
        value = jnp.dot(lines, held[first + f], preferred_element_type=jnp.float32).astype(jnp.bfloat16)
        stay_ref[f] = value[:rows]
        leave_ref[f] = value[rows:]


def project(where, mine, others, held, piece, blocks, flops=1024):
    ell = held.shape[2]
    rows = sum(mine[n].shape[1] for n, _ in blocks[0])
    vmem = pl.BlockSpec(memory_space=pltpu.VMEM)
    return pl.pallas_call(
        functools.partial(project_kernel, piece=piece, blocks=blocks),
        grid_spec=pltpu.PrefetchScalarGridSpec(
            num_scalar_prefetch=1, grid=(), in_specs=[vmem] * (2 * len(mine) + 1), out_specs=[vmem] * 2
        ),
        out_shape=[jax.ShapeDtypeStruct((len(blocks), rows, ell), jnp.bfloat16)] * 2,
        compiler_params=pltpu.CompilerParams(vmem_limit_bytes=VMEM_LIMIT),
        cost_estimate=pl.CostEstimate(flops=flops, bytes_accessed=1024, transcendentals=0),
    )(where, *mine, *others, pltpu.with_memory_space_constraint(held, pltpu.VMEM))


def contract(modes, skies):
    block = jnp.concatenate([sky[...].reshape(sky.shape[0] * ROWS, sky.shape[2]) for sky in skies], axis=0)
    return jnp.dot(modes, block, preferred_element_type=jnp.float32)


def reduce_kernel(modes_ref, *refs):
    out = refs[-1]
    out[...] = contract(modes_ref[...], refs[:-1]).astype(out.dtype).reshape(out.shape)


def by_rows(count, ell, first=0):
    return pl.BlockSpec((count, ROWS, ell), lambda g: (0, g + first // ROWS, 0))


def fixed(shape):
    return pl.BlockSpec(shape, lambda g: (0,) * len(shape))


def sky_specs(skies, first):
    return [by_rows(sky.shape[0], sky.shape[2], low) for sky, low in zip(skies, first)]


def reduce(modes, skies, first, n_modes, dtype=jnp.bfloat16):
    _, rows, ell = skies[-1].shape
    return pl.pallas_call(
        reduce_kernel,
        grid=(rows // ROWS,),
        in_specs=[fixed(modes.shape)] + sky_specs(skies, first),
        out_specs=by_rows(n_modes, ell),
        out_shape=jax.ShapeDtypeStruct((n_modes, rows, ell), dtype),
        compiler_params=pltpu.CompilerParams(vmem_limit_bytes=VMEM_LIMIT),
        cost_estimate=pl.CostEstimate(flops=1024, bytes_accessed=1024, transcendentals=0),
    )(modes, *skies)


def restore_kernel(up_ref, ratio_ref, kept_ref, came_ref, *outs, spots):
    n_modes, _, ell = came_ref.shape
    freqs = up_ref.shape[0] // ROWS // PARTS
    total = kept_ref[...] + came_ref[...].astype(jnp.float32)
    weighted = (total * ratio_ref[...]).astype(jnp.bfloat16).reshape(n_modes * ROWS, ell)
    for (j, low, high), out in zip(spots, outs):
        modes = up_ref[(j * freqs + low) * ROWS:(j * freqs + high) * ROWS, :]
        value = jnp.dot(modes, weighted, preferred_element_type=jnp.float32)
        out[...] = value.astype(jnp.bfloat16).reshape(out.shape)


def restore(kept, came, ratios, up, spots):
    n_modes, rows, ell = came.shape
    return pl.pallas_call(
        functools.partial(restore_kernel, spots=spots),
        grid=(rows // ROWS,),
        in_specs=[fixed(up.shape), fixed(ratios.shape)] + [by_rows(n_modes, ell)] * 2,
        out_specs=[by_rows(high - low, ell) for _, low, high in spots],
        out_shape=[jax.ShapeDtypeStruct((high - low, rows, ell), jnp.bfloat16) for _, low, high in spots],
        compiler_params=pltpu.CompilerParams(vmem_limit_bytes=VMEM_LIMIT),
        cost_estimate=pl.CostEstimate(flops=1024, bytes_accessed=1024, transcendentals=0),
    )(up, ratios, kept, came)


def place_kernel(where, *refs, spots, first):
    count = len(spots)
    pieces, out, sems = refs[:count], refs[-2], refs[-1]
    rows = pieces[0].shape[1]
    copies = [
        pltpu.make_async_copy(pieces[n], out.at[low:high, where[PARTS + 2 + j], first:first + rows, :], sems.at[n])
        for n, (j, low, high) in enumerate(spots)
    ]
    for copy in copies:
        copy.start()
    for copy in copies:
        copy.wait()


def place(where, pieces, spots, first, shape, into=None):
    count = len(spots)
    extra = [] if into is None else [into]
    anywhere = pl.BlockSpec(memory_space=pl.ANY)
    return pl.pallas_call(
        functools.partial(place_kernel, spots=spots, first=first),
        grid_spec=pltpu.PrefetchScalarGridSpec(
            num_scalar_prefetch=1,
            grid=(),
            in_specs=[pl.BlockSpec(memory_space=pltpu.VMEM)] * count + [anywhere] * len(extra),
            out_specs=anywhere,
            scratch_shapes=[pltpu.SemaphoreType.DMA((count,))],
        ),
        out_shape=jax.ShapeDtypeStruct(shape, jnp.bfloat16),
        input_output_aliases={count + 1: 0} if extra else {},
        compiler_params=pltpu.CompilerParams(vmem_limit_bytes=VMEM_LIMIT),
        cost_estimate=pl.CostEstimate(flops=1024, bytes_accessed=1024, transcendentals=0),
    )(where, *pieces, *extra)


def anchor_kernel(*refs):
    del refs


def anchor(values, flops):
    anywhere = pl.BlockSpec(memory_space=pl.ANY)
    return pl.pallas_call(
        anchor_kernel,
        in_specs=[anywhere] * len(values),
        out_specs=[anywhere] * len(values),
        out_shape=[jax.ShapeDtypeStruct(value.shape, value.dtype) for value in values],
        input_output_aliases={n: n for n in range(len(values))},
        compiler_params=pltpu.CompilerParams(vmem_limit_bytes=1024 * 1024),
        cost_estimate=pl.CostEstimate(flops=flops, bytes_accessed=1024, transcendentals=0),
    )(*values)


def staged(visibility, beam_transfer, tile_mask, first_block, eigen_modes, signal_noise):
    freqs, parts, rows_all, base = visibility.shape
    _, freq_total, _, ell = beam_transfer.shape
    n_modes = eigen_modes.shape[2]
    ell_tiles = ell // TILE
    z, x, p = lax.axis_index("fm"), lax.axis_index("kl"), lax.axis_index("pol")
    other = [(0, 1), (1, 0)]

    def shift_z(value, j):
        return lax.ppermute(value, "fm", [(i, (i + j) % parts) for i in range(parts)])

    def swap_z(value, j):
        return lax.ppermute(value, "fm", [(i, i ^ j) for i in range(parts)])

    def along_x(value):
        return lax.ppermute(value, "kl", other)

    def cut(j, first, rows):
        return lax.dynamic_slice(visibility, (0, (z + j) % parts, first, 0), (freqs, 1, rows, base)).reshape(freqs, rows, base)

    index = jnp.arange(2 * parts + 2, dtype=jnp.int32)
    where = jnp.where(index < parts, (z - index) % parts, z ^ (index - parts - 2))
    where = jnp.where(index == parts, (x == p).astype(jnp.int32), where)
    where = jnp.where(index == parts + 1, x * ell_tiles, where).astype(jnp.int32)
    ratio = signal_noise[0] / (1.0 + signal_noise[0])
    ratios = jnp.broadcast_to(ratio[:, None, None], (n_modes, 1, ell))
    beam = beam_transfer.reshape(freq_total, base, ell)
    shape = (freqs, parts, rows_all, ell)

    fence = lax.optimization_barrier
    most, half = rows_all - ROWS, freqs // 2
    blocks = [[(0, f)] for f in range(freqs)]
    halves = [[(f // half, f % half)] for f in range(freqs)]
    a = {j: shift_z(cut(j, 0, ROWS), j) for j in (2, 1, 3)}
    mine = [cut(0, 0, rows_all)[n:n + half] for n in (0, half)]
    others = [along_x(part) for part in mine]
    b = {j: cut(j, ROWS, most) for j in (1, 2, 3)}
    held, down, up = hold(where, tile_mask[0], first_block, beam, eigen_modes[0])
    (a[2], a[1], a[3]), b, others, down, up = fence(((a[2], a[1], a[3]), b, others, down, up))
    b[1], b[3] = shift_z(b[1], 1), shift_z(b[3], 3)
    own = project(where, mine, others, held, 0, halves, 400_000_000)
    skies = [own] + [project(where, [a[j]], [along_x(a[j])], held, j, blocks, 400_000_000) for j in (1, 2, 3)]
    gone = reduce(down, [leave for _, leave in skies], (0, 0, 0, 0), n_modes)
    stay_a = [stay for stay, _ in skies]
    b[3], b[2], stay_a, gone = fence((b[3], b[2], stay_a, gone))
    x_3 = along_x(b[3])
    x_1, = anchor([along_x(b[1])], 2_500_000_000)
    b[2] = shift_z(b[2], 2)
    kept = reduce(down, stay_a, (0, 0, 0, 0), n_modes, jnp.float32)
    spots = [(j, 0, freqs) for j in (1, 2, 3, 0)]
    outs = restore(kept, lax.ppermute(gone, "pol", other), ratios, up, spots)
    near = project(where, [b[1]], [x_1], held, 1, blocks)
    x_3, b, outs, near = fence((x_3, b, outs, near))
    first = {j: swap_z(outs[j - 1], j) for j in (1, 2, 3)}
    first[0] = outs[3]
    x_2 = along_x(b[2])
    last = project(where, [b[3]], [x_3], held, 3, blocks)
    skies = [own, near, project(where, [b[2]], [x_2], held, 2, blocks), last]
    gone = reduce(down, [leave for _, leave in skies], (ROWS, 0, 0, 0), n_modes)
    stays = [stay for stay, _ in skies]
    here, stays, gone = fence((first[0], stays, gone))
    came = lax.ppermute(gone, "pol", other)
    kept = reduce(down, stays, (ROWS, 0, 0, 0), n_modes, jnp.float32)
    first[3], first[2], first[1], kept = fence((first[3], first[2], first[1], kept))
    first[3], first[2], first[1] = anchor([first[3], first[2], first[1]], 7_500_000_000)
    outs, first[3], first[2], first[1] = fence((restore(kept, came, ratios, up, spots), first[3], first[2], first[1]))
    first[0] = here
    back = [swap_z(outs[j - 1], j) for j in (2, 3, 1)]
    result = place(where, [first[j] for j in (1, 2, 3, 0)], spots, 0, shape)
    result = place(where, [outs[3]], [spots[3]], ROWS, shape, into=result)
    return place(where, back, [spots[1], spots[2], spots[0]], ROWS, shape, into=result)


def plain(visibility, beam_transfer, tile_mask, first_block, eigen_modes, signal_noise):
    owned_modes, freq_total, base_half, ell_local = beam_transfer.shape
    base_tiles, ell_tiles = base_half // TILE, ell_local // TILE
    block_ids = lax.axis_index("kl") * ell_tiles + jnp.arange(ell_tiles, dtype=jnp.int32)
    inside = (first_block[:, None] <= block_ids[None, :]).astype(jnp.int32)
    keep_tiles = tile_mask * inside[:, None, :]
    shaped = beam_transfer.reshape(owned_modes, freq_total, base_tiles, TILE, ell_tiles, TILE)
    masked_beam = shaped * keep_tiles.astype(jnp.bfloat16)[:, None, :, None, :, None]
    masked_beam = masked_beam.reshape(owned_modes, freq_total, base_half, ell_local)
    arrived = lax.all_to_all(visibility, "fm", split_axis=1, concat_axis=0, tiled=True)
    partial_value = jnp.einsum(
        "fmrb,mfbl->fmrl",
        lax.all_gather(arrived, "kl", axis=2, tiled=True),
        masked_beam,
        preferred_element_type=jnp.float32,
    )
    sky_sum = lax.psum_scatter(
        partial_value.astype(jnp.bfloat16), "pol", scatter_dimension=2, tiled=True
    ).astype(jnp.float32)
    modes_float = eigen_modes.astype(jnp.float32)
    coeffs = jnp.einsum("mfk,fmrl->mkrl", modes_float, sky_sum, precision=lax.Precision.HIGHEST)
    ratios = signal_noise / (1.0 + signal_noise)
    weighted = (coeffs * ratios[:, :, None, None]).astype(jnp.bfloat16)
    filtered = jnp.einsum(
        "mfk,mkrl->fmrl", eigen_modes, weighted, preferred_element_type=jnp.float32
    ).astype(jnp.bfloat16)
    return lax.all_to_all(filtered, "fm", split_axis=0, concat_axis=1, tiled=True)


def per_device(*args, sizes):
    visibility, beam_transfer = args[0], args[1]
    _, modes, rows, _ = visibility.shape
    fits = (
        sizes["kl"] == 2
        and sizes["pol"] == 2
        and modes == sizes["fm"] == PARTS
        and beam_transfer.shape[0] == 1
        and rows == 3 * ROWS
        and visibility.shape[0] % 2 == 0
    )
    if not fits:
        return plain(*args)
    return staged(*args)


def solution(mesh):
    placed = (
        P(("group", "fm"), None, "kl", "pol"),
        P(("group", "fm"), None, "pol", "kl"),
        P("fm", "pol", "kl"),
        P("fm"),
        P(("group", "fm"), None, None),
        P(("group", "fm"), None),
    )
    return jax.shard_map(
        functools.partial(per_device, sizes=dict(mesh.shape)),
        mesh=mesh,
        in_specs=placed,
        out_specs=P(("group", "fm"), None, "pol", "kl"),
        check_vma=False,
    )
```

```python
import functools
import jax
import jax.numpy as jnp
from jax import lax
from jax.experimental import pallas as pl
from jax.experimental.pallas import tpu as pltpu
from jax.sharding import PartitionSpec as P

TILE = 128
PARTS = 4
ROWS = 16
VMEM_LIMIT = 24 * 1024 * 1024


def hold_kernel(where, tiles, starts, beam, modes_ref, held, down_ref, up_ref, mask, sems):
    freq, base, ell = held.shape
    n_modes = modes_ref.shape[1]
    ell_tiles, base_tiles, freqs = ell // TILE, base // TILE, freq // PARTS
    copies = [pltpu.make_async_copy(beam.at[f], held.at[f], sems.at[f]) for f in range(freq)]
    for copy in copies:
        copy.start()
    for b in range(base_tiles):
        for l in range(ell_tiles):
            kept = jnp.where(starts[0] <= where[PARTS + 1] + l, tiles[b, l], 0).astype(jnp.float32)
            mask[b * TILE:(b + 1) * TILE, l * TILE:(l + 1) * TILE] = jnp.full(
                (TILE, TILE), kept, jnp.float32
            ).astype(jnp.bfloat16)
    modes = modes_ref[...]

    def pick(shape, axis, orders=0):
        big = lax.broadcasted_iota(jnp.int32, shape, axis) // ROWS
        small = lax.broadcasted_iota(jnp.int32, shape, 1 - axis)
        if freq in shape:
            piece, within = big // freqs, big % freqs
            big = within
            for j in range(PARTS):
                big = jnp.where(piece == j, where[orders + j] * freqs + within, big)
        return jnp.where(big == small, 1.0, 0.0).astype(jnp.bfloat16)

    def lane(shape):
        rows = lax.broadcasted_iota(jnp.int32, shape, 0) % ROWS
        columns = lax.broadcasted_iota(jnp.int32, shape, 1) % ROWS
        return rows == columns

    def dot(a, b, dims):
        return lax.dot_general(a, b, (dims, ((), ())), preferred_element_type=jnp.float32)

    tall = dot(pick((n_modes * ROWS, n_modes), 0), modes, ((1,), (1,))).astype(jnp.bfloat16)
    value = dot(tall, pick((freq, freq * ROWS), 1), ((1,), (0,)))
    down_ref[...] = jnp.where(lane(value.shape), value, 0.0).astype(jnp.bfloat16)
    tall = dot(pick((freq * ROWS, freq), 0, PARTS + 2), modes, ((1,), (0,))).astype(jnp.bfloat16)
    value = dot(tall, pick((n_modes, n_modes * ROWS), 1), ((1,), (0,)))
    up_ref[...] = jnp.where(lane(value.shape), value, 0.0).astype(jnp.bfloat16)
    for f, copy in enumerate(copies):
        copy.wait()
        held[f] = held[f] * mask[...]


def hold(where, tiles, starts, beam, modes):
    freq, base, ell = beam.shape
    size, wide = freq * ROWS, modes.shape[1] * ROWS
    vmem = pl.BlockSpec(memory_space=pltpu.VMEM)
    return pl.pallas_call(
        hold_kernel,
        grid_spec=pltpu.PrefetchScalarGridSpec(
            num_scalar_prefetch=3,
            grid=(),
            in_specs=[pl.BlockSpec(memory_space=pl.ANY), vmem],
            out_specs=[vmem] * 3,
            scratch_shapes=[pltpu.VMEM((base, ell), jnp.bfloat16), pltpu.SemaphoreType.DMA((freq,))],
        ),
        out_shape=[
            pltpu.VMEM(beam.shape, beam.dtype),
            jax.ShapeDtypeStruct((wide, size), jnp.bfloat16),
            jax.ShapeDtypeStruct((size, wide), jnp.bfloat16),
        ],
        compiler_params=pltpu.CompilerParams(vmem_limit_bytes=VMEM_LIMIT),
        cost_estimate=pl.CostEstimate(flops=1024, bytes_accessed=1024, transcendentals=0),
    )(where, tiles, starts, beam, modes)


def project_kernel(where, *refs, piece, blocks):
    count = (len(refs) - 3) // 2
    mine, others = refs[:count], refs[count:2 * count]
    held, stay_ref, leave_ref = refs[2 * count:]
    freqs, rows, _ = stay_ref.shape
    first = where[piece] * freqs
    own = where[PARTS] == 1
    for f in range(freqs):
        a = jnp.concatenate([mine[n][k] for n, k in blocks[f]], axis=0)
        b = jnp.concatenate([others[n][k] for n, k in blocks[f]], axis=0)
        lines = jnp.concatenate([jnp.where(own, a, b), jnp.where(own, b, a)], axis=0)
        value = jnp.dot(lines, held[first + f], preferred_element_type=jnp.float32).astype(jnp.bfloat16)
        stay_ref[f] = value[:rows]
        leave_ref[f] = value[rows:]


def project(where, mine, others, held, piece, blocks, flops=1024):
    ell = held.shape[2]
    rows = sum(mine[n].shape[1] for n, _ in blocks[0])
    vmem = pl.BlockSpec(memory_space=pltpu.VMEM)
    return pl.pallas_call(
        functools.partial(project_kernel, piece=piece, blocks=blocks),
        grid_spec=pltpu.PrefetchScalarGridSpec(
            num_scalar_prefetch=1, grid=(), in_specs=[vmem] * (2 * len(mine) + 1), out_specs=[vmem] * 2
        ),
        out_shape=[jax.ShapeDtypeStruct((len(blocks), rows, ell), jnp.bfloat16)] * 2,
        compiler_params=pltpu.CompilerParams(vmem_limit_bytes=VMEM_LIMIT),
        cost_estimate=pl.CostEstimate(flops=flops, bytes_accessed=1024, transcendentals=0),
    )(where, *mine, *others, pltpu.with_memory_space_constraint(held, pltpu.VMEM))


def contract(modes, skies):
    block = jnp.concatenate([sky[...].reshape(sky.shape[0] * ROWS, sky.shape[2]) for sky in skies], axis=0)
    return jnp.dot(modes, block, preferred_element_type=jnp.float32)


def reduce_kernel(modes_ref, *refs):
    out = refs[-1]
    out[...] = contract(modes_ref[...], refs[:-1]).astype(out.dtype).reshape(out.shape)


def by_rows(count, ell, first=0):
    return pl.BlockSpec((count, ROWS, ell), lambda g: (0, g + first // ROWS, 0))


def fixed(shape):
    return pl.BlockSpec(shape, lambda g: (0,) * len(shape))


def sky_specs(skies, first):
    return [by_rows(sky.shape[0], sky.shape[2], low) for sky, low in zip(skies, first)]


def reduce(modes, skies, first, n_modes, dtype=jnp.bfloat16):
    _, rows, ell = skies[-1].shape
    return pl.pallas_call(
        reduce_kernel,
        grid=(rows // ROWS,),
        in_specs=[fixed(modes.shape)] + sky_specs(skies, first),
        out_specs=by_rows(n_modes, ell),
        out_shape=jax.ShapeDtypeStruct((n_modes, rows, ell), dtype),
        compiler_params=pltpu.CompilerParams(vmem_limit_bytes=VMEM_LIMIT),
        cost_estimate=pl.CostEstimate(flops=1024, bytes_accessed=1024, transcendentals=0),
    )(modes, *skies)


def restore_kernel(up_ref, ratio_ref, kept_ref, came_ref, *outs, spots):
    n_modes, _, ell = came_ref.shape
    freqs = up_ref.shape[0] // ROWS // PARTS
    total = kept_ref[...] + came_ref[...].astype(jnp.float32)
    weighted = (total * ratio_ref[...]).astype(jnp.bfloat16).reshape(n_modes * ROWS, ell)
    for (j, low, high), out in zip(spots, outs):
        modes = up_ref[(j * freqs + low) * ROWS:(j * freqs + high) * ROWS, :]
        value = jnp.dot(modes, weighted, preferred_element_type=jnp.float32)
        out[...] = value.astype(jnp.bfloat16).reshape(out.shape)


def restore(kept, came, ratios, up, spots):
    n_modes, rows, ell = came.shape
    return pl.pallas_call(
        functools.partial(restore_kernel, spots=spots),
        grid=(rows // ROWS,),
        in_specs=[fixed(up.shape), fixed(ratios.shape)] + [by_rows(n_modes, ell)] * 2,
        out_specs=[by_rows(high - low, ell) for _, low, high in spots],
        out_shape=[jax.ShapeDtypeStruct((high - low, rows, ell), jnp.bfloat16) for _, low, high in spots],
        compiler_params=pltpu.CompilerParams(vmem_limit_bytes=VMEM_LIMIT),
        cost_estimate=pl.CostEstimate(flops=1024, bytes_accessed=1024, transcendentals=0),
    )(up, ratios, kept, came)


def place_kernel(where, *refs, spots, first):
    count = len(spots)
    pieces, out, sems = refs[:count], refs[-2], refs[-1]
    rows = pieces[0].shape[1]
    copies = [
        pltpu.make_async_copy(pieces[n], out.at[low:high, where[PARTS + 2 + j], first:first + rows, :], sems.at[n])
        for n, (j, low, high) in enumerate(spots)
    ]
    for copy in copies:
        copy.start()
    for copy in copies:
        copy.wait()


def place(where, pieces, spots, first, shape, into=None):
    count = len(spots)
    extra = [] if into is None else [into]
    anywhere = pl.BlockSpec(memory_space=pl.ANY)
    return pl.pallas_call(
        functools.partial(place_kernel, spots=spots, first=first),
        grid_spec=pltpu.PrefetchScalarGridSpec(
            num_scalar_prefetch=1,
            grid=(),
            in_specs=[pl.BlockSpec(memory_space=pltpu.VMEM)] * count + [anywhere] * len(extra),
            out_specs=anywhere,
            scratch_shapes=[pltpu.SemaphoreType.DMA((count,))],
        ),
        out_shape=jax.ShapeDtypeStruct(shape, jnp.bfloat16),
        input_output_aliases={count + 1: 0} if extra else {},
        compiler_params=pltpu.CompilerParams(vmem_limit_bytes=VMEM_LIMIT),
        cost_estimate=pl.CostEstimate(flops=1024, bytes_accessed=1024, transcendentals=0),
    )(where, *pieces, *extra)


def anchor_kernel(*refs):
    del refs


def anchor(values, flops):
    anywhere = pl.BlockSpec(memory_space=pl.ANY)
    return pl.pallas_call(
        anchor_kernel,
        in_specs=[anywhere] * len(values),
        out_specs=[anywhere] * len(values),
        out_shape=[jax.ShapeDtypeStruct(value.shape, value.dtype) for value in values],
        input_output_aliases={n: n for n in range(len(values))},
        compiler_params=pltpu.CompilerParams(vmem_limit_bytes=1024 * 1024),
        cost_estimate=pl.CostEstimate(flops=flops, bytes_accessed=1024, transcendentals=0),
    )(*values)


def staged(visibility, beam_transfer, tile_mask, first_block, eigen_modes, signal_noise):
    freqs, parts, rows_all, base = visibility.shape
    _, freq_total, _, ell = beam_transfer.shape
    n_modes = eigen_modes.shape[2]
    ell_tiles = ell // TILE
    z, x, p = lax.axis_index("fm"), lax.axis_index("kl"), lax.axis_index("pol")
    other = [(0, 1), (1, 0)]

    def shift_z(value, j):
        return lax.ppermute(value, "fm", [(i, (i + j) % parts) for i in range(parts)])

    def swap_z(value, j):
        return lax.ppermute(value, "fm", [(i, i ^ j) for i in range(parts)])

    def along_x(value):
        return lax.ppermute(value, "kl", other)

    def cut(j, first, rows):
        return lax.dynamic_slice(visibility, (0, (z + j) % parts, first, 0), (freqs, 1, rows, base)).reshape(freqs, rows, base)

    index = jnp.arange(2 * parts + 2, dtype=jnp.int32)
    where = jnp.where(index < parts, (z - index) % parts, z ^ (index - parts - 2))
    where = jnp.where(index == parts, (x == p).astype(jnp.int32), where)
    where = jnp.where(index == parts + 1, x * ell_tiles, where).astype(jnp.int32)
    ratio = signal_noise[0] / (1.0 + signal_noise[0])
    ratios = jnp.broadcast_to(ratio[:, None, None], (n_modes, 1, ell))
    beam = beam_transfer.reshape(freq_total, base, ell)
    shape = (freqs, parts, rows_all, ell)

    fence = lax.optimization_barrier
    most, half = rows_all - ROWS, freqs // 2
    blocks = [[(0, f)] for f in range(freqs)]
    halves = [[(f // half, f % half)] for f in range(freqs)]
    a = {j: shift_z(cut(j, 0, ROWS), j) for j in (2, 1, 3)}
    mine = [cut(0, 0, rows_all)[n:n + half] for n in (0, half)]
    others = [along_x(part) for part in mine]
    b = {j: cut(j, ROWS, most) for j in (1, 2, 3)}
    held, down, up = hold(where, tile_mask[0], first_block, beam, eigen_modes[0])
    (a[2], a[1], a[3]), b, others, down, up = fence(((a[2], a[1], a[3]), b, others, down, up))
    b[1], b[3] = shift_z(b[1], 1), shift_z(b[3], 3)
    own = project(where, mine, others, held, 0, halves, 400_000_000)
    skies = [own] + [project(where, [a[j]], [along_x(a[j])], held, j, blocks, 400_000_000) for j in (1, 2, 3)]
    gone = reduce(down, [leave for _, leave in skies], (0, 0, 0, 0), n_modes)
    stay_a = [stay for stay, _ in skies]
    b[3], b[2], stay_a, gone = fence((b[3], b[2], stay_a, gone))
    x_3 = along_x(b[3])
    x_1, = anchor([along_x(b[1])], 2_500_000_000)
    b[2] = shift_z(b[2], 2)
    kept = reduce(down, stay_a, (0, 0, 0, 0), n_modes, jnp.float32)
    spots = [(j, 0, freqs) for j in (1, 2, 3, 0)]
    outs = restore(kept, lax.ppermute(gone, "pol", other), ratios, up, spots)
    near = project(where, [b[1]], [x_1], held, 1, blocks)
    x_3, b, outs, near = fence((x_3, b, outs, near))
    first = {j: swap_z(outs[j - 1], j) for j in (1, 2, 3)}
    first[0] = outs[3]
    x_2 = along_x(b[2])
    last = project(where, [b[3]], [x_3], held, 3, blocks)
    skies = [own, near, project(where, [b[2]], [x_2], held, 2, blocks), last]
    gone = reduce(down, [leave for _, leave in skies], (ROWS, 0, 0, 0), n_modes)
    stays = [stay for stay, _ in skies]
    here, stays, gone = fence((first[0], stays, gone))
    came = lax.ppermute(gone, "pol", other)
    kept = reduce(down, stays, (ROWS, 0, 0, 0), n_modes, jnp.float32)
    first[3], first[2], first[1], kept = fence((first[3], first[2], first[1], kept))
    first[3], first[2], first[1] = anchor([first[3], first[2], first[1]], 7_500_000_000)
    out_2, = restore(kept, came, ratios, up, [spots[1]])
    out_2, first[3], first[2], first[1] = fence((out_2, first[3], first[2], first[1]))
    first[0] = here
    out_3, out_1, out_0 = restore(kept, came, ratios, up, [spots[2], spots[0], spots[3]])
    back = [swap_z(out, j) for out, j in ((out_2, 2), (out_3, 3), (out_1, 1))]
    result = place(where, [first[j] for j in (1, 2, 3, 0)], spots, 0, shape)
    result = place(where, [out_0], [spots[3]], ROWS, shape, into=result)
    return place(where, back, [spots[1], spots[2], spots[0]], ROWS, shape, into=result)


def plain(visibility, beam_transfer, tile_mask, first_block, eigen_modes, signal_noise):
    owned_modes, freq_total, base_half, ell_local = beam_transfer.shape
    base_tiles, ell_tiles = base_half // TILE, ell_local // TILE
    block_ids = lax.axis_index("kl") * ell_tiles + jnp.arange(ell_tiles, dtype=jnp.int32)
    inside = (first_block[:, None] <= block_ids[None, :]).astype(jnp.int32)
    keep_tiles = tile_mask * inside[:, None, :]
    shaped = beam_transfer.reshape(owned_modes, freq_total, base_tiles, TILE, ell_tiles, TILE)
    masked_beam = shaped * keep_tiles.astype(jnp.bfloat16)[:, None, :, None, :, None]
    masked_beam = masked_beam.reshape(owned_modes, freq_total, base_half, ell_local)
    arrived = lax.all_to_all(visibility, "fm", split_axis=1, concat_axis=0, tiled=True)
    partial_value = jnp.einsum(
        "fmrb,mfbl->fmrl",
        lax.all_gather(arrived, "kl", axis=2, tiled=True),
        masked_beam,
        preferred_element_type=jnp.float32,
    )
    sky_sum = lax.psum_scatter(
        partial_value.astype(jnp.bfloat16), "pol", scatter_dimension=2, tiled=True
    ).astype(jnp.float32)
    modes_float = eigen_modes.astype(jnp.float32)
    coeffs = jnp.einsum("mfk,fmrl->mkrl", modes_float, sky_sum, precision=lax.Precision.HIGHEST)
    ratios = signal_noise / (1.0 + signal_noise)
    weighted = (coeffs * ratios[:, :, None, None]).astype(jnp.bfloat16)
    filtered = jnp.einsum(
        "mfk,mkrl->fmrl", eigen_modes, weighted, preferred_element_type=jnp.float32
    ).astype(jnp.bfloat16)
    return lax.all_to_all(filtered, "fm", split_axis=0, concat_axis=1, tiled=True)


def per_device(*args, sizes):
    visibility, beam_transfer = args[0], args[1]
    _, modes, rows, _ = visibility.shape
    fits = (
        sizes["kl"] == 2
        and sizes["pol"] == 2
        and modes == sizes["fm"] == PARTS
        and beam_transfer.shape[0] == 1
        and rows == 3 * ROWS
        and visibility.shape[0] % 2 == 0
    )
    if not fits:
        return plain(*args)
    return staged(*args)


def solution(mesh):
    placed = (
        P(("group", "fm"), None, "kl", "pol"),
        P(("group", "fm"), None, "pol", "kl"),
        P("fm", "pol", "kl"),
        P("fm"),
        P(("group", "fm"), None, None),
        P(("group", "fm"), None),
    )
    return jax.shard_map(
        functools.partial(per_device, sizes=dict(mesh.shape)),
        mesh=mesh,
        in_specs=placed,
        out_specs=P(("group", "fm"), None, "pol", "kl"),
        check_vma=False,
    )
```

```python
import functools
import jax
import jax.numpy as jnp
from jax import lax
from jax.experimental import pallas as pl
from jax.experimental.pallas import tpu as pltpu
from jax.sharding import PartitionSpec as P

TILE = 128
PARTS = 4
ROWS = 16
VMEM_LIMIT = 24 * 1024 * 1024


def hold_kernel(where, tiles, starts, beam, modes_ref, held, down_ref, up_ref, mask, sems):
    freq, base, ell = held.shape
    n_modes = modes_ref.shape[1]
    ell_tiles, base_tiles, freqs = ell // TILE, base // TILE, freq // PARTS
    copies = [pltpu.make_async_copy(beam.at[f], held.at[f], sems.at[f]) for f in range(freq)]
    for copy in copies:
        copy.start()
    for b in range(base_tiles):
        for l in range(ell_tiles):
            kept = jnp.where(starts[0] <= where[PARTS + 1] + l, tiles[b, l], 0).astype(jnp.float32)
            mask[b * TILE:(b + 1) * TILE, l * TILE:(l + 1) * TILE] = jnp.full(
                (TILE, TILE), kept, jnp.float32
            ).astype(jnp.bfloat16)
    modes = modes_ref[...]

    def pick(shape, axis, orders=0):
        big = lax.broadcasted_iota(jnp.int32, shape, axis) // ROWS
        small = lax.broadcasted_iota(jnp.int32, shape, 1 - axis)
        if freq in shape:
            piece, within = big // freqs, big % freqs
            big = within
            for j in range(PARTS):
                big = jnp.where(piece == j, where[orders + j] * freqs + within, big)
        return jnp.where(big == small, 1.0, 0.0).astype(jnp.bfloat16)

    def lane(shape):
        rows = lax.broadcasted_iota(jnp.int32, shape, 0) % ROWS
        columns = lax.broadcasted_iota(jnp.int32, shape, 1) % ROWS
        return rows == columns

    def dot(a, b, dims):
        return lax.dot_general(a, b, (dims, ((), ())), preferred_element_type=jnp.float32)

    tall = dot(pick((n_modes * ROWS, n_modes), 0), modes, ((1,), (1,))).astype(jnp.bfloat16)
    value = dot(tall, pick((freq, freq * ROWS), 1), ((1,), (0,)))
    down_ref[...] = jnp.where(lane(value.shape), value, 0.0).astype(jnp.bfloat16)
    tall = dot(pick((freq * ROWS, freq), 0, PARTS + 2), modes, ((1,), (0,))).astype(jnp.bfloat16)
    value = dot(tall, pick((n_modes, n_modes * ROWS), 1), ((1,), (0,)))
    up_ref[...] = jnp.where(lane(value.shape), value, 0.0).astype(jnp.bfloat16)
    for f, copy in enumerate(copies):
        copy.wait()
        held[f] = held[f] * mask[...]


def hold(where, tiles, starts, beam, modes):
    freq, base, ell = beam.shape
    size, wide = freq * ROWS, modes.shape[1] * ROWS
    vmem = pl.BlockSpec(memory_space=pltpu.VMEM)
    return pl.pallas_call(
        hold_kernel,
        grid_spec=pltpu.PrefetchScalarGridSpec(
            num_scalar_prefetch=3,
            grid=(),
            in_specs=[pl.BlockSpec(memory_space=pl.ANY), vmem],
            out_specs=[vmem] * 3,
            scratch_shapes=[pltpu.VMEM((base, ell), jnp.bfloat16), pltpu.SemaphoreType.DMA((freq,))],
        ),
        out_shape=[
            pltpu.VMEM(beam.shape, beam.dtype),
            jax.ShapeDtypeStruct((wide, size), jnp.bfloat16),
            jax.ShapeDtypeStruct((size, wide), jnp.bfloat16),
        ],
        compiler_params=pltpu.CompilerParams(vmem_limit_bytes=VMEM_LIMIT),
        cost_estimate=pl.CostEstimate(flops=1024, bytes_accessed=1024, transcendentals=0),
    )(where, tiles, starts, beam, modes)


def project_kernel(where, *refs, piece, blocks):
    count = (len(refs) - 3) // 2
    mine, others = refs[:count], refs[count:2 * count]
    held, stay_ref, leave_ref = refs[2 * count:]
    freqs, rows, _ = stay_ref.shape
    first = where[piece] * freqs
    own = where[PARTS] == 1
    for f in range(freqs):
        a = jnp.concatenate([mine[n][k] for n, k in blocks[f]], axis=0)
        b = jnp.concatenate([others[n][k] for n, k in blocks[f]], axis=0)
        lines = jnp.concatenate([jnp.where(own, a, b), jnp.where(own, b, a)], axis=0)
        value = jnp.dot(lines, held[first + f], preferred_element_type=jnp.float32).astype(jnp.bfloat16)
        stay_ref[f] = value[:rows]
        leave_ref[f] = value[rows:]


def project(where, mine, others, held, piece, blocks, flops=1024):
    ell = held.shape[2]
    rows = sum(mine[n].shape[1] for n, _ in blocks[0])
    vmem = pl.BlockSpec(memory_space=pltpu.VMEM)
    return pl.pallas_call(
        functools.partial(project_kernel, piece=piece, blocks=blocks),
        grid_spec=pltpu.PrefetchScalarGridSpec(
            num_scalar_prefetch=1, grid=(), in_specs=[vmem] * (2 * len(mine) + 1), out_specs=[vmem] * 2
        ),
        out_shape=[jax.ShapeDtypeStruct((len(blocks), rows, ell), jnp.bfloat16)] * 2,
        compiler_params=pltpu.CompilerParams(vmem_limit_bytes=VMEM_LIMIT),
        cost_estimate=pl.CostEstimate(flops=flops, bytes_accessed=1024, transcendentals=0),
    )(where, *mine, *others, pltpu.with_memory_space_constraint(held, pltpu.VMEM))


def contract(modes, skies):
    block = jnp.concatenate([sky[...].reshape(sky.shape[0] * ROWS, sky.shape[2]) for sky in skies], axis=0)
    return jnp.dot(modes, block, preferred_element_type=jnp.float32)


def reduce_kernel(modes_ref, *refs):
    out = refs[-1]
    out[...] = contract(modes_ref[...], refs[:-1]).astype(out.dtype).reshape(out.shape)


def by_rows(count, ell, first=0):
    return pl.BlockSpec((count, ROWS, ell), lambda g: (0, g + first // ROWS, 0))


def fixed(shape):
    return pl.BlockSpec(shape, lambda g: (0,) * len(shape))


def sky_specs(skies, first):
    return [by_rows(sky.shape[0], sky.shape[2], low) for sky, low in zip(skies, first)]


def reduce(modes, skies, first, n_modes, dtype=jnp.bfloat16):
    _, rows, ell = skies[-1].shape
    return pl.pallas_call(
        reduce_kernel,
        grid=(rows // ROWS,),
        in_specs=[fixed(modes.shape)] + sky_specs(skies, first),
        out_specs=by_rows(n_modes, ell),
        out_shape=jax.ShapeDtypeStruct((n_modes, rows, ell), dtype),
        compiler_params=pltpu.CompilerParams(vmem_limit_bytes=VMEM_LIMIT),
        cost_estimate=pl.CostEstimate(flops=1024, bytes_accessed=1024, transcendentals=0),
    )(modes, *skies)


def restore_kernel(up_ref, ratio_ref, kept_ref, came_ref, *outs, spots):
    n_modes, _, ell = came_ref.shape
    freqs = up_ref.shape[0] // ROWS // PARTS
    total = kept_ref[...] + came_ref[...].astype(jnp.float32)
    weighted = (total * ratio_ref[...]).astype(jnp.bfloat16).reshape(n_modes * ROWS, ell)
    for (j, low, high), out in zip(spots, outs):
        modes = up_ref[(j * freqs + low) * ROWS:(j * freqs + high) * ROWS, :]
        value = jnp.dot(modes, weighted, preferred_element_type=jnp.float32)
        out[...] = value.astype(jnp.bfloat16).reshape(out.shape)


def restore(kept, came, ratios, up, spots):
    n_modes, rows, ell = came.shape
    return pl.pallas_call(
        functools.partial(restore_kernel, spots=spots),
        grid=(rows // ROWS,),
        in_specs=[fixed(up.shape), fixed(ratios.shape)] + [by_rows(n_modes, ell)] * 2,
        out_specs=[by_rows(high - low, ell) for _, low, high in spots],
        out_shape=[jax.ShapeDtypeStruct((high - low, rows, ell), jnp.bfloat16) for _, low, high in spots],
        compiler_params=pltpu.CompilerParams(vmem_limit_bytes=VMEM_LIMIT),
        cost_estimate=pl.CostEstimate(flops=1024, bytes_accessed=1024, transcendentals=0),
    )(up, ratios, kept, came)


def place_kernel(where, *refs, spots, first):
    count = len(spots)
    pieces, out, sems = refs[:count], refs[-2], refs[-1]
    rows = pieces[0].shape[1]
    copies = [
        pltpu.make_async_copy(pieces[n], out.at[low:high, where[PARTS + 2 + j], first:first + rows, :], sems.at[n])
        for n, (j, low, high) in enumerate(spots)
    ]
    for copy in copies:
        copy.start()
    for copy in copies:
        copy.wait()


def place(where, pieces, spots, first, shape, into=None):
    count = len(spots)
    extra = [] if into is None else [into]
    anywhere = pl.BlockSpec(memory_space=pl.ANY)
    return pl.pallas_call(
        functools.partial(place_kernel, spots=spots, first=first),
        grid_spec=pltpu.PrefetchScalarGridSpec(
            num_scalar_prefetch=1,
            grid=(),
            in_specs=[pl.BlockSpec(memory_space=pltpu.VMEM)] * count + [anywhere] * len(extra),
            out_specs=anywhere,
            scratch_shapes=[pltpu.SemaphoreType.DMA((count,))],
        ),
        out_shape=jax.ShapeDtypeStruct(shape, jnp.bfloat16),
        input_output_aliases={count + 1: 0} if extra else {},
        compiler_params=pltpu.CompilerParams(vmem_limit_bytes=VMEM_LIMIT),
        cost_estimate=pl.CostEstimate(flops=1024, bytes_accessed=1024, transcendentals=0),
    )(where, *pieces, *extra)


def anchor_kernel(*refs):
    del refs


def anchor(values, flops):
    anywhere = pl.BlockSpec(memory_space=pl.ANY)
    return pl.pallas_call(
        anchor_kernel,
        in_specs=[anywhere] * len(values),
        out_specs=[anywhere] * len(values),
        out_shape=[jax.ShapeDtypeStruct(value.shape, value.dtype) for value in values],
        input_output_aliases={n: n for n in range(len(values))},
        compiler_params=pltpu.CompilerParams(vmem_limit_bytes=1024 * 1024),
        cost_estimate=pl.CostEstimate(flops=flops, bytes_accessed=1024, transcendentals=0),
    )(*values)


def staged(visibility, beam_transfer, tile_mask, first_block, eigen_modes, signal_noise):
    freqs, parts, rows_all, base = visibility.shape
    _, freq_total, _, ell = beam_transfer.shape
    n_modes = eigen_modes.shape[2]
    ell_tiles = ell // TILE
    z, x, p = lax.axis_index("fm"), lax.axis_index("kl"), lax.axis_index("pol")
    other = [(0, 1), (1, 0)]

    def shift_z(value, j):
        return lax.ppermute(value, "fm", [(i, (i + j) % parts) for i in range(parts)])

    def swap_z(value, j):
        return lax.ppermute(value, "fm", [(i, i ^ j) for i in range(parts)])

    def along_x(value):
        return lax.ppermute(value, "kl", other)

    def cut(j, first, rows):
        return lax.dynamic_slice(visibility, (0, (z + j) % parts, first, 0), (freqs, 1, rows, base)).reshape(freqs, rows, base)

    index = jnp.arange(2 * parts + 2, dtype=jnp.int32)
    where = jnp.where(index < parts, (z - index) % parts, z ^ (index - parts - 2))
    where = jnp.where(index == parts, (x == p).astype(jnp.int32), where)
    where = jnp.where(index == parts + 1, x * ell_tiles, where).astype(jnp.int32)
    ratio = signal_noise[0] / (1.0 + signal_noise[0])
    ratios = jnp.broadcast_to(ratio[:, None, None], (n_modes, 1, ell))
    beam = beam_transfer.reshape(freq_total, base, ell)
    shape = (freqs, parts, rows_all, ell)

    fence = lax.optimization_barrier
    most, half = rows_all - ROWS, freqs // 2
    blocks = [[(0, f)] for f in range(freqs)]
    halves = [[(f // half, f % half)] for f in range(freqs)]
    a = {j: shift_z(cut(j, 0, ROWS), j) for j in (2, 1, 3)}
    mine = [cut(0, 0, rows_all)[n:n + half] for n in (0, half)]
    others = [along_x(part) for part in mine]
    b = {j: cut(j, ROWS, most) for j in (1, 2, 3)}
    held, down, up = hold(where, tile_mask[0], first_block, beam, eigen_modes[0])
    (a[2], a[1], a[3]), b, others, down, up = fence(((a[2], a[1], a[3]), b, others, down, up))
    b[1], b[3] = shift_z(b[1], 1), shift_z(b[3], 3)
    own = project(where, mine, others, held, 0, halves, 400_000_000)
    skies = [own] + [project(where, [a[j]], [along_x(a[j])], held, j, blocks, 400_000_000) for j in (1, 2, 3)]
    gone = reduce(down, [leave for _, leave in skies], (0, 0, 0, 0), n_modes)
    stay_a = [stay for stay, _ in skies]
    b[3], b[2], stay_a, gone = fence((b[3], b[2], stay_a, gone))
    x_3 = along_x(b[3])
    x_1, = anchor([along_x(b[1])], 2_500_000_000)
    b[2] = shift_z(b[2], 2)
    kept = reduce(down, stay_a, (0, 0, 0, 0), n_modes, jnp.float32)
    spots = [(j, 0, freqs) for j in (1, 2, 3, 0)]
    outs = restore(kept, lax.ppermute(gone, "pol", other), ratios, up, spots)
    near = project(where, [b[1]], [x_1], held, 1, blocks)
    x_3, b, outs, near = fence((x_3, b, outs, near))
    first = {j: swap_z(outs[j - 1], j) for j in (1, 2, 3)}
    first[0] = outs[3]
    x_2 = along_x(b[2])
    last = project(where, [b[3]], [x_3], held, 3, blocks)
    skies = [own, near, project(where, [b[2]], [x_2], held, 2, blocks), last]
    gone = reduce(down, [leave for _, leave in skies], (ROWS, 0, 0, 0), n_modes)
    stays = [stay for stay, _ in skies]
    here, stays, gone = fence((first[0], stays, gone))
    came = lax.ppermute(gone, "pol", other)
    kept = reduce(down, stays, (ROWS, 0, 0, 0), n_modes, jnp.float32)
    first[2], first[3], first[1], kept = fence((first[2], first[3], first[1], kept))
    first[2], first[3], first[1] = anchor([first[2], first[3], first[1]], 7_500_000_000)
    out_2, = restore(kept, came, ratios, up, [spots[1]])
    out_2, first[2], first[3], first[1] = fence((out_2, first[2], first[3], first[1]))
    first[0] = here
    out_3, out_1, out_0 = restore(kept, came, ratios, up, [spots[2], spots[0], spots[3]])
    back = [swap_z(out, j) for out, j in ((out_2, 2), (out_3, 3), (out_1, 1))]
    result = place(where, [first[j] for j in (1, 2, 3, 0)], spots, 0, shape)
    result = place(where, [out_0], [spots[3]], ROWS, shape, into=result)
    return place(where, back, [spots[1], spots[2], spots[0]], ROWS, shape, into=result)


def plain(visibility, beam_transfer, tile_mask, first_block, eigen_modes, signal_noise):
    owned_modes, freq_total, base_half, ell_local = beam_transfer.shape
    base_tiles, ell_tiles = base_half // TILE, ell_local // TILE
    block_ids = lax.axis_index("kl") * ell_tiles + jnp.arange(ell_tiles, dtype=jnp.int32)
    inside = (first_block[:, None] <= block_ids[None, :]).astype(jnp.int32)
    keep_tiles = tile_mask * inside[:, None, :]
    shaped = beam_transfer.reshape(owned_modes, freq_total, base_tiles, TILE, ell_tiles, TILE)
    masked_beam = shaped * keep_tiles.astype(jnp.bfloat16)[:, None, :, None, :, None]
    masked_beam = masked_beam.reshape(owned_modes, freq_total, base_half, ell_local)
    arrived = lax.all_to_all(visibility, "fm", split_axis=1, concat_axis=0, tiled=True)
    partial_value = jnp.einsum(
        "fmrb,mfbl->fmrl",
        lax.all_gather(arrived, "kl", axis=2, tiled=True),
        masked_beam,
        preferred_element_type=jnp.float32,
    )
    sky_sum = lax.psum_scatter(
        partial_value.astype(jnp.bfloat16), "pol", scatter_dimension=2, tiled=True
    ).astype(jnp.float32)
    modes_float = eigen_modes.astype(jnp.float32)
    coeffs = jnp.einsum("mfk,fmrl->mkrl", modes_float, sky_sum, precision=lax.Precision.HIGHEST)
    ratios = signal_noise / (1.0 + signal_noise)
    weighted = (coeffs * ratios[:, :, None, None]).astype(jnp.bfloat16)
    filtered = jnp.einsum(
        "mfk,mkrl->fmrl", eigen_modes, weighted, preferred_element_type=jnp.float32
    ).astype(jnp.bfloat16)
    return lax.all_to_all(filtered, "fm", split_axis=0, concat_axis=1, tiled=True)


def per_device(*args, sizes):
    visibility, beam_transfer = args[0], args[1]
    _, modes, rows, _ = visibility.shape
    fits = (
        sizes["kl"] == 2
        and sizes["pol"] == 2
        and modes == sizes["fm"] == PARTS
        and beam_transfer.shape[0] == 1
        and rows == 3 * ROWS
        and visibility.shape[0] % 2 == 0
    )
    if not fits:
        return plain(*args)
    return staged(*args)


def solution(mesh):
    placed = (
        P(("group", "fm"), None, "kl", "pol"),
        P(("group", "fm"), None, "pol", "kl"),
        P("fm", "pol", "kl"),
        P("fm"),
        P(("group", "fm"), None, None),
        P(("group", "fm"), None),
    )
    return jax.shard_map(
        functools.partial(per_device, sizes=dict(mesh.shape)),
        mesh=mesh,
        in_specs=placed,
        out_specs=P(("group", "fm"), None, "pol", "kl"),
        check_vma=False,
    )
```

```python
import functools
import jax
import jax.numpy as jnp
from jax import lax
from jax.experimental import pallas as pl
from jax.experimental.pallas import tpu as pltpu
from jax.sharding import PartitionSpec as P

TILE = 128
PARTS = 4
ROWS = 16
VMEM_LIMIT = 24 * 1024 * 1024


def hold_kernel(where, tiles, starts, beam, modes_ref, held, down_ref, up_ref, mask, sems):
    freq, base, ell = held.shape
    n_modes = modes_ref.shape[1]
    ell_tiles, base_tiles, freqs = ell // TILE, base // TILE, freq // PARTS
    copies = [pltpu.make_async_copy(beam.at[f], held.at[f], sems.at[f]) for f in range(freq)]
    for copy in copies:
        copy.start()
    for b in range(base_tiles):
        for l in range(ell_tiles):
            kept = jnp.where(starts[0] <= where[PARTS + 1] + l, tiles[b, l], 0).astype(jnp.float32)
            mask[b * TILE:(b + 1) * TILE, l * TILE:(l + 1) * TILE] = jnp.full(
                (TILE, TILE), kept, jnp.float32
            ).astype(jnp.bfloat16)
    modes = modes_ref[...]

    def pick(shape, axis, orders=0):
        big = lax.broadcasted_iota(jnp.int32, shape, axis) // ROWS
        small = lax.broadcasted_iota(jnp.int32, shape, 1 - axis)
        if freq in shape:
            piece, within = big // freqs, big % freqs
            big = within
            for j in range(PARTS):
                big = jnp.where(piece == j, where[orders + j] * freqs + within, big)
        return jnp.where(big == small, 1.0, 0.0).astype(jnp.bfloat16)

    def lane(shape):
        rows = lax.broadcasted_iota(jnp.int32, shape, 0) % ROWS
        columns = lax.broadcasted_iota(jnp.int32, shape, 1) % ROWS
        return rows == columns

    def dot(a, b, dims):
        return lax.dot_general(a, b, (dims, ((), ())), preferred_element_type=jnp.float32)

    tall = dot(pick((n_modes * ROWS, n_modes), 0), modes, ((1,), (1,))).astype(jnp.bfloat16)
    value = dot(tall, pick((freq, freq * ROWS), 1), ((1,), (0,)))
    down_ref[...] = jnp.where(lane(value.shape), value, 0.0).astype(jnp.bfloat16)
    tall = dot(pick((freq * ROWS, freq), 0, PARTS + 2), modes, ((1,), (0,))).astype(jnp.bfloat16)
    value = dot(tall, pick((n_modes, n_modes * ROWS), 1), ((1,), (0,)))
    up_ref[...] = jnp.where(lane(value.shape), value, 0.0).astype(jnp.bfloat16)
    for f, copy in enumerate(copies):
        copy.wait()
        held[f] = held[f] * mask[...]


def hold(where, tiles, starts, beam, modes):
    freq, base, ell = beam.shape
    size, wide = freq * ROWS, modes.shape[1] * ROWS
    vmem = pl.BlockSpec(memory_space=pltpu.VMEM)
    return pl.pallas_call(
        hold_kernel,
        grid_spec=pltpu.PrefetchScalarGridSpec(
            num_scalar_prefetch=3,
            grid=(),
            in_specs=[pl.BlockSpec(memory_space=pl.ANY), vmem],
            out_specs=[vmem] * 3,
            scratch_shapes=[pltpu.VMEM((base, ell), jnp.bfloat16), pltpu.SemaphoreType.DMA((freq,))],
        ),
        out_shape=[
            pltpu.VMEM(beam.shape, beam.dtype),
            jax.ShapeDtypeStruct((wide, size), jnp.bfloat16),
            jax.ShapeDtypeStruct((size, wide), jnp.bfloat16),
        ],
        compiler_params=pltpu.CompilerParams(vmem_limit_bytes=VMEM_LIMIT),
        cost_estimate=pl.CostEstimate(flops=1024, bytes_accessed=1024, transcendentals=0),
    )(where, tiles, starts, beam, modes)


def project_kernel(where, *refs, piece, blocks):
    count = (len(refs) - 3) // 2
    mine, others = refs[:count], refs[count:2 * count]
    held, stay_ref, leave_ref = refs[2 * count:]
    freqs, rows, _ = stay_ref.shape
    first = where[piece] * freqs
    own = where[PARTS] == 1
    for f in range(freqs):
        a = jnp.concatenate([mine[n][k] for n, k in blocks[f]], axis=0)
        b = jnp.concatenate([others[n][k] for n, k in blocks[f]], axis=0)
        lines = jnp.concatenate([jnp.where(own, a, b), jnp.where(own, b, a)], axis=0)
        value = jnp.dot(lines, held[first + f], preferred_element_type=jnp.float32).astype(jnp.bfloat16)
        stay_ref[f] = value[:rows]
        leave_ref[f] = value[rows:]


def project(where, mine, others, held, piece, blocks, flops=1024):
    ell = held.shape[2]
    rows = sum(mine[n].shape[1] for n, _ in blocks[0])
    vmem = pl.BlockSpec(memory_space=pltpu.VMEM)
    return pl.pallas_call(
        functools.partial(project_kernel, piece=piece, blocks=blocks),
        grid_spec=pltpu.PrefetchScalarGridSpec(
            num_scalar_prefetch=1, grid=(), in_specs=[vmem] * (2 * len(mine) + 1), out_specs=[vmem] * 2
        ),
        out_shape=[jax.ShapeDtypeStruct((len(blocks), rows, ell), jnp.bfloat16)] * 2,
        compiler_params=pltpu.CompilerParams(vmem_limit_bytes=VMEM_LIMIT),
        cost_estimate=pl.CostEstimate(flops=flops, bytes_accessed=1024, transcendentals=0),
    )(where, *mine, *others, pltpu.with_memory_space_constraint(held, pltpu.VMEM))


def contract(modes, skies):
    block = jnp.concatenate([sky[...].reshape(sky.shape[0] * ROWS, sky.shape[2]) for sky in skies], axis=0)
    return jnp.dot(modes, block, preferred_element_type=jnp.float32)


def reduce_kernel(modes_ref, *refs):
    out = refs[-1]
    out[...] = contract(modes_ref[...], refs[:-1]).astype(out.dtype).reshape(out.shape)


def by_rows(count, ell, first=0):
    return pl.BlockSpec((count, ROWS, ell), lambda g: (0, g + first // ROWS, 0))


def fixed(shape):
    return pl.BlockSpec(shape, lambda g: (0,) * len(shape))


def sky_specs(skies, first):
    return [by_rows(sky.shape[0], sky.shape[2], low) for sky, low in zip(skies, first)]


def reduce(modes, skies, first, n_modes, dtype=jnp.bfloat16):
    _, rows, ell = skies[-1].shape
    return pl.pallas_call(
        reduce_kernel,
        grid=(rows // ROWS,),
        in_specs=[fixed(modes.shape)] + sky_specs(skies, first),
        out_specs=by_rows(n_modes, ell),
        out_shape=jax.ShapeDtypeStruct((n_modes, rows, ell), dtype),
        compiler_params=pltpu.CompilerParams(vmem_limit_bytes=VMEM_LIMIT),
        cost_estimate=pl.CostEstimate(flops=1024, bytes_accessed=1024, transcendentals=0),
    )(modes, *skies)


def restore_kernel(up_ref, ratio_ref, kept_ref, came_ref, *outs, spots):
    n_modes, _, ell = came_ref.shape
    freqs = up_ref.shape[0] // ROWS // PARTS
    total = kept_ref[...] + came_ref[...].astype(jnp.float32)
    weighted = (total * ratio_ref[...]).astype(jnp.bfloat16).reshape(n_modes * ROWS, ell)
    for (j, low, high), out in zip(spots, outs):
        modes = up_ref[(j * freqs + low) * ROWS:(j * freqs + high) * ROWS, :]
        value = jnp.dot(modes, weighted, preferred_element_type=jnp.float32)
        out[...] = value.astype(jnp.bfloat16).reshape(out.shape)


def restore(kept, came, ratios, up, spots):
    n_modes, rows, ell = came.shape
    return pl.pallas_call(
        functools.partial(restore_kernel, spots=spots),
        grid=(rows // ROWS,),
        in_specs=[fixed(up.shape), fixed(ratios.shape)] + [by_rows(n_modes, ell)] * 2,
        out_specs=[by_rows(high - low, ell) for _, low, high in spots],
        out_shape=[jax.ShapeDtypeStruct((high - low, rows, ell), jnp.bfloat16) for _, low, high in spots],
        compiler_params=pltpu.CompilerParams(vmem_limit_bytes=VMEM_LIMIT),
        cost_estimate=pl.CostEstimate(flops=1024, bytes_accessed=1024, transcendentals=0),
    )(up, ratios, kept, came)


def place_kernel(where, *refs, spots, first):
    count = len(spots)
    pieces, out, sems = refs[:count], refs[-2], refs[-1]
    rows = pieces[0].shape[1]
    copies = [
        pltpu.make_async_copy(
            pieces[n].at[f], out.at[low + f, where[PARTS + 2 + j], first:first + rows, :], sems.at[n, f]
        )
        for n, (j, low, high) in enumerate(spots)
        for f in range(high - low)
    ]
    for copy in copies:
        copy.start()
    for copy in copies:
        copy.wait()


def place(where, pieces, spots, first, shape, into=None):
    count = len(spots)
    extra = [] if into is None else [into]
    anywhere = pl.BlockSpec(memory_space=pl.ANY)
    return pl.pallas_call(
        functools.partial(place_kernel, spots=spots, first=first),
        grid_spec=pltpu.PrefetchScalarGridSpec(
            num_scalar_prefetch=1,
            grid=(),
            in_specs=[pl.BlockSpec(memory_space=pltpu.VMEM)] * count + [anywhere] * len(extra),
            out_specs=anywhere,
            scratch_shapes=[pltpu.SemaphoreType.DMA((count, shape[0]))],
        ),
        out_shape=jax.ShapeDtypeStruct(shape, jnp.bfloat16),
        input_output_aliases={count + 1: 0} if extra else {},
        compiler_params=pltpu.CompilerParams(vmem_limit_bytes=VMEM_LIMIT),
        cost_estimate=pl.CostEstimate(flops=1024, bytes_accessed=1024, transcendentals=0),
    )(where, *pieces, *extra)


def anchor_kernel(*refs):
    del refs


def anchor(values, flops):
    anywhere = pl.BlockSpec(memory_space=pl.ANY)
    return pl.pallas_call(
        anchor_kernel,
        in_specs=[anywhere] * len(values),
        out_specs=[anywhere] * len(values),
        out_shape=[jax.ShapeDtypeStruct(value.shape, value.dtype) for value in values],
        input_output_aliases={n: n for n in range(len(values))},
        compiler_params=pltpu.CompilerParams(vmem_limit_bytes=1024 * 1024),
        cost_estimate=pl.CostEstimate(flops=flops, bytes_accessed=1024, transcendentals=0),
    )(*values)


def staged(visibility, beam_transfer, tile_mask, first_block, eigen_modes, signal_noise):
    freqs, parts, rows_all, base = visibility.shape
    _, freq_total, _, ell = beam_transfer.shape
    n_modes = eigen_modes.shape[2]
    ell_tiles = ell // TILE
    z, x, p = lax.axis_index("fm"), lax.axis_index("kl"), lax.axis_index("pol")
    other = [(0, 1), (1, 0)]

    def shift_z(value, j):
        return lax.ppermute(value, "fm", [(i, (i + j) % parts) for i in range(parts)])

    def swap_z(value, j):
        return lax.ppermute(value, "fm", [(i, i ^ j) for i in range(parts)])

    def along_x(value):
        return lax.ppermute(value, "kl", other)

    def cut(j, first, rows):
        return lax.dynamic_slice(visibility, (0, (z + j) % parts, first, 0), (freqs, 1, rows, base)).reshape(freqs, rows, base)

    index = jnp.arange(2 * parts + 2, dtype=jnp.int32)
    where = jnp.where(index < parts, (z - index) % parts, z ^ (index - parts - 2))
    where = jnp.where(index == parts, (x == p).astype(jnp.int32), where)
    where = jnp.where(index == parts + 1, x * ell_tiles, where).astype(jnp.int32)
    ratio = signal_noise[0] / (1.0 + signal_noise[0])
    ratios = jnp.broadcast_to(ratio[:, None, None], (n_modes, 1, ell))
    beam = beam_transfer.reshape(freq_total, base, ell)
    shape = (freqs, parts, rows_all, ell)

    fence = lax.optimization_barrier
    most, half = rows_all - ROWS, freqs // 2
    blocks = [[(0, f)] for f in range(freqs)]
    halves = [[(f // half, f % half)] for f in range(freqs)]
    a = {j: shift_z(cut(j, 0, ROWS), j) for j in (2, 1, 3)}
    mine = [cut(0, 0, rows_all)[n:n + half] for n in (0, half)]
    others = [along_x(part) for part in mine]
    b = {j: cut(j, ROWS, most) for j in (1, 2, 3)}
    held, down, up = hold(where, tile_mask[0], first_block, beam, eigen_modes[0])
    (a[2], a[1], a[3]), b, others, down, up = fence(((a[2], a[1], a[3]), b, others, down, up))
    b[1], b[3] = shift_z(b[1], 1), shift_z(b[3], 3)
    own = project(where, mine, others, held, 0, halves, 400_000_000)
    skies = [own] + [project(where, [a[j]], [along_x(a[j])], held, j, blocks, 400_000_000) for j in (1, 2, 3)]
    gone = reduce(down, [leave for _, leave in skies], (0, 0, 0, 0), n_modes)
    stay_a = [stay for stay, _ in skies]
    b[3], b[2], stay_a, gone = fence((b[3], b[2], stay_a, gone))
    x_3 = along_x(b[3])
    x_1, = anchor([along_x(b[1])], 2_500_000_000)
    b[2] = shift_z(b[2], 2)
    kept = reduce(down, stay_a, (0, 0, 0, 0), n_modes, jnp.float32)
    spots = [(j, 0, freqs) for j in (1, 2, 3, 0)]
    outs = restore(kept, lax.ppermute(gone, "pol", other), ratios, up, spots)
    near = project(where, [b[1]], [x_1], held, 1, blocks)
    x_3, b, outs, near = fence((x_3, b, outs, near))
    first = {j: swap_z(outs[j - 1], j) for j in (1, 2, 3)}
    first[0] = outs[3]
    x_2 = along_x(b[2])
    last = project(where, [b[3]], [x_3], held, 3, blocks)
    skies = [own, near, project(where, [b[2]], [x_2], held, 2, blocks), last]
    gone = reduce(down, [leave for _, leave in skies], (ROWS, 0, 0, 0), n_modes)
    stays = [stay for stay, _ in skies]
    here, stays, gone = fence((first[0], stays, gone))
    came = lax.ppermute(gone, "pol", other)
    kept = reduce(down, stays, (ROWS, 0, 0, 0), n_modes, jnp.float32)
    first[3], first[2], first[1], kept = fence((first[3], first[2], first[1], kept))
    first[3], first[2], first[1] = anchor([first[3], first[2], first[1]], 7_500_000_000)
    out_2, = restore(kept, came, ratios, up, [spots[1]])
    out_2, first[3], first[2], first[1] = fence((out_2, first[3], first[2], first[1]))
    first[0] = here
    out_3, out_1, out_0 = restore(kept, came, ratios, up, [spots[2], spots[0], spots[3]])
    back = [swap_z(out, j) for out, j in ((out_2, 2), (out_3, 3), (out_1, 1))]
    result = place(where, [first[j] for j in (1, 2, 3, 0)], spots, 0, shape)
    result = place(where, [out_0], [spots[3]], ROWS, shape, into=result)
    return place(where, back, [spots[1], spots[2], spots[0]], ROWS, shape, into=result)


def plain(visibility, beam_transfer, tile_mask, first_block, eigen_modes, signal_noise):
    owned_modes, freq_total, base_half, ell_local = beam_transfer.shape
    base_tiles, ell_tiles = base_half // TILE, ell_local // TILE
    block_ids = lax.axis_index("kl") * ell_tiles + jnp.arange(ell_tiles, dtype=jnp.int32)
    inside = (first_block[:, None] <= block_ids[None, :]).astype(jnp.int32)
    keep_tiles = tile_mask * inside[:, None, :]
    shaped = beam_transfer.reshape(owned_modes, freq_total, base_tiles, TILE, ell_tiles, TILE)
    masked_beam = shaped * keep_tiles.astype(jnp.bfloat16)[:, None, :, None, :, None]
    masked_beam = masked_beam.reshape(owned_modes, freq_total, base_half, ell_local)
    arrived = lax.all_to_all(visibility, "fm", split_axis=1, concat_axis=0, tiled=True)
    partial_value = jnp.einsum(
        "fmrb,mfbl->fmrl",
        lax.all_gather(arrived, "kl", axis=2, tiled=True),
        masked_beam,
        preferred_element_type=jnp.float32,
    )
    sky_sum = lax.psum_scatter(
        partial_value.astype(jnp.bfloat16), "pol", scatter_dimension=2, tiled=True
    ).astype(jnp.float32)
    modes_float = eigen_modes.astype(jnp.float32)
    coeffs = jnp.einsum("mfk,fmrl->mkrl", modes_float, sky_sum, precision=lax.Precision.HIGHEST)
    ratios = signal_noise / (1.0 + signal_noise)
    weighted = (coeffs * ratios[:, :, None, None]).astype(jnp.bfloat16)
    filtered = jnp.einsum(
        "mfk,mkrl->fmrl", eigen_modes, weighted, preferred_element_type=jnp.float32
    ).astype(jnp.bfloat16)
    return lax.all_to_all(filtered, "fm", split_axis=0, concat_axis=1, tiled=True)


def per_device(*args, sizes):
    visibility, beam_transfer = args[0], args[1]
    _, modes, rows, _ = visibility.shape
    fits = (
        sizes["kl"] == 2
        and sizes["pol"] == 2
        and modes == sizes["fm"] == PARTS
        and beam_transfer.shape[0] == 1
        and rows == 3 * ROWS
        and visibility.shape[0] % 2 == 0
    )
    if not fits:
        return plain(*args)
    return staged(*args)


def solution(mesh):
    placed = (
        P(("group", "fm"), None, "kl", "pol"),
        P(("group", "fm"), None, "pol", "kl"),
        P("fm", "pol", "kl"),
        P("fm"),
        P(("group", "fm"), None, None),
        P(("group", "fm"), None),
    )
    return jax.shard_map(
        functools.partial(per_device, sizes=dict(mesh.shape)),
        mesh=mesh,
        in_specs=placed,
        out_specs=P(("group", "fm"), None, "pol", "kl"),
        check_vma=False,
    )
```

```python
import functools
import jax
import jax.numpy as jnp
from jax import lax
from jax.experimental import pallas as pl
from jax.experimental.pallas import tpu as pltpu
from jax.sharding import PartitionSpec as P

TILE = 128
PARTS = 4
ROWS = 16
VMEM_LIMIT = 24 * 1024 * 1024


def hold_kernel(where, tiles, starts, beam, modes_ref, held, down_ref, up_ref, mask, sems):
    freq, base, ell = held.shape
    n_modes = modes_ref.shape[1]
    ell_tiles, base_tiles, freqs = ell // TILE, base // TILE, freq // PARTS
    copies = [pltpu.make_async_copy(beam.at[f], held.at[f], sems.at[f]) for f in range(freq)]
    for copy in copies:
        copy.start()
    for b in range(base_tiles):
        for l in range(ell_tiles):
            kept = jnp.where(starts[0] <= where[PARTS + 1] + l, tiles[b, l], 0).astype(jnp.float32)
            mask[b * TILE:(b + 1) * TILE, l * TILE:(l + 1) * TILE] = jnp.full(
                (TILE, TILE), kept, jnp.float32
            ).astype(jnp.bfloat16)
    modes = modes_ref[...]

    def pick(shape, axis, orders=0):
        big = lax.broadcasted_iota(jnp.int32, shape, axis) // ROWS
        small = lax.broadcasted_iota(jnp.int32, shape, 1 - axis)
        if freq in shape:
            piece, within = big // freqs, big % freqs
            big = within
            for j in range(PARTS):
                big = jnp.where(piece == j, where[orders + j] * freqs + within, big)
        return jnp.where(big == small, 1.0, 0.0).astype(jnp.bfloat16)

    def lane(shape):
        rows = lax.broadcasted_iota(jnp.int32, shape, 0) % ROWS
        columns = lax.broadcasted_iota(jnp.int32, shape, 1) % ROWS
        return rows == columns

    def dot(a, b, dims):
        return lax.dot_general(a, b, (dims, ((), ())), preferred_element_type=jnp.float32)

    tall = dot(pick((n_modes * ROWS, n_modes), 0), modes, ((1,), (1,))).astype(jnp.bfloat16)
    value = dot(tall, pick((freq, freq * ROWS), 1), ((1,), (0,)))
    down_ref[...] = jnp.where(lane(value.shape), value, 0.0).astype(jnp.bfloat16)
    tall = dot(pick((freq * ROWS, freq), 0, PARTS + 2), modes, ((1,), (0,))).astype(jnp.bfloat16)
    value = dot(tall, pick((n_modes, n_modes * ROWS), 1), ((1,), (0,)))
    up_ref[...] = jnp.where(lane(value.shape), value, 0.0).astype(jnp.bfloat16)
    for f, copy in enumerate(copies):
        copy.wait()
        held[f] = held[f] * mask[...]


def hold(where, tiles, starts, beam, modes):
    freq, base, ell = beam.shape
    size, wide = freq * ROWS, modes.shape[1] * ROWS
    vmem = pl.BlockSpec(memory_space=pltpu.VMEM)
    return pl.pallas_call(
        hold_kernel,
        grid_spec=pltpu.PrefetchScalarGridSpec(
            num_scalar_prefetch=3,
            grid=(),
            in_specs=[pl.BlockSpec(memory_space=pl.ANY), vmem],
            out_specs=[vmem] * 3,
            scratch_shapes=[pltpu.VMEM((base, ell), jnp.bfloat16), pltpu.SemaphoreType.DMA((freq,))],
        ),
        out_shape=[
            pltpu.VMEM(beam.shape, beam.dtype),
            jax.ShapeDtypeStruct((wide, size), jnp.bfloat16),
            jax.ShapeDtypeStruct((size, wide), jnp.bfloat16),
        ],
        compiler_params=pltpu.CompilerParams(vmem_limit_bytes=VMEM_LIMIT),
        cost_estimate=pl.CostEstimate(flops=1024, bytes_accessed=1024, transcendentals=0),
    )(where, tiles, starts, beam, modes)


def project_kernel(where, *refs, piece, blocks):
    count = (len(refs) - 3) // 2
    mine, others = refs[:count], refs[count:2 * count]
    held, stay_ref, leave_ref = refs[2 * count:]
    freqs, rows, _ = stay_ref.shape
    first = where[piece] * freqs
    own = where[PARTS] == 1
    for f in range(freqs):
        a = jnp.concatenate([mine[n][k] for n, k in blocks[f]], axis=0)
        b = jnp.concatenate([others[n][k] for n, k in blocks[f]], axis=0)
        lines = jnp.concatenate([jnp.where(own, a, b), jnp.where(own, b, a)], axis=0)
        value = jnp.dot(lines, held[first + f], preferred_element_type=jnp.float32).astype(jnp.bfloat16)
        stay_ref[f] = value[:rows]
        leave_ref[f] = value[rows:]


def project(where, mine, others, held, piece, blocks, flops=1024):
    ell = held.shape[2]
    rows = sum(mine[n].shape[1] for n, _ in blocks[0])
    vmem = pl.BlockSpec(memory_space=pltpu.VMEM)
    return pl.pallas_call(
        functools.partial(project_kernel, piece=piece, blocks=blocks),
        grid_spec=pltpu.PrefetchScalarGridSpec(
            num_scalar_prefetch=1, grid=(), in_specs=[vmem] * (2 * len(mine) + 1), out_specs=[vmem] * 2
        ),
        out_shape=[jax.ShapeDtypeStruct((len(blocks), rows, ell), jnp.bfloat16)] * 2,
        compiler_params=pltpu.CompilerParams(vmem_limit_bytes=VMEM_LIMIT),
        cost_estimate=pl.CostEstimate(flops=flops, bytes_accessed=1024, transcendentals=0),
    )(where, *mine, *others, pltpu.with_memory_space_constraint(held, pltpu.VMEM))


def contract(modes, skies):
    block = jnp.concatenate([sky[...].reshape(sky.shape[0] * ROWS, sky.shape[2]) for sky in skies], axis=0)
    return jnp.dot(modes, block, preferred_element_type=jnp.float32)


def reduce_kernel(modes_ref, *refs):
    out = refs[-1]
    out[...] = contract(modes_ref[...], refs[:-1]).astype(out.dtype).reshape(out.shape)


def by_rows(count, ell, first=0):
    return pl.BlockSpec((count, ROWS, ell), lambda g: (0, g + first // ROWS, 0))


def fixed(shape):
    return pl.BlockSpec(shape, lambda g: (0,) * len(shape))


def sky_specs(skies, first):
    return [by_rows(sky.shape[0], sky.shape[2], low) for sky, low in zip(skies, first)]


def reduce(modes, skies, first, n_modes, dtype=jnp.bfloat16):
    _, rows, ell = skies[-1].shape
    return pl.pallas_call(
        reduce_kernel,
        grid=(rows // ROWS,),
        in_specs=[fixed(modes.shape)] + sky_specs(skies, first),
        out_specs=by_rows(n_modes, ell),
        out_shape=jax.ShapeDtypeStruct((n_modes, rows, ell), dtype),
        compiler_params=pltpu.CompilerParams(vmem_limit_bytes=VMEM_LIMIT),
        cost_estimate=pl.CostEstimate(flops=1024, bytes_accessed=1024, transcendentals=0),
    )(modes, *skies)


def restore_kernel(up_ref, ratio_ref, kept_ref, came_ref, *outs, spots):
    n_modes, _, ell = came_ref.shape
    freqs = up_ref.shape[0] // ROWS // PARTS
    total = kept_ref[...] + came_ref[...].astype(jnp.float32)
    weighted = (total * ratio_ref[...]).astype(jnp.bfloat16).reshape(n_modes * ROWS, ell)
    for (j, low, high), out in zip(spots, outs):
        modes = up_ref[(j * freqs + low) * ROWS:(j * freqs + high) * ROWS, :]
        value = jnp.dot(modes, weighted, preferred_element_type=jnp.float32)
        out[...] = value.astype(jnp.bfloat16).reshape(out.shape)


def restore(kept, came, ratios, up, spots):
    n_modes, rows, ell = came.shape
    return pl.pallas_call(
        functools.partial(restore_kernel, spots=spots),
        grid=(rows // ROWS,),
        in_specs=[fixed(up.shape), fixed(ratios.shape)] + [by_rows(n_modes, ell)] * 2,
        out_specs=[by_rows(high - low, ell) for _, low, high in spots],
        out_shape=[jax.ShapeDtypeStruct((high - low, rows, ell), jnp.bfloat16) for _, low, high in spots],
        compiler_params=pltpu.CompilerParams(vmem_limit_bytes=VMEM_LIMIT),
        cost_estimate=pl.CostEstimate(flops=1024, bytes_accessed=1024, transcendentals=0),
    )(up, ratios, kept, came)


def place_kernel(where, *refs, spots, first):
    count = len(spots)
    pieces, out, sems = refs[:count], refs[-2], refs[-1]
    rows = pieces[0].shape[1]
    copies = [
        pltpu.make_async_copy(pieces[n], out.at[low:high, where[PARTS + 2 + j], first:first + rows, :], sems.at[n])
        for n, (j, low, high) in enumerate(spots)
    ]
    for copy in copies:
        copy.start()
    for copy in copies:
        copy.wait()


def place(where, pieces, spots, first, shape, into=None):
    count = len(spots)
    extra = [] if into is None else [into]
    anywhere = pl.BlockSpec(memory_space=pl.ANY)
    return pl.pallas_call(
        functools.partial(place_kernel, spots=spots, first=first),
        grid_spec=pltpu.PrefetchScalarGridSpec(
            num_scalar_prefetch=1,
            grid=(),
            in_specs=[pl.BlockSpec(memory_space=pltpu.VMEM)] * count + [anywhere] * len(extra),
            out_specs=anywhere,
            scratch_shapes=[pltpu.SemaphoreType.DMA((count,))],
        ),
        out_shape=jax.ShapeDtypeStruct(shape, jnp.bfloat16),
        input_output_aliases={count + 1: 0} if extra else {},
        compiler_params=pltpu.CompilerParams(vmem_limit_bytes=VMEM_LIMIT),
        cost_estimate=pl.CostEstimate(flops=1024, bytes_accessed=1024, transcendentals=0),
    )(where, *pieces, *extra)


def anchor_kernel(*refs):
    del refs


def anchor(values, flops):
    anywhere = pl.BlockSpec(memory_space=pl.ANY)
    return pl.pallas_call(
        anchor_kernel,
        in_specs=[anywhere] * len(values),
        out_specs=[anywhere] * len(values),
        out_shape=[jax.ShapeDtypeStruct(value.shape, value.dtype) for value in values],
        input_output_aliases={n: n for n in range(len(values))},
        compiler_params=pltpu.CompilerParams(vmem_limit_bytes=1024 * 1024),
        cost_estimate=pl.CostEstimate(flops=flops, bytes_accessed=1024, transcendentals=0),
    )(*values)


def staged(visibility, beam_transfer, tile_mask, first_block, eigen_modes, signal_noise):
    freqs, parts, rows_all, base = visibility.shape
    _, freq_total, _, ell = beam_transfer.shape
    n_modes = eigen_modes.shape[2]
    ell_tiles = ell // TILE
    z, x, p = lax.axis_index("fm"), lax.axis_index("kl"), lax.axis_index("pol")
    other = [(0, 1), (1, 0)]

    def shift_z(value, j):
        return lax.ppermute(value, "fm", [(i, (i + j) % parts) for i in range(parts)])

    def swap_z(value, j):
        return lax.ppermute(value, "fm", [(i, i ^ j) for i in range(parts)])

    def along_x(value):
        return lax.ppermute(value, "kl", other)

    def cut(j, first, rows):
        return lax.dynamic_slice(visibility, (0, (z + j) % parts, first, 0), (freqs, 1, rows, base)).reshape(freqs, rows, base)

    index = jnp.arange(2 * parts + 2, dtype=jnp.int32)
    where = jnp.where(index < parts, (z - index) % parts, z ^ (index - parts - 2))
    where = jnp.where(index == parts, (x == p).astype(jnp.int32), where)
    where = jnp.where(index == parts + 1, x * ell_tiles, where).astype(jnp.int32)
    ratio = signal_noise[0] / (1.0 + signal_noise[0])
    ratios = jnp.broadcast_to(ratio[:, None, None], (n_modes, 1, ell))
    beam = beam_transfer.reshape(freq_total, base, ell)
    shape = (freqs, parts, rows_all, ell)

    fence = lax.optimization_barrier
    most, half = rows_all - ROWS, freqs // 2
    blocks = [[(0, f)] for f in range(freqs)]
    halves = [[(f // half, f % half)] for f in range(freqs)]
    a = {j: shift_z(cut(j, 0, ROWS), j) for j in (2, 1, 3)}
    mine = [cut(0, 0, rows_all)[n:n + half] for n in (0, half)]
    others = [along_x(part) for part in mine]
    b = {j: cut(j, ROWS, most) for j in (1, 2, 3)}
    held, down, up = hold(where, tile_mask[0], first_block, beam, eigen_modes[0])
    (a[2], a[1], a[3]), b, others, down, up = fence(((a[2], a[1], a[3]), b, others, down, up))
    b[1], b[3] = shift_z(b[1], 1), shift_z(b[3], 3)
    own = project(where, mine, others, held, 0, halves, 400_000_000)
    skies = [own] + [project(where, [a[j]], [along_x(a[j])], held, j, blocks, 400_000_000) for j in (1, 2, 3)]
    gone = reduce(down, [leave for _, leave in skies], (0, 0, 0, 0), n_modes)
    stay_a = [stay for stay, _ in skies]
    b[3], b[2], stay_a, gone = fence((b[3], b[2], stay_a, gone))
    x_3 = along_x(b[3])
    x_1, = anchor([along_x(b[1])], 2_500_000_000)
    b[2] = shift_z(b[2], 2)
    kept = reduce(down, stay_a, (0, 0, 0, 0), n_modes, jnp.float32)
    spots = [(j, 0, freqs) for j in (1, 2, 3, 0)]
    outs = restore(kept, lax.ppermute(gone, "pol", other), ratios, up, spots)
    near = project(where, [b[1]], [x_1], held, 1, blocks)
    last = project(where, [b[3]], [x_3], held, 3, blocks)
    last, b, outs, near = fence((last, b, outs, near))
    first = {j: swap_z(outs[j - 1], j) for j in (1, 2, 3)}
    first[0] = outs[3]
    x_2 = along_x(b[2])
    skies = [own, near, project(where, [b[2]], [x_2], held, 2, blocks), last]
    gone = reduce(down, [leave for _, leave in skies], (ROWS, 0, 0, 0), n_modes)
    stays = [stay for stay, _ in skies]
    here, stays, gone = fence((first[0], stays, gone))
    came = lax.ppermute(gone, "pol", other)
    kept = reduce(down, stays, (ROWS, 0, 0, 0), n_modes, jnp.float32)
    first[3], first[2], first[1], kept = fence((first[3], first[2], first[1], kept))
    first[3], first[2], first[1] = anchor([first[3], first[2], first[1]], 7_500_000_000)
    out_2, = restore(kept, came, ratios, up, [spots[1]])
    out_2, first[3], first[2], first[1] = fence((out_2, first[3], first[2], first[1]))
    first[0] = here
    out_3, out_1, out_0 = restore(kept, came, ratios, up, [spots[2], spots[0], spots[3]])
    back = [swap_z(out, j) for out, j in ((out_2, 2), (out_3, 3), (out_1, 1))]
    result = place(where, [first[j] for j in (1, 2, 3, 0)], spots, 0, shape)
    result = place(where, [out_0], [spots[3]], ROWS, shape, into=result)
    return place(where, back, [spots[1], spots[2], spots[0]], ROWS, shape, into=result)


def plain(visibility, beam_transfer, tile_mask, first_block, eigen_modes, signal_noise):
    owned_modes, freq_total, base_half, ell_local = beam_transfer.shape
    base_tiles, ell_tiles = base_half // TILE, ell_local // TILE
    block_ids = lax.axis_index("kl") * ell_tiles + jnp.arange(ell_tiles, dtype=jnp.int32)
    inside = (first_block[:, None] <= block_ids[None, :]).astype(jnp.int32)
    keep_tiles = tile_mask * inside[:, None, :]
    shaped = beam_transfer.reshape(owned_modes, freq_total, base_tiles, TILE, ell_tiles, TILE)
    masked_beam = shaped * keep_tiles.astype(jnp.bfloat16)[:, None, :, None, :, None]
    masked_beam = masked_beam.reshape(owned_modes, freq_total, base_half, ell_local)
    arrived = lax.all_to_all(visibility, "fm", split_axis=1, concat_axis=0, tiled=True)
    partial_value = jnp.einsum(
        "fmrb,mfbl->fmrl",
        lax.all_gather(arrived, "kl", axis=2, tiled=True),
        masked_beam,
        preferred_element_type=jnp.float32,
    )
    sky_sum = lax.psum_scatter(
        partial_value.astype(jnp.bfloat16), "pol", scatter_dimension=2, tiled=True
    ).astype(jnp.float32)
    modes_float = eigen_modes.astype(jnp.float32)
    coeffs = jnp.einsum("mfk,fmrl->mkrl", modes_float, sky_sum, precision=lax.Precision.HIGHEST)
    ratios = signal_noise / (1.0 + signal_noise)
    weighted = (coeffs * ratios[:, :, None, None]).astype(jnp.bfloat16)
    filtered = jnp.einsum(
        "mfk,mkrl->fmrl", eigen_modes, weighted, preferred_element_type=jnp.float32
    ).astype(jnp.bfloat16)
    return lax.all_to_all(filtered, "fm", split_axis=0, concat_axis=1, tiled=True)


def per_device(*args, sizes):
    visibility, beam_transfer = args[0], args[1]
    _, modes, rows, _ = visibility.shape
    fits = (
        sizes["kl"] == 2
        and sizes["pol"] == 2
        and modes == sizes["fm"] == PARTS
        and beam_transfer.shape[0] == 1
        and rows == 3 * ROWS
        and visibility.shape[0] % 2 == 0
    )
    if not fits:
        return plain(*args)
    return staged(*args)


def solution(mesh):
    placed = (
        P(("group", "fm"), None, "kl", "pol"),
        P(("group", "fm"), None, "pol", "kl"),
        P("fm", "pol", "kl"),
        P("fm"),
        P(("group", "fm"), None, None),
        P(("group", "fm"), None),
    )
    return jax.shard_map(
        functools.partial(per_device, sizes=dict(mesh.shape)),
        mesh=mesh,
        in_specs=placed,
        out_specs=P(("group", "fm"), None, "pol", "kl"),
        check_vma=False,
    )
```

```python
import functools
import jax
import jax.numpy as jnp
from jax import lax
from jax.experimental import pallas as pl
from jax.experimental.pallas import tpu as pltpu
from jax.sharding import PartitionSpec as P

TILE = 128
PARTS = 4
ROWS = 16
VMEM_LIMIT = 24 * 1024 * 1024


def hold_kernel(where, tiles, starts, beam, modes_ref, held, down_ref, up_ref, mask, sems):
    freq, base, ell = held.shape
    n_modes = modes_ref.shape[1]
    ell_tiles, base_tiles, freqs = ell // TILE, base // TILE, freq // PARTS
    copies = [pltpu.make_async_copy(beam.at[f], held.at[f], sems.at[f]) for f in range(freq)]
    for copy in copies:
        copy.start()
    for b in range(base_tiles):
        for l in range(ell_tiles):
            kept = jnp.where(starts[0] <= where[PARTS + 1] + l, tiles[b, l], 0).astype(jnp.float32)
            mask[b * TILE:(b + 1) * TILE, l * TILE:(l + 1) * TILE] = jnp.full(
                (TILE, TILE), kept, jnp.float32
            ).astype(jnp.bfloat16)
    modes = modes_ref[...]

    def pick(shape, axis, orders=0):
        big = lax.broadcasted_iota(jnp.int32, shape, axis) // ROWS
        small = lax.broadcasted_iota(jnp.int32, shape, 1 - axis)
        if freq in shape:
            piece, within = big // freqs, big % freqs
            big = within
            for j in range(PARTS):
                big = jnp.where(piece == j, where[orders + j] * freqs + within, big)
        return jnp.where(big == small, 1.0, 0.0).astype(jnp.bfloat16)

    def lane(shape):
        rows = lax.broadcasted_iota(jnp.int32, shape, 0) % ROWS
        columns = lax.broadcasted_iota(jnp.int32, shape, 1) % ROWS
        return rows == columns

    def dot(a, b, dims):
        return lax.dot_general(a, b, (dims, ((), ())), preferred_element_type=jnp.float32)

    tall = dot(pick((n_modes * ROWS, n_modes), 0), modes, ((1,), (1,))).astype(jnp.bfloat16)
    value = dot(tall, pick((freq, freq * ROWS), 1), ((1,), (0,)))
    down_ref[...] = jnp.where(lane(value.shape), value, 0.0).astype(jnp.bfloat16)
    tall = dot(pick((freq * ROWS, freq), 0, PARTS + 2), modes, ((1,), (0,))).astype(jnp.bfloat16)
    value = dot(tall, pick((n_modes, n_modes * ROWS), 1), ((1,), (0,)))
    up_ref[...] = jnp.where(lane(value.shape), value, 0.0).astype(jnp.bfloat16)
    for f, copy in enumerate(copies):
        copy.wait()
        held[f] = held[f] * mask[...]


def hold(where, tiles, starts, beam, modes):
    freq, base, ell = beam.shape
    size, wide = freq * ROWS, modes.shape[1] * ROWS
    vmem = pl.BlockSpec(memory_space=pltpu.VMEM)
    return pl.pallas_call(
        hold_kernel,
        grid_spec=pltpu.PrefetchScalarGridSpec(
            num_scalar_prefetch=3,
            grid=(),
            in_specs=[pl.BlockSpec(memory_space=pl.ANY), vmem],
            out_specs=[vmem] * 3,
            scratch_shapes=[pltpu.VMEM((base, ell), jnp.bfloat16), pltpu.SemaphoreType.DMA((freq,))],
        ),
        out_shape=[
            pltpu.VMEM(beam.shape, beam.dtype),
            jax.ShapeDtypeStruct((wide, size), jnp.bfloat16),
            jax.ShapeDtypeStruct((size, wide), jnp.bfloat16),
        ],
        compiler_params=pltpu.CompilerParams(vmem_limit_bytes=VMEM_LIMIT),
        cost_estimate=pl.CostEstimate(flops=1024, bytes_accessed=1024, transcendentals=0),
    )(where, tiles, starts, beam, modes)


def project_kernel(where, *refs, piece, blocks):
    count = (len(refs) - 3) // 2
    mine, others = refs[:count], refs[count:2 * count]
    held, stay_ref, leave_ref = refs[2 * count:]
    freqs, rows, _ = stay_ref.shape
    first = where[piece] * freqs
    own = where[PARTS] == 1
    for f in range(freqs):
        a = jnp.concatenate([mine[n][k] for n, k in blocks[f]], axis=0)
        b = jnp.concatenate([others[n][k] for n, k in blocks[f]], axis=0)
        lines = jnp.concatenate([jnp.where(own, a, b), jnp.where(own, b, a)], axis=0)
        value = jnp.dot(lines, held[first + f], preferred_element_type=jnp.float32).astype(jnp.bfloat16)
        stay_ref[f] = value[:rows]
        leave_ref[f] = value[rows:]


def project(where, mine, others, held, piece, blocks, flops=1024):
    ell = held.shape[2]
    rows = sum(mine[n].shape[1] for n, _ in blocks[0])
    vmem = pl.BlockSpec(memory_space=pltpu.VMEM)
    return pl.pallas_call(
        functools.partial(project_kernel, piece=piece, blocks=blocks),
        grid_spec=pltpu.PrefetchScalarGridSpec(
            num_scalar_prefetch=1, grid=(), in_specs=[vmem] * (2 * len(mine) + 1), out_specs=[vmem] * 2
        ),
        out_shape=[jax.ShapeDtypeStruct((len(blocks), rows, ell), jnp.bfloat16)] * 2,
        compiler_params=pltpu.CompilerParams(vmem_limit_bytes=VMEM_LIMIT),
        cost_estimate=pl.CostEstimate(flops=flops, bytes_accessed=1024, transcendentals=0),
    )(where, *mine, *others, pltpu.with_memory_space_constraint(held, pltpu.VMEM))


def contract(modes, skies):
    block = jnp.concatenate([sky[...].reshape(sky.shape[0] * ROWS, sky.shape[2]) for sky in skies], axis=0)
    return jnp.dot(modes, block, preferred_element_type=jnp.float32)


def reduce_kernel(modes_ref, *refs):
    out = refs[-1]
    out[...] = contract(modes_ref[...], refs[:-1]).astype(out.dtype).reshape(out.shape)


def by_rows(count, ell, first=0):
    return pl.BlockSpec((count, ROWS, ell), lambda g: (0, g + first // ROWS, 0))


def fixed(shape):
    return pl.BlockSpec(shape, lambda g: (0,) * len(shape))


def sky_specs(skies, first):
    return [by_rows(sky.shape[0], sky.shape[2], low) for sky, low in zip(skies, first)]


def reduce(modes, skies, first, n_modes, dtype=jnp.bfloat16):
    _, rows, ell = skies[-1].shape
    return pl.pallas_call(
        reduce_kernel,
        grid=(rows // ROWS,),
        in_specs=[fixed(modes.shape)] + sky_specs(skies, first),
        out_specs=by_rows(n_modes, ell),
        out_shape=jax.ShapeDtypeStruct((n_modes, rows, ell), dtype),
        compiler_params=pltpu.CompilerParams(vmem_limit_bytes=VMEM_LIMIT),
        cost_estimate=pl.CostEstimate(flops=1024, bytes_accessed=1024, transcendentals=0),
    )(modes, *skies)


def restore_kernel(up_ref, ratio_ref, kept_ref, came_ref, *outs, spots):
    n_modes, _, ell = came_ref.shape
    freqs = up_ref.shape[0] // ROWS // PARTS
    total = kept_ref[...] + came_ref[...].astype(jnp.float32)
    weighted = (total * ratio_ref[...]).astype(jnp.bfloat16).reshape(n_modes * ROWS, ell)
    for (j, low, high), out in zip(spots, outs):
        modes = up_ref[(j * freqs + low) * ROWS:(j * freqs + high) * ROWS, :]
        value = jnp.dot(modes, weighted, preferred_element_type=jnp.float32)
        out[...] = value.astype(jnp.bfloat16).reshape(out.shape)


def restore(kept, came, ratios, up, spots):
    n_modes, rows, ell = came.shape
    return pl.pallas_call(
        functools.partial(restore_kernel, spots=spots),
        grid=(rows // ROWS,),
        in_specs=[fixed(up.shape), fixed(ratios.shape)] + [by_rows(n_modes, ell)] * 2,
        out_specs=[by_rows(high - low, ell) for _, low, high in spots],
        out_shape=[jax.ShapeDtypeStruct((high - low, rows, ell), jnp.bfloat16) for _, low, high in spots],
        compiler_params=pltpu.CompilerParams(vmem_limit_bytes=VMEM_LIMIT),
        cost_estimate=pl.CostEstimate(flops=1024, bytes_accessed=1024, transcendentals=0),
    )(up, ratios, kept, came)


def place_kernel(where, *refs, spots, first):
    count = len(spots)
    pieces, out, sems = refs[:count], refs[-2], refs[-1]
    rows = pieces[0].shape[1]
    copies = [
        pltpu.make_async_copy(pieces[n], out.at[low:high, where[PARTS + 2 + j], first:first + rows, :], sems.at[n])
        for n, (j, low, high) in enumerate(spots)
    ]
    for copy in copies:
        copy.start()
    for copy in copies:
        copy.wait()


def place(where, pieces, spots, first, shape, into=None):
    count = len(spots)
    extra = [] if into is None else [into]
    anywhere = pl.BlockSpec(memory_space=pl.ANY)
    return pl.pallas_call(
        functools.partial(place_kernel, spots=spots, first=first),
        grid_spec=pltpu.PrefetchScalarGridSpec(
            num_scalar_prefetch=1,
            grid=(),
            in_specs=[pl.BlockSpec(memory_space=pltpu.VMEM)] * count + [anywhere] * len(extra),
            out_specs=anywhere,
            scratch_shapes=[pltpu.SemaphoreType.DMA((count,))],
        ),
        out_shape=jax.ShapeDtypeStruct(shape, jnp.bfloat16),
        input_output_aliases={count + 1: 0} if extra else {},
        compiler_params=pltpu.CompilerParams(vmem_limit_bytes=VMEM_LIMIT),
        cost_estimate=pl.CostEstimate(flops=1024, bytes_accessed=1024, transcendentals=0),
    )(where, *pieces, *extra)


def anchor_kernel(*refs):
    del refs


def anchor(values, flops):
    anywhere = pl.BlockSpec(memory_space=pl.ANY)
    return pl.pallas_call(
        anchor_kernel,
        in_specs=[anywhere] * len(values),
        out_specs=[anywhere] * len(values),
        out_shape=[jax.ShapeDtypeStruct(value.shape, value.dtype) for value in values],
        input_output_aliases={n: n for n in range(len(values))},
        compiler_params=pltpu.CompilerParams(vmem_limit_bytes=1024 * 1024),
        cost_estimate=pl.CostEstimate(flops=flops, bytes_accessed=1024, transcendentals=0),
    )(*values)


def staged(visibility, beam_transfer, tile_mask, first_block, eigen_modes, signal_noise):
    freqs, parts, rows_all, base = visibility.shape
    _, freq_total, _, ell = beam_transfer.shape
    n_modes = eigen_modes.shape[2]
    ell_tiles = ell // TILE
    z, x, p = lax.axis_index("fm"), lax.axis_index("kl"), lax.axis_index("pol")
    other = [(0, 1), (1, 0)]

    def shift_z(value, j):
        return lax.ppermute(value, "fm", [(i, (i + j) % parts) for i in range(parts)])

    def swap_z(value, j):
        return lax.ppermute(value, "fm", [(i, i ^ j) for i in range(parts)])

    def along_x(value):
        return lax.ppermute(value, "kl", other)

    def cut(j, first, rows):
        return lax.dynamic_slice(visibility, (0, (z + j) % parts, first, 0), (freqs, 1, rows, base)).reshape(freqs, rows, base)

    index = jnp.arange(2 * parts + 2, dtype=jnp.int32)
    where = jnp.where(index < parts, (z - index) % parts, z ^ (index - parts - 2))
    where = jnp.where(index == parts, (x == p).astype(jnp.int32), where)
    where = jnp.where(index == parts + 1, x * ell_tiles, where).astype(jnp.int32)
    ratio = signal_noise[0] / (1.0 + signal_noise[0])
    ratios = jnp.broadcast_to(ratio[:, None, None], (n_modes, 1, ell))
    beam = beam_transfer.reshape(freq_total, base, ell)
    shape = (freqs, parts, rows_all, ell)

    fence = lax.optimization_barrier
    most, half = rows_all - ROWS, freqs // 2
    blocks = [[(0, f)] for f in range(freqs)]
    halves = [[(f // half, f % half)] for f in range(freqs)]
    a = {j: shift_z(cut(j, 0, ROWS), j) for j in (2, 1, 3)}
    mine = [cut(0, 0, rows_all)[n:n + half] for n in (0, half)]
    others = [along_x(part) for part in mine]
    b = {j: cut(j, ROWS, most) for j in (1, 2, 3)}
    held, down, up = hold(where, tile_mask[0], first_block, beam, eigen_modes[0])
    (a[2], a[1], a[3]), b, others, down, up = fence(((a[2], a[1], a[3]), b, others, down, up))
    b[1], b[3] = shift_z(b[1], 1), shift_z(b[3], 3)
    own = project(where, mine, others, held, 0, halves, 400_000_000)
    skies = [own] + [project(where, [a[j]], [along_x(a[j])], held, j, blocks, 400_000_000) for j in (1, 2, 3)]
    gone = reduce(down, [leave for _, leave in skies], (0, 0, 0, 0), n_modes)
    stay_a = [stay for stay, _ in skies]
    b[3], b[2], stay_a, gone = fence((b[3], b[2], stay_a, gone))
    x_3 = along_x(b[3])
    x_1, = anchor([along_x(b[1])], 2_500_000_000)
    b[2], = anchor([shift_z(b[2], 2)], 2_000_000_000)
    kept = reduce(down, stay_a, (0, 0, 0, 0), n_modes, jnp.float32)
    spots = [(j, 0, freqs) for j in (1, 2, 3, 0)]
    outs = restore(kept, lax.ppermute(gone, "pol", other), ratios, up, spots)
    near = project(where, [b[1]], [x_1], held, 1, blocks)
    last = project(where, [b[3]], [x_3], held, 3, blocks)
    last, b, outs, near = fence((last, b, outs, near))
    first = {j: swap_z(outs[j - 1], j) for j in (1, 2, 3)}
    first[0] = outs[3]
    x_2 = along_x(b[2])
    skies = [own, near, project(where, [b[2]], [x_2], held, 2, blocks), last]
    gone = reduce(down, [leave for _, leave in skies], (ROWS, 0, 0, 0), n_modes)
    stays = [stay for stay, _ in skies]
    here, stays, gone = fence((first[0], stays, gone))
    came = lax.ppermute(gone, "pol", other)
    kept = reduce(down, stays, (ROWS, 0, 0, 0), n_modes, jnp.float32)
    first[3], first[2], first[1], kept = fence((first[3], first[2], first[1], kept))
    first[3], first[2], first[1] = anchor([first[3], first[2], first[1]], 7_500_000_000)
    out_2, = restore(kept, came, ratios, up, [spots[1]])
    out_2, first[3], first[2], first[1] = fence((out_2, first[3], first[2], first[1]))
    first[0] = here
    out_3, out_1, out_0 = restore(kept, came, ratios, up, [spots[2], spots[0], spots[3]])
    back = [swap_z(out, j) for out, j in ((out_2, 2), (out_3, 3), (out_1, 1))]
    result = place(where, [first[j] for j in (1, 2, 3, 0)], spots, 0, shape)
    result = place(where, [out_0], [spots[3]], ROWS, shape, into=result)
    return place(where, back, [spots[1], spots[2], spots[0]], ROWS, shape, into=result)


def plain(visibility, beam_transfer, tile_mask, first_block, eigen_modes, signal_noise):
    owned_modes, freq_total, base_half, ell_local = beam_transfer.shape
    base_tiles, ell_tiles = base_half // TILE, ell_local // TILE
    block_ids = lax.axis_index("kl") * ell_tiles + jnp.arange(ell_tiles, dtype=jnp.int32)
    inside = (first_block[:, None] <= block_ids[None, :]).astype(jnp.int32)
    keep_tiles = tile_mask * inside[:, None, :]
    shaped = beam_transfer.reshape(owned_modes, freq_total, base_tiles, TILE, ell_tiles, TILE)
    masked_beam = shaped * keep_tiles.astype(jnp.bfloat16)[:, None, :, None, :, None]
    masked_beam = masked_beam.reshape(owned_modes, freq_total, base_half, ell_local)
    arrived = lax.all_to_all(visibility, "fm", split_axis=1, concat_axis=0, tiled=True)
    partial_value = jnp.einsum(
        "fmrb,mfbl->fmrl",
        lax.all_gather(arrived, "kl", axis=2, tiled=True),
        masked_beam,
        preferred_element_type=jnp.float32,
    )
    sky_sum = lax.psum_scatter(
        partial_value.astype(jnp.bfloat16), "pol", scatter_dimension=2, tiled=True
    ).astype(jnp.float32)
    modes_float = eigen_modes.astype(jnp.float32)
    coeffs = jnp.einsum("mfk,fmrl->mkrl", modes_float, sky_sum, precision=lax.Precision.HIGHEST)
    ratios = signal_noise / (1.0 + signal_noise)
    weighted = (coeffs * ratios[:, :, None, None]).astype(jnp.bfloat16)
    filtered = jnp.einsum(
        "mfk,mkrl->fmrl", eigen_modes, weighted, preferred_element_type=jnp.float32
    ).astype(jnp.bfloat16)
    return lax.all_to_all(filtered, "fm", split_axis=0, concat_axis=1, tiled=True)


def per_device(*args, sizes):
    visibility, beam_transfer = args[0], args[1]
    _, modes, rows, _ = visibility.shape
    fits = (
        sizes["kl"] == 2
        and sizes["pol"] == 2
        and modes == sizes["fm"] == PARTS
        and beam_transfer.shape[0] == 1
        and rows == 3 * ROWS
        and visibility.shape[0] % 2 == 0
    )
    if not fits:
        return plain(*args)
    return staged(*args)


def solution(mesh):
    placed = (
        P(("group", "fm"), None, "kl", "pol"),
        P(("group", "fm"), None, "pol", "kl"),
        P("fm", "pol", "kl"),
        P("fm"),
        P(("group", "fm"), None, None),
        P(("group", "fm"), None),
    )
    return jax.shard_map(
        functools.partial(per_device, sizes=dict(mesh.shape)),
        mesh=mesh,
        in_specs=placed,
        out_specs=P(("group", "fm"), None, "pol", "kl"),
        check_vma=False,
    )
```
